256 devices in a mesh: lat: 8 (over x, y_lo), lon: 32 (over z, y_hi, core).
Axes of the slice: x: 4, y: 4 (y_hi: 2, y_lo: 2; y = y_hi * 2 + y_lo), z: 8, core: 2. Of those that a mesh axis runs over, the one named last changes fastest.
Arguments:
- field_in: bfloat16 [4, 48, 768, 192], P(None, 'lat', 'lon'), may hold values from -6 to 6
- cotangent: bfloat16 [4, 48, 768, 192], P(None, 'lat', 'lon'), may hold values from -6 to 6
- ln1_gain: float32 [192], replicated, may hold values from 0.1 to 1.9
- w_qkv: bfloat16 [192, 576], replicated, may hold values from -0.4375 to 0.4375
- w_proj: bfloat16 [192, 192], replicated, may hold values from -0.4375 to 0.4375
- ln2_gain: float32 [192], replicated, may hold values from 0.1 to 1.9
- w_up: bfloat16 [192, 768], replicated, may hold values from -0.4375 to 0.4375
- w_down: bfloat16 [768, 192], replicated, may hold values from -0.21875 to 0.21875
- bias_table: float32 [2, 8, 6, 3312], P(None, 'lat'), may hold values from -330 to 330
- region_ids: int32 [4, 48, 768], P(None, 'lat', 'lon'), may hold values from 0 to 2
- keep_flags: int32 [2, 8, 64], P(None, 'lat', 'lon'), may hold values 0 or 1
Outputs:
- block_out: bfloat16 [4, 48, 768, 192], P(None, 'lat', 'lon')
- grad_field: bfloat16 [4, 48, 768, 192], P(None, 'lat', 'lon')
- grad_bias: float32 [2, 8, 6, 3312], P(None, 'lat')
The draws below stay inside these ranges and needn't reach their ends.
All inputs are finite; a program needn't handle non-finite values. No bound on the sum of `keep_flags` on one device may be relied on, other than what follows from the above.
Results may differ from the reference program's by a relative error of at most 0.013.
Values may be sent and summed in bfloat16 or wider, within the bound.
No kernel may reach another device: no remote copies, remote signals or barrier semaphores. Data moves between devices by JAX's collectives and lax.ppermute only.
A program may use at most 128 MiB of HBM per device.

```python
import math
import jax
import jax.numpy as jnp
from jax import lax

C = 192
HEADS = 6
FF = 768
Z = 4
WZ = 2
WLAT = 6
WLON = 12
NLAT = 48
NLON = 768
NZW = 2
NLATW = 8
NLONW = 64
KTAB = 3312


def draw_bias_table(key, part):
    key = jax.random.fold_in(key, 17)
    key_base = jax.random.fold_in(key, 0)
    spread = 2 * WLON - 1
    dims_all = (NZW, NLATW, HEADS, WZ, WZ, WLAT, WLAT, spread)
    bias_vals = jax.random.normal(key_base, dims_all, jnp.float32)
    return bias_vals.reshape(NZW, NLATW, HEADS, KTAB)


def plant(entries, own_key, least, top_value):
    spot = [jax.random.randint(jax.random.fold_in(own_key, axis), (), 0, length) for axis, length in enumerate(entries.shape)]
    main_axis = entries.shape.index(max(entries.shape))
    neighbour = spot[:main_axis] + [(spot[main_axis] + 1) % entries.shape[main_axis]] + spot[main_axis + 1:]
    return entries.at[tuple(spot)].set(least).at[tuple(neighbour)].set(top_value)


def level_of(rng, dims, cuts, smallest, top_value):
    factor_of, own = 1.0, jax.random.fold_in(rng, 6)
    for position, blocks in cuts:
        heights = jnp.exp(jax.random.uniform(jax.random.fold_in(own, position), (blocks,), jnp.float32, smallest / len(cuts), top_value / len(cuts)))
        factor_of = factor_of * jnp.repeat(heights, dims[position] // blocks).reshape([-1 if axis == position else 1 for axis in range(len(dims))])
    return factor_of


def normal_values(own_key, extent, scale, most, cuts=(), kind=jnp.bfloat16):
    array = jax.random.normal(own_key, extent, jnp.float32) * scale
    if len(cuts) > 0:
        array = level_of(own_key, extent, cuts, -0.22, 0.18) * array
    return jnp.clip(array, min=-most, max=most).astype(kind)


def setup_inputs(seed: int = 0) -> dict:
    arg_keys = jax.random.split(jax.random.key(seed), 12)
    return {
        "field_in": normal_values(arg_keys[0], (Z, NLAT, NLON, C), 1.0, 6.0, ((1, 8), (2, 32))),
        "cotangent": normal_values(arg_keys[1], (Z, NLAT, NLON, C), 1.0, 6.0, ((1, 8), (2, 32))),
        "ln1_gain": jnp.clip(1.0 + 0.18 * jax.random.normal(arg_keys[2], (C,), jnp.float32), 0.1, 1.9),
        "w_qkv": normal_values(arg_keys[3], (C, 3 * C), C ** -0.5, 0.4375),
        "w_proj": normal_values(arg_keys[4], (C, C), C ** -0.5, 0.4375),
        "ln2_gain": jnp.clip(1.0 + 0.18 * jax.random.normal(arg_keys[5], (C,), jnp.float32), 0.1, 1.9),
        "w_up": normal_values(arg_keys[6], (C, FF), C ** -0.5, 0.4375),
        "w_down": normal_values(arg_keys[7], (FF, C), FF ** -0.5, 0.21875),
        "bias_table": draw_bias_table(jax.random.fold_in(arg_keys[11], 71), 0),
        "region_ids": plant(jax.random.randint(arg_keys[9], (Z, NLAT, NLON), 0, 3), jax.random.fold_in(arg_keys[9], 1), 0, 2).astype(jnp.int32),
        "keep_flags": plant((jax.random.randint(arg_keys[10], (NZW, NLATW, NLONW), 0, 5) < 4).astype(jnp.int32), jax.random.fold_in(arg_keys[10], 1), 0, 1),
    }


epsilon = 1e-05
keep_share = 0.8
gelu_coef = 0.044715
highest = lax.Precision.HIGHEST

def norm_parts(values, ln_gain):
    row_mean = lax.optimization_barrier(jnp.mean(values, axis=-1, keepdims=True))
    centred = values - row_mean
    variance = lax.optimization_barrier(jnp.mean(centred * centred, axis=-1, keepdims=True))
    inverse = lax.rsqrt(variance + epsilon)
    normed = centred * inverse
    return (normed * ln_gain, normed, inverse)

def norm_back(grad_in, ln_gain, normed, inverse):
    scaled = grad_in * ln_gain
    first_mean = lax.optimization_barrier(jnp.mean(scaled, axis=-1, keepdims=True))
    second_mean = lax.optimization_barrier(jnp.mean(scaled * normed, axis=-1, keepdims=True))
    return (scaled - first_mean - normed * second_mean) * inverse

def gelu_parts(values):
    factor = math.sqrt(2.0 / math.pi)
    tangent = jnp.tanh(factor * (values + gelu_coef * values * values * values))
    result = 0.5 * values * (1.0 + tangent)
    derivative = 0.5 * (1.0 + tangent) + 0.5 * values * (1.0 - tangent * tangent) * factor * (1.0 + 3.0 * gelu_coef * values * values)
    return (result, derivative)

def matmul(values, weight):
    flat_rows = values.reshape(-1, values.shape[-1])
    result = jnp.dot(flat_rows, weight, preferred_element_type=jnp.float32)
    return result.reshape(values.shape[:-1] + (weight.shape[1],))

def product(form, left, right):
    return jnp.einsum(form, left.astype(jnp.float32), right.astype(jnp.float32), precision=highest)

def to_windows(values):
    levels, lat_rows, lon_cols, channels = values.shape
    shaped = values.reshape(levels // WZ, WZ, lat_rows // WLAT, WLAT, lon_cols // WLON, WLON, channels)
    shaped = shaped.transpose(0, 2, 4, 1, 3, 5, 6)
    return shaped.reshape(levels // WZ, lat_rows // WLAT, lon_cols // WLON, WZ * WLAT * WLON, channels)

def from_windows(values):
    level_win, lat_win, lon_win, positions, channels = values.shape
    shaped = values.reshape(level_win, lat_win, lon_win, WZ, WLAT, WLON, channels)
    shaped = shaped.transpose(0, 3, 1, 4, 2, 5, 6)
    return shaped.reshape(level_win * WZ, lat_win * WLAT, lon_win * WLON, channels)

def lon_table():
    offsets = jnp.arange(WLON, dtype=jnp.int32)
    spread = 2 * WLON - 1
    target = offsets[:, None, None] - offsets[None, :, None] + WLON - 1
    return (jnp.arange(spread, dtype=jnp.int32)[None, None, :] == target).astype(jnp.float32)

def expand_bias(table):
    leading = table.shape[:-1]
    shaped = table.reshape(leading + (WZ, WZ, WLAT, WLAT, 2 * WLON - 1))
    expanded = jnp.einsum('...abcdr,oqr->...acobdq', shaped, lon_table(), precision=highest)
    return expanded.reshape(leading + (WZ * WLAT * WLON, WZ * WLAT * WLON))

def fold_bias(grads):
    leading = grads.shape[:-2]
    shaped = grads.reshape(leading + (WZ, WLAT, WLON, WZ, WLAT, WLON))
    folded = jnp.einsum('...acobdq,oqr->...abcdr', shaped, lon_table(), precision=highest)
    return folded.reshape(leading + (WZ * WZ * WLAT * WLAT * (2 * WLON - 1),))

def window_labels(region_ids, lat_start, lat_total):
    levels, lat_rows, lon_cols = region_ids.shape
    level_pos = jnp.arange(levels, dtype=jnp.int32)[:, None, None]
    lat_pos = lat_start + jnp.arange(lat_rows, dtype=jnp.int32)[None, :, None]
    wrapped = 2 * (level_pos >= levels - WZ // 2).astype(jnp.int32) + (lat_pos >= lat_total - WLAT // 2).astype(jnp.int32)
    labels = 4 * region_ids + wrapped
    return to_windows(labels[..., None])[..., 0]

def pair_mask(labels):
    return labels[..., :, None] == labels[..., None, :]

def head_slice(packed, part_idx, head_idx, head_dim, channels):
    offset = part_idx * channels + head_idx * head_dim
    return packed[..., offset:offset + head_dim]

def head_probs(query_h, key_h, bias_full, allowed, head_idx):
    scores = product('abcpd,abcqd->abcpq', query_h, key_h)
    scores = scores / math.sqrt(query_h.shape[-1]) + bias_full[:, :, head_idx][:, :, None]
    scores = jnp.where(allowed, scores, -jnp.inf)
    top_score = lax.optimization_barrier(jnp.max(scores, axis=-1, keepdims=True))
    weights = jnp.exp(scores - top_score)
    return weights / lax.optimization_barrier(jnp.sum(weights, axis=-1, keepdims=True))

def attention_forward(windows_in, w_qkv, w_proj, bias_full, allowed, factor):
    channels = windows_in.shape[-1]
    heads = bias_full.shape[2]
    head_dim = channels // heads
    qkv = matmul(windows_in, w_qkv).astype(jnp.bfloat16)
    pieces = []
    for head_idx in range(heads):
        query_h = head_slice(qkv, 0, head_idx, head_dim, channels)
        key_h = head_slice(qkv, 1, head_idx, head_dim, channels)
        value_h = head_slice(qkv, 2, head_idx, head_dim, channels)
        probs = head_probs(query_h, key_h, bias_full, allowed, head_idx)
        pieces.append(product('abcpq,abcqd->abcpd', probs.astype(jnp.bfloat16), value_h).astype(jnp.bfloat16))
    attended = jnp.concatenate(pieces, axis=-1)
    projected = matmul(attended, w_proj)
    return (qkv, (projected * factor).astype(jnp.bfloat16))

def attention_backward(grad_win, qkv, w_qkv, w_proj, bias_full, allowed, factor):
    channels = grad_win.shape[-1]
    heads = bias_full.shape[2]
    head_dim = channels // heads
    root = math.sqrt(head_dim)
    grad_branch = (grad_win.astype(jnp.float32) * factor).astype(jnp.bfloat16)
    grad_att = matmul(grad_branch, w_proj.T).astype(jnp.bfloat16)
    grad_query, grad_key, grad_value, bias_parts = ([], [], [], [])
    for head_idx in range(heads):
        query_h = head_slice(qkv, 0, head_idx, head_dim, channels)
        key_h = head_slice(qkv, 1, head_idx, head_dim, channels)
        value_h = head_slice(qkv, 2, head_idx, head_dim, channels)
        grad_head = head_slice(grad_att, 0, head_idx, head_dim, channels)
        probs = head_probs(query_h, key_h, bias_full, allowed, head_idx)
        probs_low = probs.astype(jnp.bfloat16)
        grad_probs = product('abcpd,abcqd->abcpq', grad_head, value_h)
        grad_scores = probs * (grad_probs - lax.optimization_barrier(jnp.sum(probs * grad_probs, axis=-1, keepdims=True)))
        grad_low = grad_scores.astype(jnp.bfloat16)
        grad_query.append((product('abcpq,abcqd->abcpd', grad_low, key_h) / root).astype(jnp.bfloat16))
        grad_key.append((product('abcpq,abcpd->abcqd', grad_low, query_h) / root).astype(jnp.bfloat16))
        grad_value.append(product('abcpq,abcpd->abcqd', probs_low, grad_head).astype(jnp.bfloat16))
        bias_parts.append(fold_bias(lax.optimization_barrier(jnp.sum(grad_scores, axis=2))))
    grad_qkv = jnp.concatenate(grad_query + grad_key + grad_value, axis=-1)
    grad_in = matmul(grad_qkv, w_qkv.T).astype(jnp.bfloat16)
    return (grad_in, jnp.stack(bias_parts, axis=2))

def mlp_both(y_sum, grad_out, ln2_gain, w_up, w_down):
    normed2, plain2, inverse2 = norm_parts(y_sum, ln2_gain)
    up_proj = matmul(normed2.astype(jnp.bfloat16), w_up)
    act_val, act_slope = gelu_parts(up_proj)
    result = (y_sum + matmul(act_val.astype(jnp.bfloat16), w_down)).astype(jnp.bfloat16)
    grad_act = matmul(grad_out, w_down.T)
    grad_up = (grad_act * act_slope).astype(jnp.bfloat16)
    grad_hidden = matmul(grad_up, w_up.T)
    grad_sum = grad_out.astype(jnp.float32) + norm_back(grad_hidden, ln2_gain, plain2, inverse2)
    return (result, grad_sum)

def swap_lead(values):
    return jnp.swapaxes(values, 0, 1)

def reference(field_in, cotangent, ln1_gain, w_qkv, w_proj, ln2_gain, w_up, w_down, bias_table, region_ids, keep_flags):
    halves = (WZ // 2, WLAT // 2, WLON // 2)
    shift_in = (-(WZ // 2), -(WLAT // 2), -(WLON // 2))
    lat_total = field_in.shape[1]
    normed1, plain1, inverse1 = norm_parts(field_in.astype(jnp.float32), ln1_gain)
    shifted = jnp.roll(normed1.astype(jnp.bfloat16), shift_in, axis=(0, 1, 2))
    labels = window_labels(region_ids, 0, lat_total)
    factor = keep_flags.astype(jnp.float32) / keep_share
    stacked = (swap_lead(to_windows(shifted)), swap_lead(bias_table), swap_lead(labels), swap_lead(factor))

    def forward_block(operands):
        win_b, table_b, labels_b, factor_b = operands
        bias_full = expand_bias(table_b[:, None])
        allowed = pair_mask(labels_b[:, None])
        qkv, branch = attention_forward(win_b[:, None], w_qkv, w_proj, bias_full, allowed, factor_b[:, None, :, None, None])
        return branch[:, 0]
    branch = swap_lead(lax.map(forward_block, stacked))
    y_sum = field_in.astype(jnp.float32) + jnp.roll(from_windows(branch), halves, axis=(0, 1, 2)).astype(jnp.float32)

    def mlp_level(operands):
        y_level, grad_level = operands
        return mlp_both(y_level, grad_level, ln2_gain, w_up, w_down)
    result, grad_sum = lax.map(mlp_level, (y_sum, cotangent))
    grad_shift = to_windows(jnp.roll(grad_sum.astype(jnp.bfloat16), shift_in, axis=(0, 1, 2)))

    def backward_block(operands):
        win_b, table_b, labels_b, factor_b, grad_b = operands
        bias_full = expand_bias(table_b[:, None])
        allowed = pair_mask(labels_b[:, None])
        qkv = matmul(win_b[:, None], w_qkv).astype(jnp.bfloat16)
        grad_in, grad_table = attention_backward(grad_b[:, None], qkv, w_qkv, w_proj, bias_full, allowed, factor_b[:, None, :, None, None])
        return (grad_in[:, 0], grad_table[:, 0])
    grad_win, grad_table = lax.map(backward_block, stacked + (swap_lead(grad_shift),))
    grad_h1 = jnp.roll(from_windows(swap_lead(grad_win)), halves, axis=(0, 1, 2))
    grad_field = (grad_sum + norm_back(grad_h1.astype(jnp.float32), ln1_gain, plain1, inverse1)).astype(jnp.bfloat16)
    return (result, grad_field, swap_lead(grad_table))
```

```python
import math

import jax
import jax.numpy as jnp
import numpy as np
from jax import lax
from jax.experimental import pallas as pl
from jax.experimental.pallas import tpu as pltpu
from jax.sharding import PartitionSpec as P

C = 192
HEADS = 6
HD = 32
FF = 768
WZ = 2
WLAT = 6
WLON = 12
SPREAD = 2 * WLON - 1
POS = WZ * WLAT * WLON
PAIR = WZ * WLAT
TAB = PAIR * SPREAD
ROWS = HEADS * POS

epsilon = 1e-05
keep_share = 0.8
gelu_coef = 0.044715
bf16 = jnp.bfloat16
f32 = jnp.float32


def shifted(block, lat_step, lon_step):
    lats, lons = lax.axis_size("lat"), lax.axis_size("lon")
    route = []
    for a in range(lats):
        for b in range(lons):
            target = ((a + lat_step) % lats) * lons + (b + lon_step) % lons
            route.append((a * lons + b, target))
    return lax.ppermute(block, ("lat", "lon"), route)


def swapped(block, distance):
    lons = lax.axis_size("lon")
    return lax.ppermute(block, "lon", [(i, i ^ distance) for i in range(lons)])


def mm(a, b):
    return lax.dot_general(a, b, (((1,), (0,)), ((), ())), preferred_element_type=f32)


def mm_nt(a, b):
    return lax.dot_general(a, b, (((1,), (1,)), ((), ())), preferred_element_type=f32)


def norm_parts(values, gain):
    row_mean = jnp.mean(values, axis=-1, keepdims=True)
    centred = values - row_mean
    variance = jnp.mean(centred * centred, axis=-1, keepdims=True)
    inverse = lax.rsqrt(variance + epsilon)
    normed = centred * inverse
    return normed * gain, normed, inverse


def norm_back(grad_in, gain, normed, inverse):
    scaled = grad_in * gain
    first_mean = jnp.mean(scaled, axis=-1, keepdims=True)
    second_mean = jnp.mean(scaled * normed, axis=-1, keepdims=True)
    return (scaled - first_mean - normed * second_mean) * inverse


def gelu_parts(values):
    factor = math.sqrt(2.0 / math.pi)
    square = values * values
    tangent = jnp.tanh(factor * (values + gelu_coef * values * square))
    half = 0.5 * (1.0 + tangent)
    result = values * half
    derivative = half + 0.5 * values * (1.0 - tangent * tangent) * (
        factor + (3.0 * gelu_coef * factor) * square
    )
    return result, derivative


def head_blocks(wide):
    return jnp.concatenate(
        [wide[h * HD : (h + 1) * HD, h * POS : (h + 1) * POS] for h in range(HEADS)], axis=0
    )


def spread_heads(rows, head_mask):
    return jnp.concatenate([rows * head_mask[h : h + 1, :] for h in range(HEADS)], axis=0)


def block_kernel(
    field_ref,
    cot_ref,
    lon_ref,
    lat_ref,
    diag_ref,
    gain1_ref,
    wqkv_t_ref,
    wproj_ref,
    gain2_ref,
    wup_ref,
    wdown_ref,
    table_ref,
    label_row_ref,
    label_col_ref,
    factor_ref,
    perm_ref,
    perm_t_ref,
    head_mask_ref,
    own_out,
    lon_out,
    lat_out,
    diag_out,
    fold_out,
    frame,
    bias,
):
    half = WLAT // 2
    cols = 2 * WLON
    edge = WLON // 2
    inner = cols - edge
    root = 1.0 / math.sqrt(HD)
    for t, own in enumerate((field_ref, cot_ref)):
        for level in range(4):
            z = (level + 1) % 4
            for i in range(half):
                row = (level * WLAT + i) * cols
                frame[t, row : row + cols, :] = jnp.concatenate(
                    [own[z, half + i].astype(f32)[edge:, :], lon_ref[t, z, i].astype(f32)], axis=0
                )
                row = (level * WLAT + half + i) * cols
                frame[t, row : row + cols, :] = jnp.concatenate(
                    [lat_ref[t, z, i].astype(f32), diag_ref[t, z, i].astype(f32)], axis=0
                )
    gain1 = gain1_ref[...]
    gain2 = gain2_ref[...]
    wq_t = wqkv_t_ref[0:C, :]
    wk_t = wqkv_t_ref[C : 2 * C, :]
    wv_t = wqkv_t_ref[2 * C : 3 * C, :]
    head_mask = head_mask_ref[...]
    perm = perm_ref[...]
    perm_t = perm_t_ref[...]
    for n in range(2):
        for o in range(WLON):
            start = PAIR * (WLON - 1 - o)
            bias[:, PAIR * o : PAIR * (o + 1), :] = table_ref[n, :, :, start : start + POS]
        bias_t = bias[...].reshape(ROWS, POS).T
        x = mm(perm, frame[0, n * 2 * POS : (n + 1) * 2 * POS, :].astype(bf16))
        cot = mm(perm, frame[1, n * 2 * POS : (n + 1) * 2 * POS, :].astype(bf16))
        scaled1, normed1, inverse1 = norm_parts(x, gain1)
        h1 = scaled1.astype(bf16)
        q_all = mm_nt(h1, wq_t).astype(bf16)
        k_all = mm_nt(h1, wk_t).astype(bf16)
        v_all = mm_nt(h1, wv_t).astype(bf16)
        saved = []
        branches = []
        for c in range(2):
            w = 2 * n + c
            rows = slice(c * POS, (c + 1) * POS)
            v_t = mm_nt(wv_t, h1[rows]).astype(bf16)
            q_wide = spread_heads(q_all[rows], head_mask)
            scores = mm_nt(k_all[rows], q_wide) * root + bias_t
            allowed = label_col_ref[:, w : w + 1] == label_row_ref[w]
            scores = jnp.where(allowed, scores, -1e30)
            weights = jnp.exp(scores - jnp.max(scores, axis=0, keepdims=True))
            probs = weights * (1.0 / jnp.sum(weights, axis=0, keepdims=True))
            probs_low = probs.astype(bf16)
            attended = head_blocks(mm(v_t, probs_low)).T.astype(bf16)
            factor = factor_ref[w]
            branches.append((mm(attended, wproj_ref[...]) * factor).astype(bf16).astype(f32))
            saved.append((q_wide, probs, probs_low))
        y_sum = x + jnp.concatenate(branches, axis=0)
        scaled2, normed2, inverse2 = norm_parts(y_sum, gain2)
        act, slope = gelu_parts(mm(scaled2.astype(bf16), wup_ref[...]))
        result = (y_sum + mm(act.astype(bf16), wdown_ref[...])).astype(bf16)
        grad_up = (mm_nt(cot.astype(bf16), wdown_ref[...]) * slope).astype(bf16)
        grad_sum = cot + norm_back(mm_nt(grad_up, wup_ref[...]), gain2, normed2, inverse2)
        grad_low_in = grad_sum.astype(bf16).astype(f32)
        folded = None
        grad_h1 = []
        for c in range(2):
            w = 2 * n + c
            rows = slice(c * POS, (c + 1) * POS)
            q_wide, probs, probs_low = saved[c]
            k_t = mm_nt(wk_t, h1[rows]).astype(bf16)
            grad_branch = (grad_low_in[rows] * factor_ref[w]).astype(bf16)
            grad_att = mm_nt(grad_branch, wproj_ref[...]).astype(bf16)
            g_wide = spread_heads(grad_att, head_mask)
            grad_probs = mm_nt(v_all[rows], g_wide)
            inner_sum = jnp.sum(probs * grad_probs, axis=0, keepdims=True)
            grad_scores = probs * (grad_probs - inner_sum)
            folded = grad_scores if folded is None else folded + grad_scores
            grad_low = grad_scores.astype(bf16)
            grad_q = (head_blocks(mm(k_t, grad_low)).T * root).astype(bf16)
            grad_k = (mm(grad_low, q_wide) * root).astype(bf16)
            grad_v = mm(probs_low, g_wide).astype(bf16)
            grad_h1.append(mm(grad_q, wq_t) + mm(grad_k, wk_t) + mm(grad_v, wv_t))
        grad_h1 = jnp.concatenate(grad_h1, axis=0).astype(bf16).astype(f32)
        grad_field = (grad_sum + norm_back(grad_h1, gain1, normed1, inverse1)).astype(bf16)
        bias[...] = folded.T.reshape(HEADS, POS, POS)
        total = None
        for o in range(WLON):
            left = PAIR * (WLON - 1 - o)
            right = TAB - POS - left
            parts = [bias[:, PAIR * o : PAIR * (o + 1), :]]
            if left:
                parts = [jnp.zeros((HEADS, PAIR, left), f32)] + parts
            if right:
                parts = parts + [jnp.zeros((HEADS, PAIR, right), f32)]
            piece = jnp.concatenate(parts, axis=2)
            total = piece if total is None else total + piece
        fold_out[n] = total
        for t, value in enumerate((result, grad_field)):
            natural = mm(perm_t, value)
            for dz in range(WZ):
                z = (2 * n + dz + 1) % 4
                for i in range(half):
                    row = (dz * WLAT + i) * cols
                    slab = natural[row : row + cols]
                    own_out[t, z, i] = slab[:inner].astype(bf16)
                    lon_out[t, z, i] = slab[inner:].astype(bf16)
                    row = (dz * WLAT + half + i) * cols
                    slab = natural[row : row + cols]
                    lat_out[t, z, i] = slab[:inner].astype(bf16)
                    diag_out[t, z, i] = slab[inner:].astype(bf16)


def finish_kernel(own_ref, lon_ref, lat_ref, diag_ref, out_ref, grad_ref):
    half = WLAT // 2
    for t, target in enumerate((out_ref, grad_ref)):
        for z in range(4):
            for i in range(half):
                target[z, i] = jnp.concatenate(
                    [diag_ref[t, z, i].astype(f32), lat_ref[t, z, i].astype(f32)], axis=0
                ).astype(bf16)
                target[z, half + i] = jnp.concatenate(
                    [lon_ref[t, z, i].astype(f32), own_ref[t, z, i].astype(f32)], axis=0
                ).astype(bf16)


def window_order():
    perm = np.zeros((2 * POS, 2 * POS), np.float32)
    for c in range(2):
        for j in range(WLON):
            for d in range(PAIR):
                perm[c * POS + j * PAIR + d, d * 2 * WLON + c * WLON + j] = 1.0
    return perm


def lon_sum(value):
    lons = lax.axis_size("lon")
    group = min(4, lons)
    others = lons // group
    me = lax.axis_index("lon") % group
    low = value.astype(bf16)
    if group < 4:
        low = low.reshape((group, 4 // group) + low.shape[1:])

    def quarter(d):
        return lax.dynamic_index_in_dim(low, me ^ d, 0, keepdims=False)

    def tree(parts):
        while len(parts) > 1:
            parts = [parts[i] + parts[i + 1] for i in range(0, len(parts), 2)]
        return parts[0]

    parts = [quarter(0)] + [swapped(quarter(d), d) for d in range(1, group)]
    mine = tree([p.astype(f32) for p in parts]).astype(bf16)
    parts = [mine] + [swapped(mine, d * group) for d in range(1, others)]
    mine = tree([p.astype(f32) for p in parts]).astype(bf16)
    parts = [mine] + [swapped(mine, d) for d in range(1, group)]
    bit = 1
    while bit < group:
        flip = (me & bit) != 0
        parts = [jnp.where(flip, parts[i ^ bit], parts[i]) for i in range(group)]
        bit *= 2
    return jnp.stack(parts, axis=0).astype(f32)


def body(
    field_in,
    cotangent,
    ln1_gain,
    w_qkv,
    w_proj,
    ln2_gain,
    w_up,
    w_down,
    bias_table,
    region_ids,
    keep_flags,
):
    levels, lat_rows, lon_cols, channels = field_in.shape
    half = WLAT // 2
    edge = WLON // 2
    both = (field_in, cotangent)
    lon_part = shifted(jnp.stack([v[:, half:, :edge] for v in both]), 0, -1)
    lat_part = shifted(jnp.stack([v[:, :half, edge:] for v in both]), -1, 0)
    diag_part = shifted(jnp.stack([v[:, :half, :edge] for v in both]), -1, -1)

    lat_start = lax.axis_index("lat") * lat_rows
    lat_total = lax.axis_size("lat") * lat_rows
    level_pos = jnp.arange(levels, dtype=jnp.int32)[:, None, None]
    lat_pos = lat_start + jnp.arange(lat_rows, dtype=jnp.int32)[None, :, None]
    labels = 4 * region_ids + (
        2 * (level_pos >= levels - WZ // 2).astype(jnp.int32)
        + (lat_pos >= lat_total - half).astype(jnp.int32)
    )
    labels = labels.reshape(2, WZ, WLAT, 2, WLON).transpose(0, 3, 4, 1, 2).reshape(4, POS)
    label_row = jnp.tile(labels, (1, HEADS)).reshape(4, 1, ROWS)
    label_col = labels.T
    factor = (keep_flags.astype(f32) / keep_share).reshape(4)

    table = bias_table.reshape(2, HEADS, WZ, WZ, WLAT, WLAT, SPREAD)[..., ::-1]
    table = table.transpose(0, 1, 2, 4, 6, 3, 5).reshape(2, HEADS, PAIR, TAB)

    perm = window_order()
    head_mask = np.repeat(np.eye(HEADS, dtype=np.float32), HD, axis=1)
    vmem = pl.BlockSpec(memory_space=pltpu.VMEM)
    smem = pl.BlockSpec(memory_space=pltpu.SMEM)
    inner = lon_cols - edge
    own, lon_back, lat_back, diag_back, fold = pl.pallas_call(
        block_kernel,
        out_shape=(
            jax.ShapeDtypeStruct((2, 4, half, inner, C), bf16),
            jax.ShapeDtypeStruct((2, 4, half, edge, C), bf16),
            jax.ShapeDtypeStruct((2, 4, half, inner, C), bf16),
            jax.ShapeDtypeStruct((2, 4, half, edge, C), bf16),
            jax.ShapeDtypeStruct((2, HEADS, PAIR, TAB), f32),
        ),
        in_specs=[vmem] * 14 + [smem] + [vmem] * 3,
        out_specs=(vmem,) * 5,
        scratch_shapes=[
            pltpu.VMEM((2, 4 * WLAT * lon_cols, C), f32),
            pltpu.VMEM((HEADS, POS, POS), f32),
        ],
        compiler_params=pltpu.CompilerParams(vmem_limit_bytes=48 * 1024 * 1024),
        name="block",
    )(
        field_in,
        cotangent,
        lon_part,
        lat_part,
        diag_part,
        ln1_gain.reshape(1, C),
        w_qkv.T,
        w_proj,
        ln2_gain.reshape(1, C),
        w_up,
        w_down,
        table,
        label_row,
        label_col,
        factor,
        jnp.asarray(perm, bf16),
        jnp.asarray(perm.T, bf16),
        jnp.asarray(head_mask, bf16),
    )
    lon_back = shifted(lon_back, 0, 1)
    lat_back = shifted(lat_back, 1, 0)
    diag_back = shifted(diag_back, 1, 1)
    grads = lon_sum(fold.reshape(4, HEADS // 2 * PAIR, TAB))
    grads = grads.reshape(2, HEADS, WZ, WLAT, SPREAD, WZ, WLAT)[:, :, :, :, ::-1]
    grads = grads.transpose(0, 1, 2, 5, 3, 6, 4).reshape(2, 1, HEADS, PAIR * TAB)
    result, grad_field = pl.pallas_call(
        finish_kernel,
        out_shape=(jax.ShapeDtypeStruct(field_in.shape, bf16),) * 2,
        in_specs=[vmem] * 4,
        out_specs=(vmem,) * 2,
        name="finish",
    )(own, lon_back, lat_back, diag_back)
    return (result, grad_field, grads)


def solution(mesh):
    placed = (
        P(None, "lat", "lon", None),
        P(None, "lat", "lon", None),
        P(),
        P(),
        P(),
        P(),
        P(),
        P(),
        P(None, "lat", None, None),
        P(None, "lat", "lon"),
        P(None, "lat", "lon"),
    )
    return jax.shard_map(
        body,
        mesh=mesh,
        in_specs=placed,
        out_specs=(
            P(None, "lat", "lon", None),
            P(None, "lat", "lon", None),
            P(None, "lat", None, None),
        ),
        check_vma=False,
    )
```

```python
import math

import jax
import jax.numpy as jnp
import numpy as np
from jax import lax
from jax.experimental import pallas as pl
from jax.experimental.pallas import tpu as pltpu
from jax.sharding import PartitionSpec as P

C = 192
HEADS = 6
HD = 32
FF = 768
WZ = 2
WLAT = 6
WLON = 12
SPREAD = 2 * WLON - 1
POS = WZ * WLAT * WLON
PAIR = WZ * WLAT
TAB = PAIR * SPREAD
ROWS = HEADS * POS
SLOTS = 16
CHUNK = 8

epsilon = 1e-05
keep_share = 0.8
gelu_coef = 0.044715
bf16 = jnp.bfloat16
f32 = jnp.float32


def shifted(block, lat_step, lon_step):
    lats, lons = lax.axis_size("lat"), lax.axis_size("lon")
    route = []
    for a in range(lats):
        for b in range(lons):
            target = ((a + lat_step) % lats) * lons + (b + lon_step) % lons
            route.append((a * lons + b, target))
    return lax.ppermute(block, ("lat", "lon"), route)


def mm(a, b):
    return lax.dot_general(a, b, (((1,), (0,)), ((), ())), preferred_element_type=f32)


def mm_nt(a, b):
    return lax.dot_general(a, b, (((1,), (1,)), ((), ())), preferred_element_type=f32)


def norm_parts(values, gain):
    row_mean = jnp.mean(values, axis=-1, keepdims=True)
    centred = values - row_mean
    variance = jnp.mean(centred * centred, axis=-1, keepdims=True)
    inverse = lax.rsqrt(variance + epsilon)
    normed = centred * inverse
    return normed * gain, normed, inverse


def norm_back(grad_in, gain, normed, inverse):
    scaled = grad_in * gain
    first_mean = jnp.mean(scaled, axis=-1, keepdims=True)
    second_mean = jnp.mean(scaled * normed, axis=-1, keepdims=True)
    return (scaled - first_mean - normed * second_mean) * inverse


def gelu_parts(values):
    factor = math.sqrt(2.0 / math.pi)
    square = values * values
    tangent = jnp.tanh(factor * (values + gelu_coef * values * square))
    half = 0.5 * (1.0 + tangent)
    result = values * half
    derivative = half + 0.5 * values * (1.0 - tangent * tangent) * (
        factor + (3.0 * gelu_coef * factor) * square
    )
    return result, derivative


def head_blocks(wide):
    return jnp.concatenate(
        [wide[h * HD : (h + 1) * HD, h * POS : (h + 1) * POS] for h in range(HEADS)], axis=0
    )


def spread_heads(rows, head_mask):
    return jnp.concatenate([rows * head_mask[h : h + 1, :] for h in range(HEADS)], axis=0)


def block_kernel(
    field_ref,
    cot_ref,
    lon_ref,
    lat_ref,
    diag_ref,
    gain1_ref,
    wqkv_t_ref,
    wproj_ref,
    gain2_ref,
    wup_ref,
    wdown_t_ref,
    bias_ref,
    label_row_ref,
    label_col_ref,
    factor_ref,
    perm_ref,
    perm_t_ref,
    head_mask_ref,
    table_perm_ref,
    chunk_perm_ref,
    own_out,
    lon_out,
    lat_out,
    diag_out,
    fold_out,
    frame,
    wide,
):
    half = WLAT // 2
    cols = 2 * WLON
    edge = WLON // 2
    inner = cols - edge
    root = 1.0 / math.sqrt(HD)
    for t, own in enumerate((field_ref, cot_ref)):
        for level in range(4):
            z = (level + 1) % 4
            for i in range(half):
                row = (level * WLAT + i) * cols
                frame[t, row : row + cols, :] = jnp.concatenate(
                    [own[z, half + i].astype(f32)[edge:, :], lon_ref[t, z, i].astype(f32)], axis=0
                )
                row = (level * WLAT + half + i) * cols
                frame[t, row : row + cols, :] = jnp.concatenate(
                    [lat_ref[t, z, i].astype(f32), diag_ref[t, z, i].astype(f32)], axis=0
                )
    spare = fold_out.shape[0] - 2 * PAIR
    if spare:
        fold_out[2 * PAIR :] = jnp.zeros((spare, CHUNK, TAB), bf16)
    gain1 = gain1_ref[...]
    gain2 = gain2_ref[...]
    wq_t = wqkv_t_ref[0:C, :]
    wk_t = wqkv_t_ref[C : 2 * C, :]
    wv_t = wqkv_t_ref[2 * C : 3 * C, :]
    head_mask = head_mask_ref[...]
    perm = perm_ref[...]
    perm_t = perm_t_ref[...]
    for n in range(2):
        x = mm(perm, frame[0, n * 2 * POS : (n + 1) * 2 * POS, :].astype(bf16))
        cot = mm(perm, frame[1, n * 2 * POS : (n + 1) * 2 * POS, :].astype(bf16))
        scaled1, normed1, inverse1 = norm_parts(x, gain1)
        h1 = scaled1.astype(bf16)
        q_all = mm_nt(h1, wq_t).astype(bf16)
        k_all = mm_nt(h1, wk_t).astype(bf16)
        v_all = mm_nt(h1, wv_t).astype(bf16)
        saved = []
        branches = []
        for c in range(2):
            w = 2 * n + c
            rows = slice(c * POS, (c + 1) * POS)
            v_t = mm_nt(wv_t, h1[rows]).astype(bf16)
            q_wide = spread_heads(q_all[rows], head_mask)
            scores = mm_nt(k_all[rows], q_wide) * root + bias_ref[n]
            allowed = label_col_ref[:, w : w + 1] == label_row_ref[w]
            scores = jnp.where(allowed, scores, -1e30)
            weights = jnp.exp(scores - jnp.max(scores, axis=0, keepdims=True))
            probs = weights * (1.0 / jnp.sum(weights, axis=0, keepdims=True))
            probs_low = probs.astype(bf16)
            attended = head_blocks(mm(v_t, probs_low)).T.astype(bf16)
            factor = factor_ref[w]
            branches.append((mm(attended, wproj_ref[...]) * factor).astype(bf16).astype(f32))
            saved.append((q_wide, probs, probs_low))
        y_sum = x + jnp.concatenate(branches, axis=0)
        scaled2, normed2, inverse2 = norm_parts(y_sum, gain2)
        act, slope = gelu_parts(mm(scaled2.astype(bf16), wup_ref[...]))
        result = (y_sum + mm_nt(act.astype(bf16), wdown_t_ref[...])).astype(bf16)
        grad_up = (mm(cot.astype(bf16), wdown_t_ref[...]) * slope).astype(bf16)
        grad_sum = cot + norm_back(mm_nt(grad_up, wup_ref[...]), gain2, normed2, inverse2)
        grad_low_in = grad_sum.astype(bf16).astype(f32)
        folded = None
        grad_h1 = []
        for c in range(2):
            w = 2 * n + c
            rows = slice(c * POS, (c + 1) * POS)
            q_wide, probs, probs_low = saved[c]
            k_t = mm_nt(wk_t, h1[rows]).astype(bf16)
            grad_branch = (grad_low_in[rows] * factor_ref[w]).astype(bf16)
            grad_att = mm_nt(grad_branch, wproj_ref[...]).astype(bf16)
            g_wide = spread_heads(grad_att, head_mask)
            grad_probs = mm_nt(v_all[rows], g_wide)
            inner_sum = jnp.sum(probs * grad_probs, axis=0, keepdims=True)
            grad_scores = probs * (grad_probs - inner_sum)
            folded = grad_scores if folded is None else folded + grad_scores
            grad_low = grad_scores.astype(bf16)
            grad_q = (head_blocks(mm(k_t, grad_low)).T * root).astype(bf16)
            grad_k = (mm(grad_low, q_wide) * root).astype(bf16)
            grad_v = mm(probs_low, g_wide).astype(bf16)
            grad_h1.append(mm(grad_q, wq_t) + mm(grad_k, wk_t) + mm(grad_v, wv_t))
        grad_h1 = jnp.concatenate(grad_h1, axis=0).astype(bf16).astype(f32)
        grad_field = (grad_sum + norm_back(grad_h1, gain1, normed1, inverse1)).astype(bf16)
        wide[...] = folded.T.reshape(HEADS, POS, POS)
        total = None
        for o in range(WLON):
            left = PAIR * (WLON - 1 - o)
            right = TAB - POS - left
            parts = [wide[:, PAIR * o : PAIR * (o + 1), :]]
            if left:
                parts = [jnp.zeros((HEADS, PAIR, left), f32)] + parts
            if right:
                parts = parts + [jnp.zeros((HEADS, PAIR, right), f32)]
            piece = jnp.concatenate(parts, axis=2)
            total = piece if total is None else total + piece
        total = jnp.concatenate([total, jnp.zeros((HEADS, SLOTS - PAIR, TAB), f32)], axis=1)
        total = total.reshape(HEADS * SLOTS, TAB).astype(bf16)
        total = mm_nt(total, table_perm_ref[...]).astype(bf16)
        total = mm(chunk_perm_ref[...], total).reshape(PAIR, CHUNK, TAB).astype(bf16)
        fold_out[n * PAIR : (n + 1) * PAIR] = total
        for t, value in enumerate((result, grad_field)):
            natural = mm(perm_t, value)
            for dz in range(WZ):
                z = (2 * n + dz + 1) % 4
                for i in range(half):
                    row = (dz * WLAT + i) * cols
                    slab = natural[row : row + cols]
                    own_out[t, z, i] = slab[:inner].astype(bf16)
                    lon_out[t, z, i] = slab[inner:].astype(bf16)
                    row = (dz * WLAT + half + i) * cols
                    slab = natural[row : row + cols]
                    lat_out[t, z, i] = slab[:inner].astype(bf16)
                    diag_out[t, z, i] = slab[inner:].astype(bf16)


def expand_kernel(table_ref, table_perm_ref, row_perm_ref, bias_out, flat, rows, wide):
    part = PAIR // WZ * SPREAD
    for k in range(2 * HEADS):
        flat[k : k + 1, :] = table_ref[k]
    rows[...] = jnp.zeros_like(rows)
    for a in range(WZ):
        for c in range(WLAT):
            pieces = []
            for b in range(WZ):
                start = ((a * WZ + b) * WLAT + c) * part
                pieces.append(flat[:, start : start + part])
            row = (a * WLAT + c) * SLOTS
            rows[row : row + 2 * HEADS, :] = jnp.concatenate(pieces, axis=1)
    left = rows[...]
    perm = table_perm_ref[...]
    total = None
    for _ in range(3):
        low = left.astype(bf16)
        left = left - low.astype(f32)
        term = mm(row_perm_ref[...], mm(low, perm).astype(bf16))
        total = term if total is None else total + term
    total = total.reshape(2 * HEADS, SLOTS, TAB)
    for o in range(WLON):
        start = PAIR * (WLON - 1 - o)
        wide[:, PAIR * o : PAIR * (o + 1), :] = total[:, :PAIR, start : start + POS]
    for n in range(2):
        bias_out[n] = wide[n * HEADS : (n + 1) * HEADS].reshape(ROWS, POS).T


def unpack_kernel(grad_ref, table_out, flat):
    part = PAIR // WZ * SPREAD
    for n in range(2):
        for a in range(WZ):
            for c in range(WLAT):
                chunk = grad_ref[n * PAIR + a * WLAT + c].astype(f32)[:HEADS]
                for b in range(WZ):
                    start = ((a * WZ + b) * WLAT + c) * part
                    flat[n * HEADS : (n + 1) * HEADS, start : start + part] = chunk[
                        :, b * part : (b + 1) * part
                    ]
    for k in range(2 * HEADS):
        table_out[k] = flat[k : k + 1, :]


def finish_kernel(own_ref, lon_ref, lat_ref, diag_ref, out_ref, grad_ref):
    half = WLAT // 2
    for t, target in enumerate((out_ref, grad_ref)):
        for z in range(4):
            for i in range(half):
                target[z, i] = jnp.concatenate(
                    [diag_ref[t, z, i].astype(f32), lat_ref[t, z, i].astype(f32)], axis=0
                ).astype(bf16)
                target[z, half + i] = jnp.concatenate(
                    [lon_ref[t, z, i].astype(f32), own_ref[t, z, i].astype(f32)], axis=0
                ).astype(bf16)


def window_order():
    perm = np.zeros((2 * POS, 2 * POS), np.float32)
    for c in range(2):
        for j in range(WLON):
            for d in range(PAIR):
                perm[c * POS + j * PAIR + d, d * 2 * WLON + c * WLON + j] = 1.0
    return perm


def table_order():
    perm = np.zeros((TAB, TAB), np.float32)
    for d in range(PAIR):
        for r in range(SPREAD):
            perm[d * SPREAD + r, (SPREAD - 1 - r) * PAIR + d] = 1.0
    return perm


def chunk_order():
    perm = np.zeros((PAIR * CHUNK, HEADS * SLOTS), np.float32)
    for h in range(HEADS):
        for k in range(PAIR):
            perm[k * CHUNK + h, h * SLOTS + k] = 1.0
    return perm


def row_order():
    perm = np.zeros((2 * HEADS * SLOTS, PAIR * SLOTS), np.float32)
    for h in range(2 * HEADS):
        for k in range(PAIR):
            perm[h * SLOTS + k, k * SLOTS + h] = 1.0
    return perm


def lon_sum(chunks):
    lons = lax.axis_size("lon")
    shares = chunks.reshape((lons, -1) + chunks.shape[1:])
    shares = lax.all_to_all(shares, "lon", 0, 0)
    share = jnp.sum(shares.astype(f32), axis=0).astype(bf16)
    shares = lax.all_to_all(jnp.broadcast_to(share, shares.shape), "lon", 0, 0)
    return shares.reshape(chunks.shape)


def body(
    field_in,
    cotangent,
    ln1_gain,
    w_qkv,
    w_proj,
    ln2_gain,
    w_up,
    w_down,
    bias_table,
    region_ids,
    keep_flags,
):
    levels, lat_rows, lon_cols, channels = field_in.shape
    half = WLAT // 2
    edge = WLON // 2
    both = (field_in, cotangent)
    lon_part = shifted(jnp.stack([v[:, half:, :edge] for v in both]), 0, -1)
    lat_part = shifted(jnp.stack([v[:, :half, edge:] for v in both]), -1, 0)
    diag_part = shifted(jnp.stack([v[:, :half, :edge] for v in both]), -1, -1)

    lat_start = lax.axis_index("lat") * lat_rows
    lat_total = lax.axis_size("lat") * lat_rows
    level_pos = jnp.arange(levels, dtype=jnp.int32)[:, None, None]
    lat_pos = lat_start + jnp.arange(lat_rows, dtype=jnp.int32)[None, :, None]
    labels = 4 * region_ids + (
        2 * (level_pos >= levels - WZ // 2).astype(jnp.int32)
        + (lat_pos >= lat_total - half).astype(jnp.int32)
    )
    labels = labels.reshape(2, WZ, WLAT, 2, WLON).transpose(0, 3, 4, 1, 2).reshape(4, POS)
    label_row = jnp.tile(labels, (1, HEADS)).reshape(4, 1, ROWS)
    label_col = labels.T
    factor = (keep_flags.astype(f32) / keep_share).reshape(4)

    perm = window_order()
    head_mask = np.repeat(np.eye(HEADS, dtype=np.float32), HD, axis=1)
    vmem = pl.BlockSpec(memory_space=pltpu.VMEM)
    smem = pl.BlockSpec(memory_space=pltpu.SMEM)
    inner = lon_cols - edge
    table_perm = jnp.asarray(table_order(), bf16)
    bias_wide = pl.pallas_call(
        expand_kernel,
        out_shape=jax.ShapeDtypeStruct((2, POS, ROWS), f32),
        in_specs=[vmem] * 3,
        out_specs=vmem,
        scratch_shapes=[
            pltpu.VMEM((2 * HEADS, PAIR * TAB), f32),
            pltpu.VMEM((PAIR * SLOTS, TAB), f32),
            pltpu.VMEM((2 * HEADS, POS, POS), f32),
        ],
        compiler_params=pltpu.CompilerParams(vmem_limit_bytes=32 * 1024 * 1024),
        name="expand",
    )(
        bias_table.reshape(2 * HEADS, 1, PAIR * TAB),
        table_perm,
        jnp.asarray(row_order(), bf16),
    )
    lons = lax.axis_size("lon")
    chunks = -(-2 * PAIR // lons) * lons
    own, lon_back, lat_back, diag_back, fold = pl.pallas_call(
        block_kernel,
        out_shape=(
            jax.ShapeDtypeStruct((2, 4, half, inner, C), bf16),
            jax.ShapeDtypeStruct((2, 4, half, edge, C), bf16),
            jax.ShapeDtypeStruct((2, 4, half, inner, C), bf16),
            jax.ShapeDtypeStruct((2, 4, half, edge, C), bf16),
            jax.ShapeDtypeStruct((chunks, CHUNK, TAB), bf16),
        ),
        in_specs=[vmem] * 14 + [smem] + [vmem] * 5,
        out_specs=(vmem,) * 5,
        scratch_shapes=[
            pltpu.VMEM((2, 4 * WLAT * lon_cols, C), f32),
            pltpu.VMEM((HEADS, POS, POS), f32),
        ],
        compiler_params=pltpu.CompilerParams(vmem_limit_bytes=48 * 1024 * 1024),
        name="block",
    )(
        field_in,
        cotangent,
        lon_part,
        lat_part,
        diag_part,
        ln1_gain.reshape(1, C),
        w_qkv.T,
        w_proj,
        ln2_gain.reshape(1, C),
        w_up,
        w_down.T,
        bias_wide,
        label_row,
        label_col,
        factor,
        jnp.asarray(perm, bf16),
        jnp.asarray(perm.T, bf16),
        jnp.asarray(head_mask, bf16),
        table_perm,
        jnp.asarray(chunk_order(), bf16),
    )
    lon_back = shifted(lon_back, 0, 1)
    lat_back = shifted(lat_back, 1, 0)
    diag_back = shifted(diag_back, 1, 1)
    grads = pl.pallas_call(
        unpack_kernel,
        out_shape=jax.ShapeDtypeStruct((2 * HEADS, 1, PAIR * TAB), f32),
        in_specs=[vmem],
        out_specs=vmem,
        scratch_shapes=[pltpu.VMEM((2 * HEADS, PAIR * TAB), f32)],
        name="unpack",
    )(lon_sum(fold))
    grads = grads.reshape(2, 1, HEADS, PAIR * TAB)
    result, grad_field = pl.pallas_call(
        finish_kernel,
        out_shape=(jax.ShapeDtypeStruct(field_in.shape, bf16),) * 2,
        in_specs=[vmem] * 4,
        out_specs=(vmem,) * 2,
        name="finish",
    )(own, lon_back, lat_back, diag_back)
    return (result, grad_field, grads)


def solution(mesh):
    placed = (
        P(None, "lat", "lon", None),
        P(None, "lat", "lon", None),
        P(),
        P(),
        P(),
        P(),
        P(),
        P(),
        P(None, "lat", None, None),
        P(None, "lat", "lon"),
        P(None, "lat", "lon"),
    )
    return jax.shard_map(
        body,
        mesh=mesh,
        in_specs=placed,
        out_specs=(
            P(None, "lat", "lon", None),
            P(None, "lat", "lon", None),
            P(None, "lat", None, None),
        ),
        check_vma=False,
    )
```

```python
import math

import jax
import jax.numpy as jnp
import numpy as np
from jax import lax
from jax.experimental import pallas as pl
from jax.experimental.pallas import tpu as pltpu
from jax.sharding import PartitionSpec as P

C = 192
HEADS = 6
HD = 32
FF = 768
WZ = 2
WLAT = 6
WLON = 12
SPREAD = 2 * WLON - 1
POS = WZ * WLAT * WLON
PAIR = WZ * WLAT
TAB = PAIR * SPREAD
ROWS = HEADS * POS
SLOTS = 16
QUARTER = PAIR * HEADS // 2
LANES = 128

epsilon = 1e-05
keep_share = 0.8
gelu_coef = 0.044715
bf16 = jnp.bfloat16
f32 = jnp.float32


def shifted(block, lat_step, lon_step):
    lats, lons = lax.axis_size("lat"), lax.axis_size("lon")
    route = []
    for a in range(lats):
        for b in range(lons):
            target = ((a + lat_step) % lats) * lons + (b + lon_step) % lons
            route.append((a * lons + b, target))
    return lax.ppermute(block, ("lat", "lon"), route)


def mm(a, b):
    return lax.dot_general(a, b, (((1,), (0,)), ((), ())), preferred_element_type=f32)


def mm_nt(a, b):
    return lax.dot_general(a, b, (((1,), (1,)), ((), ())), preferred_element_type=f32)


def norm_parts(values, gain):
    row_mean = jnp.mean(values, axis=-1, keepdims=True)
    centred = values - row_mean
    variance = jnp.mean(centred * centred, axis=-1, keepdims=True)
    inverse = lax.rsqrt(variance + epsilon)
    normed = centred * inverse
    return normed * gain, normed, inverse


def norm_back(grad_in, gain, normed, inverse):
    scaled = grad_in * gain
    first_mean = jnp.mean(scaled, axis=-1, keepdims=True)
    second_mean = jnp.mean(scaled * normed, axis=-1, keepdims=True)
    return (scaled - first_mean - normed * second_mean) * inverse


def gelu_parts(values):
    factor = math.sqrt(2.0 / math.pi)
    square = values * values
    tangent = jnp.tanh(factor * (values + gelu_coef * values * square))
    half = 0.5 * (1.0 + tangent)
    result = values * half
    derivative = half + 0.5 * values * (1.0 - tangent * tangent) * (
        factor + (3.0 * gelu_coef * factor) * square
    )
    return result, derivative


def head_blocks(wide):
    return jnp.concatenate(
        [wide[h * HD : (h + 1) * HD, h * POS : (h + 1) * POS] for h in range(HEADS)], axis=0
    )


def spread_heads(rows, head_mask):
    return jnp.concatenate([rows * head_mask[h : h + 1, :] for h in range(HEADS)], axis=0)


def put(packed, t, row, slab):
    third = packed.shape[0] // 3
    size = slab.shape[0]
    rest = C - LANES
    packed[t * third + row : t * third + row + size, :] = slab[:, :LANES]
    packed[2 * third + row : 2 * third + row + size, t * rest : (t + 1) * rest] = slab[:, LANES:]


def get(packed, t, row, size):
    third = packed.shape[0] // 3
    rest = C - LANES
    return (
        packed[t * third + row : t * third + row + size, :],
        packed[2 * third + row : 2 * third + row + size, t * rest : (t + 1) * rest],
    )


def pack_kernel(field_ref, cot_ref, lat_out, diag_out, lon_out, lat_buf, diag_buf, lon_buf):
    half = WLAT // 2
    edge = WLON // 2
    inner = 2 * WLON - edge
    for t, source in enumerate((field_ref, cot_ref)):
        for z in range(4):
            for i in range(half):
                k = z * half + i
                top = source[z, i].astype(f32)
                low = source[z, half + i].astype(f32)
                put(lat_buf, t, k * inner, top[edge:])
                put(diag_buf, t, k * edge, top[:edge])
                put(lon_buf, t, k * edge, low[:edge])
    lat_out[...] = lat_buf[...].astype(bf16)
    diag_out[...] = diag_buf[...].astype(bf16)
    lon_out[...] = lon_buf[...].astype(bf16)


def scores_kernel(
    field_ref,
    cot_ref,
    lon_ref,
    lat_ref,
    diag_ref,
    gain1_ref,
    wqkv_t_ref,
    wproj_ref,
    gain2_ref,
    wup_ref,
    wdown_t_ref,
    bias_ref,
    label_row_ref,
    label_col_ref,
    factor_ref,
    perm_ref,
    head_mask_ref,
    table_perm_ref,
    chunk_perm_ref,
    fold_out,
    x_out,
    q_out,
    kt_out,
    probs_out,
    grad_low_out,
    grad_att_out,
    grad_sum_out,
    result_out,
    frame,
    wide,
):
    half = WLAT // 2
    cols = 2 * WLON
    edge = WLON // 2
    inner = cols - edge
    root = 1.0 / math.sqrt(HD)
    lon_part = lon_ref[...].astype(f32)
    lat_part = lat_ref[...].astype(f32)
    diag_part = diag_ref[...].astype(f32)
    for t, own in enumerate((field_ref, cot_ref)):
        for level in range(4):
            z = (level + 1) % 4
            for i in range(half):
                k = z * half + i
                row = (level * WLAT + i) * cols
                frame[t, row : row + inner, :] = own[z, half + i].astype(f32)[edge:, :]
                main, rest = get(lon_part, t, k * edge, edge)
                frame[t, row + inner : row + cols, :LANES] = main
                frame[t, row + inner : row + cols, LANES:] = rest
                row = (level * WLAT + half + i) * cols
                main, rest = get(lat_part, t, k * inner, inner)
                frame[t, row : row + inner, :LANES] = main
                frame[t, row : row + inner, LANES:] = rest
                main, rest = get(diag_part, t, k * edge, edge)
                frame[t, row + inner : row + cols, :LANES] = main
                frame[t, row + inner : row + cols, LANES:] = rest
    gain1 = gain1_ref[...]
    gain2 = gain2_ref[...]
    wq_t = wqkv_t_ref[0:C, :]
    wk_t = wqkv_t_ref[C : 2 * C, :]
    wv_t = wqkv_t_ref[2 * C : 3 * C, :]
    head_mask = head_mask_ref[...]
    perm = perm_ref[...]
    for n in range(2):
        both = slice(n * 2 * POS, (n + 1) * 2 * POS)
        x = mm(perm, frame[0, both, :].astype(bf16))
        cot = mm(perm, frame[1, both, :].astype(bf16))
        x_out[both, :] = x.astype(bf16)
        h1 = norm_parts(x, gain1)[0].astype(bf16)
        q_all = mm_nt(h1, wq_t).astype(bf16)
        k_all = mm_nt(h1, wk_t).astype(bf16)
        v_all = mm_nt(h1, wv_t).astype(bf16)
        q_out[both, :] = q_all
        saved = []
        branches = []
        for c in range(2):
            w = 2 * n + c
            rows = slice(c * POS, (c + 1) * POS)
            v_t = mm_nt(wv_t, h1[rows]).astype(bf16)
            kt_out[w] = mm_nt(wk_t, h1[rows]).astype(bf16)
            q_wide = spread_heads(q_all[rows], head_mask)
            scores = mm_nt(k_all[rows], q_wide) * root + bias_ref[n]
            allowed = label_col_ref[:, w : w + 1] == label_row_ref[w]
            scores = jnp.where(allowed, scores, -1e30)
            weights = jnp.exp(scores - jnp.max(scores, axis=0, keepdims=True))
            probs = weights * (1.0 / jnp.sum(weights, axis=0, keepdims=True))
            probs_low = probs.astype(bf16)
            probs_out[w] = probs_low
            attended = head_blocks(mm(v_t, probs_low)).T.astype(bf16)
            factor = factor_ref[w]
            branches.append((mm(attended, wproj_ref[...]) * factor).astype(bf16).astype(f32))
            saved.append(probs)
        y_sum = x + jnp.concatenate(branches, axis=0)
        scaled2, normed2, inverse2 = norm_parts(y_sum, gain2)
        act, slope = gelu_parts(mm(scaled2.astype(bf16), wup_ref[...]))
        result_out[both, :] = (y_sum + mm_nt(act.astype(bf16), wdown_t_ref[...])).astype(bf16)
        grad_up = (mm(cot.astype(bf16), wdown_t_ref[...]) * slope).astype(bf16)
        grad_sum = cot + norm_back(mm_nt(grad_up, wup_ref[...]), gain2, normed2, inverse2)
        grad_sum_out[both, :] = grad_sum
        grad_low_in = grad_sum.astype(bf16).astype(f32)
        folded = None
        for c in range(2):
            w = 2 * n + c
            rows = slice(c * POS, (c + 1) * POS)
            probs = saved[c]
            grad_branch = (grad_low_in[rows] * factor_ref[w]).astype(bf16)
            grad_att = mm_nt(grad_branch, wproj_ref[...]).astype(bf16)
            grad_att_out[w * POS : (w + 1) * POS, :] = grad_att
            grad_probs = mm_nt(v_all[rows], spread_heads(grad_att, head_mask))
            inner_sum = jnp.sum(probs * grad_probs, axis=0, keepdims=True)
            grad_scores = probs * (grad_probs - inner_sum)
            folded = grad_scores if folded is None else folded + grad_scores
            grad_low_out[w] = grad_scores.astype(bf16)
        wide[...] = folded.T.reshape(HEADS, POS, POS)
        total = None
        for o in range(WLON):
            left = PAIR * (WLON - 1 - o)
            right = TAB - POS - left
            parts = [wide[:, PAIR * o : PAIR * (o + 1), :]]
            if left:
                parts = [jnp.zeros((HEADS, PAIR, left), f32)] + parts
            if right:
                parts = parts + [jnp.zeros((HEADS, PAIR, right), f32)]
            piece = jnp.concatenate(parts, axis=2)
            total = piece if total is None else total + piece
        total = jnp.concatenate([total, jnp.zeros((HEADS, SLOTS - PAIR, TAB), f32)], axis=1)
        total = total.reshape(HEADS * SLOTS, TAB).astype(bf16)
        total = mm_nt(total, table_perm_ref[...]).astype(bf16)
        total = mm(chunk_perm_ref[...], total)
        fold_out[2 * n] = total[:QUARTER].astype(bf16)
        fold_out[2 * n + 1] = total[QUARTER:].astype(bf16)


def inputs_kernel(
    x_ref,
    q_ref,
    kt_ref,
    probs_ref,
    grad_low_ref,
    grad_att_ref,
    grad_sum_ref,
    result_ref,
    gain1_ref,
    wqkv_t_ref,
    perm_t_ref,
    head_mask_ref,
    own_out,
    lat_out,
    diag_out,
    lon_out,
    lat_buf,
    diag_buf,
    lon_buf,
):
    half = WLAT // 2
    cols = 2 * WLON
    edge = WLON // 2
    inner = cols - edge
    root = 1.0 / math.sqrt(HD)
    gain1 = gain1_ref[...]
    wq_t = wqkv_t_ref[0:C, :]
    wk_t = wqkv_t_ref[C : 2 * C, :]
    wv_t = wqkv_t_ref[2 * C : 3 * C, :]
    head_mask = head_mask_ref[...]
    perm_t = perm_t_ref[...]
    for n in range(2):
        both = slice(n * 2 * POS, (n + 1) * 2 * POS)
        _, normed1, inverse1 = norm_parts(x_ref[both, :].astype(f32), gain1)
        grad_h1 = []
        for c in range(2):
            w = 2 * n + c
            rows = slice(w * POS, (w + 1) * POS)
            grad_low = grad_low_ref[w]
            q_wide = spread_heads(q_ref[rows, :], head_mask)
            g_wide = spread_heads(grad_att_ref[rows, :], head_mask)
            grad_q = (head_blocks(mm(kt_ref[w], grad_low)).T * root).astype(bf16)
            grad_k = (mm(grad_low, q_wide) * root).astype(bf16)
            grad_v = mm(probs_ref[w], g_wide).astype(bf16)
            grad_h1.append(mm(grad_q, wq_t) + mm(grad_k, wk_t) + mm(grad_v, wv_t))
        grad_h1 = jnp.concatenate(grad_h1, axis=0).astype(bf16).astype(f32)
        grad_sum = grad_sum_ref[both, :]
        grad_field = (grad_sum + norm_back(grad_h1, gain1, normed1, inverse1)).astype(bf16)
        for t, value in enumerate((result_ref[both, :], grad_field)):
            natural = mm(perm_t, value)
            for dz in range(WZ):
                z = (2 * n + dz + 1) % 4
                for i in range(half):
                    k = z * half + i
                    row = (dz * WLAT + i) * cols
                    slab = natural[row : row + cols]
                    own_out[t, z, i] = slab[:inner].astype(bf16)
                    put(lon_buf, t, k * edge, slab[inner:])
                    row = (dz * WLAT + half + i) * cols
                    slab = natural[row : row + cols]
                    put(lat_buf, t, k * inner, slab[:inner])
                    put(diag_buf, t, k * edge, slab[inner:])
    lat_out[...] = lat_buf[...].astype(bf16)
    diag_out[...] = diag_buf[...].astype(bf16)
    lon_out[...] = lon_buf[...].astype(bf16)


def expand_kernel(table_ref, table_perm_ref, row_perm_ref, bias_out, flat, rows, wide):
    part = PAIR // WZ * SPREAD
    for k in range(2 * HEADS):
        flat[k : k + 1, :] = table_ref[k]
    rows[...] = jnp.zeros_like(rows)
    for a in range(WZ):
        for c in range(WLAT):
            pieces = []
            for b in range(WZ):
                start = ((a * WZ + b) * WLAT + c) * part
                pieces.append(flat[:, start : start + part])
            row = (a * WLAT + c) * SLOTS
            rows[row : row + 2 * HEADS, :] = jnp.concatenate(pieces, axis=1)
    left = rows[...]
    perm = table_perm_ref[...]
    total = None
    for _ in range(3):
        low = left.astype(bf16)
        left = left - low.astype(f32)
        term = mm(row_perm_ref[...], mm(low, perm).astype(bf16))
        total = term if total is None else total + term
    total = total.reshape(2 * HEADS, SLOTS, TAB)
    for o in range(WLON):
        start = PAIR * (WLON - 1 - o)
        wide[:, PAIR * o : PAIR * (o + 1), :] = total[:, :PAIR, start : start + POS]
    for n in range(2):
        bias_out[n] = wide[n * HEADS : (n + 1) * HEADS].reshape(ROWS, POS).T


def unpack_kernel(grad_ref, table_out, flat):
    part = PAIR // WZ * SPREAD
    for n in range(2):
        halves = [grad_ref[2 * n + k].astype(f32) for k in range(2)]
        for a in range(WZ):
            for c in range(WLAT):
                row = c * HEADS
                chunk = halves[a][row : row + HEADS]
                for b in range(WZ):
                    start = ((a * WZ + b) * WLAT + c) * part
                    flat[n * HEADS : (n + 1) * HEADS, start : start + part] = chunk[
                        :, b * part : (b + 1) * part
                    ]
    for k in range(2 * HEADS):
        table_out[k] = flat[k : k + 1, :]


def finish_kernel(own_ref, lat_ref, diag_ref, lon_ref, out_ref, grad_ref):
    half = WLAT // 2
    edge = WLON // 2
    inner = 2 * WLON - edge
    lat_part = lat_ref[...].astype(f32)
    diag_part = diag_ref[...].astype(f32)
    lon_part = lon_ref[...].astype(f32)
    for t, target in enumerate((out_ref, grad_ref)):
        for z in range(4):
            for i in range(half):
                k = z * half + i
                parts = (get(diag_part, t, k * edge, edge), get(lat_part, t, k * inner, inner))
                slab = [jnp.concatenate([parts[0][j], parts[1][j]], axis=0) for j in range(2)]
                target[z, i] = jnp.concatenate(slab, axis=1).astype(bf16)
                slab = jnp.concatenate(get(lon_part, t, k * edge, edge), axis=1)
                own = own_ref[t, z, i].astype(f32)
                target[z, half + i] = jnp.concatenate([slab, own], axis=0).astype(bf16)


def window_order():
    perm = np.zeros((2 * POS, 2 * POS), np.float32)
    for c in range(2):
        for j in range(WLON):
            for d in range(PAIR):
                perm[c * POS + j * PAIR + d, d * 2 * WLON + c * WLON + j] = 1.0
    return perm


def table_order():
    perm = np.zeros((TAB, TAB), np.float32)
    for d in range(PAIR):
        for r in range(SPREAD):
            perm[d * SPREAD + r, (SPREAD - 1 - r) * PAIR + d] = 1.0
    return perm


def chunk_order():
    perm = np.zeros((PAIR * HEADS, HEADS * SLOTS), np.float32)
    for h in range(HEADS):
        for k in range(PAIR):
            perm[k * HEADS + h, h * SLOTS + k] = 1.0
    return perm


def row_order():
    perm = np.zeros((2 * HEADS * SLOTS, PAIR * SLOTS), np.float32)
    for h in range(2 * HEADS):
        for k in range(PAIR):
            perm[h * SLOTS + k, k * SLOTS + h] = 1.0
    return perm


def lon_sum(quarters):
    lons = lax.axis_size("lon")
    me = lax.axis_index("lon")
    bits = [(me >> k) & 1 for k in range(2)]

    def swapped(block, distance):
        return lax.ppermute(block, "lon", [(i, i ^ distance) for i in range(lons)])

    def pick(value, bit):
        return lax.dynamic_index_in_dim(value, bit, 0, keepdims=False)

    def add(a, b):
        return (a.astype(f32) + b.astype(f32)).astype(bf16)

    def gathered(value, distance, bit):
        other = swapped(value, distance)
        first = jnp.where(bit == 0, value, other)
        second = jnp.where(bit == 0, other, value)
        return jnp.stack([first, second])

    pairs = quarters.reshape((2, 2) + quarters.shape[1:])
    value = add(pick(pairs, bits[0]), swapped(pick(pairs, 1 - bits[0]), 1))
    value = add(pick(value, bits[1]), swapped(pick(value, 1 - bits[1]), 2))
    distance = 4
    while distance < lons:
        value = add(value, swapped(value, distance))
        distance *= 2
    value = gathered(value, 2, bits[1])
    value = gathered(value, 1, bits[0])
    return value.reshape(quarters.shape)


def body(
    field_in,
    cotangent,
    ln1_gain,
    w_qkv,
    w_proj,
    ln2_gain,
    w_up,
    w_down,
    bias_table,
    region_ids,
    keep_flags,
):
    levels, lat_rows, lon_cols, channels = field_in.shape
    half = WLAT // 2
    edge = WLON // 2
    inner = lon_cols - edge
    vmem = pl.BlockSpec(memory_space=pltpu.VMEM)
    smem = pl.BlockSpec(memory_space=pltpu.SMEM)
    sizes = [3 * levels * half * size for size in (inner, edge, edge)]
    packed = tuple(jax.ShapeDtypeStruct((size, LANES), bf16) for size in sizes)
    buffers = [pltpu.VMEM((size, LANES), f32) for size in sizes]
    lat_part, diag_part, lon_part = pl.pallas_call(
        pack_kernel,
        out_shape=packed,
        in_specs=[vmem] * 2,
        out_specs=(vmem,) * 3,
        scratch_shapes=buffers,
        name="pack",
    )(field_in, cotangent)
    lat_part = shifted(lat_part, -1, 0)
    diag_part = shifted(diag_part, -1, -1)
    lon_part = shifted(lon_part, 0, -1)

    lat_start = lax.axis_index("lat") * lat_rows
    lat_total = lax.axis_size("lat") * lat_rows
    level_pos = jnp.arange(levels, dtype=jnp.int32)[:, None, None]
    lat_pos = lat_start + jnp.arange(lat_rows, dtype=jnp.int32)[None, :, None]
    labels = 4 * region_ids + (
        2 * (level_pos >= levels - WZ // 2).astype(jnp.int32)
        + (lat_pos >= lat_total - half).astype(jnp.int32)
    )
    labels = labels.reshape(2, WZ, WLAT, 2, WLON).transpose(0, 3, 4, 1, 2).reshape(4, POS)
    label_row = jnp.tile(labels, (1, HEADS)).reshape(4, 1, ROWS)
    label_col = labels.T
    factor = (keep_flags.astype(f32) / keep_share).reshape(4)

    perm = window_order()
    head_mask = np.repeat(np.eye(HEADS, dtype=np.float32), HD, axis=1)
    table_perm = jnp.asarray(table_order(), bf16)
    bias_wide = pl.pallas_call(
        expand_kernel,
        out_shape=jax.ShapeDtypeStruct((2, POS, ROWS), f32),
        in_specs=[vmem] * 3,
        out_specs=vmem,
        scratch_shapes=[
            pltpu.VMEM((2 * HEADS, PAIR * TAB), f32),
            pltpu.VMEM((PAIR * SLOTS, TAB), f32),
            pltpu.VMEM((2 * HEADS, POS, POS), f32),
        ],
        compiler_params=pltpu.CompilerParams(vmem_limit_bytes=32 * 1024 * 1024),
        name="expand",
    )(
        bias_table.reshape(2 * HEADS, 1, PAIR * TAB),
        table_perm,
        jnp.asarray(row_order(), bf16),
    )
    positions = levels * lat_rows * lon_cols
    weights_t = w_qkv.T
    gain1 = ln1_gain.reshape(1, C)
    head_mask = jnp.asarray(head_mask, bf16)
    fold, *saved = pl.pallas_call(
        scores_kernel,
        out_shape=(
            jax.ShapeDtypeStruct((4, QUARTER, TAB), bf16),
            jax.ShapeDtypeStruct((positions, C), bf16),
            jax.ShapeDtypeStruct((positions, C), bf16),
            jax.ShapeDtypeStruct((4, C, POS), bf16),
            jax.ShapeDtypeStruct((4, POS, ROWS), bf16),
            jax.ShapeDtypeStruct((4, POS, ROWS), bf16),
            jax.ShapeDtypeStruct((positions, C), bf16),
            jax.ShapeDtypeStruct((positions, C), f32),
            jax.ShapeDtypeStruct((positions, C), bf16),
        ),
        in_specs=[vmem] * 14 + [smem] + [vmem] * 4,
        out_specs=(vmem,) * 9,
        scratch_shapes=[
            pltpu.VMEM((2, positions, C), f32),
            pltpu.VMEM((HEADS, POS, POS), f32),
        ],
        compiler_params=pltpu.CompilerParams(vmem_limit_bytes=48 * 1024 * 1024),
        name="scores",
    )(
        field_in,
        cotangent,
        lon_part,
        lat_part,
        diag_part,
        gain1,
        weights_t,
        w_proj,
        ln2_gain.reshape(1, C),
        w_up,
        w_down.T,
        bias_wide,
        label_row,
        label_col,
        factor,
        jnp.asarray(perm, bf16),
        head_mask,
        table_perm,
        jnp.asarray(chunk_order(), bf16),
    )
    own, lat_back, diag_back, lon_back = pl.pallas_call(
        inputs_kernel,
        out_shape=(jax.ShapeDtypeStruct((2, levels, half, inner, C), bf16),) + packed,
        in_specs=[vmem] * 12,
        out_specs=(vmem,) * 4,
        scratch_shapes=buffers,
        compiler_params=pltpu.CompilerParams(vmem_limit_bytes=32 * 1024 * 1024),
        cost_estimate=pl.CostEstimate(
            flops=1_000_000_000, bytes_accessed=8_000_000, transcendentals=0
        ),
        name="inputs",
    )(*saved, gain1, weights_t, jnp.asarray(perm.T, bf16), head_mask)
    lat_back = shifted(lat_back, 1, 0)
    diag_back = shifted(diag_back, 1, 1)
    lon_back = shifted(lon_back, 0, 1)
    grads = pl.pallas_call(
        unpack_kernel,
        out_shape=jax.ShapeDtypeStruct((2 * HEADS, 1, PAIR * TAB), f32),
        in_specs=[vmem],
        out_specs=vmem,
        scratch_shapes=[pltpu.VMEM((2 * HEADS, PAIR * TAB), f32)],
        name="unpack",
    )(lon_sum(fold))
    grads = grads.reshape(2, 1, HEADS, PAIR * TAB)
    result, grad_field = pl.pallas_call(
        finish_kernel,
        out_shape=(jax.ShapeDtypeStruct(field_in.shape, bf16),) * 2,
        in_specs=[vmem] * 4,
        out_specs=(vmem,) * 2,
        name="finish",
    )(own, lat_back, diag_back, lon_back)
    return (result, grad_field, grads)


def solution(mesh):
    placed = (
        P(None, "lat", "lon", None),
        P(None, "lat", "lon", None),
        P(),
        P(),
        P(),
        P(),
        P(),
        P(),
        P(None, "lat", None, None),
        P(None, "lat", "lon"),
        P(None, "lat", "lon"),
    )
    return jax.shard_map(
        body,
        mesh=mesh,
        in_specs=placed,
        out_specs=(
            P(None, "lat", "lon", None),
            P(None, "lat", "lon", None),
            P(None, "lat", None, None),
        ),
        check_vma=False,
    )
```

```python
import math

import jax
import jax.numpy as jnp
import numpy as np
from jax import lax
from jax.experimental import pallas as pl
from jax.experimental.pallas import tpu as pltpu
from jax.sharding import PartitionSpec as P

C = 192
HEADS = 6
HD = 32
FF = 768
WZ = 2
WLAT = 6
WLON = 12
SPREAD = 2 * WLON - 1
POS = WZ * WLAT * WLON
PAIR = WZ * WLAT
TAB = PAIR * SPREAD
ROWS = HEADS * POS
SLOTS = 16
QUARTER = PAIR * HEADS // 2
LANES = 128

epsilon = 1e-05
keep_share = 0.8
LOG2E = math.log2(math.e)
gelu_coef = 0.044715
VMEM_BYTES = 16 * 1024 * 1024
bf16 = jnp.bfloat16
f32 = jnp.float32


def shifted(block, lat_step, lon_step):
    lats, lons = lax.axis_size("lat"), lax.axis_size("lon")
    route = []
    for a in range(lats):
        for b in range(lons):
            target = ((a + lat_step) % lats) * lons + (b + lon_step) % lons
            route.append((a * lons + b, target))
    return lax.ppermute(block, ("lat", "lon"), route)


def mm(a, b):
    return lax.dot_general(a, b, (((1,), (0,)), ((), ())), preferred_element_type=f32)


def mm_nt(a, b):
    return lax.dot_general(a, b, (((1,), (1,)), ((), ())), preferred_element_type=f32)


def norm_parts(values, gain):
    row_mean = jnp.mean(values, axis=-1, keepdims=True)
    centred = values - row_mean
    variance = jnp.mean(centred * centred, axis=-1, keepdims=True)
    inverse = lax.rsqrt(variance + epsilon)
    normed = centred * inverse
    return normed * gain, normed, inverse


def norm_back(grad_in, gain, normed, inverse):
    scaled = grad_in * gain
    first_mean = jnp.mean(scaled, axis=-1, keepdims=True)
    second_mean = jnp.mean(scaled * normed, axis=-1, keepdims=True)
    return (scaled - first_mean - normed * second_mean) * inverse


def gelu_parts(values):
    factor = math.sqrt(2.0 / math.pi)
    square = values * values
    tangent = jnp.tanh(values * (factor + (gelu_coef * factor) * square))
    half = 0.5 + 0.5 * tangent
    result = values * half
    derivative = half + result * (1.0 - tangent) * (factor + (3.0 * gelu_coef * factor) * square)
    return result, derivative


def head_blocks(wide):
    return jnp.concatenate(
        [wide[h * HD : (h + 1) * HD, h * POS : (h + 1) * POS] for h in range(HEADS)], axis=0
    )


def spread_heads(rows, head_mask):
    return jnp.concatenate([rows * head_mask[h : h + 1, :] for h in range(HEADS)], axis=0)


def put(packed, t, row, slab):
    third = packed.shape[0] // 3
    size = slab.shape[0]
    rest = C - LANES
    packed[t * third + row : t * third + row + size, :] = slab[:, :LANES]
    packed[2 * third + row : 2 * third + row + size, t * rest : (t + 1) * rest] = slab[:, LANES:]


def get(packed, t, row, size):
    third = packed.shape[0] // 3
    rest = C - LANES
    return (
        packed[t * third + row : t * third + row + size, :],
        packed[2 * third + row : 2 * third + row + size, t * rest : (t + 1) * rest],
    )


def pack_lat_kernel(field_ref, cot_ref, lat_out, lat_buf):
    half = WLAT // 2
    edge = WLON // 2
    inner = 2 * WLON - edge
    for t, source in enumerate((field_ref, cot_ref)):
        for z in range(4):
            for i in range(half):
                put(lat_buf, t, (z * half + i) * inner, source[z, i].astype(f32)[edge:])
    lat_out[...] = lat_buf[...].astype(bf16)


def pack_edge_kernel(field_ref, cot_ref, after_ref, diag_out, lon_out, diag_buf, lon_buf):
    half = WLAT // 2
    edge = WLON // 2
    for t, source in enumerate((field_ref, cot_ref)):
        for z in range(4):
            for i in range(half):
                row = (z * half + i) * edge
                put(diag_buf, t, row, source[z, i].astype(f32)[:edge])
                put(lon_buf, t, row, source[z, half + i].astype(f32)[:edge])
    diag_out[...] = diag_buf[...].astype(bf16)
    lon_out[...] = lon_buf[...].astype(bf16)


def scores_kernel(
    field_ref,
    cot_ref,
    lon_ref,
    lat_ref,
    diag_ref,
    gain1_ref,
    wqkv_t_ref,
    wproj_ref,
    gain2_ref,
    wup_ref,
    wdown_t_ref,
    bias_ref,
    label_row_ref,
    label_col_ref,
    factor_ref,
    perm_ref,
    head_mask_ref,
    table_perm_ref,
    chunk_perm_ref,
    fold_out,
    x_out,
    q_out,
    kt_out,
    probs_out,
    grad_low_out,
    grad_att_out,
    grad_sum_out,
    result_out,
    frame,
    wide,
):
    half = WLAT // 2
    cols = 2 * WLON
    edge = WLON // 2
    inner = cols - edge
    root = 1.0 / math.sqrt(HD)
    lon_part = lon_ref[...].astype(f32)
    lat_part = lat_ref[...].astype(f32)
    diag_part = diag_ref[...].astype(f32)
    for t, own in enumerate((field_ref, cot_ref)):
        for level in range(4):
            z = (level + 1) % 4
            for i in range(half):
                k = z * half + i
                row = (level * WLAT + i) * cols
                frame[t, row : row + inner, :] = own[z, half + i].astype(f32)[edge:, :]
                main, rest = get(lon_part, t, k * edge, edge)
                frame[t, row + inner : row + cols, :LANES] = main
                frame[t, row + inner : row + cols, LANES:] = rest
                row = (level * WLAT + half + i) * cols
                main, rest = get(lat_part, t, k * inner, inner)
                frame[t, row : row + inner, :LANES] = main
                frame[t, row : row + inner, LANES:] = rest
                main, rest = get(diag_part, t, k * edge, edge)
                frame[t, row + inner : row + cols, :LANES] = main
                frame[t, row + inner : row + cols, LANES:] = rest
    gain1 = gain1_ref[...]
    gain2 = gain2_ref[...]
    wq_t = wqkv_t_ref[0:C, :]
    wk_t = wqkv_t_ref[C : 2 * C, :]
    wv_t = wqkv_t_ref[2 * C : 3 * C, :]
    head_mask = head_mask_ref[...]
    perm = perm_ref[...]
    for n in range(2):
        both = slice(n * 2 * POS, (n + 1) * 2 * POS)
        x = mm(perm, frame[0, both, :].astype(bf16))
        cot = mm(perm, frame[1, both, :].astype(bf16))
        x_out[both, :] = x.astype(bf16)
        h1 = norm_parts(x, gain1)[0].astype(bf16)
        q_all = mm_nt(h1, wq_t).astype(bf16)
        k_all = mm_nt(h1, wk_t).astype(bf16)
        v_all = mm_nt(h1, wv_t).astype(bf16)
        q_out[both, :] = q_all
        saved = []
        branches = []
        for c in range(2):
            w = 2 * n + c
            rows = slice(c * POS, (c + 1) * POS)
            v_t = mm_nt(wv_t, h1[rows]).astype(bf16)
            kt_out[w] = mm_nt(wk_t, h1[rows]).astype(bf16)
            q_wide = spread_heads(q_all[rows], head_mask)
            scores = mm_nt(k_all[rows], q_wide) * (root * LOG2E) + bias_ref[n]
            allowed = label_col_ref[:, w : w + 1] == label_row_ref[w]
            scores = jnp.where(allowed, scores, -1e30)
            weights = jnp.exp2(scores - jnp.max(scores, axis=0, keepdims=True))
            probs = weights * (1.0 / jnp.sum(weights, axis=0, keepdims=True))
            probs_low = probs.astype(bf16)
            probs_out[w] = probs_low
            attended = head_blocks(mm(v_t, probs_low)).T.astype(bf16)
            factor = factor_ref[w]
            branches.append((mm(attended, wproj_ref[...]) * factor).astype(bf16).astype(f32))
            saved.append(probs)
        y_sum = x + jnp.concatenate(branches, axis=0)
        scaled2, normed2, inverse2 = norm_parts(y_sum, gain2)
        act, slope = gelu_parts(mm(scaled2.astype(bf16), wup_ref[...]))
        result_out[both, :] = (y_sum + mm_nt(act.astype(bf16), wdown_t_ref[...])).astype(bf16)
        grad_up = (mm(cot.astype(bf16), wdown_t_ref[...]) * slope).astype(bf16)
        grad_sum = cot + norm_back(mm_nt(grad_up, wup_ref[...]), gain2, normed2, inverse2)
        grad_sum_out[both, :] = grad_sum
        grad_low_in = grad_sum.astype(bf16).astype(f32)
        folded = None
        for c in range(2):
            w = 2 * n + c
            rows = slice(c * POS, (c + 1) * POS)
            probs = saved[c]
            grad_branch = (grad_low_in[rows] * factor_ref[w]).astype(bf16)
            grad_att = mm_nt(grad_branch, wproj_ref[...]).astype(bf16)
            grad_att_out[w * POS : (w + 1) * POS, :] = grad_att
            grad_probs = mm_nt(v_all[rows], spread_heads(grad_att, head_mask))
            inner_sum = jnp.sum(probs * grad_probs, axis=0, keepdims=True)
            grad_scores = probs * (grad_probs - inner_sum)
            folded = grad_scores if folded is None else folded + grad_scores
            grad_low_out[w] = grad_scores.astype(bf16)
        wide[...] = folded.T.reshape(HEADS, POS, POS)
        total = None
        for o in range(WLON):
            left = PAIR * (WLON - 1 - o)
            right = TAB - POS - left
            parts = [wide[:, PAIR * o : PAIR * (o + 1), :]]
            if left:
                parts = [jnp.zeros((HEADS, PAIR, left), f32)] + parts
            if right:
                parts = parts + [jnp.zeros((HEADS, PAIR, right), f32)]
            piece = jnp.concatenate(parts, axis=2)
            total = piece if total is None else total + piece
        total = jnp.concatenate([total, jnp.zeros((HEADS, SLOTS - PAIR, TAB), f32)], axis=1)
        total = total.reshape(HEADS * SLOTS, TAB).astype(bf16)
        total = mm_nt(total, table_perm_ref[...]).astype(bf16)
        total = mm(chunk_perm_ref[...], total)
        fold_out[2 * n] = total[:QUARTER].astype(bf16)
        fold_out[2 * n + 1] = total[QUARTER:].astype(bf16)


def inputs_kernel(
    x_ref,
    q_ref,
    kt_ref,
    probs_ref,
    grad_low_ref,
    grad_att_ref,
    grad_sum_ref,
    result_ref,
    gain1_ref,
    wqkv_t_ref,
    perm_t_ref,
    head_mask_ref,
    own_out,
    lat_out,
    diag_out,
    lon_out,
    lat_buf,
    diag_buf,
    lon_buf,
):
    half = WLAT // 2
    cols = 2 * WLON
    edge = WLON // 2
    inner = cols - edge
    root = 1.0 / math.sqrt(HD)
    gain1 = gain1_ref[...]
    wq_t = wqkv_t_ref[0:C, :]
    wk_t = wqkv_t_ref[C : 2 * C, :]
    wv_t = wqkv_t_ref[2 * C : 3 * C, :]
    head_mask = head_mask_ref[...]
    perm_t = perm_t_ref[...]
    for n in range(2):
        both = slice(n * 2 * POS, (n + 1) * 2 * POS)
        _, normed1, inverse1 = norm_parts(x_ref[both, :].astype(f32), gain1)
        grad_h1 = []
        for c in range(2):
            w = 2 * n + c
            rows = slice(w * POS, (w + 1) * POS)
            grad_low = grad_low_ref[w]
            q_wide = spread_heads(q_ref[rows, :], head_mask)
            g_wide = spread_heads(grad_att_ref[rows, :], head_mask)
            grad_q = (head_blocks(mm(kt_ref[w], grad_low)).T * root).astype(bf16)
            grad_k = (mm(grad_low, q_wide) * root).astype(bf16)
            grad_v = mm(probs_ref[w], g_wide).astype(bf16)
            grad_h1.append(mm(grad_q, wq_t) + mm(grad_k, wk_t) + mm(grad_v, wv_t))
        grad_h1 = jnp.concatenate(grad_h1, axis=0).astype(bf16).astype(f32)
        grad_sum = grad_sum_ref[both, :]
        grad_field = (grad_sum + norm_back(grad_h1, gain1, normed1, inverse1)).astype(bf16)
        for t, value in enumerate((result_ref[both, :], grad_field)):
            natural = mm(perm_t, value)
            for dz in range(WZ):
                z = (2 * n + dz + 1) % 4
                for i in range(half):
                    k = z * half + i
                    row = (dz * WLAT + i) * cols
                    slab = natural[row : row + cols]
                    own_out[t, z, i] = slab[:inner].astype(bf16)
                    put(lon_buf, t, k * edge, slab[inner:])
                    row = (dz * WLAT + half + i) * cols
                    slab = natural[row : row + cols]
                    put(lat_buf, t, k * inner, slab[:inner])
                    put(diag_buf, t, k * edge, slab[inner:])
    lat_out[...] = lat_buf[...].astype(bf16)
    diag_out[...] = diag_buf[...].astype(bf16)
    lon_out[...] = lon_buf[...].astype(bf16)


def expand_kernel(table_ref, table_perm_ref, row_perm_ref, bias_out, flat, rows, wide):
    part = PAIR // WZ * SPREAD
    for k in range(2 * HEADS):
        flat[k : k + 1, :] = table_ref[k]
    rows[...] = jnp.zeros_like(rows)
    for a in range(WZ):
        for c in range(WLAT):
            pieces = []
            for b in range(WZ):
                start = ((a * WZ + b) * WLAT + c) * part
                pieces.append(flat[:, start : start + part])
            row = (a * WLAT + c) * SLOTS
            rows[row : row + 2 * HEADS, :] = jnp.concatenate(pieces, axis=1)
    left = rows[...]
    perm = table_perm_ref[...]
    total = None
    for _ in range(3):
        low = left.astype(bf16)
        left = left - low.astype(f32)
        term = mm(row_perm_ref[...], mm(low, perm).astype(bf16))
        total = term if total is None else total + term
    total = total.reshape(2 * HEADS, SLOTS, TAB)
    for o in range(WLON):
        start = PAIR * (WLON - 1 - o)
        wide[:, PAIR * o : PAIR * (o + 1), :] = total[:, :PAIR, start : start + POS]
    for n in range(2):
        bias_out[n] = wide[n * HEADS : (n + 1) * HEADS].reshape(ROWS, POS).T * LOG2E


def unpack_kernel(grad_ref, table_out, flat):
    part = PAIR // WZ * SPREAD
    for n in range(2):
        halves = [grad_ref[2 * n + k].astype(f32) for k in range(2)]
        for a in range(WZ):
            for c in range(WLAT):
                row = c * HEADS
                chunk = halves[a][row : row + HEADS]
                for b in range(WZ):
                    start = ((a * WZ + b) * WLAT + c) * part
                    flat[n * HEADS : (n + 1) * HEADS, start : start + part] = chunk[
                        :, b * part : (b + 1) * part
                    ]
    for k in range(2 * HEADS):
        table_out[k] = flat[k : k + 1, :]


def finish_kernel(own_ref, lat_ref, diag_ref, lon_ref, out_ref, grad_ref):
    half = WLAT // 2
    edge = WLON // 2
    inner = 2 * WLON - edge
    lat_part = lat_ref[...].astype(f32)
    diag_part = diag_ref[...].astype(f32)
    lon_part = lon_ref[...].astype(f32)
    for t, target in enumerate((out_ref, grad_ref)):
        for z in range(4):
            for i in range(half):
                k = z * half + i
                parts = (get(diag_part, t, k * edge, edge), get(lat_part, t, k * inner, inner))
                slab = [jnp.concatenate([parts[0][j], parts[1][j]], axis=0) for j in range(2)]
                target[z, i] = jnp.concatenate(slab, axis=1).astype(bf16)
                slab = jnp.concatenate(get(lon_part, t, k * edge, edge), axis=1)
                own = own_ref[t, z, i].astype(f32)
                target[z, half + i] = jnp.concatenate([slab, own], axis=0).astype(bf16)


def window_order():
    perm = np.zeros((2 * POS, 2 * POS), np.float32)
    for c in range(2):
        for j in range(WLON):
            for d in range(PAIR):
                perm[c * POS + j * PAIR + d, d * 2 * WLON + c * WLON + j] = 1.0
    return perm


def table_order():
    perm = np.zeros((TAB, TAB), np.float32)
    for d in range(PAIR):
        for r in range(SPREAD):
            perm[d * SPREAD + r, (SPREAD - 1 - r) * PAIR + d] = 1.0
    return perm


def chunk_order():
    perm = np.zeros((PAIR * HEADS, HEADS * SLOTS), np.float32)
    for h in range(HEADS):
        for k in range(PAIR):
            perm[k * HEADS + h, h * SLOTS + k] = 1.0
    return perm


def row_order():
    perm = np.zeros((2 * HEADS * SLOTS, PAIR * SLOTS), np.float32)
    for h in range(2 * HEADS):
        for k in range(PAIR):
            perm[h * SLOTS + k, k * SLOTS + h] = 1.0
    return perm


def lon_sum(quarters):
    lons = lax.axis_size("lon")
    near = [[4 * k + j for j in range(4)] for k in range(lons // 4)]
    far = [[4 * k + j for k in range(lons // 4)] for j in range(4)]

    def exchange(parts, groups):
        return lax.all_to_all(parts, "lon", 0, 0, axis_index_groups=groups)

    def total(parts):
        return jnp.sum(parts.astype(f32), axis=0).astype(bf16)

    def copies(part, count):
        return jnp.broadcast_to(part, (count,) + part.shape)

    quarter = total(exchange(quarters, near))
    quarter = total(exchange(copies(quarter, lons // 4), far))
    return exchange(copies(quarter, 4), near)


def body(
    field_in,
    cotangent,
    ln1_gain,
    w_qkv,
    w_proj,
    ln2_gain,
    w_up,
    w_down,
    bias_table,
    region_ids,
    keep_flags,
):
    levels, lat_rows, lon_cols, channels = field_in.shape
    half = WLAT // 2
    edge = WLON // 2
    inner = lon_cols - edge
    vmem = pl.BlockSpec(memory_space=pltpu.VMEM)
    smem = pl.BlockSpec(memory_space=pltpu.SMEM)
    sizes = [3 * levels * half * size for size in (inner, edge, edge)]
    packed = tuple(jax.ShapeDtypeStruct((size, LANES), bf16) for size in sizes)
    buffers = [pltpu.VMEM((size, LANES), f32) for size in sizes]
    params = pltpu.CompilerParams(vmem_limit_bytes=VMEM_BYTES)
    lat_part = pl.pallas_call(
        pack_lat_kernel,
        out_shape=packed[0],
        in_specs=[vmem] * 2,
        out_specs=vmem,
        scratch_shapes=buffers[:1],
        compiler_params=params,
        name="pack_lat",
    )(field_in, cotangent)
    diag_part, lon_part = pl.pallas_call(
        pack_edge_kernel,
        out_shape=packed[1:],
        in_specs=[vmem] * 2 + [pl.BlockSpec(memory_space=pl.ANY)],
        out_specs=(vmem,) * 2,
        scratch_shapes=buffers[1:],
        compiler_params=params,
        name="pack_edge",
    )(field_in, cotangent, lat_part)
    lat_part = shifted(lat_part, -1, 0)
    diag_part = shifted(diag_part, -1, -1)
    lon_part = shifted(lon_part, 0, -1)

    lat_start = lax.axis_index("lat") * lat_rows
    lat_total = lax.axis_size("lat") * lat_rows
    level_pos = jnp.arange(levels, dtype=jnp.int32)[:, None, None]
    lat_pos = lat_start + jnp.arange(lat_rows, dtype=jnp.int32)[None, :, None]
    labels = 4 * region_ids + (
        2 * (level_pos >= levels - WZ // 2).astype(jnp.int32)
        + (lat_pos >= lat_total - half).astype(jnp.int32)
    )
    labels = labels.reshape(2, WZ, WLAT, 2, WLON).transpose(0, 3, 4, 1, 2).reshape(4, POS)
    label_row = jnp.tile(labels, (1, HEADS)).reshape(4, 1, ROWS)
    label_col = labels.T
    factor = (keep_flags.astype(f32) / keep_share).reshape(4)

    perm = window_order()
    head_mask = np.repeat(np.eye(HEADS, dtype=np.float32), HD, axis=1)
    table_perm = jnp.asarray(table_order(), bf16)
    bias_wide = pl.pallas_call(
        expand_kernel,
        out_shape=jax.ShapeDtypeStruct((2, POS, ROWS), f32),
        in_specs=[vmem] * 3,
        out_specs=vmem,
        scratch_shapes=[
            pltpu.VMEM((2 * HEADS, PAIR * TAB), f32),
            pltpu.VMEM((PAIR * SLOTS, TAB), f32),
            pltpu.VMEM((2 * HEADS, POS, POS), f32),
        ],
        compiler_params=params,
        name="expand",
    )(
        bias_table.reshape(2 * HEADS, 1, PAIR * TAB),
        table_perm,
        jnp.asarray(row_order(), bf16),
    )
    positions = levels * lat_rows * lon_cols
    weights_t = w_qkv.T
    gain1 = ln1_gain.reshape(1, C)
    head_mask = jnp.asarray(head_mask, bf16)
    fold, *saved = pl.pallas_call(
        scores_kernel,
        out_shape=(
            jax.ShapeDtypeStruct((4, QUARTER, TAB), bf16),
            jax.ShapeDtypeStruct((positions, C), bf16),
            jax.ShapeDtypeStruct((positions, C), bf16),
            jax.ShapeDtypeStruct((4, C, POS), bf16),
            jax.ShapeDtypeStruct((4, POS, ROWS), bf16),
            jax.ShapeDtypeStruct((4, POS, ROWS), bf16),
            jax.ShapeDtypeStruct((positions, C), bf16),
            jax.ShapeDtypeStruct((positions, C), f32),
            jax.ShapeDtypeStruct((positions, C), bf16),
        ),
        in_specs=[vmem] * 14 + [smem] + [vmem] * 4,
        out_specs=(vmem,) * 9,
        scratch_shapes=[
            pltpu.VMEM((2, positions, C), f32),
            pltpu.VMEM((HEADS, POS, POS), f32),
        ],
        compiler_params=params,
        name="scores",
    )(
        field_in,
        cotangent,
        lon_part,
        lat_part,
        diag_part,
        gain1,
        weights_t,
        w_proj,
        ln2_gain.reshape(1, C),
        w_up,
        w_down.T,
        bias_wide,
        label_row,
        label_col,
        factor,
        jnp.asarray(perm, bf16),
        head_mask,
        table_perm,
        jnp.asarray(chunk_order(), bf16),
    )
    own, lat_back, diag_back, lon_back = pl.pallas_call(
        inputs_kernel,
        out_shape=(jax.ShapeDtypeStruct((2, levels, half, inner, C), bf16),) + packed,
        in_specs=[vmem] * 12,
        out_specs=(vmem,) * 4,
        scratch_shapes=buffers,
        compiler_params=params,
        cost_estimate=pl.CostEstimate(
            flops=1_000_000_000, bytes_accessed=8_000_000, transcendentals=0
        ),
        name="inputs",
    )(*saved, gain1, weights_t, jnp.asarray(perm.T, bf16), head_mask)
    lat_back = shifted(lat_back, 1, 0)
    diag_back = shifted(diag_back, 1, 1)
    lon_back = shifted(lon_back, 0, 1)
    grads = pl.pallas_call(
        unpack_kernel,
        out_shape=jax.ShapeDtypeStruct((2 * HEADS, 1, PAIR * TAB), f32),
        in_specs=[vmem],
        out_specs=vmem,
        scratch_shapes=[pltpu.VMEM((2 * HEADS, PAIR * TAB), f32)],
        compiler_params=params,
        name="unpack",
    )(lon_sum(fold))
    grads = grads.reshape(2, 1, HEADS, PAIR * TAB)
    result, grad_field = pl.pallas_call(
        finish_kernel,
        out_shape=(jax.ShapeDtypeStruct(field_in.shape, bf16),) * 2,
        in_specs=[vmem] * 4,
        out_specs=(vmem,) * 2,
        compiler_params=params,
        name="finish",
    )(own, lat_back, diag_back, lon_back)
    return (result, grad_field, grads)


def solution(mesh):
    placed = (
        P(None, "lat", "lon", None),
        P(None, "lat", "lon", None),
        P(),
        P(),
        P(),
        P(),
        P(),
        P(),
        P(None, "lat", None, None),
        P(None, "lat", "lon"),
        P(None, "lat", "lon"),
    )
    return jax.shard_map(
        body,
        mesh=mesh,
        in_specs=placed,
        out_specs=(
            P(None, "lat", "lon", None),
            P(None, "lat", "lon", None),
            P(None, "lat", None, None),
        ),
        check_vma=False,
    )
```

```python
import math

import jax
import jax.numpy as jnp
import numpy as np
from jax import lax
from jax.experimental import pallas as pl
from jax.experimental.pallas import tpu as pltpu
from jax.sharding import PartitionSpec as P

C = 192
HEADS = 6
HD = 32
FF = 768
WZ = 2
WLAT = 6
WLON = 12
SPREAD = 2 * WLON - 1
POS = WZ * WLAT * WLON
PAIR = WZ * WLAT
TAB = PAIR * SPREAD
ROWS = HEADS * POS
SLOTS = 16
QUARTER = PAIR * HEADS // 2
LANES = 128

epsilon = 1e-05
keep_share = 0.8
LOG2E = math.log2(math.e)
gelu_coef = 0.044715
VMEM_BYTES = 16 * 1024 * 1024
bf16 = jnp.bfloat16
f32 = jnp.float32


def shifted(block, lat_step, lon_step):
    lats, lons = lax.axis_size("lat"), lax.axis_size("lon")
    route = []
    for a in range(lats):
        for b in range(lons):
            target = ((a + lat_step) % lats) * lons + (b + lon_step) % lons
            route.append((a * lons + b, target))
    return lax.ppermute(block, ("lat", "lon"), route)


def mm(a, b):
    return lax.dot_general(a, b, (((1,), (0,)), ((), ())), preferred_element_type=f32)


def mm_nt(a, b):
    return lax.dot_general(a, b, (((1,), (1,)), ((), ())), preferred_element_type=f32)


def norm_parts(values, gain):
    row_mean = jnp.mean(values, axis=-1, keepdims=True)
    centred = values - row_mean
    variance = jnp.mean(centred * centred, axis=-1, keepdims=True)
    inverse = lax.rsqrt(variance + epsilon)
    normed = centred * inverse
    return normed * gain, normed, inverse


def norm_back(grad_in, gain, normed, inverse):
    scaled = grad_in * gain
    first_mean = jnp.mean(scaled, axis=-1, keepdims=True)
    second_mean = jnp.mean(scaled * normed, axis=-1, keepdims=True)
    return (scaled - first_mean - normed * second_mean) * inverse


def gelu_parts(values):
    factor = math.sqrt(2.0 / math.pi)
    square = values * values
    tangent = jnp.tanh(values * (factor + (gelu_coef * factor) * square))
    half = 0.5 + 0.5 * tangent
    result = values * half
    derivative = half + result * (1.0 - tangent) * (factor + (3.0 * gelu_coef * factor) * square)
    return result, derivative


def head_blocks(wide):
    return jnp.concatenate(
        [wide[h * HD : (h + 1) * HD, h * POS : (h + 1) * POS] for h in range(HEADS)], axis=0
    )


def spread_heads(rows, head_mask):
    return jnp.concatenate([rows * head_mask[h : h + 1, :] for h in range(HEADS)], axis=0)


def put(packed, t, row, slab):
    third = packed.shape[0] // 3
    size = slab.shape[0]
    rest = C - LANES
    packed[t * third + row : t * third + row + size, :] = slab[:, :LANES]
    packed[2 * third + row : 2 * third + row + size, t * rest : (t + 1) * rest] = slab[:, LANES:]


def get(packed, t, row, size):
    third = packed.shape[0] // 3
    rest = C - LANES
    return (
        packed[t * third + row : t * third + row + size, :],
        packed[2 * third + row : 2 * third + row + size, t * rest : (t + 1) * rest],
    )


def pack_lat_kernel(field_ref, cot_ref, lat_out, lat_buf, rows, arrived):
    half = WLAT // 2
    edge = WLON // 2
    inner = 2 * WLON - edge
    sources = (field_ref, cot_ref)
    copies = [
        pltpu.make_async_copy(sources[t].at[:, pl.ds(0, half)], rows.at[t], arrived.at[t])
        for t in range(2)
    ]
    for copy in copies:
        copy.start()
    for t in range(2):
        copies[t].wait()
        for z in range(4):
            for i in range(half):
                put(lat_buf, t, (z * half + i) * inner, rows[t, z, i].astype(f32)[edge:])
    lat_out[...] = lat_buf[...].astype(bf16)


def pack_edge_kernel(field_ref, cot_ref, after_ref, diag_out, lon_out, diag_buf, lon_buf):
    half = WLAT // 2
    edge = WLON // 2
    for t, source in enumerate((field_ref, cot_ref)):
        for z in range(4):
            for i in range(half):
                row = (z * half + i) * edge
                put(diag_buf, t, row, source[z, i].astype(f32)[:edge])
                put(lon_buf, t, row, source[z, half + i].astype(f32)[:edge])
    diag_out[...] = diag_buf[...].astype(bf16)
    lon_out[...] = lon_buf[...].astype(bf16)


def scores_kernel(
    field_ref,
    cot_ref,
    lon_ref,
    lat_ref,
    diag_ref,
    gain1_ref,
    wqkv_t_ref,
    wproj_ref,
    gain2_ref,
    wup_ref,
    wdown_t_ref,
    bias_ref,
    label_row_ref,
    label_col_ref,
    keep_ref,
    perm_ref,
    head_mask_ref,
    table_perm_ref,
    chunk_perm_ref,
    fold_out,
    x_out,
    probs_out,
    grad_low_out,
    grad_sum_out,
    result_out,
    frame,
    wide,
):
    half = WLAT // 2
    cols = 2 * WLON
    edge = WLON // 2
    inner = cols - edge
    root = 1.0 / math.sqrt(HD)
    lon_part = lon_ref[...].astype(f32)
    lat_part = lat_ref[...].astype(f32)
    diag_part = diag_ref[...].astype(f32)
    for t, own in enumerate((field_ref, cot_ref)):
        for level in range(4):
            z = (level + 1) % 4
            for i in range(half):
                k = z * half + i
                row = (level * WLAT + i) * cols
                frame[t, row : row + inner, :] = own[z, half + i].astype(f32)[edge:, :]
                main, rest = get(lon_part, t, k * edge, edge)
                frame[t, row + inner : row + cols, :LANES] = main
                frame[t, row + inner : row + cols, LANES:] = rest
                row = (level * WLAT + half + i) * cols
                main, rest = get(lat_part, t, k * inner, inner)
                frame[t, row : row + inner, :LANES] = main
                frame[t, row : row + inner, LANES:] = rest
                main, rest = get(diag_part, t, k * edge, edge)
                frame[t, row + inner : row + cols, :LANES] = main
                frame[t, row + inner : row + cols, LANES:] = rest
    gain1 = gain1_ref[...]
    gain2 = gain2_ref[...]
    wq_t = wqkv_t_ref[0:C, :]
    wk_t = wqkv_t_ref[C : 2 * C, :]
    wv_t = wqkv_t_ref[2 * C : 3 * C, :]
    head_mask = head_mask_ref[...]
    perm = perm_ref[...]
    for n in range(2):
        both = slice(n * 2 * POS, (n + 1) * 2 * POS)
        x = mm(perm, frame[0, both, :].astype(bf16))
        cot = mm(perm, frame[1, both, :].astype(bf16))
        x_out[both, :] = x.astype(bf16)
        h1 = norm_parts(x, gain1)[0].astype(bf16)
        q_all = mm_nt(h1, wq_t).astype(bf16)
        k_all = mm_nt(h1, wk_t).astype(bf16)
        v_all = mm_nt(h1, wv_t).astype(bf16)
        saved = []
        branches = []
        for c in range(2):
            w = 2 * n + c
            rows = slice(c * POS, (c + 1) * POS)
            v_t = mm_nt(wv_t, h1[rows]).astype(bf16)
            q_wide = spread_heads(q_all[rows], head_mask)
            scores = mm_nt(k_all[rows], q_wide) * (root * LOG2E) + bias_ref[n]
            allowed = label_col_ref[:, w : w + 1] == label_row_ref[w : w + 1, :]
            scores = jnp.where(allowed, scores, -1e30)
            weights = jnp.exp2(scores - jnp.max(scores, axis=0, keepdims=True))
            probs = weights * (1.0 / jnp.sum(weights, axis=0, keepdims=True))
            probs_low = probs.astype(bf16)
            probs_out[w] = probs_low
            attended = head_blocks(mm(v_t, probs_low)).T.astype(bf16)
            factor = keep_ref[n, 0, c].astype(f32) * (1.0 / keep_share)
            branches.append((mm(attended, wproj_ref[...]) * factor).astype(bf16).astype(f32))
            saved.append(probs)
        y_sum = x + jnp.concatenate(branches, axis=0)
        scaled2, normed2, inverse2 = norm_parts(y_sum, gain2)
        act, slope = gelu_parts(mm(scaled2.astype(bf16), wup_ref[...]))
        result_out[both, :] = (y_sum + mm_nt(act.astype(bf16), wdown_t_ref[...])).astype(bf16)
        grad_up = (mm(cot.astype(bf16), wdown_t_ref[...]) * slope).astype(bf16)
        grad_sum = cot + norm_back(mm_nt(grad_up, wup_ref[...]), gain2, normed2, inverse2)
        grad_sum_out[both, :] = grad_sum
        grad_low_in = grad_sum.astype(bf16).astype(f32)
        folded = None
        for c in range(2):
            w = 2 * n + c
            rows = slice(c * POS, (c + 1) * POS)
            probs = saved[c]
            factor = keep_ref[n, 0, c].astype(f32) * (1.0 / keep_share)
            grad_branch = (grad_low_in[rows] * factor).astype(bf16)
            grad_att = mm_nt(grad_branch, wproj_ref[...]).astype(bf16)
            grad_probs = mm_nt(v_all[rows], spread_heads(grad_att, head_mask))
            inner_sum = jnp.sum(probs * grad_probs, axis=0, keepdims=True)
            grad_scores = probs * (grad_probs - inner_sum)
            folded = grad_scores if folded is None else folded + grad_scores
            grad_low_out[w] = grad_scores.astype(bf16)
        wide[...] = folded.T.reshape(HEADS, POS, POS)
        total = None
        for o in range(WLON):
            left = PAIR * (WLON - 1 - o)
            right = TAB - POS - left
            parts = [wide[:, PAIR * o : PAIR * (o + 1), :]]
            if left:
                parts = [jnp.zeros((HEADS, PAIR, left), f32)] + parts
            if right:
                parts = parts + [jnp.zeros((HEADS, PAIR, right), f32)]
            piece = jnp.concatenate(parts, axis=2)
            total = piece if total is None else total + piece
        total = jnp.concatenate([total, jnp.zeros((HEADS, SLOTS - PAIR, TAB), f32)], axis=1)
        total = total.reshape(HEADS * SLOTS, TAB).astype(bf16)
        total = mm_nt(total, table_perm_ref[...]).astype(bf16)
        total = mm(chunk_perm_ref[...], total)
        fold_out[2 * n] = total[:QUARTER].astype(bf16)
        fold_out[2 * n + 1] = total[QUARTER:].astype(bf16)


def inputs_kernel(
    x_ref,
    probs_ref,
    grad_low_ref,
    grad_sum_ref,
    result_ref,
    gain1_ref,
    wqkv_t_ref,
    wproj_ref,
    keep_ref,
    perm_t_ref,
    head_mask_ref,
    own_out,
    lat_out,
    diag_out,
    lon_out,
    lat_buf,
    diag_buf,
    lon_buf,
):
    half = WLAT // 2
    cols = 2 * WLON
    edge = WLON // 2
    inner = cols - edge
    root = 1.0 / math.sqrt(HD)
    gain1 = gain1_ref[...]
    wq_t = wqkv_t_ref[0:C, :]
    wk_t = wqkv_t_ref[C : 2 * C, :]
    wv_t = wqkv_t_ref[2 * C : 3 * C, :]
    head_mask = head_mask_ref[...]
    perm_t = perm_t_ref[...]
    for n in range(2):
        both = slice(n * 2 * POS, (n + 1) * 2 * POS)
        scaled1, normed1, inverse1 = norm_parts(x_ref[both, :].astype(f32), gain1)
        h1 = scaled1.astype(bf16)
        q_all = mm_nt(h1, wq_t).astype(bf16)
        grad_sum = grad_sum_ref[both, :]
        grad_low_in = grad_sum.astype(bf16).astype(f32)
        grad_h1 = []
        for c in range(2):
            w = 2 * n + c
            rows = slice(c * POS, (c + 1) * POS)
            grad_low = grad_low_ref[w]
            k_t = mm_nt(wk_t, h1[rows]).astype(bf16)
            factor = keep_ref[n, 0, c].astype(f32) * (1.0 / keep_share)
            grad_branch = (grad_low_in[rows] * factor).astype(bf16)
            grad_att = mm_nt(grad_branch, wproj_ref[...]).astype(bf16)
            q_wide = spread_heads(q_all[rows], head_mask)
            g_wide = spread_heads(grad_att, head_mask)
            grad_q = (head_blocks(mm(k_t, grad_low)).T * root).astype(bf16)
            grad_k = (mm(grad_low, q_wide) * root).astype(bf16)
            grad_v = mm(probs_ref[w], g_wide).astype(bf16)
            grad_h1.append(mm(grad_q, wq_t) + mm(grad_k, wk_t) + mm(grad_v, wv_t))
        grad_h1 = jnp.concatenate(grad_h1, axis=0).astype(bf16).astype(f32)
        grad_field = (grad_sum + norm_back(grad_h1, gain1, normed1, inverse1)).astype(bf16)
        for t, value in enumerate((result_ref[both, :], grad_field)):
            natural = mm(perm_t, value)
            for dz in range(WZ):
                z = (2 * n + dz + 1) % 4
                for i in range(half):
                    k = z * half + i
                    row = (dz * WLAT + i) * cols
                    slab = natural[row : row + cols]
                    own_out[t, z, i] = slab[:inner].astype(bf16)
                    put(lon_buf, t, k * edge, slab[inner:])
                    row = (dz * WLAT + half + i) * cols
                    slab = natural[row : row + cols]
                    put(lat_buf, t, k * inner, slab[:inner])
                    put(diag_buf, t, k * edge, slab[inner:])
    lat_out[...] = lat_buf[...].astype(bf16)
    diag_out[...] = diag_buf[...].astype(bf16)
    lon_out[...] = lon_buf[...].astype(bf16)


def prepare_kernel(
    table_ref,
    table_perm_ref,
    row_perm_ref,
    region_ref,
    wqkv_ref,
    bias_out,
    label_row_out,
    label_col_out,
    wqkv_t_out,
    flat,
    rows,
    wide,
    marks,
):
    wqkv_t_out[...] = wqkv_ref[...].astype(f32).T.astype(bf16)
    last = lax.axis_index("lat") == lax.axis_size("lat") - 1
    level = lax.broadcasted_iota(jnp.int32, (4, 2 * WLON), 0)
    for i in range(WLAT):
        wrapped = 2 * (level >= 4 - WZ // 2).astype(jnp.int32)
        if i >= WLAT // 2:
            wrapped = wrapped + last.astype(jnp.int32)
        marks[4 * i : 4 * (i + 1), :] = (4 * region_ref[i] + wrapped).astype(f32)
    place = lax.broadcasted_iota(jnp.int32, (POS, 4 * WLAT), 0)
    lane = lax.broadcasted_iota(jnp.int32, (POS, 4 * WLAT), 1)
    lon = (place * 43691) >> 19
    pair = place - PAIR * lon
    upper = (pair >= WLAT).astype(jnp.int32)
    source = 4 * (pair - WLAT * upper) + upper
    columns = []
    for n in range(2):
        chosen = mm((lane == source + WZ * n).astype(f32).astype(bf16), marks[...].astype(bf16))
        for c in range(2):
            own = jnp.where(lane == lon + WLON * c, chosen, 0.0)
            columns.append(jnp.sum(own, axis=1, keepdims=True))
    label_col_out[...] = jnp.concatenate(columns, axis=1)
    spread = jnp.concatenate([jnp.broadcast_to(v, (POS, LANES)) for v in columns], axis=1).T
    labels = jnp.concatenate([spread[k * LANES : k * LANES + 1] for k in range(4)], axis=0)
    label_row_out[...] = jnp.concatenate([labels] * HEADS, axis=1)
    part = PAIR // WZ * SPREAD
    for k in range(2 * HEADS):
        flat[k : k + 1, :] = table_ref[k]
    rows[...] = jnp.zeros_like(rows)
    for a in range(WZ):
        for c in range(WLAT):
            pieces = []
            for b in range(WZ):
                start = ((a * WZ + b) * WLAT + c) * part
                pieces.append(flat[:, start : start + part])
            row = (a * WLAT + c) * SLOTS
            rows[row : row + 2 * HEADS, :] = jnp.concatenate(pieces, axis=1)
    left = rows[...]
    perm = table_perm_ref[...]
    total = None
    for _ in range(3):
        low = left.astype(bf16)
        left = left - low.astype(f32)
        term = mm(row_perm_ref[...], mm(low, perm).astype(bf16))
        total = term if total is None else total + term
    total = total.reshape(2 * HEADS, SLOTS, TAB)
    for o in range(WLON):
        start = PAIR * (WLON - 1 - o)
        wide[:, PAIR * o : PAIR * (o + 1), :] = total[:, :PAIR, start : start + POS]
    for n in range(2):
        bias_out[n] = wide[n * HEADS : (n + 1) * HEADS].reshape(ROWS, POS).T * LOG2E


def unpack_kernel(grad_ref, table_out, flat):
    part = PAIR // WZ * SPREAD
    for n in range(2):
        halves = [grad_ref[2 * n + k].astype(f32) for k in range(2)]
        for a in range(WZ):
            for c in range(WLAT):
                row = c * HEADS
                chunk = halves[a][row : row + HEADS]
                for b in range(WZ):
                    start = ((a * WZ + b) * WLAT + c) * part
                    flat[n * HEADS : (n + 1) * HEADS, start : start + part] = chunk[
                        :, b * part : (b + 1) * part
                    ]
    for k in range(2 * HEADS):
        table_out[k] = flat[k : k + 1, :]


def add_kernel(parts_ref, copies_out):
    total = parts_ref[0].astype(f32)
    for k in range(1, parts_ref.shape[0]):
        total = total + parts_ref[k].astype(f32)
    total = total.astype(bf16)
    for k in range(copies_out.shape[0]):
        copies_out[k] = total


def finish_kernel(own_ref, lat_ref, diag_ref, lon_ref, out_ref, grad_ref):
    half = WLAT // 2
    edge = WLON // 2
    inner = 2 * WLON - edge
    lat_part = lat_ref[...].astype(f32)
    diag_part = diag_ref[...].astype(f32)
    lon_part = lon_ref[...].astype(f32)
    for t, target in enumerate((out_ref, grad_ref)):
        for z in range(4):
            for i in range(half):
                k = z * half + i
                parts = (get(diag_part, t, k * edge, edge), get(lat_part, t, k * inner, inner))
                slab = [jnp.concatenate([parts[0][j], parts[1][j]], axis=0) for j in range(2)]
                target[z, i] = jnp.concatenate(slab, axis=1).astype(bf16)
                slab = jnp.concatenate(get(lon_part, t, k * edge, edge), axis=1)
                own = own_ref[t, z, i].astype(f32)
                target[z, half + i] = jnp.concatenate([slab, own], axis=0).astype(bf16)


def window_order():
    perm = np.zeros((2 * POS, 2 * POS), np.float32)
    for c in range(2):
        for j in range(WLON):
            for d in range(PAIR):
                perm[c * POS + j * PAIR + d, d * 2 * WLON + c * WLON + j] = 1.0
    return perm


def table_order():
    perm = np.zeros((TAB, TAB), np.float32)
    for d in range(PAIR):
        for r in range(SPREAD):
            perm[d * SPREAD + r, (SPREAD - 1 - r) * PAIR + d] = 1.0
    return perm


def chunk_order():
    perm = np.zeros((PAIR * HEADS, HEADS * SLOTS), np.float32)
    for h in range(HEADS):
        for k in range(PAIR):
            perm[k * HEADS + h, h * SLOTS + k] = 1.0
    return perm


def row_order():
    perm = np.zeros((2 * HEADS * SLOTS, PAIR * SLOTS), np.float32)
    for h in range(2 * HEADS):
        for k in range(PAIR):
            perm[h * SLOTS + k, k * SLOTS + h] = 1.0
    return perm


def lon_sum(quarters):
    lons = lax.axis_size("lon")
    near = [[4 * k + j for j in range(4)] for k in range(lons // 4)]
    far = [[4 * k + j for k in range(lons // 4)] for j in range(4)]

    def exchange(parts, groups):
        return lax.all_to_all(parts, "lon", 0, 0, axis_index_groups=groups)

    def added(parts, copies):
        vmem = pl.BlockSpec(memory_space=pltpu.VMEM)
        return pl.pallas_call(
            add_kernel,
            out_shape=jax.ShapeDtypeStruct((copies,) + parts.shape[1:], bf16),
            in_specs=[vmem],
            out_specs=vmem,
            compiler_params=pltpu.CompilerParams(vmem_limit_bytes=VMEM_BYTES),
            name="add",
        )(parts)

    parts = exchange(quarters, near)
    parts = exchange(added(parts, lons // 4), far)
    return exchange(added(parts, 4), near)


def body(
    field_in,
    cotangent,
    ln1_gain,
    w_qkv,
    w_proj,
    ln2_gain,
    w_up,
    w_down,
    bias_table,
    region_ids,
    keep_flags,
):
    levels, lat_rows, lon_cols, channels = field_in.shape
    half = WLAT // 2
    edge = WLON // 2
    inner = lon_cols - edge
    vmem = pl.BlockSpec(memory_space=pltpu.VMEM)
    smem = pl.BlockSpec(memory_space=pltpu.SMEM)
    sizes = [3 * levels * half * size for size in (inner, edge, edge)]
    packed = tuple(jax.ShapeDtypeStruct((size, LANES), bf16) for size in sizes)
    buffers = [pltpu.VMEM((size, LANES), f32) for size in sizes]
    params = pltpu.CompilerParams(vmem_limit_bytes=VMEM_BYTES)
    lat_part = pl.pallas_call(
        pack_lat_kernel,
        out_shape=packed[0],
        in_specs=[pl.BlockSpec(memory_space=pltpu.HBM)] * 2,
        out_specs=vmem,
        scratch_shapes=buffers[:1]
        + [pltpu.VMEM((2, levels, half, lon_cols, C), bf16), pltpu.SemaphoreType.DMA((2,))],
        compiler_params=params,
        name="pack_lat",
    )(field_in, cotangent)
    diag_part, lon_part = pl.pallas_call(
        pack_edge_kernel,
        out_shape=packed[1:],
        in_specs=[vmem] * 2 + [pl.BlockSpec(memory_space=pl.ANY)],
        out_specs=(vmem,) * 2,
        scratch_shapes=buffers[1:],
        compiler_params=params,
        name="pack_edge",
    )(field_in, cotangent, lat_part)
    lat_part = shifted(lat_part, -1, 0)
    diag_part = shifted(diag_part, -1, -1)
    lon_part = shifted(lon_part, 0, -1)

    perm = window_order()
    head_mask = np.repeat(np.eye(HEADS, dtype=np.float32), HD, axis=1)
    table_perm = jnp.asarray(table_order(), bf16)
    bias_wide, label_row, label_col, weights_t = pl.pallas_call(
        prepare_kernel,
        out_shape=(
            jax.ShapeDtypeStruct((2, POS, ROWS), f32),
            jax.ShapeDtypeStruct((4, ROWS), f32),
            jax.ShapeDtypeStruct((POS, 4), f32),
            jax.ShapeDtypeStruct((3 * C, C), bf16),
        ),
        in_specs=[vmem] * 5,
        out_specs=(vmem,) * 4,
        scratch_shapes=[
            pltpu.VMEM((2 * HEADS, PAIR * TAB), f32),
            pltpu.VMEM((PAIR * SLOTS, TAB), f32),
            pltpu.VMEM((2 * HEADS, POS, POS), f32),
            pltpu.VMEM((4 * WLAT, 2 * WLON), f32),
        ],
        compiler_params=params,
        name="prepare",
    )(
        bias_table.reshape(2 * HEADS, 1, PAIR * TAB),
        table_perm,
        jnp.asarray(row_order(), bf16),
        region_ids.transpose(1, 0, 2),
        w_qkv,
    )
    positions = levels * lat_rows * lon_cols
    gain1 = ln1_gain.reshape(1, C)
    head_mask = jnp.asarray(head_mask, bf16)
    fold, *saved = pl.pallas_call(
        scores_kernel,
        out_shape=(
            jax.ShapeDtypeStruct((4, QUARTER, TAB), bf16),
            jax.ShapeDtypeStruct((positions, C), bf16),
            jax.ShapeDtypeStruct((4, POS, ROWS), bf16),
            jax.ShapeDtypeStruct((4, POS, ROWS), bf16),
            jax.ShapeDtypeStruct((positions, C), f32),
            jax.ShapeDtypeStruct((positions, C), bf16),
        ),
        in_specs=[vmem] * 14 + [smem] + [vmem] * 4,
        out_specs=(vmem,) * 6,
        scratch_shapes=[
            pltpu.VMEM((2, positions, C), f32),
            pltpu.VMEM((HEADS, POS, POS), f32),
        ],
        compiler_params=params,
        name="scores",
    )(
        field_in,
        cotangent,
        lon_part,
        lat_part,
        diag_part,
        gain1,
        weights_t,
        w_proj,
        ln2_gain.reshape(1, C),
        w_up,
        w_down.T,
        bias_wide,
        label_row,
        label_col,
        keep_flags,
        jnp.asarray(perm, bf16),
        head_mask,
        table_perm,
        jnp.asarray(chunk_order(), bf16),
    )
    own, lat_back, diag_back, lon_back = pl.pallas_call(
        inputs_kernel,
        out_shape=(jax.ShapeDtypeStruct((2, levels, half, inner, C), bf16),) + packed,
        in_specs=[vmem] * 8 + [smem] + [vmem] * 2,
        out_specs=(vmem,) * 4,
        scratch_shapes=buffers,
        compiler_params=params,
        cost_estimate=pl.CostEstimate(
            flops=1_000_000_000, bytes_accessed=8_000_000, transcendentals=0
        ),
        name="inputs",
    )(*saved, gain1, weights_t, w_proj, keep_flags, jnp.asarray(perm.T, bf16), head_mask)
    lat_back = shifted(lat_back, 1, 0)
    diag_back = shifted(diag_back, 1, 1)
    lon_back = shifted(lon_back, 0, 1)
    grads = pl.pallas_call(
        unpack_kernel,
        out_shape=jax.ShapeDtypeStruct((2 * HEADS, 1, PAIR * TAB), f32),
        in_specs=[vmem],
        out_specs=vmem,
        scratch_shapes=[pltpu.VMEM((2 * HEADS, PAIR * TAB), f32)],
        compiler_params=params,
        name="unpack",
    )(lon_sum(fold))
    grads = grads.reshape(2, 1, HEADS, PAIR * TAB)
    result, grad_field = pl.pallas_call(
        finish_kernel,
        out_shape=(jax.ShapeDtypeStruct(field_in.shape, bf16),) * 2,
        in_specs=[vmem] * 4,
        out_specs=(vmem,) * 2,
        compiler_params=params,
        name="finish",
    )(own, lat_back, diag_back, lon_back)
    return (result, grad_field, grads)


def solution(mesh):
    placed = (
        P(None, "lat", "lon", None),
        P(None, "lat", "lon", None),
        P(),
        P(),
        P(),
        P(),
        P(),
        P(),
        P(None, "lat", None, None),
        P(None, "lat", "lon"),
        P(None, "lat", "lon"),
    )
    return jax.shard_map(
        body,
        mesh=mesh,
        in_specs=placed,
        out_specs=(
            P(None, "lat", "lon", None),
            P(None, "lat", "lon", None),
            P(None, "lat", None, None),
        ),
        check_vma=False,
    )
```

```python
import math

import jax
import jax.numpy as jnp
import numpy as np
from jax import lax
from jax.experimental import pallas as pl
from jax.experimental.pallas import tpu as pltpu
from jax.sharding import PartitionSpec as P

C = 192
HEADS = 6
HD = 32
FF = 768
WZ = 2
WLAT = 6
WLON = 12
SPREAD = 2 * WLON - 1
POS = WZ * WLAT * WLON
PAIR = WZ * WLAT
TAB = PAIR * SPREAD
ROWS = HEADS * POS
SLOTS = 16
QUARTER = PAIR * HEADS // 2
LANES = 128

epsilon = 1e-05
keep_share = 0.8
LOG2E = math.log2(math.e)
gelu_coef = 0.044715
VMEM_BYTES = 16 * 1024 * 1024
bf16 = jnp.bfloat16
f32 = jnp.float32


def shifted(block, lat_step, lon_step):
    lats, lons = lax.axis_size("lat"), lax.axis_size("lon")
    route = []
    for a in range(lats):
        for b in range(lons):
            target = ((a + lat_step) % lats) * lons + (b + lon_step) % lons
            route.append((a * lons + b, target))
    return lax.ppermute(block, ("lat", "lon"), route)


def mm(a, b):
    return lax.dot_general(a, b, (((1,), (0,)), ((), ())), preferred_element_type=f32)


def mm_nt(a, b):
    return lax.dot_general(a, b, (((1,), (1,)), ((), ())), preferred_element_type=f32)


def norm_parts(values, gain):
    row_mean = jnp.mean(values, axis=-1, keepdims=True)
    centred = values - row_mean
    variance = jnp.mean(centred * centred, axis=-1, keepdims=True)
    inverse = lax.rsqrt(variance + epsilon)
    normed = centred * inverse
    return normed * gain, normed, inverse


def norm_back(grad_in, gain, normed, inverse):
    scaled = grad_in * gain
    first_mean = jnp.mean(scaled, axis=-1, keepdims=True)
    second_mean = jnp.mean(scaled * normed, axis=-1, keepdims=True)
    return (scaled - first_mean - normed * second_mean) * inverse


def gelu_parts(values):
    factor = math.sqrt(2.0 / math.pi)
    square = values * values
    tangent = jnp.tanh(values * (factor + (gelu_coef * factor) * square))
    half = 0.5 + 0.5 * tangent
    result = values * half
    derivative = half + result * (1.0 - tangent) * (factor + (3.0 * gelu_coef * factor) * square)
    return result, derivative


def head_blocks(wide):
    return jnp.concatenate(
        [wide[h * HD : (h + 1) * HD, h * POS : (h + 1) * POS] for h in range(HEADS)], axis=0
    )


def spread_heads(rows, head_mask):
    return jnp.concatenate([rows * head_mask[h : h + 1, :] for h in range(HEADS)], axis=0)


def put(packed, t, row, slab):
    third = packed.shape[0] // 3
    size = slab.shape[0]
    rest = C - LANES
    packed[t * third + row : t * third + row + size, :] = slab[:, :LANES]
    packed[2 * third + row : 2 * third + row + size, t * rest : (t + 1) * rest] = slab[:, LANES:]


def get(packed, t, row, size):
    third = packed.shape[0] // 3
    rest = C - LANES
    return (
        packed[t * third + row : t * third + row + size, :],
        packed[2 * third + row : 2 * third + row + size, t * rest : (t + 1) * rest],
    )


def pack_lat_kernel(field_ref, cot_ref, lat_out, lat_buf, rows, arrived):
    half = WLAT // 2
    edge = WLON // 2
    inner = 2 * WLON - edge
    sources = (field_ref, cot_ref)
    copies = [
        pltpu.make_async_copy(sources[t].at[:, pl.ds(0, half)], rows.at[t], arrived.at[t])
        for t in range(2)
    ]
    for copy in copies:
        copy.start()
    for t in range(2):
        copies[t].wait()
        for z in range(4):
            for i in range(half):
                put(lat_buf, t, (z * half + i) * inner, rows[t, z, i].astype(f32)[edge:])
    lat_out[...] = lat_buf[...].astype(bf16)


def pack_edge_kernel(field_ref, cot_ref, after_ref, diag_out, lon_out, diag_buf, lon_buf):
    half = WLAT // 2
    edge = WLON // 2
    for t, source in enumerate((field_ref, cot_ref)):
        for z in range(4):
            for i in range(half):
                row = (z * half + i) * edge
                put(diag_buf, t, row, source[z, i].astype(f32)[:edge])
                put(lon_buf, t, row, source[z, half + i].astype(f32)[:edge])
    diag_out[...] = diag_buf[...].astype(bf16)
    lon_out[...] = lon_buf[...].astype(bf16)


def block_kernel(
    field_ref,
    cot_ref,
    lon_ref,
    lat_ref,
    diag_ref,
    gain1_ref,
    wqkv_t_ref,
    wproj_ref,
    gain2_ref,
    wup_ref,
    wdown_t_ref,
    bias_ref,
    label_row_ref,
    label_col_ref,
    keep_ref,
    perm_ref,
    head_mask_ref,
    table_perm_ref,
    chunk_perm_ref,
    perm_t_ref,
    fold_out,
    own_out,
    lat_out,
    diag_out,
    lon_out,
    frame,
    wide,
    lat_buf,
    diag_buf,
    lon_buf,
):
    half = WLAT // 2
    cols = 2 * WLON
    edge = WLON // 2
    inner = cols - edge
    root = 1.0 / math.sqrt(HD)
    lon_part = lon_ref[...].astype(f32)
    lat_part = lat_ref[...].astype(f32)
    diag_part = diag_ref[...].astype(f32)
    for t, own in enumerate((field_ref, cot_ref)):
        for level in range(4):
            z = (level + 1) % 4
            for i in range(half):
                k = z * half + i
                row = (level * WLAT + i) * cols
                frame[t, row : row + inner, :] = own[z, half + i].astype(f32)[edge:, :]
                main, rest = get(lon_part, t, k * edge, edge)
                frame[t, row + inner : row + cols, :LANES] = main
                frame[t, row + inner : row + cols, LANES:] = rest
                row = (level * WLAT + half + i) * cols
                main, rest = get(lat_part, t, k * inner, inner)
                frame[t, row : row + inner, :LANES] = main
                frame[t, row : row + inner, LANES:] = rest
                main, rest = get(diag_part, t, k * edge, edge)
                frame[t, row + inner : row + cols, :LANES] = main
                frame[t, row + inner : row + cols, LANES:] = rest
    gain1 = gain1_ref[...]
    gain2 = gain2_ref[...]
    wq_t = wqkv_t_ref[0:C, :]
    wk_t = wqkv_t_ref[C : 2 * C, :]
    wv_t = wqkv_t_ref[2 * C : 3 * C, :]
    head_mask = head_mask_ref[...]
    perm = perm_ref[...]
    perm_t = perm_t_ref[...]
    for n in range(2):
        both = slice(n * 2 * POS, (n + 1) * 2 * POS)
        x = mm(perm, frame[0, both, :].astype(bf16))
        cot = mm(perm, frame[1, both, :].astype(bf16))
        scaled1, normed1, inverse1 = norm_parts(x, gain1)
        h1 = scaled1.astype(bf16)
        q_all = mm_nt(h1, wq_t).astype(bf16)
        k_all = mm_nt(h1, wk_t).astype(bf16)
        v_all = mm_nt(h1, wv_t).astype(bf16)
        saved = []
        branches = []
        for c in range(2):
            w = 2 * n + c
            rows = slice(c * POS, (c + 1) * POS)
            v_t = mm_nt(wv_t, h1[rows]).astype(bf16)
            q_wide = spread_heads(q_all[rows], head_mask)
            scores = mm_nt(k_all[rows], q_wide) * (root * LOG2E) + bias_ref[n]
            allowed = label_col_ref[:, w : w + 1] == label_row_ref[w : w + 1, :]
            scores = jnp.where(allowed, scores, -1e30)
            weights = jnp.exp2(scores - jnp.max(scores, axis=0, keepdims=True))
            probs = weights * (1.0 / jnp.sum(weights, axis=0, keepdims=True))
            probs_low = probs.astype(bf16)
            attended = head_blocks(mm(v_t, probs_low)).T.astype(bf16)
            factor = keep_ref[n, 0, c].astype(f32) * (1.0 / keep_share)
            branches.append((mm(attended, wproj_ref[...]) * factor).astype(bf16).astype(f32))
            saved.append((q_wide, probs, probs_low))
        y_sum = x + jnp.concatenate(branches, axis=0)
        scaled2, normed2, inverse2 = norm_parts(y_sum, gain2)
        act, slope = gelu_parts(mm(scaled2.astype(bf16), wup_ref[...]))
        result = (y_sum + mm_nt(act.astype(bf16), wdown_t_ref[...])).astype(bf16)
        grad_up = (mm(cot.astype(bf16), wdown_t_ref[...]) * slope).astype(bf16)
        grad_sum = cot + norm_back(mm_nt(grad_up, wup_ref[...]), gain2, normed2, inverse2)
        grad_low_in = grad_sum.astype(bf16).astype(f32)
        folded = None
        grad_h1 = []
        for c in range(2):
            rows = slice(c * POS, (c + 1) * POS)
            q_wide, probs, probs_low = saved[c]
            factor = keep_ref[n, 0, c].astype(f32) * (1.0 / keep_share)
            grad_branch = (grad_low_in[rows] * factor).astype(bf16)
            grad_att = mm_nt(grad_branch, wproj_ref[...]).astype(bf16)
            g_wide = spread_heads(grad_att, head_mask)
            grad_probs = mm_nt(v_all[rows], g_wide)
            inner_sum = jnp.sum(probs * grad_probs, axis=0, keepdims=True)
            grad_scores = probs * (grad_probs - inner_sum)
            folded = grad_scores if folded is None else folded + grad_scores
            grad_low = grad_scores.astype(bf16)
            k_t = mm_nt(wk_t, h1[rows]).astype(bf16)
            grad_q = (head_blocks(mm(k_t, grad_low)).T * root).astype(bf16)
            grad_k = (mm(grad_low, q_wide) * root).astype(bf16)
            grad_v = mm(probs_low, g_wide).astype(bf16)
            grad_h1.append(mm(grad_q, wq_t) + mm(grad_k, wk_t) + mm(grad_v, wv_t))
        wide[...] = folded.T.reshape(HEADS, POS, POS)
        total = None
        for o in range(WLON):
            left = PAIR * (WLON - 1 - o)
            right = TAB - POS - left
            parts = [wide[:, PAIR * o : PAIR * (o + 1), :]]
            if left:
                parts = [jnp.zeros((HEADS, PAIR, left), f32)] + parts
            if right:
                parts = parts + [jnp.zeros((HEADS, PAIR, right), f32)]
            piece = jnp.concatenate(parts, axis=2)
            total = piece if total is None else total + piece
        total = jnp.concatenate([total, jnp.zeros((HEADS, SLOTS - PAIR, TAB), f32)], axis=1)
        total = total.reshape(HEADS * SLOTS, TAB).astype(bf16)
        total = mm_nt(total, table_perm_ref[...]).astype(bf16)
        total = mm(chunk_perm_ref[...], total)
        fold_out[2 * n] = total[:QUARTER].astype(bf16)
        fold_out[2 * n + 1] = total[QUARTER:].astype(bf16)
        grad_h1 = jnp.concatenate(grad_h1, axis=0).astype(bf16).astype(f32)
        grad_field = (grad_sum + norm_back(grad_h1, gain1, normed1, inverse1)).astype(bf16)
        for t, value in enumerate((result, grad_field)):
            natural = mm(perm_t, value)
            for dz in range(WZ):
                z = (2 * n + dz + 1) % 4
                for i in range(half):
                    k = z * half + i
                    row = (dz * WLAT + i) * cols
                    slab = natural[row : row + cols]
                    own_out[t, z, i] = slab[:inner].astype(bf16)
                    put(lon_buf, t, k * edge, slab[inner:])
                    row = (dz * WLAT + half + i) * cols
                    slab = natural[row : row + cols]
                    put(lat_buf, t, k * inner, slab[:inner])
                    put(diag_buf, t, k * edge, slab[inner:])
    lat_out[...] = lat_buf[...].astype(bf16)
    diag_out[...] = diag_buf[...].astype(bf16)
    lon_out[...] = lon_buf[...].astype(bf16)


def prepare_kernel(
    table_ref,
    table_perm_ref,
    row_perm_ref,
    region_ref,
    wqkv_ref,
    bias_out,
    label_row_out,
    label_col_out,
    wqkv_t_out,
    flat,
    rows,
    wide,
    marks,
):
    wqkv_t_out[...] = wqkv_ref[...].astype(f32).T.astype(bf16)
    last = lax.axis_index("lat") == lax.axis_size("lat") - 1
    level = lax.broadcasted_iota(jnp.int32, (4, 2 * WLON), 0)
    for i in range(WLAT):
        wrapped = 2 * (level >= 4 - WZ // 2).astype(jnp.int32)
        if i >= WLAT // 2:
            wrapped = wrapped + last.astype(jnp.int32)
        marks[4 * i : 4 * (i + 1), :] = (4 * region_ref[i] + wrapped).astype(f32)
    place = lax.broadcasted_iota(jnp.int32, (POS, 4 * WLAT), 0)
    lane = lax.broadcasted_iota(jnp.int32, (POS, 4 * WLAT), 1)
    lon = (place * 43691) >> 19
    pair = place - PAIR * lon
    upper = (pair >= WLAT).astype(jnp.int32)
    source = 4 * (pair - WLAT * upper) + upper
    columns = []
    for n in range(2):
        chosen = mm((lane == source + WZ * n).astype(f32).astype(bf16), marks[...].astype(bf16))
        for c in range(2):
            own = jnp.where(lane == lon + WLON * c, chosen, 0.0)
            columns.append(jnp.sum(own, axis=1, keepdims=True))
    label_col_out[...] = jnp.concatenate(columns, axis=1)
    spread = jnp.concatenate([jnp.broadcast_to(v, (POS, LANES)) for v in columns], axis=1).T
    labels = jnp.concatenate([spread[k * LANES : k * LANES + 1] for k in range(4)], axis=0)
    label_row_out[...] = jnp.concatenate([labels] * HEADS, axis=1)
    part = PAIR // WZ * SPREAD
    for k in range(2 * HEADS):
        flat[k : k + 1, :] = table_ref[k]
    rows[...] = jnp.zeros_like(rows)
    for a in range(WZ):
        for c in range(WLAT):
            pieces = []
            for b in range(WZ):
                start = ((a * WZ + b) * WLAT + c) * part
                pieces.append(flat[:, start : start + part])
            row = (a * WLAT + c) * SLOTS
            rows[row : row + 2 * HEADS, :] = jnp.concatenate(pieces, axis=1)
    left = rows[...]
    perm = table_perm_ref[...]
    total = None
    for _ in range(3):
        low = left.astype(bf16)
        left = left - low.astype(f32)
        term = mm(row_perm_ref[...], mm(low, perm).astype(bf16))
        total = term if total is None else total + term
    total = total.reshape(2 * HEADS, SLOTS, TAB)
    for o in range(WLON):
        start = PAIR * (WLON - 1 - o)
        wide[:, PAIR * o : PAIR * (o + 1), :] = total[:, :PAIR, start : start + POS]
    for n in range(2):
        bias_out[n] = wide[n * HEADS : (n + 1) * HEADS].reshape(ROWS, POS).T * LOG2E


def unpack_kernel(grad_ref, table_out, flat):
    part = PAIR // WZ * SPREAD
    for n in range(2):
        halves = [grad_ref[2 * n + k].astype(f32) for k in range(2)]
        for a in range(WZ):
            for c in range(WLAT):
                row = c * HEADS
                chunk = halves[a][row : row + HEADS]
                for b in range(WZ):
                    start = ((a * WZ + b) * WLAT + c) * part
                    flat[n * HEADS : (n + 1) * HEADS, start : start + part] = chunk[
                        :, b * part : (b + 1) * part
                    ]
    for k in range(2 * HEADS):
        table_out[k] = flat[k : k + 1, :]


def add_kernel(parts_ref, copies_out):
    total = parts_ref[0].astype(f32)
    for k in range(1, parts_ref.shape[0]):
        total = total + parts_ref[k].astype(f32)
    total = total.astype(bf16)
    for k in range(copies_out.shape[0]):
        copies_out[k] = total


def finish_kernel(own_ref, lat_ref, diag_ref, lon_ref, out_ref, grad_ref):
    half = WLAT // 2
    edge = WLON // 2
    inner = 2 * WLON - edge
    lat_part = lat_ref[...].astype(f32)
    diag_part = diag_ref[...].astype(f32)
    lon_part = lon_ref[...].astype(f32)
    for t, target in enumerate((out_ref, grad_ref)):
        for z in range(4):
            for i in range(half):
                k = z * half + i
                parts = (get(diag_part, t, k * edge, edge), get(lat_part, t, k * inner, inner))
                slab = [jnp.concatenate([parts[0][j], parts[1][j]], axis=0) for j in range(2)]
                target[z, i] = jnp.concatenate(slab, axis=1).astype(bf16)
                slab = jnp.concatenate(get(lon_part, t, k * edge, edge), axis=1)
                own = own_ref[t, z, i].astype(f32)
                target[z, half + i] = jnp.concatenate([slab, own], axis=0).astype(bf16)


def window_order():
    perm = np.zeros((2 * POS, 2 * POS), np.float32)
    for c in range(2):
        for j in range(WLON):
            for d in range(PAIR):
                perm[c * POS + j * PAIR + d, d * 2 * WLON + c * WLON + j] = 1.0
    return perm


def table_order():
    perm = np.zeros((TAB, TAB), np.float32)
    for d in range(PAIR):
        for r in range(SPREAD):
            perm[d * SPREAD + r, (SPREAD - 1 - r) * PAIR + d] = 1.0
    return perm


def chunk_order():
    perm = np.zeros((PAIR * HEADS, HEADS * SLOTS), np.float32)
    for h in range(HEADS):
        for k in range(PAIR):
            perm[k * HEADS + h, h * SLOTS + k] = 1.0
    return perm


def row_order():
    perm = np.zeros((2 * HEADS * SLOTS, PAIR * SLOTS), np.float32)
    for h in range(2 * HEADS):
        for k in range(PAIR):
            perm[h * SLOTS + k, k * SLOTS + h] = 1.0
    return perm


def lon_sum(quarters, after):
    lons = lax.axis_size("lon")
    near = [[4 * k + j for j in range(4)] for k in range(lons // 4)]
    far = [[4 * k + j for k in range(lons // 4)] for j in range(4)]

    def exchange(parts, groups):
        return lax.all_to_all(parts, "lon", 0, 0, axis_index_groups=groups)

    def added(parts, copies):
        vmem = pl.BlockSpec(memory_space=pltpu.VMEM)
        return pl.pallas_call(
            add_kernel,
            out_shape=jax.ShapeDtypeStruct((copies,) + parts.shape[1:], bf16),
            in_specs=[vmem],
            out_specs=vmem,
            compiler_params=pltpu.CompilerParams(vmem_limit_bytes=VMEM_BYTES),
            name="add",
        )(parts)

    parts = added(exchange(quarters, near), lons // 4)
    parts, after = lax.optimization_barrier((parts, after))
    parts = exchange(parts, far)
    return exchange(added(parts, 4), near), after


def body(
    field_in,
    cotangent,
    ln1_gain,
    w_qkv,
    w_proj,
    ln2_gain,
    w_up,
    w_down,
    bias_table,
    region_ids,
    keep_flags,
):
    levels, lat_rows, lon_cols, channels = field_in.shape
    half = WLAT // 2
    edge = WLON // 2
    inner = lon_cols - edge
    vmem = pl.BlockSpec(memory_space=pltpu.VMEM)
    smem = pl.BlockSpec(memory_space=pltpu.SMEM)
    sizes = [3 * levels * half * size for size in (inner, edge, edge)]
    packed = tuple(jax.ShapeDtypeStruct((size, LANES), bf16) for size in sizes)
    buffers = [pltpu.VMEM((size, LANES), f32) for size in sizes]
    params = pltpu.CompilerParams(vmem_limit_bytes=VMEM_BYTES)
    lat_part = pl.pallas_call(
        pack_lat_kernel,
        out_shape=packed[0],
        in_specs=[pl.BlockSpec(memory_space=pltpu.HBM)] * 2,
        out_specs=vmem,
        scratch_shapes=buffers[:1]
        + [pltpu.VMEM((2, levels, half, lon_cols, C), bf16), pltpu.SemaphoreType.DMA((2,))],
        compiler_params=params,
        name="pack_lat",
    )(field_in, cotangent)
    diag_part, lon_part = pl.pallas_call(
        pack_edge_kernel,
        out_shape=packed[1:],
        in_specs=[vmem] * 2 + [pl.BlockSpec(memory_space=pl.ANY)],
        out_specs=(vmem,) * 2,
        scratch_shapes=buffers[1:],
        compiler_params=params,
        name="pack_edge",
    )(field_in, cotangent, lat_part)
    lat_part = shifted(lat_part, -1, 0)
    diag_part = shifted(diag_part, -1, -1)
    lon_part = shifted(lon_part, 0, -1)

    perm = window_order()
    head_mask = np.repeat(np.eye(HEADS, dtype=np.float32), HD, axis=1)
    table_perm = jnp.asarray(table_order(), bf16)
    bias_wide, label_row, label_col, weights_t = pl.pallas_call(
        prepare_kernel,
        out_shape=(
            jax.ShapeDtypeStruct((2, POS, ROWS), f32),
            jax.ShapeDtypeStruct((4, ROWS), f32),
            jax.ShapeDtypeStruct((POS, 4), f32),
            jax.ShapeDtypeStruct((3 * C, C), bf16),
        ),
        in_specs=[vmem] * 5,
        out_specs=(vmem,) * 4,
        scratch_shapes=[
            pltpu.VMEM((2 * HEADS, PAIR * TAB), f32),
            pltpu.VMEM((PAIR * SLOTS, TAB), f32),
            pltpu.VMEM((2 * HEADS, POS, POS), f32),
            pltpu.VMEM((4 * WLAT, 2 * WLON), f32),
        ],
        compiler_params=params,
        name="prepare",
    )(
        bias_table.reshape(2 * HEADS, 1, PAIR * TAB),
        table_perm,
        jnp.asarray(row_order(), bf16),
        region_ids.transpose(1, 0, 2),
        w_qkv,
    )
    positions = levels * lat_rows * lon_cols
    gain1 = ln1_gain.reshape(1, C)
    head_mask = jnp.asarray(head_mask, bf16)
    fold, own, *strips = pl.pallas_call(
        block_kernel,
        out_shape=(
            jax.ShapeDtypeStruct((4, QUARTER, TAB), bf16),
            jax.ShapeDtypeStruct((2, levels, half, inner, C), bf16),
        )
        + packed,
        in_specs=[vmem] * 14 + [smem] + [vmem] * 5,
        out_specs=(vmem,) * 5,
        scratch_shapes=[
            pltpu.VMEM((2, positions, C), f32),
            pltpu.VMEM((HEADS, POS, POS), f32),
        ]
        + buffers,
        compiler_params=params,
        name="block",
    )(
        field_in,
        cotangent,
        lon_part,
        lat_part,
        diag_part,
        gain1,
        weights_t,
        w_proj,
        ln2_gain.reshape(1, C),
        w_up,
        w_down.T,
        bias_wide,
        label_row,
        label_col,
        keep_flags,
        jnp.asarray(perm, bf16),
        head_mask,
        table_perm,
        jnp.asarray(chunk_order(), bf16),
        jnp.asarray(perm.T, bf16),
    )
    grads, (lat_back, diag_back, lon_back) = lon_sum(fold, strips)
    lat_back = shifted(lat_back, 1, 0)
    diag_back = shifted(diag_back, 1, 1)
    lon_back = shifted(lon_back, 0, 1)
    grads = pl.pallas_call(
        unpack_kernel,
        out_shape=jax.ShapeDtypeStruct((2 * HEADS, 1, PAIR * TAB), f32),
        in_specs=[vmem],
        out_specs=vmem,
        scratch_shapes=[pltpu.VMEM((2 * HEADS, PAIR * TAB), f32)],
        compiler_params=params,
        name="unpack",
    )(grads)
    grads = grads.reshape(2, 1, HEADS, PAIR * TAB)
    result, grad_field = pl.pallas_call(
        finish_kernel,
        out_shape=(jax.ShapeDtypeStruct(field_in.shape, bf16),) * 2,
        in_specs=[vmem] * 4,
        out_specs=(vmem,) * 2,
        compiler_params=params,
        name="finish",
    )(own, lat_back, diag_back, lon_back)
    return (result, grad_field, grads)


def solution(mesh):
    placed = (
        P(None, "lat", "lon", None),
        P(None, "lat", "lon", None),
        P(),
        P(),
        P(),
        P(),
        P(),
        P(),
        P(None, "lat", None, None),
        P(None, "lat", "lon"),
        P(None, "lat", "lon"),
    )
    return jax.shard_map(
        body,
        mesh=mesh,
        in_specs=placed,
        out_specs=(
            P(None, "lat", "lon", None),
            P(None, "lat", "lon", None),
            P(None, "lat", None, None),
        ),
        check_vma=False,
    )
```

```python
import math

import jax
import jax.numpy as jnp
from jax import lax
from jax.experimental import pallas as pl
from jax.experimental.pallas import tpu as pltpu
from jax.sharding import PartitionSpec as P

C = 192
HEADS = 6
HD = 32
FF = 768
WZ = 2
WLAT = 6
WLON = 12
SPREAD = 2 * WLON - 1
POS = WZ * WLAT * WLON
PAIR = WZ * WLAT
TAB = PAIR * SPREAD
ROWS = HEADS * POS
SLOTS = 16
QUARTER = PAIR * HEADS // 2
REST = 20
DENSE = 80
LANES = 128

epsilon = 1e-05
keep_share = 0.8
LOG2E = math.log2(math.e)
gelu_coef = 0.044715
VMEM_BYTES = 16 * 1024 * 1024
bf16 = jnp.bfloat16
f32 = jnp.float32


def shifted(block, lat_step, lon_step):
    lats, lons = lax.axis_size("lat"), lax.axis_size("lon")
    route = []
    for a in range(lats):
        for b in range(lons):
            target = ((a + lat_step) % lats) * lons + (b + lon_step) % lons
            route.append((a * lons + b, target))
    return lax.ppermute(block, ("lat", "lon"), route)


def mm(a, b):
    return lax.dot_general(a, b, (((1,), (0,)), ((), ())), preferred_element_type=f32)


def mm_nt(a, b):
    return lax.dot_general(a, b, (((1,), (1,)), ((), ())), preferred_element_type=f32)


def norm_parts(values, gain):
    row_mean = jnp.mean(values, axis=-1, keepdims=True)
    centred = values - row_mean
    variance = jnp.mean(centred * centred, axis=-1, keepdims=True)
    inverse = lax.rsqrt(variance + epsilon)
    normed = centred * inverse
    return normed * gain, normed, inverse


def norm_back(grad_in, gain, normed, inverse):
    scaled = grad_in * gain
    first_mean = jnp.mean(scaled, axis=-1, keepdims=True)
    second_mean = jnp.mean(scaled * normed, axis=-1, keepdims=True)
    return (scaled - first_mean - normed * second_mean) * inverse


def gelu_parts(values):
    factor = math.sqrt(2.0 / math.pi)
    square = values * values
    tangent = jnp.tanh(values * (factor + (gelu_coef * factor) * square))
    half = 0.5 + 0.5 * tangent
    result = values * half
    derivative = half + result * (1.0 - tangent) * (factor + (3.0 * gelu_coef * factor) * square)
    return result, derivative


def head_blocks(wide):
    return jnp.concatenate(
        [wide[h * HD : (h + 1) * HD, h * POS : (h + 1) * POS] for h in range(HEADS)], axis=0
    )


def spread_heads(rows, head_mask):
    return jnp.concatenate([rows * head_mask[h : h + 1, :] for h in range(HEADS)], axis=0)


def quotient(values, divisor):
    return (values * (2**20 // divisor + 1)) >> 20


def one_hot(rows, columns, target):
    row = lax.broadcasted_iota(jnp.int32, (rows, columns), 0)
    column = lax.broadcasted_iota(jnp.int32, (rows, columns), 1)
    return (column == target(row)).astype(f32).astype(bf16)


def window_order():
    def target(row):
        c = (row >= POS).astype(jnp.int32)
        row = row - POS * c
        j = quotient(row, PAIR)
        return (row - PAIR * j) * (2 * WLON) + c * WLON + j

    return one_hot(2 * POS, 2 * POS, target)


def natural_order():
    def target(row):
        pair = quotient(row, 2 * WLON)
        lon = row - 2 * WLON * pair
        c = (lon >= WLON).astype(jnp.int32)
        return c * POS + (lon - WLON * c) * PAIR + pair

    return one_hot(2 * POS, 2 * POS, target)


def table_order():
    def target(row):
        pair = quotient(row, SPREAD)
        return (SPREAD - 1 - (row - SPREAD * pair)) * PAIR + pair

    return one_hot(TAB, TAB, target)


def chunk_order():
    def target(row):
        pair = quotient(row, HEADS)
        return (row - HEADS * pair) * SLOTS + pair

    return one_hot(PAIR * HEADS, HEADS * SLOTS, target)


def row_order():
    def target(row):
        head = quotient(row, SLOTS)
        return (row - SLOTS * head) * SLOTS + head

    return one_hot(2 * HEADS * SLOTS, PAIR * SLOTS, target)


def put(packed, t, row, slab):
    third = packed.shape[0] // 3
    size = slab.shape[0]
    rest = C - LANES
    packed[t * third + row : t * third + row + size, :] = slab[:, :LANES]
    packed[2 * third + row : 2 * third + row + size, t * rest : (t + 1) * rest] = slab[:, LANES:]


def get(packed, t, row, size):
    third = packed.shape[0] // 3
    rest = C - LANES
    return (
        packed[t * third + row : t * third + row + size, :],
        packed[2 * third + row : 2 * third + row + size, t * rest : (t + 1) * rest],
    )


def pack_lat_kernel(field_ref, cot_ref, lat_out, lat_buf, rows, arrived):
    half = WLAT // 2
    edge = WLON // 2
    inner = 2 * WLON - edge
    sources = (field_ref, cot_ref)
    copies = [
        pltpu.make_async_copy(sources[t].at[:, pl.ds(0, half)], rows.at[t], arrived.at[t])
        for t in range(2)
    ]
    for copy in copies:
        copy.start()
    for t in range(2):
        copies[t].wait()
        for z in range(4):
            for i in range(half):
                put(lat_buf, t, (z * half + i) * inner, rows[t, z, i].astype(f32)[edge:])
    lat_out[...] = lat_buf[...].astype(bf16)


def pack_edge_kernel(field_ref, cot_ref, after_ref, diag_out, lon_out, diag_buf, lon_buf):
    half = WLAT // 2
    edge = WLON // 2
    for t, source in enumerate((field_ref, cot_ref)):
        for z in range(4):
            for i in range(half):
                row = (z * half + i) * edge
                put(diag_buf, t, row, source[z, i].astype(f32)[:edge])
                put(lon_buf, t, row, source[z, half + i].astype(f32)[:edge])
    diag_out[...] = diag_buf[...].astype(bf16)
    lon_out[...] = lon_buf[...].astype(bf16)


def block_kernel(
    field_ref,
    cot_ref,
    lon_ref,
    lat_ref,
    diag_ref,
    gain1_ref,
    wqkv_t_ref,
    wproj_ref,
    gain2_ref,
    wup_ref,
    wdown_t_ref,
    bias_ref,
    label_row_ref,
    label_col_ref,
    keep_ref,
    fold_out,
    own_out,
    lat_out,
    diag_out,
    lon_out,
    frame,
    wide,
    dense,
    lat_buf,
    diag_buf,
    lon_buf,
):
    half = WLAT // 2
    cols = 2 * WLON
    edge = WLON // 2
    inner = cols - edge
    root = 1.0 / math.sqrt(HD)
    lon_part = lon_ref[...].astype(f32)
    lat_part = lat_ref[...].astype(f32)
    diag_part = diag_ref[...].astype(f32)
    for t, own in enumerate((field_ref, cot_ref)):
        for level in range(4):
            z = (level + 1) % 4
            for i in range(half):
                k = z * half + i
                row = (level * WLAT + i) * cols
                frame[t, row : row + inner, :] = own[z, half + i].astype(f32)[edge:, :]
                main, rest = get(lon_part, t, k * edge, edge)
                frame[t, row + inner : row + cols, :LANES] = main
                frame[t, row + inner : row + cols, LANES:] = rest
                row = (level * WLAT + half + i) * cols
                main, rest = get(lat_part, t, k * inner, inner)
                frame[t, row : row + inner, :LANES] = main
                frame[t, row : row + inner, LANES:] = rest
                main, rest = get(diag_part, t, k * edge, edge)
                frame[t, row + inner : row + cols, :LANES] = main
                frame[t, row + inner : row + cols, LANES:] = rest
    gain1 = gain1_ref[...]
    gain2 = gain2_ref[...]
    wq_t = wqkv_t_ref[0:C, :]
    wk_t = wqkv_t_ref[C : 2 * C, :]
    wv_t = wqkv_t_ref[2 * C : 3 * C, :]
    head = lax.broadcasted_iota(jnp.int32, (HEADS, C), 0)
    head_mask = (lax.broadcasted_iota(jnp.int32, (HEADS, C), 1) >> 5) == head
    head_mask = head_mask.astype(f32).astype(bf16)
    perm = window_order()
    perm_t = natural_order()
    table_perm = table_order()
    chunk_perm = chunk_order()
    dense[...] = jnp.zeros_like(dense)
    for n in range(2):
        both = slice(n * 2 * POS, (n + 1) * 2 * POS)
        x = mm(perm, frame[0, both, :].astype(bf16))
        cot = mm(perm, frame[1, both, :].astype(bf16))
        scaled1, normed1, inverse1 = norm_parts(x, gain1)
        h1 = scaled1.astype(bf16)
        q_all = mm_nt(h1, wq_t).astype(bf16)
        k_all = mm_nt(h1, wk_t).astype(bf16)
        v_all = mm_nt(h1, wv_t).astype(bf16)
        saved = []
        branches = []
        for c in range(2):
            w = 2 * n + c
            rows = slice(c * POS, (c + 1) * POS)
            v_t = mm_nt(wv_t, h1[rows]).astype(bf16)
            q_wide = spread_heads(q_all[rows], head_mask)
            scores = mm_nt(k_all[rows], q_wide) * (root * LOG2E) + bias_ref[n]
            allowed = label_col_ref[:, w : w + 1] == label_row_ref[w : w + 1, :]
            scores = jnp.where(allowed, scores, -1e30)
            weights = jnp.exp2(scores - jnp.max(scores, axis=0, keepdims=True))
            probs = weights * (1.0 / jnp.sum(weights, axis=0, keepdims=True))
            probs_low = probs.astype(bf16)
            attended = head_blocks(mm(v_t, probs_low)).T.astype(bf16)
            factor = keep_ref[n, 0, c].astype(f32) * (1.0 / keep_share)
            branches.append((mm(attended, wproj_ref[...]) * factor).astype(bf16).astype(f32))
            saved.append((q_wide, probs, probs_low))
        y_sum = x + jnp.concatenate(branches, axis=0)
        scaled2, normed2, inverse2 = norm_parts(y_sum, gain2)
        act, slope = gelu_parts(mm(scaled2.astype(bf16), wup_ref[...]))
        result = (y_sum + mm_nt(act.astype(bf16), wdown_t_ref[...])).astype(bf16)
        grad_up = (mm(cot.astype(bf16), wdown_t_ref[...]) * slope).astype(bf16)
        grad_sum = cot + norm_back(mm_nt(grad_up, wup_ref[...]), gain2, normed2, inverse2)
        grad_low_in = grad_sum.astype(bf16).astype(f32)
        folded = None
        grad_h1 = []
        for c in range(2):
            rows = slice(c * POS, (c + 1) * POS)
            q_wide, probs, probs_low = saved[c]
            factor = keep_ref[n, 0, c].astype(f32) * (1.0 / keep_share)
            grad_branch = (grad_low_in[rows] * factor).astype(bf16)
            grad_att = mm_nt(grad_branch, wproj_ref[...]).astype(bf16)
            g_wide = spread_heads(grad_att, head_mask)
            grad_probs = mm_nt(v_all[rows], g_wide)
            inner_sum = jnp.sum(probs * grad_probs, axis=0, keepdims=True)
            grad_scores = probs * (grad_probs - inner_sum)
            folded = grad_scores if folded is None else folded + grad_scores
            grad_low = grad_scores.astype(bf16)
            k_t = mm_nt(wk_t, h1[rows]).astype(bf16)
            grad_q = (head_blocks(mm(k_t, grad_low)).T * root).astype(bf16)
            grad_k = (mm(grad_low, q_wide) * root).astype(bf16)
            grad_v = mm(probs_low, g_wide).astype(bf16)
            grad_h1.append(mm(grad_q, wq_t) + mm(grad_k, wk_t) + mm(grad_v, wv_t))
        wide[...] = folded.T.reshape(HEADS, POS, POS)
        total = None
        for o in range(WLON):
            left = PAIR * (WLON - 1 - o)
            right = TAB - POS - left
            parts = [wide[:, PAIR * o : PAIR * (o + 1), :]]
            if left:
                parts = [jnp.zeros((HEADS, PAIR, left), f32)] + parts
            if right:
                parts = parts + [jnp.zeros((HEADS, PAIR, right), f32)]
            piece = jnp.concatenate(parts, axis=2)
            total = piece if total is None else total + piece
        total = jnp.concatenate([total, jnp.zeros((HEADS, SLOTS - PAIR, TAB), f32)], axis=1)
        total = total.reshape(HEADS * SLOTS, TAB).astype(bf16)
        total = mm_nt(total, table_perm).astype(bf16)
        total = mm(chunk_perm, total)
        for k in range(2):
            part = total[k * QUARTER : (k + 1) * QUARTER]
            dense[:QUARTER, :] = part[:, :LANES]
            dense[QUARTER : 2 * QUARTER, :] = part[:, LANES : 2 * LANES]
            rest = [part[HEADS * g : HEADS * (g + 1), 2 * LANES :] for g in range(WLAT)]
            dense[2 * QUARTER : 2 * QUARTER + HEADS, : WLAT * REST] = jnp.concatenate(rest, axis=1)
            fold_out[2 * n + k] = dense[...].astype(bf16)
        grad_h1 = jnp.concatenate(grad_h1, axis=0).astype(bf16).astype(f32)
        grad_field = (grad_sum + norm_back(grad_h1, gain1, normed1, inverse1)).astype(bf16)
        for t, value in enumerate((result, grad_field)):
            natural = mm(perm_t, value)
            for dz in range(WZ):
                z = (2 * n + dz + 1) % 4
                for i in range(half):
                    k = z * half + i
                    row = (dz * WLAT + i) * cols
                    slab = natural[row : row + cols]
                    own_out[t, z, i] = slab[:inner].astype(bf16)
                    put(lon_buf, t, k * edge, slab[inner:])
                    row = (dz * WLAT + half + i) * cols
                    slab = natural[row : row + cols]
                    put(lat_buf, t, k * inner, slab[:inner])
                    put(diag_buf, t, k * edge, slab[inner:])
    lat_out[...] = lat_buf[...].astype(bf16)
    diag_out[...] = diag_buf[...].astype(bf16)
    lon_out[...] = lon_buf[...].astype(bf16)


def prepare_kernel(
    table_ref,
    region_ref,
    wqkv_ref,
    bias_out,
    label_row_out,
    label_col_out,
    wqkv_t_out,
    flat,
    rows,
    wide,
    marks,
):
    wqkv_t_out[...] = wqkv_ref[...].astype(f32).T.astype(bf16)
    last = lax.axis_index("lat") == lax.axis_size("lat") - 1
    level = lax.broadcasted_iota(jnp.int32, (4, 2 * WLON), 0)
    for i in range(WLAT):
        wrapped = 2 * (level >= 4 - WZ // 2).astype(jnp.int32)
        if i >= WLAT // 2:
            wrapped = wrapped + last.astype(jnp.int32)
        marks[4 * i : 4 * (i + 1), :] = (4 * region_ref[i] + wrapped).astype(f32)
    place = lax.broadcasted_iota(jnp.int32, (POS, 4 * WLAT), 0)
    lane = lax.broadcasted_iota(jnp.int32, (POS, 4 * WLAT), 1)
    lon = quotient(place, PAIR)
    pair = place - PAIR * lon
    upper = (pair >= WLAT).astype(jnp.int32)
    source = 4 * (pair - WLAT * upper) + upper
    columns = []
    for n in range(2):
        chosen = mm((lane == source + WZ * n).astype(f32).astype(bf16), marks[...].astype(bf16))
        for c in range(2):
            own = jnp.where(lane == lon + WLON * c, chosen, 0.0)
            columns.append(jnp.sum(own, axis=1, keepdims=True))
    label_col_out[...] = jnp.concatenate(columns, axis=1)
    spread = jnp.concatenate([jnp.broadcast_to(v, (POS, LANES)) for v in columns], axis=1).T
    labels = jnp.concatenate([spread[k * LANES : k * LANES + 1] for k in range(4)], axis=0)
    label_row_out[...] = jnp.concatenate([labels] * HEADS, axis=1)
    part = PAIR // WZ * SPREAD
    for k in range(2 * HEADS):
        flat[k : k + 1, :] = table_ref[k]
    rows[...] = jnp.zeros_like(rows)
    for a in range(WZ):
        for c in range(WLAT):
            pieces = []
            for b in range(WZ):
                start = ((a * WZ + b) * WLAT + c) * part
                pieces.append(flat[:, start : start + part])
            row = (a * WLAT + c) * SLOTS
            rows[row : row + 2 * HEADS, :] = jnp.concatenate(pieces, axis=1)
    left = rows[...]
    perm = table_order()
    row_perm = row_order()
    total = None
    for _ in range(3):
        low = left.astype(bf16)
        left = left - low.astype(f32)
        term = mm(row_perm, mm(low, perm).astype(bf16))
        total = term if total is None else total + term
    total = total.reshape(2 * HEADS, SLOTS, TAB)
    for o in range(WLON):
        start = PAIR * (WLON - 1 - o)
        wide[:, PAIR * o : PAIR * (o + 1), :] = total[:, :PAIR, start : start + POS]
    for n in range(2):
        bias_out[n] = wide[n * HEADS : (n + 1) * HEADS].reshape(ROWS, POS).T * LOG2E


def unpack_kernel(grad_ref, table_out, flat):
    part = PAIR // WZ * SPREAD
    for n in range(2):
        halves = []
        for k in range(2):
            dense = grad_ref[2 * n + k].astype(f32)
            rest = dense[2 * QUARTER : 2 * QUARTER + HEADS]
            rest = [rest[:, g * REST : (g + 1) * REST] for g in range(WLAT)]
            rest = jnp.concatenate(rest, axis=0)
            parts = [dense[:QUARTER], dense[QUARTER : 2 * QUARTER], rest]
            halves.append(jnp.concatenate(parts, axis=1))
        for a in range(WZ):
            for c in range(WLAT):
                row = c * HEADS
                chunk = halves[a][row : row + HEADS]
                for b in range(WZ):
                    start = ((a * WZ + b) * WLAT + c) * part
                    flat[n * HEADS : (n + 1) * HEADS, start : start + part] = chunk[
                        :, b * part : (b + 1) * part
                    ]
    for k in range(2 * HEADS):
        table_out[k] = flat[k : k + 1, :]


def add_kernel(parts_ref, copies_out):
    total = parts_ref[0].astype(f32)
    for k in range(1, parts_ref.shape[0]):
        total = total + parts_ref[k].astype(f32)
    total = total.astype(bf16)
    for k in range(copies_out.shape[0]):
        copies_out[k] = total


def finish_kernel(own_ref, lat_ref, diag_ref, lon_ref, out_ref, grad_ref):
    half = WLAT // 2
    edge = WLON // 2
    inner = 2 * WLON - edge
    lat_part = lat_ref[...].astype(f32)
    diag_part = diag_ref[...].astype(f32)
    lon_part = lon_ref[...].astype(f32)
    for t, target in enumerate((out_ref, grad_ref)):
        for z in range(4):
            for i in range(half):
                k = z * half + i
                parts = (get(diag_part, t, k * edge, edge), get(lat_part, t, k * inner, inner))
                slab = [jnp.concatenate([parts[0][j], parts[1][j]], axis=0) for j in range(2)]
                target[z, i] = jnp.concatenate(slab, axis=1).astype(bf16)
                slab = jnp.concatenate(get(lon_part, t, k * edge, edge), axis=1)
                own = own_ref[t, z, i].astype(f32)
                target[z, half + i] = jnp.concatenate([slab, own], axis=0).astype(bf16)


def lon_sum(quarters, strips):
    lons = lax.axis_size("lon")
    near = [[4 * k + j for j in range(4)] for k in range(lons // 4)]
    far = [[4 * k + j for k in range(lons // 4)] for j in range(4)]

    def exchange(parts, groups):
        return lax.all_to_all(parts, "lon", 0, 0, axis_index_groups=groups)

    def added(parts, copies):
        vmem = pl.BlockSpec(memory_space=pltpu.VMEM)
        return pl.pallas_call(
            add_kernel,
            out_shape=jax.ShapeDtypeStruct((copies,) + parts.shape[1:], bf16),
            in_specs=[vmem],
            out_specs=vmem,
            compiler_params=pltpu.CompilerParams(vmem_limit_bytes=VMEM_BYTES),
            name="add",
        )(parts)

    parts = added(exchange(quarters, near), lons // 4)
    parts, strips = lax.optimization_barrier((parts, strips))
    steps = ((1, 0), (1, 1), (0, 1))
    strips = [shifted(strip, *step) for strip, step in zip(strips, steps)]
    parts = exchange(parts, far)
    parts, strips = lax.optimization_barrier((added(parts, 4), strips))
    return exchange(parts, near), strips


def body(
    field_in,
    cotangent,
    ln1_gain,
    w_qkv,
    w_proj,
    ln2_gain,
    w_up,
    w_down,
    bias_table,
    region_ids,
    keep_flags,
):
    levels, lat_rows, lon_cols, channels = field_in.shape
    half = WLAT // 2
    edge = WLON // 2
    inner = lon_cols - edge
    vmem = pl.BlockSpec(memory_space=pltpu.VMEM)
    smem = pl.BlockSpec(memory_space=pltpu.SMEM)
    sizes = [3 * levels * half * size for size in (inner, edge, edge)]
    packed = tuple(jax.ShapeDtypeStruct((size, LANES), bf16) for size in sizes)
    buffers = [pltpu.VMEM((size, LANES), f32) for size in sizes]
    params = pltpu.CompilerParams(vmem_limit_bytes=VMEM_BYTES)
    lat_part = pl.pallas_call(
        pack_lat_kernel,
        out_shape=packed[0],
        in_specs=[pl.BlockSpec(memory_space=pltpu.HBM)] * 2,
        out_specs=vmem,
        scratch_shapes=buffers[:1]
        + [pltpu.VMEM((2, levels, half, lon_cols, C), bf16), pltpu.SemaphoreType.DMA((2,))],
        compiler_params=params,
        name="pack_lat",
    )(field_in, cotangent)
    diag_part, lon_part = pl.pallas_call(
        pack_edge_kernel,
        out_shape=packed[1:],
        in_specs=[vmem] * 2 + [pl.BlockSpec(memory_space=pl.ANY)],
        out_specs=(vmem,) * 2,
        scratch_shapes=buffers[1:],
        compiler_params=params,
        name="pack_edge",
    )(field_in, cotangent, lat_part)
    lat_part = shifted(lat_part, -1, 0)
    diag_part = shifted(diag_part, -1, -1)
    lon_part = shifted(lon_part, 0, -1)

    bias_wide, label_row, label_col, weights_t = pl.pallas_call(
        prepare_kernel,
        out_shape=(
            jax.ShapeDtypeStruct((2, POS, ROWS), f32),
            jax.ShapeDtypeStruct((4, ROWS), f32),
            jax.ShapeDtypeStruct((POS, 4), f32),
            jax.ShapeDtypeStruct((3 * C, C), bf16),
        ),
        in_specs=[vmem] * 3,
        out_specs=(vmem,) * 4,
        scratch_shapes=[
            pltpu.VMEM((2 * HEADS, PAIR * TAB), f32),
            pltpu.VMEM((PAIR * SLOTS, TAB), f32),
            pltpu.VMEM((2 * HEADS, POS, POS), f32),
            pltpu.VMEM((4 * WLAT, 2 * WLON), f32),
        ],
        compiler_params=params,
        name="prepare",
    )(
        bias_table.reshape(2 * HEADS, 1, PAIR * TAB),
        region_ids.transpose(1, 0, 2),
        w_qkv,
    )
    positions = levels * lat_rows * lon_cols
    gain1 = ln1_gain.reshape(1, C)
    fold, own, *strips = pl.pallas_call(
        block_kernel,
        out_shape=(
            jax.ShapeDtypeStruct((4, DENSE, LANES), bf16),
            jax.ShapeDtypeStruct((2, levels, half, inner, C), bf16),
        )
        + packed,
        in_specs=[vmem] * 14 + [smem],
        out_specs=(vmem,) * 5,
        scratch_shapes=[
            pltpu.VMEM((2, positions, C), f32),
            pltpu.VMEM((HEADS, POS, POS), f32),
            pltpu.VMEM((DENSE, LANES), f32),
        ]
        + buffers,
        compiler_params=params,
        name="block",
    )(
        field_in,
        cotangent,
        lon_part,
        lat_part,
        diag_part,
        gain1,
        weights_t,
        w_proj,
        ln2_gain.reshape(1, C),
        w_up,
        w_down.T,
        bias_wide,
        label_row,
        label_col,
        keep_flags,
    )
    grads, (lat_back, diag_back, lon_back) = lon_sum(fold, strips)
    grads = pl.pallas_call(
        unpack_kernel,
        out_shape=jax.ShapeDtypeStruct((2 * HEADS, 1, PAIR * TAB), f32),
        in_specs=[vmem],
        out_specs=vmem,
        scratch_shapes=[pltpu.VMEM((2 * HEADS, PAIR * TAB), f32)],
        compiler_params=params,
        name="unpack",
    )(grads)
    grads = grads.reshape(2, 1, HEADS, PAIR * TAB)
    result, grad_field = pl.pallas_call(
        finish_kernel,
        out_shape=(jax.ShapeDtypeStruct(field_in.shape, bf16),) * 2,
        in_specs=[vmem] * 4,
        out_specs=(vmem,) * 2,
        compiler_params=params,
        name="finish",
    )(own, lat_back, diag_back, lon_back)
    return (result, grad_field, grads)


def solution(mesh):
    placed = (
        P(None, "lat", "lon", None),
        P(None, "lat", "lon", None),
        P(),
        P(),
        P(),
        P(),
        P(),
        P(),
        P(None, "lat", None, None),
        P(None, "lat", "lon"),
        P(None, "lat", "lon"),
    )
    return jax.shard_map(
        body,
        mesh=mesh,
        in_specs=placed,
        out_specs=(
            P(None, "lat", "lon", None),
            P(None, "lat", "lon", None),
            P(None, "lat", None, None),
        ),
        check_vma=False,
    )
```

```python
import math

import jax
import jax.numpy as jnp
from jax import lax
from jax.experimental import pallas as pl
from jax.experimental.pallas import tpu as pltpu
from jax.sharding import PartitionSpec as P

C = 192
HEADS = 6
HD = 32
FF = 768
WZ = 2
WLAT = 6
WLON = 12
SPREAD = 2 * WLON - 1
POS = WZ * WLAT * WLON
PAIR = WZ * WLAT
TAB = PAIR * SPREAD
ROWS = HEADS * POS
SLOTS = 16
QUARTER = PAIR * HEADS // 2
REST = 20
DENSE = 80
LANES = 128

epsilon = 1e-05
keep_share = 0.8
LOG2E = math.log2(math.e)
gelu_coef = 0.044715
VMEM_BYTES = 16 * 1024 * 1024
bf16 = jnp.bfloat16
f32 = jnp.float32


def shifted(block, lat_step, lon_step):
    lats, lons = lax.axis_size("lat"), lax.axis_size("lon")
    route = []
    for a in range(lats):
        for b in range(lons):
            target = ((a + lat_step) % lats) * lons + (b + lon_step) % lons
            route.append((a * lons + b, target))
    return lax.ppermute(block, ("lat", "lon"), route)


def mm(a, b):
    return lax.dot_general(a, b, (((1,), (0,)), ((), ())), preferred_element_type=f32)


def mm_nt(a, b):
    return lax.dot_general(a, b, (((1,), (1,)), ((), ())), preferred_element_type=f32)


def norm_parts(values, gain):
    row_mean = jnp.mean(values, axis=-1, keepdims=True)
    centred = values - row_mean
    variance = jnp.mean(centred * centred, axis=-1, keepdims=True)
    inverse = lax.rsqrt(variance + epsilon)
    normed = centred * inverse
    return normed * gain, normed, inverse


def norm_back(grad_in, gain, normed, inverse):
    scaled = grad_in * gain
    first_mean = jnp.mean(scaled, axis=-1, keepdims=True)
    second_mean = jnp.mean(scaled * normed, axis=-1, keepdims=True)
    return (scaled - first_mean - normed * second_mean) * inverse


def gelu_parts(values):
    factor = math.sqrt(2.0 / math.pi)
    square = values * values
    tangent = jnp.tanh(values * (factor + (gelu_coef * factor) * square))
    half = 0.5 + 0.5 * tangent
    result = values * half
    derivative = half + result * (1.0 - tangent) * (factor + (3.0 * gelu_coef * factor) * square)
    return result, derivative


def head_blocks(wide):
    return jnp.concatenate(
        [wide[h * HD : (h + 1) * HD, h * POS : (h + 1) * POS] for h in range(HEADS)], axis=0
    )


def spread_heads(rows, head_mask):
    return jnp.concatenate([rows * head_mask[h : h + 1, :] for h in range(HEADS)], axis=0)


def quotient(values, divisor):
    return (values * (2**20 // divisor + 1)) >> 20


def one_hot(rows, columns, target):
    row = lax.broadcasted_iota(jnp.int32, (rows, 1), 0)
    column = lax.broadcasted_iota(jnp.int32, (rows, columns), 1)
    return (column == target(row)).astype(f32).astype(bf16)


def window_order():
    def target(row):
        c = (row >= POS).astype(jnp.int32)
        row = row - POS * c
        j = quotient(row, PAIR)
        return (row - PAIR * j) * (2 * WLON) + c * WLON + j

    return one_hot(2 * POS, 2 * POS, target)


def natural_order():
    def target(row):
        pair = quotient(row, 2 * WLON)
        lon = row - 2 * WLON * pair
        c = (lon >= WLON).astype(jnp.int32)
        return c * POS + (lon - WLON * c) * PAIR + pair

    return one_hot(2 * POS, 2 * POS, target)


def table_order():
    def target(row):
        pair = quotient(row, SPREAD)
        return (SPREAD - 1 - (row - SPREAD * pair)) * PAIR + pair

    return one_hot(TAB, TAB, target)


def chunk_order():
    def target(row):
        pair = quotient(row, HEADS)
        return (row - HEADS * pair) * SLOTS + pair

    return one_hot(PAIR * HEADS, HEADS * SLOTS, target)


def row_order():
    def target(row):
        head = quotient(row, SLOTS)
        return (row - SLOTS * head) * SLOTS + head

    return one_hot(2 * HEADS * SLOTS, PAIR * SLOTS, target)


def put(packed, t, row, slab):
    third = packed.shape[0] // 3
    size = slab.shape[0]
    rest = C - LANES
    packed[t * third + row : t * third + row + size, :] = slab[:, :LANES]
    packed[2 * third + row : 2 * third + row + size, t * rest : (t + 1) * rest] = slab[:, LANES:]


def get(packed, t, row, size):
    third = packed.shape[0] // 3
    rest = C - LANES
    return (
        packed[t * third + row : t * third + row + size, :],
        packed[2 * third + row : 2 * third + row + size, t * rest : (t + 1) * rest],
    )


def pack_lat_kernel(field_ref, cot_ref, lat_out, lat_buf, rows, arrived):
    half = WLAT // 2
    edge = WLON // 2
    inner = 2 * WLON - edge
    sources = (field_ref, cot_ref)
    copies = [
        pltpu.make_async_copy(sources[t].at[:, pl.ds(0, half)], rows.at[t], arrived.at[t])
        for t in range(2)
    ]
    for copy in copies:
        copy.start()
    for t in range(2):
        copies[t].wait()
        for z in range(4):
            for i in range(half):
                put(lat_buf, t, (z * half + i) * inner, rows[t, z, i].astype(f32)[edge:])
    lat_out[...] = lat_buf[...].astype(bf16)


def pack_edge_kernel(field_ref, cot_ref, after_ref, diag_out, lon_out, diag_buf, lon_buf):
    half = WLAT // 2
    edge = WLON // 2
    for t, source in enumerate((field_ref, cot_ref)):
        for z in range(4):
            for i in range(half):
                row = (z * half + i) * edge
                put(diag_buf, t, row, source[z, i].astype(f32)[:edge])
                put(lon_buf, t, row, source[z, half + i].astype(f32)[:edge])
    diag_out[...] = diag_buf[...].astype(bf16)
    lon_out[...] = lon_buf[...].astype(bf16)


def block_kernel(
    field_ref,
    cot_ref,
    lon_ref,
    lat_ref,
    diag_ref,
    gain1_ref,
    wqkv_t_ref,
    wproj_ref,
    gain2_ref,
    wup_ref,
    wdown_t_ref,
    bias_ref,
    label_row_ref,
    label_col_ref,
    keep_ref,
    fold_out,
    own_out,
    lat_out,
    diag_out,
    lon_out,
    frame,
    wide,
    dense,
    lat_buf,
    diag_buf,
    lon_buf,
):
    half = WLAT // 2
    cols = 2 * WLON
    edge = WLON // 2
    inner = cols - edge
    root = 1.0 / math.sqrt(HD)
    lon_part = lon_ref[...].astype(f32)
    lat_part = lat_ref[...].astype(f32)
    diag_part = diag_ref[...].astype(f32)
    for t, own in enumerate((field_ref, cot_ref)):
        for level in range(4):
            z = (level + 1) % 4
            for i in range(half):
                k = z * half + i
                row = (level * WLAT + i) * cols
                frame[t, row : row + inner, :] = own[z, half + i].astype(f32)[edge:, :]
                main, rest = get(lon_part, t, k * edge, edge)
                frame[t, row + inner : row + cols, :LANES] = main
                frame[t, row + inner : row + cols, LANES:] = rest
                row = (level * WLAT + half + i) * cols
                main, rest = get(lat_part, t, k * inner, inner)
                frame[t, row : row + inner, :LANES] = main
                frame[t, row : row + inner, LANES:] = rest
                main, rest = get(diag_part, t, k * edge, edge)
                frame[t, row + inner : row + cols, :LANES] = main
                frame[t, row + inner : row + cols, LANES:] = rest
    gain1 = gain1_ref[...]
    gain2 = gain2_ref[...]
    wq_t = wqkv_t_ref[0:C, :]
    wk_t = wqkv_t_ref[C : 2 * C, :]
    wv_t = wqkv_t_ref[2 * C : 3 * C, :]
    head = lax.broadcasted_iota(jnp.int32, (HEADS, C), 0)
    head_mask = (lax.broadcasted_iota(jnp.int32, (HEADS, C), 1) >> 5) == head
    head_mask = head_mask.astype(f32).astype(bf16)
    perm = window_order()
    perm_t = natural_order()
    table_perm = table_order()
    chunk_perm = chunk_order()
    dense[...] = jnp.zeros_like(dense)
    for n in range(2):
        both = slice(n * 2 * POS, (n + 1) * 2 * POS)
        x = mm(perm, frame[0, both, :].astype(bf16))
        cot = mm(perm, frame[1, both, :].astype(bf16))
        scaled1, normed1, inverse1 = norm_parts(x, gain1)
        h1 = scaled1.astype(bf16)
        q_all = mm_nt(h1, wq_t).astype(bf16)
        k_all = mm_nt(h1, wk_t).astype(bf16)
        v_all = mm_nt(h1, wv_t).astype(bf16)
        saved = []
        branches = []
        for c in range(2):
            w = 2 * n + c
            rows = slice(c * POS, (c + 1) * POS)
            v_t = mm_nt(wv_t, h1[rows]).astype(bf16)
            q_wide = spread_heads(q_all[rows], head_mask)
            scores = mm_nt(k_all[rows], q_wide) * (root * LOG2E) + bias_ref[n]
            allowed = label_col_ref[:, w : w + 1] == label_row_ref[w : w + 1, :]
            scores = jnp.where(allowed, scores, -1e30)
            weights = jnp.exp2(scores - jnp.max(scores, axis=0, keepdims=True))
            probs = weights * (1.0 / jnp.sum(weights, axis=0, keepdims=True))
            probs_low = probs.astype(bf16)
            attended = head_blocks(mm(v_t, probs_low)).T.astype(bf16)
            factor = keep_ref[n, 0, c].astype(f32) * (1.0 / keep_share)
            branches.append((mm(attended, wproj_ref[...]) * factor).astype(bf16).astype(f32))
            saved.append((q_wide, probs, probs_low))
        y_sum = x + jnp.concatenate(branches, axis=0)
        scaled2, normed2, inverse2 = norm_parts(y_sum, gain2)
        act, slope = gelu_parts(mm(scaled2.astype(bf16), wup_ref[...]))
        result = (y_sum + mm_nt(act.astype(bf16), wdown_t_ref[...])).astype(bf16)
        grad_up = (mm(cot.astype(bf16), wdown_t_ref[...]) * slope).astype(bf16)
        grad_sum = cot + norm_back(mm_nt(grad_up, wup_ref[...]), gain2, normed2, inverse2)
        grad_low_in = grad_sum.astype(bf16).astype(f32)
        folded = None
        grad_h1 = []
        for c in range(2):
            rows = slice(c * POS, (c + 1) * POS)
            q_wide, probs, probs_low = saved[c]
            factor = keep_ref[n, 0, c].astype(f32) * (1.0 / keep_share)
            grad_branch = (grad_low_in[rows] * factor).astype(bf16)
            grad_att = mm_nt(grad_branch, wproj_ref[...]).astype(bf16)
            g_wide = spread_heads(grad_att, head_mask)
            grad_probs = mm_nt(v_all[rows], g_wide)
            inner_sum = jnp.sum(probs * grad_probs, axis=0, keepdims=True)
            grad_scores = probs * (grad_probs - inner_sum)
            folded = grad_scores if folded is None else folded + grad_scores
            grad_low = grad_scores.astype(bf16)
            k_t = mm_nt(wk_t, h1[rows]).astype(bf16)
            grad_q = (head_blocks(mm(k_t, grad_low)).T * root).astype(bf16)
            grad_k = (mm(grad_low, q_wide) * root).astype(bf16)
            grad_v = mm(probs_low, g_wide).astype(bf16)
            grad_h1.append(mm(grad_q, wq_t) + mm(grad_k, wk_t) + mm(grad_v, wv_t))
        wide[...] = folded.T.reshape(HEADS, POS, POS)
        total = None
        for o in range(WLON):
            left = PAIR * (WLON - 1 - o)
            right = TAB - POS - left
            parts = [wide[:, PAIR * o : PAIR * (o + 1), :]]
            if left:
                parts = [jnp.zeros((HEADS, PAIR, left), f32)] + parts
            if right:
                parts = parts + [jnp.zeros((HEADS, PAIR, right), f32)]
            piece = jnp.concatenate(parts, axis=2)
            total = piece if total is None else total + piece
        total = jnp.concatenate([total, jnp.zeros((HEADS, SLOTS - PAIR, TAB), f32)], axis=1)
        total = total.reshape(HEADS * SLOTS, TAB).astype(bf16)
        total = mm_nt(total, table_perm).astype(bf16)
        total = mm(chunk_perm, total)
        for k in range(2):
            part = total[k * QUARTER : (k + 1) * QUARTER]
            dense[:QUARTER, :] = part[:, :LANES]
            dense[QUARTER : 2 * QUARTER, :] = part[:, LANES : 2 * LANES]
            rest = [part[HEADS * g : HEADS * (g + 1), 2 * LANES :] for g in range(WLAT)]
            dense[2 * QUARTER : 2 * QUARTER + HEADS, : WLAT * REST] = jnp.concatenate(rest, axis=1)
            count = fold_out.shape[0] // 4
            size = DENSE // count
            spare = jnp.zeros((fold_out.shape[1] - size, LANES), f32)
            for j in range(count):
                share = jnp.concatenate([dense[j * size : (j + 1) * size, :], spare], axis=0)
                fold_out[(2 * n + k) * count + j] = share.astype(bf16)
        grad_h1 = jnp.concatenate(grad_h1, axis=0).astype(bf16).astype(f32)
        grad_field = (grad_sum + norm_back(grad_h1, gain1, normed1, inverse1)).astype(bf16)
        for t, value in enumerate((result, grad_field)):
            natural = mm(perm_t, value)
            for dz in range(WZ):
                z = (2 * n + dz + 1) % 4
                for i in range(half):
                    k = z * half + i
                    row = (dz * WLAT + i) * cols
                    slab = natural[row : row + cols]
                    own_out[t, z, i] = slab[:inner].astype(bf16)
                    put(lon_buf, t, k * edge, slab[inner:])
                    row = (dz * WLAT + half + i) * cols
                    slab = natural[row : row + cols]
                    put(lat_buf, t, k * inner, slab[:inner])
                    put(diag_buf, t, k * edge, slab[inner:])
    lat_out[...] = lat_buf[...].astype(bf16)
    diag_out[...] = diag_buf[...].astype(bf16)
    lon_out[...] = lon_buf[...].astype(bf16)


def prepare_kernel(
    table_ref,
    region_ref,
    wqkv_ref,
    bias_out,
    label_row_out,
    label_col_out,
    wqkv_t_out,
    flat,
    rows,
    wide,
    marks,
):
    wqkv_t_out[...] = wqkv_ref[...].astype(f32).T.astype(bf16)
    last = lax.axis_index("lat") == lax.axis_size("lat") - 1
    level = lax.broadcasted_iota(jnp.int32, (4, 2 * WLON), 0)
    for i in range(WLAT):
        wrapped = 2 * (level >= 4 - WZ // 2).astype(jnp.int32)
        if i >= WLAT // 2:
            wrapped = wrapped + last.astype(jnp.int32)
        marks[4 * i : 4 * (i + 1), :] = (4 * region_ref[i] + wrapped).astype(f32)
    place = lax.broadcasted_iota(jnp.int32, (POS, 4 * WLAT), 0)
    lane = lax.broadcasted_iota(jnp.int32, (POS, 4 * WLAT), 1)
    lon = quotient(place, PAIR)
    pair = place - PAIR * lon
    upper = (pair >= WLAT).astype(jnp.int32)
    source = 4 * (pair - WLAT * upper) + upper
    columns = []
    for n in range(2):
        chosen = mm((lane == source + WZ * n).astype(f32).astype(bf16), marks[...].astype(bf16))
        for c in range(2):
            own = jnp.where(lane == lon + WLON * c, chosen, 0.0)
            columns.append(jnp.sum(own, axis=1, keepdims=True))
    label_col_out[...] = jnp.concatenate(columns, axis=1)
    spread = jnp.concatenate([jnp.broadcast_to(v, (POS, LANES)) for v in columns], axis=1).T
    labels = jnp.concatenate([spread[k * LANES : k * LANES + 1] for k in range(4)], axis=0)
    label_row_out[...] = jnp.concatenate([labels] * HEADS, axis=1)
    part = PAIR // WZ * SPREAD
    for k in range(2 * HEADS):
        flat[k : k + 1, :] = table_ref[k]
    rows[...] = jnp.zeros_like(rows)
    for a in range(WZ):
        for c in range(WLAT):
            pieces = []
            for b in range(WZ):
                start = ((a * WZ + b) * WLAT + c) * part
                pieces.append(flat[:, start : start + part])
            row = (a * WLAT + c) * SLOTS
            rows[row : row + 2 * HEADS, :] = jnp.concatenate(pieces, axis=1)
    left = rows[...]
    perm = table_order()
    row_perm = row_order()
    total = None
    for _ in range(3):
        low = left.astype(bf16)
        left = left - low.astype(f32)
        term = mm(row_perm, mm(low, perm).astype(bf16))
        total = term if total is None else total + term
    total = total.reshape(2 * HEADS, SLOTS, TAB)
    for o in range(WLON):
        start = PAIR * (WLON - 1 - o)
        wide[:, PAIR * o : PAIR * (o + 1), :] = total[:, :PAIR, start : start + POS]
    for n in range(2):
        bias_out[n] = wide[n * HEADS : (n + 1) * HEADS].reshape(ROWS, POS).T * LOG2E


def unpack_kernel(grad_ref, table_out, flat):
    part = PAIR // WZ * SPREAD
    for n in range(2):
        halves = []
        for k in range(2):
            count = grad_ref.shape[0] // 4
            size = DENSE // count
            shares = [grad_ref[(2 * n + k) * count + j].astype(f32)[:size] for j in range(count)]
            dense = jnp.concatenate(shares, axis=0)
            rest = dense[2 * QUARTER : 2 * QUARTER + HEADS]
            rest = [rest[:, g * REST : (g + 1) * REST] for g in range(WLAT)]
            rest = jnp.concatenate(rest, axis=0)
            parts = [dense[:QUARTER], dense[QUARTER : 2 * QUARTER], rest]
            halves.append(jnp.concatenate(parts, axis=1))
        for a in range(WZ):
            for c in range(WLAT):
                row = c * HEADS
                chunk = halves[a][row : row + HEADS]
                for b in range(WZ):
                    start = ((a * WZ + b) * WLAT + c) * part
                    flat[n * HEADS : (n + 1) * HEADS, start : start + part] = chunk[
                        :, b * part : (b + 1) * part
                    ]
    for k in range(2 * HEADS):
        table_out[k] = flat[k : k + 1, :]


def add_kernel(parts_ref, copies_out):
    total = parts_ref[0].astype(f32)
    for k in range(1, parts_ref.shape[0]):
        total = total + parts_ref[k].astype(f32)
    total = total.astype(bf16)
    for k in range(copies_out.shape[0]):
        copies_out[k] = total


def finish_kernel(own_ref, lat_ref, diag_ref, lon_ref, out_ref, grad_ref):
    half = WLAT // 2
    edge = WLON // 2
    inner = 2 * WLON - edge
    lat_part = lat_ref[...].astype(f32)
    diag_part = diag_ref[...].astype(f32)
    lon_part = lon_ref[...].astype(f32)
    for t, target in enumerate((out_ref, grad_ref)):
        for z in range(4):
            for i in range(half):
                k = z * half + i
                parts = (get(diag_part, t, k * edge, edge), get(lat_part, t, k * inner, inner))
                slab = [jnp.concatenate([parts[0][j], parts[1][j]], axis=0) for j in range(2)]
                target[z, i] = jnp.concatenate(slab, axis=1).astype(bf16)
                slab = jnp.concatenate(get(lon_part, t, k * edge, edge), axis=1)
                own = own_ref[t, z, i].astype(f32)
                target[z, half + i] = jnp.concatenate([slab, own], axis=0).astype(bf16)


def lon_sum(shares, strips):
    def exchange(parts):
        return lax.all_to_all(parts, "lon", 0, 0)

    vmem = pl.BlockSpec(memory_space=pltpu.VMEM)
    parts = pl.pallas_call(
        add_kernel,
        out_shape=jax.ShapeDtypeStruct(shares.shape, bf16),
        in_specs=[vmem],
        out_specs=vmem,
        compiler_params=pltpu.CompilerParams(vmem_limit_bytes=VMEM_BYTES),
        name="add",
    )(exchange(shares))
    parts, strips = lax.optimization_barrier((parts, strips))
    steps = ((1, 0), (1, 1), (0, 1))
    strips = [shifted(strip, *step) for strip, step in zip(strips, steps)]
    return exchange(parts), strips


def body(
    field_in,
    cotangent,
    ln1_gain,
    w_qkv,
    w_proj,
    ln2_gain,
    w_up,
    w_down,
    bias_table,
    region_ids,
    keep_flags,
):
    levels, lat_rows, lon_cols, channels = field_in.shape
    half = WLAT // 2
    edge = WLON // 2
    inner = lon_cols - edge
    vmem = pl.BlockSpec(memory_space=pltpu.VMEM)
    smem = pl.BlockSpec(memory_space=pltpu.SMEM)
    sizes = [3 * levels * half * size for size in (inner, edge, edge)]
    packed = tuple(jax.ShapeDtypeStruct((size, LANES), bf16) for size in sizes)
    buffers = [pltpu.VMEM((size, LANES), f32) for size in sizes]
    params = pltpu.CompilerParams(vmem_limit_bytes=VMEM_BYTES)
    lat_part = pl.pallas_call(
        pack_lat_kernel,
        out_shape=packed[0],
        in_specs=[pl.BlockSpec(memory_space=pltpu.HBM)] * 2,
        out_specs=vmem,
        scratch_shapes=buffers[:1]
        + [pltpu.VMEM((2, levels, half, lon_cols, C), bf16), pltpu.SemaphoreType.DMA((2,))],
        compiler_params=params,
        name="pack_lat",
    )(field_in, cotangent)
    diag_part, lon_part = pl.pallas_call(
        pack_edge_kernel,
        out_shape=packed[1:],
        in_specs=[vmem] * 2 + [pl.BlockSpec(memory_space=pl.ANY)],
        out_specs=(vmem,) * 2,
        scratch_shapes=buffers[1:],
        compiler_params=params,
        name="pack_edge",
    )(field_in, cotangent, lat_part)
    lat_part = shifted(lat_part, -1, 0)
    diag_part = shifted(diag_part, -1, -1)
    lon_part = shifted(lon_part, 0, -1)

    bias_wide, label_row, label_col, weights_t = pl.pallas_call(
        prepare_kernel,
        out_shape=(
            jax.ShapeDtypeStruct((2, POS, ROWS), f32),
            jax.ShapeDtypeStruct((4, ROWS), f32),
            jax.ShapeDtypeStruct((POS, 4), f32),
            jax.ShapeDtypeStruct((3 * C, C), bf16),
        ),
        in_specs=[vmem] * 3,
        out_specs=(vmem,) * 4,
        scratch_shapes=[
            pltpu.VMEM((2 * HEADS, PAIR * TAB), f32),
            pltpu.VMEM((PAIR * SLOTS, TAB), f32),
            pltpu.VMEM((2 * HEADS, POS, POS), f32),
            pltpu.VMEM((4 * WLAT, 2 * WLON), f32),
        ],
        compiler_params=params,
        name="prepare",
    )(
        bias_table.reshape(2 * HEADS, 1, PAIR * TAB),
        region_ids.transpose(1, 0, 2),
        w_qkv,
    )
    positions = levels * lat_rows * lon_cols
    lons = lax.axis_size("lon")
    share_rows = -(-4 * DENSE // lons // 16) * 16
    gain1 = ln1_gain.reshape(1, C)
    fold, own, *strips = pl.pallas_call(
        block_kernel,
        out_shape=(
            jax.ShapeDtypeStruct((lons, share_rows, LANES), bf16),
            jax.ShapeDtypeStruct((2, levels, half, inner, C), bf16),
        )
        + packed,
        in_specs=[vmem] * 14 + [smem],
        out_specs=(vmem,) * 5,
        scratch_shapes=[
            pltpu.VMEM((2, positions, C), f32),
            pltpu.VMEM((HEADS, POS, POS), f32),
            pltpu.VMEM((DENSE, LANES), f32),
        ]
        + buffers,
        compiler_params=params,
        name="block",
    )(
        field_in,
        cotangent,
        lon_part,
        lat_part,
        diag_part,
        gain1,
        weights_t,
        w_proj,
        ln2_gain.reshape(1, C),
        w_up,
        w_down.T,
        bias_wide,
        label_row,
        label_col,
        keep_flags,
    )
    grads, (lat_back, diag_back, lon_back) = lon_sum(fold, strips)
    grads = pl.pallas_call(
        unpack_kernel,
        out_shape=jax.ShapeDtypeStruct((2 * HEADS, 1, PAIR * TAB), f32),
        in_specs=[vmem],
        out_specs=vmem,
        scratch_shapes=[pltpu.VMEM((2 * HEADS, PAIR * TAB), f32)],
        compiler_params=params,
        name="unpack",
    )(grads)
    grads = grads.reshape(2, 1, HEADS, PAIR * TAB)
    result, grad_field = pl.pallas_call(
        finish_kernel,
        out_shape=(jax.ShapeDtypeStruct(field_in.shape, bf16),) * 2,
        in_specs=[vmem] * 4,
        out_specs=(vmem,) * 2,
        compiler_params=params,
        name="finish",
    )(own, lat_back, diag_back, lon_back)
    return (result, grad_field, grads)


def solution(mesh):
    placed = (
        P(None, "lat", "lon", None),
        P(None, "lat", "lon", None),
        P(),
        P(),
        P(),
        P(),
        P(),
        P(),
        P(None, "lat", None, None),
        P(None, "lat", "lon"),
        P(None, "lat", "lon"),
    )
    return jax.shard_map(
        body,
        mesh=mesh,
        in_specs=placed,
        out_specs=(
            P(None, "lat", "lon", None),
            P(None, "lat", "lon", None),
            P(None, "lat", None, None),
        ),
        check_vma=False,
    )
```

```python
import math

import jax
import jax.numpy as jnp
from jax import lax
from jax.experimental import pallas as pl
from jax.experimental.pallas import tpu as pltpu
from jax.sharding import PartitionSpec as P

C = 192
HEADS = 6
HD = 32
FF = 768
WZ = 2
WLAT = 6
WLON = 12
SPREAD = 2 * WLON - 1
POS = WZ * WLAT * WLON
PAIR = WZ * WLAT
TAB = PAIR * SPREAD
ROWS = HEADS * POS
SLOTS = 16
QUARTER = PAIR * HEADS // 2
REST = 20
DENSE = 80
LANES = 128

epsilon = 1e-05
keep_share = 0.8
LOG2E = math.log2(math.e)
gelu_coef = 0.044715
VMEM_BYTES = 16 * 1024 * 1024
bf16 = jnp.bfloat16
f32 = jnp.float32


def shifted(block, lat_step, lon_step):
    lats, lons = lax.axis_size("lat"), lax.axis_size("lon")
    route = []
    for a in range(lats):
        for b in range(lons):
            target = ((a + lat_step) % lats) * lons + (b + lon_step) % lons
            route.append((a * lons + b, target))
    return lax.ppermute(block, ("lat", "lon"), route)


def mm(a, b):
    return lax.dot_general(a, b, (((1,), (0,)), ((), ())), preferred_element_type=f32)


def mm_nt(a, b):
    return lax.dot_general(a, b, (((1,), (1,)), ((), ())), preferred_element_type=f32)


def norm_parts(values, gain):
    row_mean = jnp.mean(values, axis=-1, keepdims=True)
    centred = values - row_mean
    variance = jnp.mean(centred * centred, axis=-1, keepdims=True)
    inverse = lax.rsqrt(variance + epsilon)
    normed = centred * inverse
    return normed * gain, normed, inverse


def norm_back(grad_in, gain, normed, inverse):
    scaled = grad_in * gain
    first_mean = jnp.mean(scaled, axis=-1, keepdims=True)
    second_mean = jnp.mean(scaled * normed, axis=-1, keepdims=True)
    return (scaled - first_mean - normed * second_mean) * inverse


def gelu_parts(values):
    factor = math.sqrt(2.0 / math.pi)
    square = values * values
    tangent = jnp.tanh(values * (factor + (gelu_coef * factor) * square))
    half = 0.5 + 0.5 * tangent
    result = values * half
    derivative = half + result * (1.0 - tangent) * (factor + (3.0 * gelu_coef * factor) * square)
    return result, derivative


def head_blocks(wide):
    return jnp.concatenate(
        [wide[h * HD : (h + 1) * HD, h * POS : (h + 1) * POS] for h in range(HEADS)], axis=0
    )


def spread_heads(rows, head_mask):
    return jnp.concatenate([rows * head_mask[h : h + 1, :] for h in range(HEADS)], axis=0)


def quotient(values, divisor):
    return (values * (2**20 // divisor + 1)) >> 20


def one_hot(rows, columns, target):
    row = lax.broadcasted_iota(jnp.int32, (rows, 1), 0)
    column = lax.broadcasted_iota(jnp.int32, (rows, columns), 1)
    return (column == target(row)).astype(f32).astype(bf16)


def window_order():
    def target(row):
        c = (row >= POS).astype(jnp.int32)
        row = row - POS * c
        j = quotient(row, PAIR)
        return (row - PAIR * j) * (2 * WLON) + c * WLON + j

    return one_hot(2 * POS, 2 * POS, target)


def natural_order():
    def target(row):
        pair = quotient(row, 2 * WLON)
        lon = row - 2 * WLON * pair
        c = (lon >= WLON).astype(jnp.int32)
        return c * POS + (lon - WLON * c) * PAIR + pair

    return one_hot(2 * POS, 2 * POS, target)


def table_order():
    def target(row):
        pair = quotient(row, SPREAD)
        return (SPREAD - 1 - (row - SPREAD * pair)) * PAIR + pair

    return one_hot(TAB, TAB, target)


def chunk_order():
    def target(row):
        pair = quotient(row, HEADS)
        return (row - HEADS * pair) * SLOTS + pair

    return one_hot(PAIR * HEADS, HEADS * SLOTS, target)


def row_order():
    def target(row):
        head = quotient(row, SLOTS)
        return (row - SLOTS * head) * SLOTS + head

    return one_hot(2 * HEADS * SLOTS, PAIR * SLOTS, target)


def put(packed, t, row, slab):
    third = packed.shape[0] // 3
    size = slab.shape[0]
    rest = C - LANES
    packed[t * third + row : t * third + row + size, :] = slab[:, :LANES]
    packed[2 * third + row : 2 * third + row + size, t * rest : (t + 1) * rest] = slab[:, LANES:]


def get(packed, t, row, size):
    third = packed.shape[0] // 3
    rest = C - LANES
    return (
        packed[t * third + row : t * third + row + size, :],
        packed[2 * third + row : 2 * third + row + size, t * rest : (t + 1) * rest],
    )


def pack_lat_kernel(field_ref, cot_ref, lat_out, lat_buf, rows, arrived):
    half = WLAT // 2
    edge = WLON // 2
    inner = 2 * WLON - edge
    sources = (field_ref, cot_ref)
    copies = [
        pltpu.make_async_copy(sources[t].at[:, pl.ds(0, half)], rows.at[t], arrived.at[t])
        for t in range(2)
    ]
    for copy in copies:
        copy.start()
    for t in range(2):
        copies[t].wait()
        for z in range(4):
            for i in range(half):
                put(lat_buf, t, (z * half + i) * inner, rows[t, z, i].astype(f32)[edge:])
    lat_out[...] = lat_buf[...].astype(bf16)


def pack_edge_kernel(field_ref, cot_ref, after_ref, diag_out, lon_out, diag_buf, lon_buf):
    half = WLAT // 2
    edge = WLON // 2
    for t, source in enumerate((field_ref, cot_ref)):
        for z in range(4):
            for i in range(half):
                row = (z * half + i) * edge
                put(diag_buf, t, row, source[z, i].astype(f32)[:edge])
                put(lon_buf, t, row, source[z, half + i].astype(f32)[:edge])
    diag_out[...] = diag_buf[...].astype(bf16)
    lon_out[...] = lon_buf[...].astype(bf16)


def block_kernel(
    field_ref,
    cot_ref,
    lon_ref,
    lat_ref,
    diag_ref,
    gains_ref,
    wqkv_t_ref,
    wproj_ref,
    wup_ref,
    wdown_t_ref,
    bias_ref,
    label_row_ref,
    label_col_ref,
    keep_ref,
    fold_out,
    own_out,
    lat_out,
    diag_out,
    lon_out,
    frame,
    wide,
    dense,
    lat_buf,
    diag_buf,
    lon_buf,
):
    half = WLAT // 2
    cols = 2 * WLON
    edge = WLON // 2
    inner = cols - edge
    root = 1.0 / math.sqrt(HD)
    lon_part = lon_ref[...].astype(f32)
    lat_part = lat_ref[...].astype(f32)
    diag_part = diag_ref[...].astype(f32)
    for t, own in enumerate((field_ref, cot_ref)):
        for level in range(4):
            z = (level + 1) % 4
            for i in range(half):
                k = z * half + i
                row = (level * WLAT + i) * cols
                frame[t, row : row + inner, :] = own[z, half + i].astype(f32)[edge:, :]
                main, rest = get(lon_part, t, k * edge, edge)
                frame[t, row + inner : row + cols, :LANES] = main
                frame[t, row + inner : row + cols, LANES:] = rest
                row = (level * WLAT + half + i) * cols
                main, rest = get(lat_part, t, k * inner, inner)
                frame[t, row : row + inner, :LANES] = main
                frame[t, row : row + inner, LANES:] = rest
                main, rest = get(diag_part, t, k * edge, edge)
                frame[t, row + inner : row + cols, :LANES] = main
                frame[t, row + inner : row + cols, LANES:] = rest
    gain1 = gains_ref[0:1, :]
    gain2 = gains_ref[1:2, :]
    wq_t = wqkv_t_ref[0:C, :]
    wk_t = wqkv_t_ref[C : 2 * C, :]
    wv_t = wqkv_t_ref[2 * C : 3 * C, :]
    head = lax.broadcasted_iota(jnp.int32, (HEADS, C), 0)
    head_mask = (lax.broadcasted_iota(jnp.int32, (HEADS, C), 1) >> 5) == head
    head_mask = head_mask.astype(f32).astype(bf16)
    perm = window_order()
    perm_t = natural_order()
    table_perm = table_order()
    chunk_perm = chunk_order()
    dense[...] = jnp.zeros_like(dense)
    for n in range(2):
        both = slice(n * 2 * POS, (n + 1) * 2 * POS)
        x = mm(perm, frame[0, both, :].astype(bf16))
        cot = mm(perm, frame[1, both, :].astype(bf16))
        scaled1, normed1, inverse1 = norm_parts(x, gain1)
        h1 = scaled1.astype(bf16)
        q_all = mm_nt(h1, wq_t).astype(bf16)
        k_all = mm_nt(h1, wk_t).astype(bf16)
        v_all = mm_nt(h1, wv_t).astype(bf16)
        saved = []
        branches = []
        for c in range(2):
            w = 2 * n + c
            rows = slice(c * POS, (c + 1) * POS)
            v_t = mm_nt(wv_t, h1[rows]).astype(bf16)
            q_wide = spread_heads(q_all[rows], head_mask)
            scores = mm_nt(k_all[rows], q_wide) * (root * LOG2E) + bias_ref[n]
            allowed = label_col_ref[:, w : w + 1] == label_row_ref[w : w + 1, :]
            scores = jnp.where(allowed, scores, -1e30)
            weights = jnp.exp2(scores - jnp.max(scores, axis=0, keepdims=True))
            probs = weights * (1.0 / jnp.sum(weights, axis=0, keepdims=True))
            probs_low = probs.astype(bf16)
            attended = head_blocks(mm(v_t, probs_low)).T.astype(bf16)
            factor = keep_ref[n, 0, c].astype(f32) * (1.0 / keep_share)
            branches.append((mm(attended, wproj_ref[...]) * factor).astype(bf16).astype(f32))
            saved.append((q_wide, probs, probs_low))
        y_sum = x + jnp.concatenate(branches, axis=0)
        scaled2, normed2, inverse2 = norm_parts(y_sum, gain2)
        act, slope = gelu_parts(mm(scaled2.astype(bf16), wup_ref[...]))
        result = (y_sum + mm_nt(act.astype(bf16), wdown_t_ref[...])).astype(bf16)
        grad_up = (mm(cot.astype(bf16), wdown_t_ref[...]) * slope).astype(bf16)
        grad_sum = cot + norm_back(mm_nt(grad_up, wup_ref[...]), gain2, normed2, inverse2)
        grad_low_in = grad_sum.astype(bf16).astype(f32)
        folded = None
        grad_h1 = []
        for c in range(2):
            rows = slice(c * POS, (c + 1) * POS)
            q_wide, probs, probs_low = saved[c]
            factor = keep_ref[n, 0, c].astype(f32) * (1.0 / keep_share)
            grad_branch = (grad_low_in[rows] * factor).astype(bf16)
            grad_att = mm_nt(grad_branch, wproj_ref[...]).astype(bf16)
            g_wide = spread_heads(grad_att, head_mask)
            grad_probs = mm_nt(v_all[rows], g_wide)
            inner_sum = jnp.sum(probs * grad_probs, axis=0, keepdims=True)
            grad_scores = probs * (grad_probs - inner_sum)
            folded = grad_scores if folded is None else folded + grad_scores
            grad_low = grad_scores.astype(bf16)
            k_t = mm_nt(wk_t, h1[rows]).astype(bf16)
            grad_q = (head_blocks(mm(k_t, grad_low)).T * root).astype(bf16)
            grad_k = (mm(grad_low, q_wide) * root).astype(bf16)
            grad_v = mm(probs_low, g_wide).astype(bf16)
            grad_h1.append(mm(grad_q, wq_t) + mm(grad_k, wk_t) + mm(grad_v, wv_t))
        wide[...] = folded.T.reshape(HEADS, POS, POS)
        total = None
        for o in range(WLON):
            left = PAIR * (WLON - 1 - o)
            right = TAB - POS - left
            parts = [wide[:, PAIR * o : PAIR * (o + 1), :]]
            if left:
                parts = [jnp.zeros((HEADS, PAIR, left), f32)] + parts
            if right:
                parts = parts + [jnp.zeros((HEADS, PAIR, right), f32)]
            piece = jnp.concatenate(parts, axis=2)
            total = piece if total is None else total + piece
        total = jnp.concatenate([total, jnp.zeros((HEADS, SLOTS - PAIR, TAB), f32)], axis=1)
        total = total.reshape(HEADS * SLOTS, TAB).astype(bf16)
        total = mm_nt(total, table_perm).astype(bf16)
        total = mm(chunk_perm, total)
        for k in range(2):
            part = total[k * QUARTER : (k + 1) * QUARTER]
            dense[:QUARTER, :] = part[:, :LANES]
            dense[QUARTER : 2 * QUARTER, :] = part[:, LANES : 2 * LANES]
            rest = [part[HEADS * g : HEADS * (g + 1), 2 * LANES :] for g in range(WLAT)]
            dense[2 * QUARTER : 2 * QUARTER + HEADS, : WLAT * REST] = jnp.concatenate(rest, axis=1)
            fold_out[2 * n + k] = dense[...].astype(bf16)
        grad_h1 = jnp.concatenate(grad_h1, axis=0).astype(bf16).astype(f32)
        grad_field = (grad_sum + norm_back(grad_h1, gain1, normed1, inverse1)).astype(bf16)
        for t, value in enumerate((result, grad_field)):
            natural = mm(perm_t, value)
            for dz in range(WZ):
                z = (2 * n + dz + 1) % 4
                for i in range(half):
                    k = z * half + i
                    row = (dz * WLAT + i) * cols
                    slab = natural[row : row + cols]
                    own_out[t, z, i] = slab[:inner].astype(bf16)
                    put(lon_buf, t, k * edge, slab[inner:])
                    row = (dz * WLAT + half + i) * cols
                    slab = natural[row : row + cols]
                    put(lat_buf, t, k * inner, slab[:inner])
                    put(diag_buf, t, k * edge, slab[inner:])
    lat_out[...] = lat_buf[...].astype(bf16)
    diag_out[...] = diag_buf[...].astype(bf16)
    lon_out[...] = lon_buf[...].astype(bf16)


def prepare_kernel(
    table_ref,
    region_ref,
    wqkv_ref,
    gain1_ref,
    gain2_ref,
    bias_out,
    label_row_out,
    label_col_out,
    wqkv_t_out,
    gains_out,
    flat,
    rows,
    wide,
    marks,
):
    wqkv_t_out[...] = wqkv_ref[...].astype(f32).T.astype(bf16)
    gains_out[0:1, :] = gain1_ref[...]
    gains_out[1:2, :] = gain2_ref[...]
    last = lax.axis_index("lat") == lax.axis_size("lat") - 1
    level = lax.broadcasted_iota(jnp.int32, (4, 2 * WLON), 0)
    for i in range(WLAT):
        wrapped = 2 * (level >= 4 - WZ // 2).astype(jnp.int32)
        if i >= WLAT // 2:
            wrapped = wrapped + last.astype(jnp.int32)
        marks[4 * i : 4 * (i + 1), :] = (4 * region_ref[i] + wrapped).astype(f32)
    place = lax.broadcasted_iota(jnp.int32, (POS, 4 * WLAT), 0)
    lane = lax.broadcasted_iota(jnp.int32, (POS, 4 * WLAT), 1)
    lon = quotient(place, PAIR)
    pair = place - PAIR * lon
    upper = (pair >= WLAT).astype(jnp.int32)
    source = 4 * (pair - WLAT * upper) + upper
    columns = []
    for n in range(2):
        chosen = mm((lane == source + WZ * n).astype(f32).astype(bf16), marks[...].astype(bf16))
        for c in range(2):
            own = jnp.where(lane == lon + WLON * c, chosen, 0.0)
            columns.append(jnp.sum(own, axis=1, keepdims=True))
    label_col_out[...] = jnp.concatenate(columns, axis=1)
    spread = jnp.concatenate([jnp.broadcast_to(v, (POS, LANES)) for v in columns], axis=1).T
    labels = jnp.concatenate([spread[k * LANES : k * LANES + 1] for k in range(4)], axis=0)
    label_row_out[...] = jnp.concatenate([labels] * HEADS, axis=1)
    part = PAIR // WZ * SPREAD
    for k in range(2 * HEADS):
        flat[k : k + 1, :] = table_ref[k]
    rows[...] = jnp.zeros_like(rows)
    for a in range(WZ):
        for c in range(WLAT):
            pieces = []
            for b in range(WZ):
                start = ((a * WZ + b) * WLAT + c) * part
                pieces.append(flat[:, start : start + part])
            row = (a * WLAT + c) * SLOTS
            rows[row : row + 2 * HEADS, :] = jnp.concatenate(pieces, axis=1)
    left = rows[...]
    perm = table_order()
    row_perm = row_order()
    total = None
    for _ in range(3):
        low = left.astype(bf16)
        left = left - low.astype(f32)
        term = mm(row_perm, mm(low, perm).astype(bf16))
        total = term if total is None else total + term
    total = total.reshape(2 * HEADS, SLOTS, TAB)
    for o in range(WLON):
        start = PAIR * (WLON - 1 - o)
        wide[:, PAIR * o : PAIR * (o + 1), :] = total[:, :PAIR, start : start + POS]
    for n in range(2):
        bias_out[n] = wide[n * HEADS : (n + 1) * HEADS].reshape(ROWS, POS).T * LOG2E


def unpack_kernel(mine_ref, other_ref, table_out, flat):
    odd = (lax.axis_index("lon") & 1) != 0
    part = PAIR // WZ * SPREAD
    for n in range(2):
        halves = []
        for k in range(2):
            mine = mine_ref[n].astype(f32)
            other = other_ref[n].astype(f32)
            dense = jnp.where(odd == (k == 1), mine, other)
            rest = dense[2 * QUARTER : 2 * QUARTER + HEADS]
            rest = [rest[:, g * REST : (g + 1) * REST] for g in range(WLAT)]
            rest = jnp.concatenate(rest, axis=0)
            parts = [dense[:QUARTER], dense[QUARTER : 2 * QUARTER], rest]
            halves.append(jnp.concatenate(parts, axis=1))
        for a in range(WZ):
            for c in range(WLAT):
                row = c * HEADS
                chunk = halves[a][row : row + HEADS]
                for b in range(WZ):
                    start = ((a * WZ + b) * WLAT + c) * part
                    flat[n * HEADS : (n + 1) * HEADS, start : start + part] = chunk[
                        :, b * part : (b + 1) * part
                    ]
    for k in range(2 * HEADS):
        table_out[k] = flat[k : k + 1, :]


def add_kernel(*refs):
    copies_out = refs[-1]
    parts = [ref[k].astype(f32) for ref in refs[:-1] for k in range(ref.shape[0])]
    while len(parts) > 1:
        parts = [parts[k] + parts[k + 1] for k in range(0, len(parts), 2)]
    total = parts[0].astype(bf16)
    for k in range(copies_out.shape[0]):
        copies_out[k] = total


def finish_kernel(own_ref, lat_ref, diag_ref, lon_ref, out_ref, grad_ref):
    half = WLAT // 2
    edge = WLON // 2
    inner = 2 * WLON - edge
    lat_part = lat_ref[...].astype(f32)
    diag_part = diag_ref[...].astype(f32)
    lon_part = lon_ref[...].astype(f32)
    for t, target in enumerate((out_ref, grad_ref)):
        for z in range(4):
            for i in range(half):
                k = z * half + i
                parts = (get(diag_part, t, k * edge, edge), get(lat_part, t, k * inner, inner))
                slab = [jnp.concatenate([parts[0][j], parts[1][j]], axis=0) for j in range(2)]
                target[z, i] = jnp.concatenate(slab, axis=1).astype(bf16)
                slab = jnp.concatenate(get(lon_part, t, k * edge, edge), axis=1)
                own = own_ref[t, z, i].astype(f32)
                target[z, half + i] = jnp.concatenate([slab, own], axis=0).astype(bf16)


def lon_sum(quarters, strips):
    lons = lax.axis_size("lon")
    me = lax.axis_index("lon")
    bits = [(me >> k) & 1 for k in range(2)]
    far = [[4 * k + j for k in range(lons // 4)] for j in range(4)]

    def swapped(block, distance):
        return lax.ppermute(block, "lon", [(i, i ^ distance) for i in range(lons)])

    def pick(value, bit, axis):
        return lax.dynamic_index_in_dim(value, bit, axis, keepdims=False)

    def added(parts, copies):
        vmem = pl.BlockSpec(memory_space=pltpu.VMEM)
        return pl.pallas_call(
            add_kernel,
            out_shape=jax.ShapeDtypeStruct((copies,) + parts[0].shape[1:], bf16),
            in_specs=[vmem] * len(parts),
            out_specs=vmem,
            compiler_params=pltpu.CompilerParams(vmem_limit_bytes=VMEM_BYTES),
            name="add",
        )(*parts)

    value = quarters.reshape((2, 2) + quarters.shape[1:])
    other = swapped(pick(value, 1 - bits[0], 1), 1)
    value = pick(value, bits[0], 1).astype(f32) + other.astype(f32)
    value = value.astype(bf16)
    other = swapped(pick(value, 1 - bits[1], 0), 2)
    parts = added((pick(value, bits[1], 0)[None], other[None]), lons // 4)
    parts, strips = lax.optimization_barrier((parts, strips))
    steps = ((1, 0), (1, 1), (0, 1))
    strips = [shifted(strip, *step) for strip, step in zip(strips, steps)]
    parts = lax.all_to_all(parts, "lon", 0, 0, axis_index_groups=far)
    value, strips = lax.optimization_barrier((added((parts,), 1)[0], strips))
    other = swapped(value, 2)
    lower = jnp.where(bits[1] == 0, value, other)
    upper = jnp.where(bits[1] == 0, other, value)
    value = jnp.stack([lower, upper])
    return (value, swapped(value, 1)), strips


def body(
    field_in,
    cotangent,
    ln1_gain,
    w_qkv,
    w_proj,
    ln2_gain,
    w_up,
    w_down,
    bias_table,
    region_ids,
    keep_flags,
):
    levels, lat_rows, lon_cols, channels = field_in.shape
    half = WLAT // 2
    edge = WLON // 2
    inner = lon_cols - edge
    vmem = pl.BlockSpec(memory_space=pltpu.VMEM)
    smem = pl.BlockSpec(memory_space=pltpu.SMEM)
    sizes = [3 * levels * half * size for size in (inner, edge, edge)]
    packed = tuple(jax.ShapeDtypeStruct((size, LANES), bf16) for size in sizes)
    buffers = [pltpu.VMEM((size, LANES), f32) for size in sizes]
    params = pltpu.CompilerParams(vmem_limit_bytes=VMEM_BYTES)
    lat_part = pl.pallas_call(
        pack_lat_kernel,
        out_shape=packed[0],
        in_specs=[pl.BlockSpec(memory_space=pltpu.HBM)] * 2,
        out_specs=vmem,
        scratch_shapes=buffers[:1]
        + [pltpu.VMEM((2, levels, half, lon_cols, C), bf16), pltpu.SemaphoreType.DMA((2,))],
        compiler_params=params,
        name="pack_lat",
    )(field_in, cotangent)
    diag_part, lon_part = pl.pallas_call(
        pack_edge_kernel,
        out_shape=packed[1:],
        in_specs=[vmem] * 2 + [pl.BlockSpec(memory_space=pl.ANY)],
        out_specs=(vmem,) * 2,
        scratch_shapes=buffers[1:],
        compiler_params=params,
        name="pack_edge",
    )(field_in, cotangent, lat_part)
    lat_part = shifted(lat_part, -1, 0)
    diag_part = shifted(diag_part, -1, -1)
    lon_part = shifted(lon_part, 0, -1)

    bias_wide, label_row, label_col, weights_t, gains = pl.pallas_call(
        prepare_kernel,
        out_shape=(
            jax.ShapeDtypeStruct((2, POS, ROWS), f32),
            jax.ShapeDtypeStruct((4, ROWS), f32),
            jax.ShapeDtypeStruct((POS, 4), f32),
            jax.ShapeDtypeStruct((3 * C, C), bf16),
            jax.ShapeDtypeStruct((2, C), f32),
        ),
        in_specs=[vmem] * 5,
        out_specs=(vmem,) * 5,
        scratch_shapes=[
            pltpu.VMEM((2 * HEADS, PAIR * TAB), f32),
            pltpu.VMEM((PAIR * SLOTS, TAB), f32),
            pltpu.VMEM((2 * HEADS, POS, POS), f32),
            pltpu.VMEM((4 * WLAT, 2 * WLON), f32),
        ],
        compiler_params=params,
        name="prepare",
    )(
        bias_table.reshape(2 * HEADS, 1, PAIR * TAB),
        region_ids.transpose(1, 0, 2),
        w_qkv,
        ln1_gain.reshape(1, C),
        ln2_gain.reshape(1, C),
    )
    positions = levels * lat_rows * lon_cols
    fold, own, *strips = pl.pallas_call(
        block_kernel,
        out_shape=(
            jax.ShapeDtypeStruct((4, DENSE, LANES), bf16),
            jax.ShapeDtypeStruct((2, levels, half, inner, C), bf16),
        )
        + packed,
        in_specs=[vmem] * 13 + [smem],
        out_specs=(vmem,) * 5,
        scratch_shapes=[
            pltpu.VMEM((2, positions, C), f32),
            pltpu.VMEM((HEADS, POS, POS), f32),
            pltpu.VMEM((DENSE, LANES), f32),
        ]
        + buffers,
        compiler_params=params,
        name="block",
    )(
        field_in,
        cotangent,
        lon_part,
        lat_part,
        diag_part,
        gains,
        weights_t,
        w_proj,
        w_up,
        w_down.T,
        bias_wide,
        label_row,
        label_col,
        keep_flags,
    )
    halves, (lat_back, diag_back, lon_back) = lon_sum(fold, strips)
    grads = pl.pallas_call(
        unpack_kernel,
        out_shape=jax.ShapeDtypeStruct((2 * HEADS, 1, PAIR * TAB), f32),
        in_specs=[vmem] * 2,
        out_specs=vmem,
        scratch_shapes=[pltpu.VMEM((2 * HEADS, PAIR * TAB), f32)],
        compiler_params=params,
        name="unpack",
    )(*halves)
    grads = grads.reshape(2, 1, HEADS, PAIR * TAB)
    result, grad_field = pl.pallas_call(
        finish_kernel,
        out_shape=(jax.ShapeDtypeStruct(field_in.shape, bf16),) * 2,
        in_specs=[vmem] * 4,
        out_specs=(vmem,) * 2,
        compiler_params=params,
        name="finish",
    )(own, lat_back, diag_back, lon_back)
    return (result, grad_field, grads)


def solution(mesh):
    placed = (
        P(None, "lat", "lon", None),
        P(None, "lat", "lon", None),
        P(),
        P(),
        P(),
        P(),
        P(),
        P(),
        P(None, "lat", None, None),
        P(None, "lat", "lon"),
        P(None, "lat", "lon"),
    )
    return jax.shard_map(
        body,
        mesh=mesh,
        in_specs=placed,
        out_specs=(
            P(None, "lat", "lon", None),
            P(None, "lat", "lon", None),
            P(None, "lat", None, None),
        ),
        check_vma=False,
    )
```

```python
import math

import jax
import jax.numpy as jnp
from jax import lax
from jax.experimental import pallas as pl
from jax.experimental.pallas import tpu as pltpu
from jax.sharding import PartitionSpec as P

C = 192
HEADS = 6
HD = 32
FF = 768
WZ = 2
WLAT = 6
WLON = 12
SPREAD = 2 * WLON - 1
POS = WZ * WLAT * WLON
PAIR = WZ * WLAT
TAB = PAIR * SPREAD
ROWS = HEADS * POS
SLOTS = 16
QUARTER = PAIR * HEADS // 2
REST = 20
LN_ROWS = 96
GELU_ROWS = 48
LANE_CUTS = [(k, min(k + 256, ROWS)) for k in range(0, ROWS, 256)]
DENSE = 80
LANES = 128

epsilon = 1e-05
keep_share = 0.8
LOG2E = math.log2(math.e)
gelu_coef = 0.044715
VMEM_BYTES = 16 * 1024 * 1024
bf16 = jnp.bfloat16
f32 = jnp.float32


def shifted(block, lat_step, lon_step):
    lats, lons = lax.axis_size("lat"), lax.axis_size("lon")
    route = []
    for a in range(lats):
        for b in range(lons):
            target = ((a + lat_step) % lats) * lons + (b + lon_step) % lons
            route.append((a * lons + b, target))
    return lax.ppermute(block, ("lat", "lon"), route)


def mm(a, b):
    return lax.dot_general(a, b, (((1,), (0,)), ((), ())), preferred_element_type=f32)


def mm_nt(a, b):
    return lax.dot_general(a, b, (((1,), (1,)), ((), ())), preferred_element_type=f32)


def norm_parts(values, gain):
    row_mean = jnp.mean(values, axis=-1, keepdims=True)
    centred = values - row_mean
    variance = jnp.mean(centred * centred, axis=-1, keepdims=True)
    inverse = lax.rsqrt(variance + epsilon)
    normed = centred * inverse
    return normed * gain, normed, inverse


def norm_back(grad_in, gain, normed, inverse):
    scaled = grad_in * gain
    first_mean = jnp.mean(scaled, axis=-1, keepdims=True)
    second_mean = jnp.mean(scaled * normed, axis=-1, keepdims=True)
    return (scaled - first_mean - normed * second_mean) * inverse


def gelu_parts(values):
    factor = math.sqrt(2.0 / math.pi)
    square = values * values
    tangent = jnp.tanh(values * (factor + (gelu_coef * factor) * square))
    half = 0.5 + 0.5 * tangent
    result = values * half
    derivative = half + result * (1.0 - tangent) * (factor + (3.0 * gelu_coef * factor) * square)
    return result.astype(bf16), derivative


def by_rows(function, size, *arrays):
    rows = arrays[0].shape[0]
    parts = [function(*(v[r : r + size] for v in arrays)) for r in range(0, rows, size)]
    return tuple(jnp.concatenate(part, axis=0) for part in zip(*parts))


def masked_softmax(scores, bias, allowed):
    scores = scores * (LOG2E / math.sqrt(HD)) + bias
    scores = jnp.where(allowed, scores, -1e30)
    weights = jnp.exp2(scores - jnp.max(scores, axis=0, keepdims=True))
    return weights * (1.0 / jnp.sum(weights, axis=0, keepdims=True))


def head_blocks(wide):
    return jnp.concatenate(
        [wide[h * HD : (h + 1) * HD, h * POS : (h + 1) * POS] for h in range(HEADS)], axis=0
    )


def spread_heads(rows, head_mask):
    return jnp.concatenate([rows * head_mask[h : h + 1, :] for h in range(HEADS)], axis=0)


def quotient(values, divisor):
    return (values * (2**20 // divisor + 1)) >> 20


def one_hot(rows, columns, target):
    row = lax.broadcasted_iota(jnp.int32, (rows, 1), 0)
    column = lax.broadcasted_iota(jnp.int32, (rows, columns), 1)
    return (column == target(row)).astype(f32).astype(bf16)


def window_order():
    def target(row):
        c = (row >= POS).astype(jnp.int32)
        row = row - POS * c
        j = quotient(row, PAIR)
        return (row - PAIR * j) * (2 * WLON) + c * WLON + j

    return one_hot(2 * POS, 2 * POS, target)


def natural_order():
    def target(row):
        pair = quotient(row, 2 * WLON)
        lon = row - 2 * WLON * pair
        c = (lon >= WLON).astype(jnp.int32)
        return c * POS + (lon - WLON * c) * PAIR + pair

    return one_hot(2 * POS, 2 * POS, target)


def table_order():
    def target(row):
        pair = quotient(row, SPREAD)
        return (SPREAD - 1 - (row - SPREAD * pair)) * PAIR + pair

    return one_hot(TAB, TAB, target)


def chunk_order():
    def target(row):
        pair = quotient(row, HEADS)
        return (row - HEADS * pair) * SLOTS + pair

    return one_hot(PAIR * HEADS, HEADS * SLOTS, target)


def row_order():
    def target(row):
        head = quotient(row, SLOTS)
        return (row - SLOTS * head) * SLOTS + head

    return one_hot(2 * HEADS * SLOTS, PAIR * SLOTS, target)


def put(packed, t, row, slab):
    third = packed.shape[0] // 3
    size = slab.shape[0]
    rest = C - LANES
    packed[t * third + row : t * third + row + size, :] = slab[:, :LANES]
    packed[2 * third + row : 2 * third + row + size, t * rest : (t + 1) * rest] = slab[:, LANES:]


def get(packed, t, row, size):
    third = packed.shape[0] // 3
    rest = C - LANES
    return (
        packed[t * third + row : t * third + row + size, :],
        packed[2 * third + row : 2 * third + row + size, t * rest : (t + 1) * rest],
    )


def pack_lat_kernel(field_ref, cot_ref, lat_out, lat_buf, rows, arrived):
    half = WLAT // 2
    edge = WLON // 2
    inner = 2 * WLON - edge
    sources = (field_ref, cot_ref)
    copies = [
        pltpu.make_async_copy(sources[t].at[:, pl.ds(0, half)], rows.at[t], arrived.at[t])
        for t in range(2)
    ]
    for copy in copies:
        copy.start()
    for t in range(2):
        copies[t].wait()
        for z in range(4):
            for i in range(half):
                put(lat_buf, t, (z * half + i) * inner, rows[t, z, i].astype(f32)[edge:])
    lat_out[...] = lat_buf[...].astype(bf16)


def pack_edge_kernel(field_ref, cot_ref, after_ref, diag_out, lon_out, diag_buf, lon_buf):
    half = WLAT // 2
    edge = WLON // 2
    for t, source in enumerate((field_ref, cot_ref)):
        for z in range(4):
            for i in range(half):
                row = (z * half + i) * edge
                put(diag_buf, t, row, source[z, i].astype(f32)[:edge])
                put(lon_buf, t, row, source[z, half + i].astype(f32)[:edge])
    diag_out[...] = diag_buf[...].astype(bf16)
    lon_out[...] = lon_buf[...].astype(bf16)


def block_kernel(
    field_ref,
    cot_ref,
    lon_ref,
    lat_ref,
    diag_ref,
    gains_ref,
    wqkv_t_ref,
    wproj_ref,
    wup_ref,
    wdown_t_ref,
    bias_ref,
    label_row_ref,
    label_col_ref,
    fold_out,
    own_out,
    lat_out,
    diag_out,
    lon_out,
    frame,
    wide,
    dense,
    lat_buf,
    diag_buf,
    lon_buf,
):
    half = WLAT // 2
    cols = 2 * WLON
    edge = WLON // 2
    inner = cols - edge
    root = 1.0 / math.sqrt(HD)
    lon_part = lon_ref[...].astype(f32)
    lat_part = lat_ref[...].astype(f32)
    diag_part = diag_ref[...].astype(f32)
    for t, own in enumerate((field_ref, cot_ref)):
        for level in range(4):
            z = (level + 1) % 4
            for i in range(half):
                k = z * half + i
                row = (level * WLAT + i) * cols
                frame[t, row : row + inner, :] = own[z, half + i].astype(f32)[edge:, :]
                main, rest = get(lon_part, t, k * edge, edge)
                frame[t, row + inner : row + cols, :LANES] = main
                frame[t, row + inner : row + cols, LANES:] = rest
                row = (level * WLAT + half + i) * cols
                main, rest = get(lat_part, t, k * inner, inner)
                frame[t, row : row + inner, :LANES] = main
                frame[t, row : row + inner, LANES:] = rest
                main, rest = get(diag_part, t, k * edge, edge)
                frame[t, row + inner : row + cols, :LANES] = main
                frame[t, row + inner : row + cols, LANES:] = rest
    gain1 = gains_ref[0:1, :]
    gain2 = gains_ref[1:2, :]
    wq_t = wqkv_t_ref[0:C, :]
    wk_t = wqkv_t_ref[C : 2 * C, :]
    wv_t = wqkv_t_ref[2 * C : 3 * C, :]
    head = lax.broadcasted_iota(jnp.int32, (HEADS, C), 0)
    head_mask = (lax.broadcasted_iota(jnp.int32, (HEADS, C), 1) >> 5) == head
    head_mask = head_mask.astype(f32).astype(bf16)
    perm = window_order()
    perm_t = natural_order()
    table_perm = table_order()
    chunk_perm = chunk_order()
    dense[...] = jnp.zeros_like(dense)
    for n in range(2):
        both = slice(n * 2 * POS, (n + 1) * 2 * POS)
        x = mm(perm, frame[0, both, :].astype(bf16))
        cot = mm(perm, frame[1, both, :].astype(bf16))
        scaled1, normed1, inverse1 = by_rows(lambda v: norm_parts(v, gain1), LN_ROWS, x)
        h1 = scaled1.astype(bf16)
        q_all = mm_nt(h1, wq_t).astype(bf16)
        k_all = mm_nt(h1, wk_t).astype(bf16)
        v_all = mm_nt(h1, wv_t).astype(bf16)
        saved = []
        branches = []
        for c in range(2):
            w = 2 * n + c
            rows = slice(c * POS, (c + 1) * POS)
            v_t = mm_nt(wv_t, h1[rows]).astype(bf16)
            q_wide = spread_heads(q_all[rows], head_mask)
            label_col = label_col_ref[:, w : w + 1]
            probs = []
            for low, high in LANE_CUTS:
                scores = mm_nt(k_all[rows], q_wide[low:high])
                allowed = label_col == label_row_ref[w : w + 1, low:high]
                probs.append(masked_softmax(scores, bias_ref[n, :, low:high], allowed))
            probs_low = jnp.concatenate([part.astype(bf16) for part in probs], axis=1)
            attended = head_blocks(mm(v_t, probs_low)).astype(bf16).T
            factor = gains_ref[2 + w : 3 + w, :]
            branches.append((mm(attended, wproj_ref[...]) * factor).astype(bf16).astype(f32))
            saved.append((q_wide, probs, probs_low))
        y_sum = x + jnp.concatenate(branches, axis=0)
        scaled2, normed2, inverse2 = by_rows(lambda v: norm_parts(v, gain2), LN_ROWS, y_sum)
        act, slope = by_rows(gelu_parts, GELU_ROWS, mm(scaled2.astype(bf16), wup_ref[...]))
        result = (y_sum + mm_nt(act, wdown_t_ref[...])).astype(bf16)
        grad_up = (mm(cot.astype(bf16), wdown_t_ref[...]) * slope).astype(bf16)
        grad_hidden = mm_nt(grad_up, wup_ref[...])
        (grad_sum,) = by_rows(
            lambda v, g, normed, inverse: (v + norm_back(g, gain2, normed, inverse),),
            LN_ROWS,
            cot,
            grad_hidden,
            normed2,
            inverse2,
        )
        grad_low_in = grad_sum.astype(bf16).astype(f32)
        folded = [None] * len(LANE_CUTS)
        grad_h1 = []
        for c in range(2):
            rows = slice(c * POS, (c + 1) * POS)
            q_wide, probs, probs_low = saved[c]
            factor = gains_ref[2 + 2 * n + c : 3 + 2 * n + c, :]
            grad_branch = (grad_low_in[rows] * factor).astype(bf16)
            grad_att = mm_nt(grad_branch, wproj_ref[...]).astype(bf16)
            g_wide = spread_heads(grad_att, head_mask)
            grad_low = []
            for k, (low, high) in enumerate(LANE_CUTS):
                grad_probs = mm_nt(v_all[rows], g_wide[low:high])
                inner_sum = jnp.sum(probs[k] * grad_probs, axis=0, keepdims=True)
                grad_scores = probs[k] * (grad_probs - inner_sum)
                folded[k] = grad_scores if c == 0 else folded[k] + grad_scores
                grad_low.append(grad_scores.astype(bf16))
            grad_low = jnp.concatenate(grad_low, axis=1)
            k_t = mm_nt(wk_t, h1[rows]).astype(bf16)
            grad_q = (head_blocks(mm(k_t, grad_low)) * root).astype(bf16).T
            grad_k = (mm(grad_low, q_wide) * root).astype(bf16)
            grad_v = mm(probs_low, g_wide).astype(bf16)
            grad_h1.append(mm(grad_q, wq_t) + mm(grad_k, wk_t) + mm(grad_v, wv_t))
        folded = jnp.concatenate([part.astype(bf16) for part in folded], axis=1)
        wide[...] = folded.T.astype(f32).reshape(HEADS, POS, POS)
        total = None
        for o in range(WLON):
            left = PAIR * (WLON - 1 - o)
            right = TAB - POS - left
            parts = [wide[:, PAIR * o : PAIR * (o + 1), :]]
            if left:
                parts = [jnp.zeros((HEADS, PAIR, left), f32)] + parts
            if right:
                parts = parts + [jnp.zeros((HEADS, PAIR, right), f32)]
            piece = jnp.concatenate(parts, axis=2)
            total = piece if total is None else total + piece
        total = jnp.concatenate([total, jnp.zeros((HEADS, SLOTS - PAIR, TAB), f32)], axis=1)
        total = total.reshape(HEADS * SLOTS, TAB).astype(bf16)
        total = mm_nt(total, table_perm).astype(bf16)
        total = mm(chunk_perm, total)
        for k in range(2):
            part = total[k * QUARTER : (k + 1) * QUARTER]
            dense[:QUARTER, :] = part[:, :LANES]
            dense[QUARTER : 2 * QUARTER, :] = part[:, LANES : 2 * LANES]
            rest = [part[HEADS * g : HEADS * (g + 1), 2 * LANES :] for g in range(WLAT)]
            dense[2 * QUARTER : 2 * QUARTER + HEADS, : WLAT * REST] = jnp.concatenate(rest, axis=1)
            fold_out[2 * n + k] = dense[...].astype(bf16)
        grad_h1 = jnp.concatenate(grad_h1, axis=0).astype(bf16).astype(f32)
        (grad_field,) = by_rows(
            lambda v, g, normed, inverse: (
                (v + norm_back(g, gain1, normed, inverse)).astype(bf16),
            ),
            LN_ROWS,
            grad_sum,
            grad_h1,
            normed1,
            inverse1,
        )
        for t, value in enumerate((result, grad_field)):
            natural = mm(perm_t, value)
            for dz in range(WZ):
                z = (2 * n + dz + 1) % 4
                for i in range(half):
                    k = z * half + i
                    row = (dz * WLAT + i) * cols
                    slab = natural[row : row + cols]
                    own_out[t, z, i] = slab[:inner].astype(bf16)
                    put(lon_buf, t, k * edge, slab[inner:])
                    row = (dz * WLAT + half + i) * cols
                    slab = natural[row : row + cols]
                    put(lat_buf, t, k * inner, slab[:inner])
                    put(diag_buf, t, k * edge, slab[inner:])
    lat_out[...] = lat_buf[...].astype(bf16)
    diag_out[...] = diag_buf[...].astype(bf16)
    lon_out[...] = lon_buf[...].astype(bf16)


def prepare_kernel(
    table_ref,
    region_ref,
    wqkv_ref,
    gain1_ref,
    gain2_ref,
    keep_ref,
    bias_out,
    label_row_out,
    label_col_out,
    wqkv_t_out,
    gains_out,
    flat,
    rows,
    wide,
    marks,
):
    wqkv_t_out[...] = wqkv_ref[...].astype(f32).T.astype(bf16)
    gains_out[0:1, :] = gain1_ref[...]
    gains_out[1:2, :] = gain2_ref[...]
    for n in range(2):
        for c in range(2):
            factor = keep_ref[n, 0, c].astype(f32) * (1.0 / keep_share)
            row = 2 + 2 * n + c
            gains_out[row : row + 1, :] = jnp.full((1, C), factor, f32)
    last = lax.axis_index("lat") == lax.axis_size("lat") - 1
    level = lax.broadcasted_iota(jnp.int32, (4, 2 * WLON), 0)
    for i in range(WLAT):
        wrapped = 2 * (level >= 4 - WZ // 2).astype(jnp.int32)
        if i >= WLAT // 2:
            wrapped = wrapped + last.astype(jnp.int32)
        marks[4 * i : 4 * (i + 1), :] = (4 * region_ref[i] + wrapped).astype(f32)
    place = lax.broadcasted_iota(jnp.int32, (POS, 4 * WLAT), 0)
    lane = lax.broadcasted_iota(jnp.int32, (POS, 4 * WLAT), 1)
    lon = quotient(place, PAIR)
    pair = place - PAIR * lon
    upper = (pair >= WLAT).astype(jnp.int32)
    source = 4 * (pair - WLAT * upper) + upper
    columns = []
    for n in range(2):
        chosen = mm((lane == source + WZ * n).astype(f32).astype(bf16), marks[...].astype(bf16))
        for c in range(2):
            own = jnp.where(lane == lon + WLON * c, chosen, 0.0)
            columns.append(jnp.sum(own, axis=1, keepdims=True))
    label_col_out[...] = jnp.concatenate(columns, axis=1)
    spread = jnp.concatenate([jnp.broadcast_to(v, (POS, LANES)) for v in columns], axis=1).T
    labels = jnp.concatenate([spread[k * LANES : k * LANES + 1] for k in range(4)], axis=0)
    label_row_out[...] = jnp.concatenate([labels] * HEADS, axis=1)
    part = PAIR // WZ * SPREAD
    for k in range(2 * HEADS):
        flat[k : k + 1, :] = table_ref[k]
    rows[...] = jnp.zeros_like(rows)
    for a in range(WZ):
        for c in range(WLAT):
            pieces = []
            for b in range(WZ):
                start = ((a * WZ + b) * WLAT + c) * part
                pieces.append(flat[:, start : start + part])
            row = (a * WLAT + c) * SLOTS
            rows[row : row + 2 * HEADS, :] = jnp.concatenate(pieces, axis=1)
    left = rows[...]
    perm = table_order()
    row_perm = row_order()
    total = None
    for _ in range(3):
        low = left.astype(bf16)
        left = left - low.astype(f32)
        term = mm(row_perm, mm(low, perm).astype(bf16))
        total = term if total is None else total + term
    total = total.reshape(2 * HEADS, SLOTS, TAB)
    for o in range(WLON):
        start = PAIR * (WLON - 1 - o)
        wide[:, PAIR * o : PAIR * (o + 1), :] = total[:, :PAIR, start : start + POS]
    for n in range(2):
        bias_out[n] = wide[n * HEADS : (n + 1) * HEADS].reshape(ROWS, POS).T * LOG2E


def unpack_kernel(mine_ref, other_ref, table_out, flat):
    odd = (lax.axis_index("lon") & 1) != 0
    part = PAIR // WZ * SPREAD
    for n in range(2):
        halves = []
        for k in range(2):
            mine = mine_ref[n].astype(f32)
            other = other_ref[n].astype(f32)
            dense = jnp.where(odd == (k == 1), mine, other)
            rest = dense[2 * QUARTER : 2 * QUARTER + HEADS]
            rest = [rest[:, g * REST : (g + 1) * REST] for g in range(WLAT)]
            rest = jnp.concatenate(rest, axis=0)
            parts = [dense[:QUARTER], dense[QUARTER : 2 * QUARTER], rest]
            halves.append(jnp.concatenate(parts, axis=1))
        for a in range(WZ):
            for c in range(WLAT):
                row = c * HEADS
                chunk = halves[a][row : row + HEADS]
                for b in range(WZ):
                    start = ((a * WZ + b) * WLAT + c) * part
                    flat[n * HEADS : (n + 1) * HEADS, start : start + part] = chunk[
                        :, b * part : (b + 1) * part
                    ]
    for k in range(2 * HEADS):
        table_out[k] = flat[k : k + 1, :]


def add_kernel(*refs):
    copies_out = refs[-1]
    parts = [ref[k].astype(f32) for ref in refs[:-1] for k in range(ref.shape[0])]
    while len(parts) > 1:
        parts = [parts[k] + parts[k + 1] for k in range(0, len(parts), 2)]
    total = parts[0].astype(bf16)
    for k in range(copies_out.shape[0]):
        copies_out[k] = total


def finish_kernel(own_ref, lat_ref, diag_ref, lon_ref, out_ref, grad_ref):
    half = WLAT // 2
    edge = WLON // 2
    inner = 2 * WLON - edge
    lat_part = lat_ref[...].astype(f32)
    diag_part = diag_ref[...].astype(f32)
    lon_part = lon_ref[...].astype(f32)
    for t, target in enumerate((out_ref, grad_ref)):
        for z in range(4):
            for i in range(half):
                k = z * half + i
                parts = (get(diag_part, t, k * edge, edge), get(lat_part, t, k * inner, inner))
                slab = [jnp.concatenate([parts[0][j], parts[1][j]], axis=0) for j in range(2)]
                target[z, i] = jnp.concatenate(slab, axis=1).astype(bf16)
                slab = jnp.concatenate(get(lon_part, t, k * edge, edge), axis=1)
                own = own_ref[t, z, i].astype(f32)
                target[z, half + i] = jnp.concatenate([slab, own], axis=0).astype(bf16)


def lon_sum(quarters, strips):
    lons = lax.axis_size("lon")
    me = lax.axis_index("lon")
    bits = [(me >> k) & 1 for k in range(2)]
    far = [[4 * k + j for k in range(lons // 4)] for j in range(4)]

    def swapped(block, distance):
        return lax.ppermute(block, "lon", [(i, i ^ distance) for i in range(lons)])

    def pick(value, bit, axis):
        return lax.dynamic_index_in_dim(value, bit, axis, keepdims=False)

    def added(parts, copies):
        vmem = pl.BlockSpec(memory_space=pltpu.VMEM)
        return pl.pallas_call(
            add_kernel,
            out_shape=jax.ShapeDtypeStruct((copies,) + parts[0].shape[1:], bf16),
            in_specs=[vmem] * len(parts),
            out_specs=vmem,
            compiler_params=pltpu.CompilerParams(vmem_limit_bytes=VMEM_BYTES),
            name="add",
        )(*parts)

    value = quarters.reshape((2, 2) + quarters.shape[1:])
    other = swapped(pick(value, 1 - bits[0], 1), 1)
    value = pick(value, bits[0], 1).astype(f32) + other.astype(f32)
    value = value.astype(bf16)
    other = swapped(pick(value, 1 - bits[1], 0), 2)
    parts = added((pick(value, bits[1], 0)[None], other[None]), lons // 4)
    parts, strips = lax.optimization_barrier((parts, strips))
    steps = ((1, 0), (1, 1), (0, 1))
    strips = [shifted(strip, *step) for strip, step in zip(strips, steps)]
    parts = lax.all_to_all(parts, "lon", 0, 0, axis_index_groups=far)
    value, strips = lax.optimization_barrier((added((parts,), 1)[0], strips))
    other = swapped(value, 2)
    lower = jnp.where(bits[1] == 0, value, other)
    upper = jnp.where(bits[1] == 0, other, value)
    value = jnp.stack([lower, upper])
    return (value, swapped(value, 1)), strips


def body(
    field_in,
    cotangent,
    ln1_gain,
    w_qkv,
    w_proj,
    ln2_gain,
    w_up,
    w_down,
    bias_table,
    region_ids,
    keep_flags,
):
    levels, lat_rows, lon_cols, channels = field_in.shape
    half = WLAT // 2
    edge = WLON // 2
    inner = lon_cols - edge
    vmem = pl.BlockSpec(memory_space=pltpu.VMEM)
    smem = pl.BlockSpec(memory_space=pltpu.SMEM)
    sizes = [3 * levels * half * size for size in (inner, edge, edge)]
    packed = tuple(jax.ShapeDtypeStruct((size, LANES), bf16) for size in sizes)
    buffers = [pltpu.VMEM((size, LANES), f32) for size in sizes]
    params = pltpu.CompilerParams(vmem_limit_bytes=VMEM_BYTES)
    lat_part = pl.pallas_call(
        pack_lat_kernel,
        out_shape=packed[0],
        in_specs=[pl.BlockSpec(memory_space=pltpu.HBM)] * 2,
        out_specs=vmem,
        scratch_shapes=buffers[:1]
        + [pltpu.VMEM((2, levels, half, lon_cols, C), bf16), pltpu.SemaphoreType.DMA((2,))],
        compiler_params=params,
        name="pack_lat",
    )(field_in, cotangent)
    diag_part, lon_part = pl.pallas_call(
        pack_edge_kernel,
        out_shape=packed[1:],
        in_specs=[vmem] * 2 + [pl.BlockSpec(memory_space=pl.ANY)],
        out_specs=(vmem,) * 2,
        scratch_shapes=buffers[1:],
        compiler_params=params,
        name="pack_edge",
    )(field_in, cotangent, lat_part)
    lat_part = shifted(lat_part, -1, 0)
    diag_part = shifted(diag_part, -1, -1)
    lon_part = shifted(lon_part, 0, -1)

    bias_wide, label_row, label_col, weights_t, gains = pl.pallas_call(
        prepare_kernel,
        out_shape=(
            jax.ShapeDtypeStruct((2, POS, ROWS), f32),
            jax.ShapeDtypeStruct((4, ROWS), f32),
            jax.ShapeDtypeStruct((POS, 4), f32),
            jax.ShapeDtypeStruct((3 * C, C), bf16),
            jax.ShapeDtypeStruct((6, C), f32),
        ),
        in_specs=[vmem] * 5 + [smem],
        out_specs=(vmem,) * 5,
        scratch_shapes=[
            pltpu.VMEM((2 * HEADS, PAIR * TAB), f32),
            pltpu.VMEM((PAIR * SLOTS, TAB), f32),
            pltpu.VMEM((2 * HEADS, POS, POS), f32),
            pltpu.VMEM((4 * WLAT, 2 * WLON), f32),
        ],
        compiler_params=params,
        name="prepare",
    )(
        bias_table.reshape(2 * HEADS, 1, PAIR * TAB),
        region_ids.transpose(1, 0, 2),
        w_qkv,
        ln1_gain.reshape(1, C),
        ln2_gain.reshape(1, C),
        keep_flags,
    )
    positions = levels * lat_rows * lon_cols
    fold, own, *strips = pl.pallas_call(
        block_kernel,
        out_shape=(
            jax.ShapeDtypeStruct((4, DENSE, LANES), bf16),
            jax.ShapeDtypeStruct((2, levels, half, inner, C), bf16),
        )
        + packed,
        in_specs=[vmem] * 13,
        out_specs=(vmem,) * 5,
        scratch_shapes=[
            pltpu.VMEM((2, positions, C), f32),
            pltpu.VMEM((HEADS, POS, POS), f32),
            pltpu.VMEM((DENSE, LANES), f32),
        ]
        + buffers,
        compiler_params=params,
        name="block",
    )(
        field_in,
        cotangent,
        lon_part,
        lat_part,
        diag_part,
        gains,
        weights_t,
        w_proj,
        w_up,
        w_down.T,
        bias_wide,
        label_row,
        label_col,
    )
    halves, (lat_back, diag_back, lon_back) = lon_sum(fold, strips)
    grads = pl.pallas_call(
        unpack_kernel,
        out_shape=jax.ShapeDtypeStruct((2 * HEADS, 1, PAIR * TAB), f32),
        in_specs=[vmem] * 2,
        out_specs=vmem,
        scratch_shapes=[pltpu.VMEM((2 * HEADS, PAIR * TAB), f32)],
        compiler_params=params,
        name="unpack",
    )(*halves)
    grads = grads.reshape(2, 1, HEADS, PAIR * TAB)
    result, grad_field = pl.pallas_call(
        finish_kernel,
        out_shape=(jax.ShapeDtypeStruct(field_in.shape, bf16),) * 2,
        in_specs=[vmem] * 4,
        out_specs=(vmem,) * 2,
        compiler_params=params,
        name="finish",
    )(own, lat_back, diag_back, lon_back)
    return (result, grad_field, grads)


def solution(mesh):
    placed = (
        P(None, "lat", "lon", None),
        P(None, "lat", "lon", None),
        P(),
        P(),
        P(),
        P(),
        P(),
        P(),
        P(None, "lat", None, None),
        P(None, "lat", "lon"),
        P(None, "lat", "lon"),
    )
    return jax.shard_map(
        body,
        mesh=mesh,
        in_specs=placed,
        out_specs=(
            P(None, "lat", "lon", None),
            P(None, "lat", "lon", None),
            P(None, "lat", None, None),
        ),
        check_vma=False,
    )
```

```python
import math

import jax
import jax.numpy as jnp
from jax import lax
from jax.experimental import pallas as pl
from jax.experimental.pallas import tpu as pltpu
from jax.sharding import PartitionSpec as P

C = 192
HEADS = 6
HD = 32
FF = 768
WZ = 2
WLAT = 6
WLON = 12
SPREAD = 2 * WLON - 1
POS = WZ * WLAT * WLON
PAIR = WZ * WLAT
TAB = PAIR * SPREAD
ROWS = HEADS * POS
SLOTS = 16
QUARTER = PAIR * HEADS // 2
REST = 20
LN_ROWS = 96
GELU_ROWS = 48
LANE_CUTS = [(k, min(k + 256, ROWS)) for k in range(0, ROWS, 256)]
DENSE = 80
LANES = 128

epsilon = 1e-05
keep_share = 0.8
LOG2E = math.log2(math.e)
gelu_coef = 0.044715
VMEM_BYTES = 16 * 1024 * 1024
bf16 = jnp.bfloat16
f32 = jnp.float32


def shifted(block, lat_step, lon_step):
    lats, lons = lax.axis_size("lat"), lax.axis_size("lon")
    route = []
    for a in range(lats):
        for b in range(lons):
            target = ((a + lat_step) % lats) * lons + (b + lon_step) % lons
            route.append((a * lons + b, target))
    return lax.ppermute(block, ("lat", "lon"), route)


def mm(a, b):
    return lax.dot_general(a, b, (((1,), (0,)), ((), ())), preferred_element_type=f32)


def mm_nt(a, b):
    return lax.dot_general(a, b, (((1,), (1,)), ((), ())), preferred_element_type=f32)


def norm_parts(values, gain):
    row_mean = jnp.mean(values, axis=-1, keepdims=True)
    centred = values - row_mean
    variance = jnp.mean(centred * centred, axis=-1, keepdims=True)
    inverse = lax.rsqrt(variance + epsilon)
    normed = centred * inverse
    return normed * gain, normed, inverse


def norm_back(grad_in, gain, normed, inverse):
    scaled = grad_in * gain
    first_mean = jnp.mean(scaled, axis=-1, keepdims=True)
    second_mean = jnp.mean(scaled * normed, axis=-1, keepdims=True)
    return (scaled - first_mean - normed * second_mean) * inverse


def gelu_parts(values):
    factor = math.sqrt(2.0 / math.pi)
    square = values * values
    tangent = jnp.tanh(values * (factor + (gelu_coef * factor) * square))
    half = 0.5 + 0.5 * tangent
    result = values * half
    derivative = half + result * (1.0 - tangent) * (factor + (3.0 * gelu_coef * factor) * square)
    return result.astype(bf16), derivative


def by_rows(function, size, *arrays):
    rows = arrays[0].shape[0]
    parts = [function(*(v[r : r + size] for v in arrays)) for r in range(0, rows, size)]
    return tuple(jnp.concatenate(part, axis=0) for part in zip(*parts))


def masked_softmax(scores, bias, allowed):
    scores = scores * (LOG2E / math.sqrt(HD)) + bias
    scores = jnp.where(allowed, scores, -1e30)
    weights = jnp.exp2(scores - jnp.max(scores, axis=0, keepdims=True))
    return weights * (1.0 / jnp.sum(weights, axis=0, keepdims=True))


def head_blocks(wide):
    return jnp.concatenate(
        [wide[h * HD : (h + 1) * HD, h * POS : (h + 1) * POS] for h in range(HEADS)], axis=0
    )


def spread_heads(rows, head_mask):
    return jnp.concatenate([rows * head_mask[h : h + 1, :] for h in range(HEADS)], axis=0)


def quotient(values, divisor):
    return (values * (2**20 // divisor + 1)) >> 20


def one_hot(rows, columns, target):
    row = lax.broadcasted_iota(jnp.int32, (rows, 1), 0)
    column = lax.broadcasted_iota(jnp.int32, (rows, columns), 1)
    return (column == target(row)).astype(f32).astype(bf16)


def window_sources(n, from_strips):
    half, edge = WLAT // 2, WLON // 2
    inner = 2 * WLON - edge

    def target(row):
        c = (row >= POS).astype(jnp.int32)
        row = row - POS * c
        j = quotient(row, PAIR)
        pair = row - PAIR * j
        dz = (pair >= WLAT).astype(jnp.int32)
        i = pair - WLAT * dz
        lon = c * WLON + j
        upper = i < half
        if not from_strips:
            own = (half * dz + i) * (2 * WLON) + lon + edge
            return jnp.where(upper & (lon < inner), own, -1)
        slab = ((2 * n + dz + 1) & 3) * half + jnp.where(upper, i, i - half)
        lat = slab * inner + lon
        corner = 4 * half * inner + slab * edge + lon - inner
        corner = jnp.where(upper, corner, corner + 4 * half * edge)
        return jnp.where(lon < inner, jnp.where(upper, -1, lat), corner)

    columns = 4 * half * (inner + 2 * edge) if from_strips else 2 * half * 2 * WLON
    return one_hot(2 * POS, columns, target)


def output_sources():
    half, edge = WLAT // 2, WLON // 2
    inner = 2 * WLON - edge
    wide, narrow = 4 * half * inner, 4 * half * edge

    def target(row):
        narrow_row = row >= 2 * wide
        row = jnp.where(narrow_row, row - 2 * wide, row)
        size = jnp.where(narrow_row, narrow, wide)
        second = row >= size
        row = jnp.where(second, row - size, row)
        slab = jnp.where(narrow_row, quotient(row, edge), quotient(row, inner))
        lon = jnp.where(narrow_row, row - slab * edge + inner, row - slab * inner)
        z = quotient(slab, half)
        i = slab - half * z + jnp.where(second, half, 0)
        level = (z + 3) & 3
        c = (lon >= WLON).astype(jnp.int32)
        pair = (level & 1) * WLAT + i
        return (level >> 1) * (2 * POS) + c * POS + (lon - WLON * c) * PAIR + pair

    return one_hot(4 * POS, 4 * POS, target)


def table_order():
    def target(row):
        pair = quotient(row, SPREAD)
        return (SPREAD - 1 - (row - SPREAD * pair)) * PAIR + pair

    return one_hot(TAB, TAB, target)


def chunk_order():
    def target(row):
        pair = quotient(row, HEADS)
        return (row - HEADS * pair) * SLOTS + pair

    return one_hot(PAIR * HEADS, HEADS * SLOTS, target)


def row_order():
    def target(row):
        head = quotient(row, SLOTS)
        return (row - SLOTS * head) * SLOTS + head

    return one_hot(2 * HEADS * SLOTS, PAIR * SLOTS, target)


def put(packed, t, row, slab):
    third = packed.shape[0] // 3
    size = slab.shape[0]
    rest = C - LANES
    packed[t * third + row : t * third + row + size, :] = slab[:, :LANES]
    packed[2 * third + row : 2 * third + row + size, t * rest : (t + 1) * rest] = slab[:, LANES:]


def get(packed, t, row, size):
    third = packed.shape[0] // 3
    rest = C - LANES
    return (
        packed[t * third + row : t * third + row + size, :],
        packed[2 * third + row : 2 * third + row + size, t * rest : (t + 1) * rest],
    )


def pack_lat_kernel(field_ref, cot_ref, lat_out, lat_buf, rows, arrived):
    half = WLAT // 2
    edge = WLON // 2
    inner = 2 * WLON - edge
    sources = (field_ref, cot_ref)
    copies = [
        pltpu.make_async_copy(sources[t].at[:, pl.ds(0, half)], rows.at[t], arrived.at[t])
        for t in range(2)
    ]
    for copy in copies:
        copy.start()
    for t in range(2):
        copies[t].wait()
        for z in range(4):
            for i in range(half):
                put(lat_buf, t, (z * half + i) * inner, rows[t, z, i].astype(f32)[edge:])
    lat_out[...] = lat_buf[...].astype(bf16)


def pack_edge_kernel(field_ref, cot_ref, after_ref, diag_out, lon_out, diag_buf, lon_buf):
    half = WLAT // 2
    edge = WLON // 2
    for t, source in enumerate((field_ref, cot_ref)):
        for z in range(4):
            for i in range(half):
                row = (z * half + i) * edge
                put(diag_buf, t, row, source[z, i].astype(f32)[:edge])
                put(lon_buf, t, row, source[z, half + i].astype(f32)[:edge])
    diag_out[...] = diag_buf[...].astype(bf16)
    lon_out[...] = lon_buf[...].astype(bf16)


def block_kernel(
    field_ref,
    cot_ref,
    lon_ref,
    lat_ref,
    diag_ref,
    gains_ref,
    wqkv_t_ref,
    wproj_ref,
    wup_ref,
    wdown_t_ref,
    bias_ref,
    label_row_ref,
    label_col_ref,
    fold_out,
    own_out,
    lat_out,
    diag_out,
    lon_out,
    wide,
    dense,
):
    half = WLAT // 2
    root = 1.0 / math.sqrt(HD)
    pieces = [ref[...].astype(f32) for ref in (lat_ref, lon_ref, diag_ref)]
    thirds = []
    for k in range(3):
        sizes = [piece.shape[0] // 3 for piece in pieces]
        third = [piece[k * size : (k + 1) * size] for piece, size in zip(pieces, sizes)]
        thirds.append(jnp.concatenate(third, axis=0).astype(bf16))
    strips = jnp.concatenate(thirds, axis=1)
    narrow = C - LANES
    gain1 = gains_ref[0:1, :]
    gain2 = gains_ref[1:2, :]
    wq_t = wqkv_t_ref[0:C, :]
    wk_t = wqkv_t_ref[C : 2 * C, :]
    wv_t = wqkv_t_ref[2 * C : 3 * C, :]
    head = lax.broadcasted_iota(jnp.int32, (HEADS, C), 0)
    head_mask = (lax.broadcasted_iota(jnp.int32, (HEADS, C), 1) >> 5) == head
    head_mask = head_mask.astype(f32).astype(bf16)
    table_perm = table_order()
    chunk_perm = chunk_order()
    dense[...] = jnp.zeros_like(dense)
    results = []
    for n in range(2):
        moved = mm(window_sources(n, True), strips)
        own_rows = window_sources(n, False)
        inputs = []
        for t, own in enumerate((field_ref, cot_ref)):
            levels = [(2 * n + dz + 1) % 4 for dz in range(WZ)]
            slabs = [own[z, half + i].astype(f32) for z in levels for i in range(half)]
            slabs = mm(own_rows, jnp.concatenate(slabs, axis=0).astype(bf16))
            main = moved[:, t * LANES : (t + 1) * LANES]
            side = moved[:, 2 * LANES + t * narrow : 2 * LANES + (t + 1) * narrow]
            inputs.append(slabs + jnp.concatenate([main, side], axis=1))
        x, cot = inputs
        scaled1, normed1, inverse1 = by_rows(lambda v: norm_parts(v, gain1), LN_ROWS, x)
        h1 = scaled1.astype(bf16)
        q_all = mm_nt(h1, wq_t).astype(bf16)
        k_all = mm_nt(h1, wk_t).astype(bf16)
        v_all = mm_nt(h1, wv_t).astype(bf16)
        saved = []
        branches = []
        for c in range(2):
            w = 2 * n + c
            rows = slice(c * POS, (c + 1) * POS)
            v_t = mm_nt(wv_t, h1[rows]).astype(bf16)
            q_wide = spread_heads(q_all[rows], head_mask)
            label_col = label_col_ref[:, w : w + 1]
            probs = []
            for low, high in LANE_CUTS:
                scores = mm_nt(k_all[rows], q_wide[low:high])
                allowed = label_col == label_row_ref[w : w + 1, low:high]
                probs.append(masked_softmax(scores, bias_ref[n, :, low:high], allowed))
            probs_low = jnp.concatenate([part.astype(bf16) for part in probs], axis=1)
            attended = head_blocks(mm(v_t, probs_low)).astype(bf16).T
            factor = gains_ref[2 + w : 3 + w, :]
            branches.append((mm(attended, wproj_ref[...]) * factor).astype(bf16).astype(f32))
            saved.append((q_wide, probs, probs_low))
        y_sum = x + jnp.concatenate(branches, axis=0)
        scaled2, normed2, inverse2 = by_rows(lambda v: norm_parts(v, gain2), LN_ROWS, y_sum)
        act, slope = by_rows(gelu_parts, GELU_ROWS, mm(scaled2.astype(bf16), wup_ref[...]))
        result = (y_sum + mm_nt(act, wdown_t_ref[...])).astype(bf16)
        grad_up = (mm(cot.astype(bf16), wdown_t_ref[...]) * slope).astype(bf16)
        grad_hidden = mm_nt(grad_up, wup_ref[...])
        (grad_sum,) = by_rows(
            lambda v, g, normed, inverse: (v + norm_back(g, gain2, normed, inverse),),
            LN_ROWS,
            cot,
            grad_hidden,
            normed2,
            inverse2,
        )
        grad_low_in = grad_sum.astype(bf16).astype(f32)
        folded = [None] * len(LANE_CUTS)
        grad_h1 = []
        for c in range(2):
            rows = slice(c * POS, (c + 1) * POS)
            q_wide, probs, probs_low = saved[c]
            factor = gains_ref[2 + 2 * n + c : 3 + 2 * n + c, :]
            grad_branch = (grad_low_in[rows] * factor).astype(bf16)
            grad_att = mm_nt(grad_branch, wproj_ref[...]).astype(bf16)
            g_wide = spread_heads(grad_att, head_mask)
            grad_low = []
            for k, (low, high) in enumerate(LANE_CUTS):
                grad_probs = mm_nt(v_all[rows], g_wide[low:high])
                inner_sum = jnp.sum(probs[k] * grad_probs, axis=0, keepdims=True)
                grad_scores = probs[k] * (grad_probs - inner_sum)
                folded[k] = grad_scores if c == 0 else folded[k] + grad_scores
                grad_low.append(grad_scores.astype(bf16))
            grad_low = jnp.concatenate(grad_low, axis=1)
            k_t = mm_nt(wk_t, h1[rows]).astype(bf16)
            grad_q = (head_blocks(mm(k_t, grad_low)) * root).astype(bf16).T
            grad_k = (mm(grad_low, q_wide) * root).astype(bf16)
            grad_v = mm(probs_low, g_wide).astype(bf16)
            grad_h1.append(mm(grad_q, wq_t) + mm(grad_k, wk_t) + mm(grad_v, wv_t))
        folded = jnp.concatenate([part.astype(bf16) for part in folded], axis=1)
        wide[...] = folded.T.astype(f32).reshape(HEADS, POS, POS)
        total = None
        for o in range(WLON):
            left = PAIR * (WLON - 1 - o)
            right = TAB - POS - left
            parts = [wide[:, PAIR * o : PAIR * (o + 1), :]]
            if left:
                parts = [jnp.zeros((HEADS, PAIR, left), f32)] + parts
            if right:
                parts = parts + [jnp.zeros((HEADS, PAIR, right), f32)]
            piece = jnp.concatenate(parts, axis=2)
            total = piece if total is None else total + piece
        total = jnp.concatenate([total, jnp.zeros((HEADS, SLOTS - PAIR, TAB), f32)], axis=1)
        total = total.reshape(HEADS * SLOTS, TAB).astype(bf16)
        total = mm_nt(total, table_perm).astype(bf16)
        total = mm(chunk_perm, total)
        for k in range(2):
            part = total[k * QUARTER : (k + 1) * QUARTER]
            dense[:QUARTER, :] = part[:, :LANES]
            dense[QUARTER : 2 * QUARTER, :] = part[:, LANES : 2 * LANES]
            rest = [part[HEADS * g : HEADS * (g + 1), 2 * LANES :] for g in range(WLAT)]
            dense[2 * QUARTER : 2 * QUARTER + HEADS, : WLAT * REST] = jnp.concatenate(rest, axis=1)
            fold_out[2 * n + k] = dense[...].astype(bf16)
        grad_h1 = jnp.concatenate(grad_h1, axis=0).astype(bf16).astype(f32)
        (grad_field,) = by_rows(
            lambda v, g, normed, inverse: (
                (v + norm_back(g, gain1, normed, inverse)).astype(bf16),
            ),
            LN_ROWS,
            grad_sum,
            grad_h1,
            normed1,
            inverse1,
        )
        results.append((result, grad_field))
    order = output_sources()
    outputs = [mm(order, jnp.concatenate(parts, axis=0)) for parts in zip(*results)]
    row = 0
    for out in (own_out, lat_out, lon_out, diag_out):
        size = out.shape[0] // 3
        cuts = [value[row : row + size] for value in outputs]
        side = jnp.concatenate([cut[:, LANES:] for cut in cuts], axis=1)
        cuts = [cut[:, :LANES] for cut in cuts] + [side]
        out[...] = jnp.concatenate(cuts, axis=0).astype(bf16)
        row += size


def prepare_kernel(
    table_ref,
    region_ref,
    wqkv_ref,
    gain1_ref,
    gain2_ref,
    keep_ref,
    bias_out,
    label_row_out,
    label_col_out,
    wqkv_t_out,
    gains_out,
    flat,
    rows,
    wide,
    marks,
):
    wqkv_t_out[...] = wqkv_ref[...].astype(f32).T.astype(bf16)
    gains_out[0:1, :] = gain1_ref[...]
    gains_out[1:2, :] = gain2_ref[...]
    for n in range(2):
        for c in range(2):
            factor = keep_ref[n, 0, c].astype(f32) * (1.0 / keep_share)
            row = 2 + 2 * n + c
            gains_out[row : row + 1, :] = jnp.full((1, C), factor, f32)
    last = lax.axis_index("lat") == lax.axis_size("lat") - 1
    level = lax.broadcasted_iota(jnp.int32, (4, 2 * WLON), 0)
    for i in range(WLAT):
        wrapped = 2 * (level >= 4 - WZ // 2).astype(jnp.int32)
        if i >= WLAT // 2:
            wrapped = wrapped + last.astype(jnp.int32)
        marks[4 * i : 4 * (i + 1), :] = (4 * region_ref[i] + wrapped).astype(f32)
    place = lax.broadcasted_iota(jnp.int32, (POS, 4 * WLAT), 0)
    lane = lax.broadcasted_iota(jnp.int32, (POS, 4 * WLAT), 1)
    lon = quotient(place, PAIR)
    pair = place - PAIR * lon
    upper = (pair >= WLAT).astype(jnp.int32)
    source = 4 * (pair - WLAT * upper) + upper
    columns = []
    for n in range(2):
        chosen = mm((lane == source + WZ * n).astype(f32).astype(bf16), marks[...].astype(bf16))
        for c in range(2):
            own = jnp.where(lane == lon + WLON * c, chosen, 0.0)
            columns.append(jnp.sum(own, axis=1, keepdims=True))
    label_col_out[...] = jnp.concatenate(columns, axis=1)
    spread = jnp.concatenate([jnp.broadcast_to(v, (POS, LANES)) for v in columns], axis=1).T
    labels = jnp.concatenate([spread[k * LANES : k * LANES + 1] for k in range(4)], axis=0)
    label_row_out[...] = jnp.concatenate([labels] * HEADS, axis=1)
    part = PAIR // WZ * SPREAD
    for k in range(2 * HEADS):
        flat[k : k + 1, :] = table_ref[k]
    rows[...] = jnp.zeros_like(rows)
    for a in range(WZ):
        for c in range(WLAT):
            pieces = []
            for b in range(WZ):
                start = ((a * WZ + b) * WLAT + c) * part
                pieces.append(flat[:, start : start + part])
            row = (a * WLAT + c) * SLOTS
            rows[row : row + 2 * HEADS, :] = jnp.concatenate(pieces, axis=1)
    left = rows[...]
    perm = table_order()
    row_perm = row_order()
    total = None
    for _ in range(3):
        low = left.astype(bf16)
        left = left - low.astype(f32)
        term = mm(row_perm, mm(low, perm).astype(bf16))
        total = term if total is None else total + term
    total = total.reshape(2 * HEADS, SLOTS, TAB)
    for o in range(WLON):
        start = PAIR * (WLON - 1 - o)
        wide[:, PAIR * o : PAIR * (o + 1), :] = total[:, :PAIR, start : start + POS]
    for n in range(2):
        bias_out[n] = wide[n * HEADS : (n + 1) * HEADS].reshape(ROWS, POS).T * LOG2E


def unpack_kernel(mine_ref, other_ref, table_out, flat):
    odd = (lax.axis_index("lon") & 1) != 0
    part = PAIR // WZ * SPREAD
    for n in range(2):
        halves = []
        for k in range(2):
            mine = mine_ref[n].astype(f32)
            other = other_ref[n].astype(f32)
            dense = jnp.where(odd == (k == 1), mine, other)
            rest = dense[2 * QUARTER : 2 * QUARTER + HEADS]
            rest = [rest[:, g * REST : (g + 1) * REST] for g in range(WLAT)]
            rest = jnp.concatenate(rest, axis=0)
            parts = [dense[:QUARTER], dense[QUARTER : 2 * QUARTER], rest]
            halves.append(jnp.concatenate(parts, axis=1))
        for a in range(WZ):
            for c in range(WLAT):
                row = c * HEADS
                chunk = halves[a][row : row + HEADS]
                for b in range(WZ):
                    start = ((a * WZ + b) * WLAT + c) * part
                    flat[n * HEADS : (n + 1) * HEADS, start : start + part] = chunk[
                        :, b * part : (b + 1) * part
                    ]
    for k in range(2 * HEADS):
        table_out[k] = flat[k : k + 1, :]


def add_kernel(*refs):
    copies_out = refs[-1]
    parts = [ref[k].astype(f32) for ref in refs[:-1] for k in range(ref.shape[0])]
    while len(parts) > 1:
        parts = [parts[k] + parts[k + 1] for k in range(0, len(parts), 2)]
    total = parts[0].astype(bf16)
    for k in range(copies_out.shape[0]):
        copies_out[k] = total


def finish_kernel(own_ref, lat_ref, diag_ref, lon_ref, out_ref, grad_ref):
    half = WLAT // 2
    edge = WLON // 2
    inner = 2 * WLON - edge
    lat_part = lat_ref[...].astype(f32)
    diag_part = diag_ref[...].astype(f32)
    lon_part = lon_ref[...].astype(f32)
    own_part = own_ref[...].astype(f32)
    for t, target in enumerate((out_ref, grad_ref)):
        for z in range(4):
            for i in range(half):
                k = z * half + i
                parts = (get(diag_part, t, k * edge, edge), get(lat_part, t, k * inner, inner))
                slab = [jnp.concatenate([parts[0][j], parts[1][j]], axis=0) for j in range(2)]
                target[z, i] = jnp.concatenate(slab, axis=1).astype(bf16)
                slab = jnp.concatenate(get(lon_part, t, k * edge, edge), axis=1)
                own = jnp.concatenate(get(own_part, t, k * inner, inner), axis=1)
                target[z, half + i] = jnp.concatenate([slab, own], axis=0).astype(bf16)


def lon_sum(quarters, strips):
    lons = lax.axis_size("lon")
    me = lax.axis_index("lon")
    bits = [(me >> k) & 1 for k in range(2)]
    far = [[4 * k + j for k in range(lons // 4)] for j in range(4)]

    def swapped(block, distance):
        return lax.ppermute(block, "lon", [(i, i ^ distance) for i in range(lons)])

    def pick(value, bit, axis):
        return lax.dynamic_index_in_dim(value, bit, axis, keepdims=False)

    def added(parts, copies):
        vmem = pl.BlockSpec(memory_space=pltpu.VMEM)
        return pl.pallas_call(
            add_kernel,
            out_shape=jax.ShapeDtypeStruct((copies,) + parts[0].shape[1:], bf16),
            in_specs=[vmem] * len(parts),
            out_specs=vmem,
            compiler_params=pltpu.CompilerParams(vmem_limit_bytes=VMEM_BYTES),
            name="add",
        )(*parts)

    value = quarters.reshape((2, 2) + quarters.shape[1:])
    other = swapped(pick(value, 1 - bits[0], 1), 1)
    value = pick(value, bits[0], 1).astype(f32) + other.astype(f32)
    value = value.astype(bf16)
    other = swapped(pick(value, 1 - bits[1], 0), 2)
    parts = added((pick(value, bits[1], 0)[None], other[None]), lons // 4)
    parts, strips = lax.optimization_barrier((parts, strips))
    steps = ((1, 0), (1, 1), (0, 1))
    strips = [shifted(strip, *step) for strip, step in zip(strips, steps)]
    parts = lax.all_to_all(parts, "lon", 0, 0, axis_index_groups=far)
    value, strips = lax.optimization_barrier((added((parts,), 1)[0], strips))
    other = swapped(value, 2)
    lower = jnp.where(bits[1] == 0, value, other)
    upper = jnp.where(bits[1] == 0, other, value)
    value = jnp.stack([lower, upper])
    return (value, swapped(value, 1)), strips


def body(
    field_in,
    cotangent,
    ln1_gain,
    w_qkv,
    w_proj,
    ln2_gain,
    w_up,
    w_down,
    bias_table,
    region_ids,
    keep_flags,
):
    levels, lat_rows, lon_cols, channels = field_in.shape
    half = WLAT // 2
    edge = WLON // 2
    inner = lon_cols - edge
    vmem = pl.BlockSpec(memory_space=pltpu.VMEM)
    smem = pl.BlockSpec(memory_space=pltpu.SMEM)
    sizes = [3 * levels * half * size for size in (inner, edge, edge)]
    packed = tuple(jax.ShapeDtypeStruct((size, LANES), bf16) for size in sizes)
    buffers = [pltpu.VMEM((size, LANES), f32) for size in sizes]
    params = pltpu.CompilerParams(vmem_limit_bytes=VMEM_BYTES)
    lat_part = pl.pallas_call(
        pack_lat_kernel,
        out_shape=packed[0],
        in_specs=[pl.BlockSpec(memory_space=pltpu.HBM)] * 2,
        out_specs=vmem,
        scratch_shapes=buffers[:1]
        + [pltpu.VMEM((2, levels, half, lon_cols, C), bf16), pltpu.SemaphoreType.DMA((2,))],
        compiler_params=params,
        name="pack_lat",
    )(field_in, cotangent)
    diag_part, lon_part = pl.pallas_call(
        pack_edge_kernel,
        out_shape=packed[1:],
        in_specs=[vmem] * 2 + [pl.BlockSpec(memory_space=pl.ANY)],
        out_specs=(vmem,) * 2,
        scratch_shapes=buffers[1:],
        compiler_params=params,
        name="pack_edge",
    )(field_in, cotangent, lat_part)
    lat_part = shifted(lat_part, -1, 0)
    diag_part = shifted(diag_part, -1, -1)
    lon_part = shifted(lon_part, 0, -1)

    bias_wide, label_row, label_col, weights_t, gains = pl.pallas_call(
        prepare_kernel,
        out_shape=(
            jax.ShapeDtypeStruct((2, POS, ROWS), f32),
            jax.ShapeDtypeStruct((4, ROWS), f32),
            jax.ShapeDtypeStruct((POS, 4), f32),
            jax.ShapeDtypeStruct((3 * C, C), bf16),
            jax.ShapeDtypeStruct((6, C), f32),
        ),
        in_specs=[vmem] * 5 + [smem],
        out_specs=(vmem,) * 5,
        scratch_shapes=[
            pltpu.VMEM((2 * HEADS, PAIR * TAB), f32),
            pltpu.VMEM((PAIR * SLOTS, TAB), f32),
            pltpu.VMEM((2 * HEADS, POS, POS), f32),
            pltpu.VMEM((4 * WLAT, 2 * WLON), f32),
        ],
        compiler_params=params,
        name="prepare",
    )(
        bias_table.reshape(2 * HEADS, 1, PAIR * TAB),
        region_ids.transpose(1, 0, 2),
        w_qkv,
        ln1_gain.reshape(1, C),
        ln2_gain.reshape(1, C),
        keep_flags,
    )
    fold, own, *strips = pl.pallas_call(
        block_kernel,
        out_shape=(
            jax.ShapeDtypeStruct((4, DENSE, LANES), bf16),
            packed[0],
        )
        + packed,
        in_specs=[vmem] * 13,
        out_specs=(vmem,) * 5,
        scratch_shapes=[
            pltpu.VMEM((HEADS, POS, POS), f32),
            pltpu.VMEM((DENSE, LANES), f32),
        ],
        compiler_params=params,
        name="block",
    )(
        field_in,
        cotangent,
        lon_part,
        lat_part,
        diag_part,
        gains,
        weights_t,
        w_proj,
        w_up,
        w_down.T,
        bias_wide,
        label_row,
        label_col,
    )
    halves, (lat_back, diag_back, lon_back) = lon_sum(fold, strips)
    grads = pl.pallas_call(
        unpack_kernel,
        out_shape=jax.ShapeDtypeStruct((2 * HEADS, 1, PAIR * TAB), f32),
        in_specs=[vmem] * 2,
        out_specs=vmem,
        scratch_shapes=[pltpu.VMEM((2 * HEADS, PAIR * TAB), f32)],
        compiler_params=params,
        name="unpack",
    )(*halves)
    grads = grads.reshape(2, 1, HEADS, PAIR * TAB)
    result, grad_field = pl.pallas_call(
        finish_kernel,
        out_shape=(jax.ShapeDtypeStruct(field_in.shape, bf16),) * 2,
        in_specs=[vmem] * 4,
        out_specs=(vmem,) * 2,
        compiler_params=params,
        name="finish",
    )(own, lat_back, diag_back, lon_back)
    return (result, grad_field, grads)


def solution(mesh):
    placed = (
        P(None, "lat", "lon", None),
        P(None, "lat", "lon", None),
        P(),
        P(),
        P(),
        P(),
        P(),
        P(),
        P(None, "lat", None, None),
        P(None, "lat", "lon"),
        P(None, "lat", "lon"),
    )
    return jax.shard_map(
        body,
        mesh=mesh,
        in_specs=placed,
        out_specs=(
            P(None, "lat", "lon", None),
            P(None, "lat", "lon", None),
            P(None, "lat", None, None),
        ),
        check_vma=False,
    )
```

```python
import math

import jax
import jax.numpy as jnp
from jax import lax
from jax.experimental import pallas as pl
from jax.experimental.pallas import tpu as pltpu
from jax.sharding import PartitionSpec as P

C = 192
HEADS = 6
HD = 32
FF = 768
WZ = 2
WLAT = 6
WLON = 12
SPREAD = 2 * WLON - 1
POS = WZ * WLAT * WLON
PAIR = WZ * WLAT
TAB = PAIR * SPREAD
ROWS = HEADS * POS
SLOTS = 16
QUARTER = PAIR * HEADS // 2
REST = 20
LN_ROWS = 96
GELU_ROWS = 48
LANE_CUTS = [(k, min(k + 256, ROWS)) for k in range(0, ROWS, 256)]
DENSE = 80
LANES = 128

epsilon = 1e-05
keep_share = 0.8
LOG2E = math.log2(math.e)
gelu_coef = 0.044715
VMEM_BYTES = 16 * 1024 * 1024
bf16 = jnp.bfloat16
f32 = jnp.float32


def shifted(block, lat_step, lon_step):
    lats, lons = lax.axis_size("lat"), lax.axis_size("lon")
    route = []
    for a in range(lats):
        for b in range(lons):
            target = ((a + lat_step) % lats) * lons + (b + lon_step) % lons
            route.append((a * lons + b, target))
    return lax.ppermute(block, ("lat", "lon"), route)


def mm(a, b):
    return lax.dot_general(a, b, (((1,), (0,)), ((), ())), preferred_element_type=f32)


def mm_nt(a, b):
    return lax.dot_general(a, b, (((1,), (1,)), ((), ())), preferred_element_type=f32)


def norm_parts(values, gain):
    row_mean = jnp.mean(values, axis=-1, keepdims=True)
    centred = values - row_mean
    variance = jnp.mean(centred * centred, axis=-1, keepdims=True)
    inverse = lax.rsqrt(variance + epsilon)
    normed = centred * inverse
    return normed * gain, normed, inverse


def norm_back(grad_in, gain, normed, inverse):
    scaled = grad_in * gain
    first_mean = jnp.mean(scaled, axis=-1, keepdims=True)
    second_mean = jnp.mean(scaled * normed, axis=-1, keepdims=True)
    return (scaled - first_mean - normed * second_mean) * inverse


def gelu_parts(values):
    factor = math.sqrt(2.0 / math.pi)
    square = values * values
    tangent = jnp.tanh(values * (factor + (gelu_coef * factor) * square))
    half = 0.5 + 0.5 * tangent
    result = values * half
    derivative = half + result * (1.0 - tangent) * (factor + (3.0 * gelu_coef * factor) * square)
    return result.astype(bf16), derivative


def by_rows(function, size, *arrays):
    rows = arrays[0].shape[0]
    parts = [function(*(v[r : r + size] for v in arrays)) for r in range(0, rows, size)]
    return tuple(jnp.concatenate(part, axis=0) for part in zip(*parts))


def masked_softmax(scores, bias, allowed):
    scores = scores * (LOG2E / math.sqrt(HD)) + bias
    scores = jnp.where(allowed, scores, -1e30)
    weights = jnp.exp2(scores - jnp.max(scores, axis=0, keepdims=True))
    return weights * (1.0 / jnp.sum(weights, axis=0, keepdims=True))


def head_blocks(wide):
    return jnp.concatenate(
        [wide[h * HD : (h + 1) * HD, h * POS : (h + 1) * POS] for h in range(HEADS)], axis=0
    )


def spread_heads(rows, head_mask):
    return jnp.concatenate([rows * head_mask[h : h + 1, :] for h in range(HEADS)], axis=0)


def quotient(values, divisor):
    return (values * (2**20 // divisor + 1)) >> 20


def one_hot(rows, columns, target):
    row = lax.broadcasted_iota(jnp.int32, (rows, 1), 0)
    column = lax.broadcasted_iota(jnp.int32, (rows, columns), 1)
    return (column == target(row)).astype(f32).astype(bf16)


def window_order():
    def target(row):
        c = (row >= POS).astype(jnp.int32)
        row = row - POS * c
        j = quotient(row, PAIR)
        return (row - PAIR * j) * (2 * WLON) + c * WLON + j

    return one_hot(2 * POS, 2 * POS, target)


def natural_order():
    def target(row):
        pair = quotient(row, 2 * WLON)
        lon = row - 2 * WLON * pair
        c = (lon >= WLON).astype(jnp.int32)
        return c * POS + (lon - WLON * c) * PAIR + pair

    return one_hot(2 * POS, 2 * POS, target)


def table_order():
    def target(row):
        pair = quotient(row, SPREAD)
        return (SPREAD - 1 - (row - SPREAD * pair)) * PAIR + pair

    return one_hot(TAB, TAB, target)


def chunk_order():
    def target(row):
        pair = quotient(row, HEADS)
        return (row - HEADS * pair) * SLOTS + pair

    return one_hot(PAIR * HEADS, HEADS * SLOTS, target)


def row_order():
    def target(row):
        head = quotient(row, SLOTS)
        return (row - SLOTS * head) * SLOTS + head

    return one_hot(2 * HEADS * SLOTS, PAIR * SLOTS, target)


def put(packed, t, row, slab):
    third = packed.shape[0] // 3
    size = slab.shape[0]
    rest = C - LANES
    packed[t * third + row : t * third + row + size, :] = slab[:, :LANES]
    packed[2 * third + row : 2 * third + row + size, t * rest : (t + 1) * rest] = slab[:, LANES:]


def get(packed, t, row, size):
    third = packed.shape[0] // 3
    rest = C - LANES
    return (
        packed[t * third + row : t * third + row + size, :],
        packed[2 * third + row : 2 * third + row + size, t * rest : (t + 1) * rest],
    )


def pack_lat_kernel(field_ref, cot_ref, lat_out, lat_buf, rows, arrived):
    half = WLAT // 2
    edge = WLON // 2
    inner = 2 * WLON - edge
    sources = (field_ref, cot_ref)
    copies = [
        pltpu.make_async_copy(sources[t].at[:, pl.ds(0, half)], rows.at[t], arrived.at[t])
        for t in range(2)
    ]
    for copy in copies:
        copy.start()
    for t in range(2):
        copies[t].wait()
        for z in range(4):
            for i in range(half):
                put(lat_buf, t, (z * half + i) * inner, rows[t, z, i].astype(f32)[edge:])
    lat_out[...] = lat_buf[...].astype(bf16)


def pack_edge_kernel(field_ref, cot_ref, after_ref, diag_out, lon_out, diag_buf, lon_buf):
    half = WLAT // 2
    edge = WLON // 2
    for t, source in enumerate((field_ref, cot_ref)):
        for z in range(4):
            for i in range(half):
                row = (z * half + i) * edge
                put(diag_buf, t, row, source[z, i].astype(f32)[:edge])
                put(lon_buf, t, row, source[z, half + i].astype(f32)[:edge])
    diag_out[...] = diag_buf[...].astype(bf16)
    lon_out[...] = lon_buf[...].astype(bf16)


def scores_kernel(
    field_ref,
    cot_ref,
    lon_ref,
    lat_ref,
    diag_ref,
    gains_ref,
    wqkv_t_ref,
    wproj_ref,
    wup_ref,
    wdown_t_ref,
    bias_ref,
    label_row_ref,
    label_col_ref,
    fold_out,
    x_out,
    probs_out,
    grad_low_out,
    grad_sum_out,
    result_out,
    frame,
    wide,
    dense,
):
    half = WLAT // 2
    cols = 2 * WLON
    edge = WLON // 2
    inner = cols - edge
    root = 1.0 / math.sqrt(HD)
    lon_part = lon_ref[...].astype(f32)
    lat_part = lat_ref[...].astype(f32)
    diag_part = diag_ref[...].astype(f32)
    for t, own in enumerate((field_ref, cot_ref)):
        for level in range(4):
            z = (level + 1) % 4
            for i in range(half):
                k = z * half + i
                row = (level * WLAT + i) * cols
                frame[t, row : row + inner, :] = own[z, half + i].astype(f32)[edge:, :]
                main, rest = get(lon_part, t, k * edge, edge)
                frame[t, row + inner : row + cols, :LANES] = main
                frame[t, row + inner : row + cols, LANES:] = rest
                row = (level * WLAT + half + i) * cols
                main, rest = get(lat_part, t, k * inner, inner)
                frame[t, row : row + inner, :LANES] = main
                frame[t, row : row + inner, LANES:] = rest
                main, rest = get(diag_part, t, k * edge, edge)
                frame[t, row + inner : row + cols, :LANES] = main
                frame[t, row + inner : row + cols, LANES:] = rest
    gain1 = gains_ref[0:1, :]
    gain2 = gains_ref[1:2, :]
    wq_t = wqkv_t_ref[0:C, :]
    wk_t = wqkv_t_ref[C : 2 * C, :]
    wv_t = wqkv_t_ref[2 * C : 3 * C, :]
    head = lax.broadcasted_iota(jnp.int32, (HEADS, C), 0)
    head_mask = (lax.broadcasted_iota(jnp.int32, (HEADS, C), 1) >> 5) == head
    head_mask = head_mask.astype(f32).astype(bf16)
    perm = window_order()
    table_perm = table_order()
    chunk_perm = chunk_order()
    dense[...] = jnp.zeros_like(dense)
    for n in range(2):
        both = slice(n * 2 * POS, (n + 1) * 2 * POS)
        x = mm(perm, frame[0, both, :].astype(bf16))
        cot = mm(perm, frame[1, both, :].astype(bf16))
        x_out[both, :] = x.astype(bf16)
        (scaled1,) = by_rows(lambda v: norm_parts(v, gain1)[:1], LN_ROWS, x)
        h1 = scaled1.astype(bf16)
        q_all = mm_nt(h1, wq_t).astype(bf16)
        k_all = mm_nt(h1, wk_t).astype(bf16)
        v_all = mm_nt(h1, wv_t).astype(bf16)
        saved = []
        branches = []
        for c in range(2):
            w = 2 * n + c
            rows = slice(c * POS, (c + 1) * POS)
            v_t = mm_nt(wv_t, h1[rows]).astype(bf16)
            q_wide = spread_heads(q_all[rows], head_mask)
            label_col = label_col_ref[:, w : w + 1]
            probs = []
            for low, high in LANE_CUTS:
                scores = mm_nt(k_all[rows], q_wide[low:high])
                allowed = label_col == label_row_ref[w : w + 1, low:high]
                probs.append(masked_softmax(scores, bias_ref[n, :, low:high], allowed))
            probs_low = jnp.concatenate([part.astype(bf16) for part in probs], axis=1)
            probs_out[w] = probs_low
            attended = head_blocks(mm(v_t, probs_low)).astype(bf16).T
            factor = gains_ref[2 + w : 3 + w, :]
            branches.append((mm(attended, wproj_ref[...]) * factor).astype(bf16).astype(f32))
            saved.append(probs)
        y_sum = x + jnp.concatenate(branches, axis=0)
        scaled2, normed2, inverse2 = by_rows(lambda v: norm_parts(v, gain2), LN_ROWS, y_sum)
        act, slope = by_rows(gelu_parts, GELU_ROWS, mm(scaled2.astype(bf16), wup_ref[...]))
        result_out[both, :] = (y_sum + mm_nt(act, wdown_t_ref[...])).astype(bf16)
        grad_up = (mm(cot.astype(bf16), wdown_t_ref[...]) * slope).astype(bf16)
        grad_hidden = mm_nt(grad_up, wup_ref[...])
        (grad_sum,) = by_rows(
            lambda v, g, normed, inverse: (v + norm_back(g, gain2, normed, inverse),),
            LN_ROWS,
            cot,
            grad_hidden,
            normed2,
            inverse2,
        )
        grad_sum_low = grad_sum.astype(bf16)
        grad_sum_out[both, :] = grad_sum_low
        grad_low_in = grad_sum_low.astype(f32)
        folded = [None] * len(LANE_CUTS)
        for c in range(2):
            rows = slice(c * POS, (c + 1) * POS)
            probs = saved[c]
            factor = gains_ref[2 + 2 * n + c : 3 + 2 * n + c, :]
            grad_branch = (grad_low_in[rows] * factor).astype(bf16)
            grad_att = mm_nt(grad_branch, wproj_ref[...]).astype(bf16)
            g_wide = spread_heads(grad_att, head_mask)
            grad_low = []
            for k, (low, high) in enumerate(LANE_CUTS):
                grad_probs = mm_nt(v_all[rows], g_wide[low:high])
                inner_sum = jnp.sum(probs[k] * grad_probs, axis=0, keepdims=True)
                grad_scores = probs[k] * (grad_probs - inner_sum)
                folded[k] = grad_scores if c == 0 else folded[k] + grad_scores
                grad_low.append(grad_scores.astype(bf16))
            grad_low_out[2 * n + c] = jnp.concatenate(grad_low, axis=1)
        folded = jnp.concatenate([part.astype(bf16) for part in folded], axis=1)
        wide[...] = folded.T.astype(f32).reshape(HEADS, POS, POS)
        total = None
        for o in range(WLON):
            left = PAIR * (WLON - 1 - o)
            right = TAB - POS - left
            parts = [wide[:, PAIR * o : PAIR * (o + 1), :]]
            if left:
                parts = [jnp.zeros((HEADS, PAIR, left), f32)] + parts
            if right:
                parts = parts + [jnp.zeros((HEADS, PAIR, right), f32)]
            piece = jnp.concatenate(parts, axis=2)
            total = piece if total is None else total + piece
        total = jnp.concatenate([total, jnp.zeros((HEADS, SLOTS - PAIR, TAB), f32)], axis=1)
        total = total.reshape(HEADS * SLOTS, TAB).astype(bf16)
        total = mm_nt(total, table_perm).astype(bf16)
        total = mm(chunk_perm, total)
        for k in range(2):
            part = total[k * QUARTER : (k + 1) * QUARTER]
            dense[:QUARTER, :] = part[:, :LANES]
            dense[QUARTER : 2 * QUARTER, :] = part[:, LANES : 2 * LANES]
            rest = [part[HEADS * g : HEADS * (g + 1), 2 * LANES :] for g in range(WLAT)]
            dense[2 * QUARTER : 2 * QUARTER + HEADS, : WLAT * REST] = jnp.concatenate(rest, axis=1)
            fold_out[2 * n + k] = dense[...].astype(bf16)


def rest_kernel(
    x_ref,
    probs_ref,
    grad_low_ref,
    grad_sum_ref,
    result_ref,
    gains_ref,
    wqkv_t_ref,
    wproj_ref,
    own_out,
    lat_out,
    diag_out,
    lon_out,
    lat_buf,
    diag_buf,
    lon_buf,
):
    half = WLAT // 2
    cols = 2 * WLON
    edge = WLON // 2
    inner = cols - edge
    root = 1.0 / math.sqrt(HD)
    gain1 = gains_ref[0:1, :]
    wq_t = wqkv_t_ref[0:C, :]
    wk_t = wqkv_t_ref[C : 2 * C, :]
    wv_t = wqkv_t_ref[2 * C : 3 * C, :]
    head = lax.broadcasted_iota(jnp.int32, (HEADS, C), 0)
    head_mask = (lax.broadcasted_iota(jnp.int32, (HEADS, C), 1) >> 5) == head
    head_mask = head_mask.astype(f32).astype(bf16)
    perm_t = natural_order()
    for n in range(2):
        both = slice(n * 2 * POS, (n + 1) * 2 * POS)
        x = x_ref[both, :].astype(f32)
        scaled1, normed1, inverse1 = by_rows(lambda v: norm_parts(v, gain1), LN_ROWS, x)
        h1 = scaled1.astype(bf16)
        q_all = mm_nt(h1, wq_t).astype(bf16)
        grad_sum = grad_sum_ref[both, :].astype(f32)
        grad_h1 = []
        for c in range(2):
            w = 2 * n + c
            rows = slice(c * POS, (c + 1) * POS)
            q_wide = spread_heads(q_all[rows], head_mask)
            grad_branch = (grad_sum[rows] * gains_ref[2 + w : 3 + w, :]).astype(bf16)
            grad_att = mm_nt(grad_branch, wproj_ref[...]).astype(bf16)
            g_wide = spread_heads(grad_att, head_mask)
            grad_low = grad_low_ref[w]
            k_t = mm_nt(wk_t, h1[rows]).astype(bf16)
            grad_q = (head_blocks(mm(k_t, grad_low)) * root).astype(bf16).T
            grad_k = (mm(grad_low, q_wide) * root).astype(bf16)
            grad_v = mm(probs_ref[w], g_wide).astype(bf16)
            grad_h1.append(mm(grad_q, wq_t) + mm(grad_k, wk_t) + mm(grad_v, wv_t))
        grad_h1 = jnp.concatenate(grad_h1, axis=0).astype(bf16).astype(f32)
        (grad_field,) = by_rows(
            lambda v, g, normed, inverse: (
                (v + norm_back(g, gain1, normed, inverse)).astype(bf16),
            ),
            LN_ROWS,
            grad_sum,
            grad_h1,
            normed1,
            inverse1,
        )
        for t, value in enumerate((result_ref[both, :], grad_field)):
            natural = mm(perm_t, value)
            for dz in range(WZ):
                z = (2 * n + dz + 1) % 4
                for i in range(half):
                    k = z * half + i
                    row = (dz * WLAT + i) * cols
                    slab = natural[row : row + cols]
                    own_out[t, z, i] = slab[:inner].astype(bf16)
                    put(lon_buf, t, k * edge, slab[inner:])
                    row = (dz * WLAT + half + i) * cols
                    slab = natural[row : row + cols]
                    put(lat_buf, t, k * inner, slab[:inner])
                    put(diag_buf, t, k * edge, slab[inner:])
    lat_out[...] = lat_buf[...].astype(bf16)
    diag_out[...] = diag_buf[...].astype(bf16)
    lon_out[...] = lon_buf[...].astype(bf16)


def prepare_kernel(
    table_ref,
    region_ref,
    wqkv_ref,
    gain1_ref,
    gain2_ref,
    keep_ref,
    bias_out,
    label_row_out,
    label_col_out,
    wqkv_t_out,
    gains_out,
    flat,
    rows,
    wide,
    marks,
):
    wqkv_t_out[...] = wqkv_ref[...].astype(f32).T.astype(bf16)
    gains_out[0:1, :] = gain1_ref[...]
    gains_out[1:2, :] = gain2_ref[...]
    for n in range(2):
        for c in range(2):
            factor = keep_ref[n, 0, c].astype(f32) * (1.0 / keep_share)
            row = 2 + 2 * n + c
            gains_out[row : row + 1, :] = jnp.full((1, C), factor, f32)
    last = lax.axis_index("lat") == lax.axis_size("lat") - 1
    level = lax.broadcasted_iota(jnp.int32, (4, 2 * WLON), 0)
    for i in range(WLAT):
        wrapped = 2 * (level >= 4 - WZ // 2).astype(jnp.int32)
        if i >= WLAT // 2:
            wrapped = wrapped + last.astype(jnp.int32)
        marks[4 * i : 4 * (i + 1), :] = (4 * region_ref[i] + wrapped).astype(f32)
    place = lax.broadcasted_iota(jnp.int32, (POS, 4 * WLAT), 0)
    lane = lax.broadcasted_iota(jnp.int32, (POS, 4 * WLAT), 1)
    lon = quotient(place, PAIR)
    pair = place - PAIR * lon
    upper = (pair >= WLAT).astype(jnp.int32)
    source = 4 * (pair - WLAT * upper) + upper
    columns = []
    for n in range(2):
        chosen = mm((lane == source + WZ * n).astype(f32).astype(bf16), marks[...].astype(bf16))
        for c in range(2):
            own = jnp.where(lane == lon + WLON * c, chosen, 0.0)
            columns.append(jnp.sum(own, axis=1, keepdims=True))
    label_col_out[...] = jnp.concatenate(columns, axis=1)
    spread = jnp.concatenate([jnp.broadcast_to(v, (POS, LANES)) for v in columns], axis=1).T
    labels = jnp.concatenate([spread[k * LANES : k * LANES + 1] for k in range(4)], axis=0)
    label_row_out[...] = jnp.concatenate([labels] * HEADS, axis=1)
    part = PAIR // WZ * SPREAD
    for k in range(2 * HEADS):
        flat[k : k + 1, :] = table_ref[k]
    rows[...] = jnp.zeros_like(rows)
    for a in range(WZ):
        for c in range(WLAT):
            pieces = []
            for b in range(WZ):
                start = ((a * WZ + b) * WLAT + c) * part
                pieces.append(flat[:, start : start + part])
            row = (a * WLAT + c) * SLOTS
            rows[row : row + 2 * HEADS, :] = jnp.concatenate(pieces, axis=1)
    left = rows[...]
    perm = table_order()
    row_perm = row_order()
    total = None
    for _ in range(3):
        low = left.astype(bf16)
        left = left - low.astype(f32)
        term = mm(row_perm, mm(low, perm).astype(bf16))
        total = term if total is None else total + term
    total = total.reshape(2 * HEADS, SLOTS, TAB)
    for o in range(WLON):
        start = PAIR * (WLON - 1 - o)
        wide[:, PAIR * o : PAIR * (o + 1), :] = total[:, :PAIR, start : start + POS]
    for n in range(2):
        bias_out[n] = wide[n * HEADS : (n + 1) * HEADS].reshape(ROWS, POS).T * LOG2E


def unpack_kernel(mine_ref, other_ref, table_out, flat):
    odd = (lax.axis_index("lon") & 1) != 0
    part = PAIR // WZ * SPREAD
    for n in range(2):
        halves = []
        for k in range(2):
            mine = mine_ref[n].astype(f32)
            other = other_ref[n].astype(f32)
            dense = jnp.where(odd == (k == 1), mine, other)
            rest = dense[2 * QUARTER : 2 * QUARTER + HEADS]
            rest = [rest[:, g * REST : (g + 1) * REST] for g in range(WLAT)]
            rest = jnp.concatenate(rest, axis=0)
            parts = [dense[:QUARTER], dense[QUARTER : 2 * QUARTER], rest]
            halves.append(jnp.concatenate(parts, axis=1))
        for a in range(WZ):
            for c in range(WLAT):
                row = c * HEADS
                chunk = halves[a][row : row + HEADS]
                for b in range(WZ):
                    start = ((a * WZ + b) * WLAT + c) * part
                    flat[n * HEADS : (n + 1) * HEADS, start : start + part] = chunk[
                        :, b * part : (b + 1) * part
                    ]
    for k in range(2 * HEADS):
        table_out[k] = flat[k : k + 1, :]


def add_kernel(*refs):
    copies_out = refs[-1]
    parts = [ref[k].astype(f32) for ref in refs[:-1] for k in range(ref.shape[0])]
    while len(parts) > 1:
        parts = [parts[k] + parts[k + 1] for k in range(0, len(parts), 2)]
    total = parts[0].astype(bf16)
    for k in range(copies_out.shape[0]):
        copies_out[k] = total


def finish_kernel(own_ref, lat_ref, diag_ref, lon_ref, out_ref, grad_ref):
    half = WLAT // 2
    edge = WLON // 2
    inner = 2 * WLON - edge
    lat_part = lat_ref[...].astype(f32)
    diag_part = diag_ref[...].astype(f32)
    lon_part = lon_ref[...].astype(f32)
    for t, target in enumerate((out_ref, grad_ref)):
        for z in range(4):
            for i in range(half):
                k = z * half + i
                parts = (get(diag_part, t, k * edge, edge), get(lat_part, t, k * inner, inner))
                slab = [jnp.concatenate([parts[0][j], parts[1][j]], axis=0) for j in range(2)]
                target[z, i] = jnp.concatenate(slab, axis=1).astype(bf16)
                slab = jnp.concatenate(get(lon_part, t, k * edge, edge), axis=1)
                own = own_ref[t, z, i].astype(f32)
                target[z, half + i] = jnp.concatenate([slab, own], axis=0).astype(bf16)


def lon_sum(quarters, saved, rest_of_backward):
    lons = lax.axis_size("lon")
    me = lax.axis_index("lon")
    bits = [(me >> k) & 1 for k in range(2)]
    far = [[4 * k + j for k in range(lons // 4)] for j in range(4)]

    def swapped(block, distance):
        return lax.ppermute(block, "lon", [(i, i ^ distance) for i in range(lons)])

    def pick(value, bit, axis):
        return lax.dynamic_index_in_dim(value, bit, axis, keepdims=False)

    def added(parts, copies):
        vmem = pl.BlockSpec(memory_space=pltpu.VMEM)
        return pl.pallas_call(
            add_kernel,
            out_shape=jax.ShapeDtypeStruct((copies,) + parts[0].shape[1:], bf16),
            in_specs=[vmem] * len(parts),
            out_specs=vmem,
            compiler_params=pltpu.CompilerParams(vmem_limit_bytes=VMEM_BYTES),
            name="add",
        )(*parts)

    value = quarters.reshape((2, 2) + quarters.shape[1:])
    other = swapped(pick(value, 1 - bits[0], 1), 1)
    value = pick(value, bits[0], 1).astype(f32) + other.astype(f32)
    value, saved = lax.optimization_barrier((value.astype(bf16), saved))
    other = swapped(pick(value, 1 - bits[1], 0), 2)
    own, *strips = rest_of_backward(saved)
    parts = added((pick(value, bits[1], 0)[None], other[None]), lons // 4)
    parts, strips = lax.optimization_barrier((parts, strips))
    steps = ((1, 0), (1, 1), (0, 1))
    strips = [shifted(strip, *step) for strip, step in zip(strips, steps)]
    parts = lax.all_to_all(parts, "lon", 0, 0, axis_index_groups=far)
    value, strips = lax.optimization_barrier((added((parts,), 1)[0], strips))
    other = swapped(value, 2)
    lower = jnp.where(bits[1] == 0, value, other)
    upper = jnp.where(bits[1] == 0, other, value)
    value = jnp.stack([lower, upper])
    return (value, swapped(value, 1)), own, strips


def body(
    field_in,
    cotangent,
    ln1_gain,
    w_qkv,
    w_proj,
    ln2_gain,
    w_up,
    w_down,
    bias_table,
    region_ids,
    keep_flags,
):
    levels, lat_rows, lon_cols, channels = field_in.shape
    half = WLAT // 2
    edge = WLON // 2
    inner = lon_cols - edge
    vmem = pl.BlockSpec(memory_space=pltpu.VMEM)
    smem = pl.BlockSpec(memory_space=pltpu.SMEM)
    sizes = [3 * levels * half * size for size in (inner, edge, edge)]
    packed = tuple(jax.ShapeDtypeStruct((size, LANES), bf16) for size in sizes)
    buffers = [pltpu.VMEM((size, LANES), f32) for size in sizes]
    params = pltpu.CompilerParams(vmem_limit_bytes=VMEM_BYTES)
    lat_part = pl.pallas_call(
        pack_lat_kernel,
        out_shape=packed[0],
        in_specs=[pl.BlockSpec(memory_space=pltpu.HBM)] * 2,
        out_specs=vmem,
        scratch_shapes=buffers[:1]
        + [pltpu.VMEM((2, levels, half, lon_cols, C), bf16), pltpu.SemaphoreType.DMA((2,))],
        compiler_params=params,
        name="pack_lat",
    )(field_in, cotangent)
    diag_part, lon_part = pl.pallas_call(
        pack_edge_kernel,
        out_shape=packed[1:],
        in_specs=[vmem] * 2 + [pl.BlockSpec(memory_space=pl.ANY)],
        out_specs=(vmem,) * 2,
        scratch_shapes=buffers[1:],
        compiler_params=params,
        name="pack_edge",
    )(field_in, cotangent, lat_part)
    lat_part = shifted(lat_part, -1, 0)
    diag_part = shifted(diag_part, -1, -1)
    lon_part = shifted(lon_part, 0, -1)

    bias_wide, label_row, label_col, weights_t, gains = pl.pallas_call(
        prepare_kernel,
        out_shape=(
            jax.ShapeDtypeStruct((2, POS, ROWS), f32),
            jax.ShapeDtypeStruct((4, ROWS), f32),
            jax.ShapeDtypeStruct((POS, 4), f32),
            jax.ShapeDtypeStruct((3 * C, C), bf16),
            jax.ShapeDtypeStruct((6, C), f32),
        ),
        in_specs=[vmem] * 5 + [smem],
        out_specs=(vmem,) * 5,
        scratch_shapes=[
            pltpu.VMEM((2 * HEADS, PAIR * TAB), f32),
            pltpu.VMEM((PAIR * SLOTS, TAB), f32),
            pltpu.VMEM((2 * HEADS, POS, POS), f32),
            pltpu.VMEM((4 * WLAT, 2 * WLON), f32),
        ],
        compiler_params=params,
        name="prepare",
    )(
        bias_table.reshape(2 * HEADS, 1, PAIR * TAB),
        region_ids.transpose(1, 0, 2),
        w_qkv,
        ln1_gain.reshape(1, C),
        ln2_gain.reshape(1, C),
        keep_flags,
    )
    positions = levels * lat_rows * lon_cols
    fold, *saved = pl.pallas_call(
        scores_kernel,
        out_shape=(
            jax.ShapeDtypeStruct((4, DENSE, LANES), bf16),
            jax.ShapeDtypeStruct((positions, C), bf16),
            jax.ShapeDtypeStruct((4, POS, ROWS), bf16),
            jax.ShapeDtypeStruct((4, POS, ROWS), bf16),
            jax.ShapeDtypeStruct((positions, C), bf16),
            jax.ShapeDtypeStruct((positions, C), bf16),
        ),
        in_specs=[vmem] * 13,
        out_specs=(vmem,) * 6,
        scratch_shapes=[
            pltpu.VMEM((2, positions, C), f32),
            pltpu.VMEM((HEADS, POS, POS), f32),
            pltpu.VMEM((DENSE, LANES), f32),
        ],
        compiler_params=params,
        name="scores",
    )(
        field_in,
        cotangent,
        lon_part,
        lat_part,
        diag_part,
        gains,
        weights_t,
        w_proj,
        w_up,
        w_down.T,
        bias_wide,
        label_row,
        label_col,
    )

    def rest_of_backward(saved):
        return pl.pallas_call(
            rest_kernel,
            out_shape=(jax.ShapeDtypeStruct((2, levels, half, inner, C), bf16),) + packed,
            in_specs=[vmem] * 8,
            out_specs=(vmem,) * 4,
            scratch_shapes=buffers,
            compiler_params=params,
            cost_estimate=pl.CostEstimate(
                flops=1_000_000_000, bytes_accessed=8_000_000, transcendentals=0
            ),
            name="rest",
        )(*saved, gains, weights_t, w_proj)

    halves, own, (lat_back, diag_back, lon_back) = lon_sum(fold, saved, rest_of_backward)
    grads = pl.pallas_call(
        unpack_kernel,
        out_shape=jax.ShapeDtypeStruct((2 * HEADS, 1, PAIR * TAB), f32),
        in_specs=[vmem] * 2,
        out_specs=vmem,
        scratch_shapes=[pltpu.VMEM((2 * HEADS, PAIR * TAB), f32)],
        compiler_params=params,
        name="unpack",
    )(*halves)
    grads = grads.reshape(2, 1, HEADS, PAIR * TAB)
    result, grad_field = pl.pallas_call(
        finish_kernel,
        out_shape=(jax.ShapeDtypeStruct(field_in.shape, bf16),) * 2,
        in_specs=[vmem] * 4,
        out_specs=(vmem,) * 2,
        compiler_params=params,
        name="finish",
    )(own, lat_back, diag_back, lon_back)
    return (result, grad_field, grads)


def solution(mesh):
    placed = (
        P(None, "lat", "lon", None),
        P(None, "lat", "lon", None),
        P(),
        P(),
        P(),
        P(),
        P(),
        P(),
        P(None, "lat", None, None),
        P(None, "lat", "lon"),
        P(None, "lat", "lon"),
    )
    return jax.shard_map(
        body,
        mesh=mesh,
        in_specs=placed,
        out_specs=(
            P(None, "lat", "lon", None),
            P(None, "lat", "lon", None),
            P(None, "lat", None, None),
        ),
        check_vma=False,
    )
```

```python
import math

import jax
import jax.numpy as jnp
from jax import lax
from jax.experimental import pallas as pl
from jax.experimental.pallas import tpu as pltpu
from jax.sharding import PartitionSpec as P

C = 192
HEADS = 6
HD = 32
FF = 768
WZ = 2
WLAT = 6
WLON = 12
SPREAD = 2 * WLON - 1
POS = WZ * WLAT * WLON
PAIR = WZ * WLAT
TAB = PAIR * SPREAD
ROWS = HEADS * POS
SLOTS = 16
QUARTER = PAIR * HEADS // 2
REST = 20
LN_ROWS = 96
GELU_ROWS = 48
LANE_CUTS = [(k, min(k + 256, ROWS)) for k in range(0, ROWS, 256)]
DENSE = 80
LANES = 128

epsilon = 1e-05
keep_share = 0.8
LOG2E = math.log2(math.e)
gelu_coef = 0.044715
VMEM_BYTES = 16 * 1024 * 1024
bf16 = jnp.bfloat16
f32 = jnp.float32


def shifted(block, lat_step, lon_step):
    lats, lons = lax.axis_size("lat"), lax.axis_size("lon")
    route = []
    for a in range(lats):
        for b in range(lons):
            target = ((a + lat_step) % lats) * lons + (b + lon_step) % lons
            route.append((a * lons + b, target))
    return lax.ppermute(block, ("lat", "lon"), route)


def mm(a, b):
    return lax.dot_general(a, b, (((1,), (0,)), ((), ())), preferred_element_type=f32)


def mm_nt(a, b):
    return lax.dot_general(a, b, (((1,), (1,)), ((), ())), preferred_element_type=f32)


def norm_parts(values, gain):
    row_mean = jnp.mean(values, axis=-1, keepdims=True)
    centred = values - row_mean
    variance = jnp.mean(centred * centred, axis=-1, keepdims=True)
    inverse = lax.rsqrt(variance + epsilon)
    normed = centred * inverse
    return normed * gain, normed, inverse


def norm_back(grad_in, gain, normed, inverse):
    scaled = grad_in * gain
    first_mean = jnp.mean(scaled, axis=-1, keepdims=True)
    second_mean = jnp.mean(scaled * normed, axis=-1, keepdims=True)
    return (scaled - first_mean - normed * second_mean) * inverse


def gelu_parts(values):
    factor = math.sqrt(2.0 / math.pi)
    square = values * values
    tangent = jnp.tanh(values * (factor + (gelu_coef * factor) * square))
    half = 0.5 + 0.5 * tangent
    result = values * half
    derivative = half + result * (1.0 - tangent) * (factor + (3.0 * gelu_coef * factor) * square)
    return result.astype(bf16), derivative


def by_rows(function, size, *arrays):
    rows = arrays[0].shape[0]
    parts = [function(*(v[r : r + size] for v in arrays)) for r in range(0, rows, size)]
    return tuple(jnp.concatenate(part, axis=0) for part in zip(*parts))


def masked_softmax(scores, bias, allowed):
    scores = scores * (LOG2E / math.sqrt(HD)) + bias
    scores = jnp.where(allowed, scores, -1e30)
    weights = jnp.exp2(scores - jnp.max(scores, axis=0, keepdims=True))
    return weights * (1.0 / jnp.sum(weights, axis=0, keepdims=True))


def head_blocks(wide):
    return jnp.concatenate(
        [wide[h * HD : (h + 1) * HD, h * POS : (h + 1) * POS] for h in range(HEADS)], axis=0
    )


def spread_heads(rows, head_mask):
    return jnp.concatenate([rows * head_mask[h : h + 1, :] for h in range(HEADS)], axis=0)


def quotient(values, divisor):
    return (values * (2**20 // divisor + 1)) >> 20


def one_hot(rows, columns, target):
    row = lax.broadcasted_iota(jnp.int32, (rows, 1), 0)
    column = lax.broadcasted_iota(jnp.int32, (rows, columns), 1)
    return (column == target(row)).astype(f32).astype(bf16)


def window_order():
    def target(row):
        c = (row >= POS).astype(jnp.int32)
        row = row - POS * c
        j = quotient(row, PAIR)
        return (row - PAIR * j) * (2 * WLON) + c * WLON + j

    return one_hot(2 * POS, 2 * POS, target)


def natural_order():
    def target(row):
        pair = quotient(row, 2 * WLON)
        lon = row - 2 * WLON * pair
        c = (lon >= WLON).astype(jnp.int32)
        return c * POS + (lon - WLON * c) * PAIR + pair

    return one_hot(2 * POS, 2 * POS, target)


def table_order():
    def target(row):
        pair = quotient(row, SPREAD)
        return (SPREAD - 1 - (row - SPREAD * pair)) * PAIR + pair

    return one_hot(TAB, TAB, target)


def chunk_order():
    def target(row):
        pair = quotient(row, HEADS)
        return (row - HEADS * pair) * SLOTS + pair

    return one_hot(PAIR * HEADS, HEADS * SLOTS, target)


def row_order():
    def target(row):
        head = quotient(row, SLOTS)
        return (row - SLOTS * head) * SLOTS + head

    return one_hot(2 * HEADS * SLOTS, PAIR * SLOTS, target)


def put(packed, t, row, slab):
    third = packed.shape[0] // 3
    size = slab.shape[0]
    rest = C - LANES
    packed[t * third + row : t * third + row + size, :] = slab[:, :LANES]
    packed[2 * third + row : 2 * third + row + size, t * rest : (t + 1) * rest] = slab[:, LANES:]


def get(packed, t, row, size):
    third = packed.shape[0] // 3
    rest = C - LANES
    return (
        packed[t * third + row : t * third + row + size, :],
        packed[2 * third + row : 2 * third + row + size, t * rest : (t + 1) * rest],
    )


def pack_lat_kernel(field_ref, cot_ref, lat_out, lat_buf, rows, arrived):
    half = WLAT // 2
    edge = WLON // 2
    inner = 2 * WLON - edge
    sources = (field_ref, cot_ref)
    copies = [
        pltpu.make_async_copy(sources[t].at[:, pl.ds(0, half)], rows.at[t], arrived.at[t])
        for t in range(2)
    ]
    for copy in copies:
        copy.start()
    for t in range(2):
        copies[t].wait()
        for z in range(4):
            for i in range(half):
                put(lat_buf, t, (z * half + i) * inner, rows[t, z, i].astype(f32)[edge:])
    lat_out[...] = lat_buf[...].astype(bf16)


def pack_edge_kernel(field_ref, cot_ref, after_ref, diag_out, lon_out, diag_buf, lon_buf):
    half = WLAT // 2
    edge = WLON // 2
    for t, source in enumerate((field_ref, cot_ref)):
        for z in range(4):
            for i in range(half):
                row = (z * half + i) * edge
                put(diag_buf, t, row, source[z, i].astype(f32)[:edge])
                put(lon_buf, t, row, source[z, half + i].astype(f32)[:edge])
    diag_out[...] = diag_buf[...].astype(bf16)
    lon_out[...] = lon_buf[...].astype(bf16)


def scores_kernel(
    field_ref,
    cot_ref,
    lon_ref,
    lat_ref,
    diag_ref,
    gains_ref,
    wqkv_t_ref,
    wproj_ref,
    wup_ref,
    wdown_t_ref,
    bias_ref,
    label_row_ref,
    label_col_ref,
    keep_out,
    send_out,
    x_out,
    probs_out,
    grad_low_out,
    grad_sum_out,
    result_out,
    frame,
    wide,
    dense,
):
    half = WLAT // 2
    cols = 2 * WLON
    edge = WLON // 2
    inner = cols - edge
    root = 1.0 / math.sqrt(HD)
    lon_part = lon_ref[...].astype(f32)
    lat_part = lat_ref[...].astype(f32)
    diag_part = diag_ref[...].astype(f32)
    for t, own in enumerate((field_ref, cot_ref)):
        for level in range(4):
            z = (level + 1) % 4
            for i in range(half):
                k = z * half + i
                row = (level * WLAT + i) * cols
                frame[t, row : row + inner, :] = own[z, half + i].astype(f32)[edge:, :]
                main, rest = get(lon_part, t, k * edge, edge)
                frame[t, row + inner : row + cols, :LANES] = main
                frame[t, row + inner : row + cols, LANES:] = rest
                row = (level * WLAT + half + i) * cols
                main, rest = get(lat_part, t, k * inner, inner)
                frame[t, row : row + inner, :LANES] = main
                frame[t, row : row + inner, LANES:] = rest
                main, rest = get(diag_part, t, k * edge, edge)
                frame[t, row + inner : row + cols, :LANES] = main
                frame[t, row + inner : row + cols, LANES:] = rest
    gain1 = gains_ref[0:1, :]
    gain2 = gains_ref[1:2, :]
    wq_t = wqkv_t_ref[0:C, :]
    wk_t = wqkv_t_ref[C : 2 * C, :]
    wv_t = wqkv_t_ref[2 * C : 3 * C, :]
    head = lax.broadcasted_iota(jnp.int32, (HEADS, C), 0)
    head_mask = (lax.broadcasted_iota(jnp.int32, (HEADS, C), 1) >> 5) == head
    head_mask = head_mask.astype(f32).astype(bf16)
    perm = window_order()
    table_perm = table_order()
    chunk_perm = chunk_order()
    dense[...] = jnp.zeros_like(dense)
    odd = jnp.broadcast_to(gains_ref[6:7, :LANES], (DENSE, LANES)) > 0.5
    for n in range(2):
        both = slice(n * 2 * POS, (n + 1) * 2 * POS)
        x = mm(perm, frame[0, both, :].astype(bf16))
        cot = mm(perm, frame[1, both, :].astype(bf16))
        x_out[both, :] = x.astype(bf16)
        (scaled1,) = by_rows(lambda v: norm_parts(v, gain1)[:1], LN_ROWS, x)
        h1 = scaled1.astype(bf16)
        q_all = mm_nt(h1, wq_t).astype(bf16)
        k_all = mm_nt(h1, wk_t).astype(bf16)
        v_all = mm_nt(h1, wv_t).astype(bf16)
        saved = []
        branches = []
        for c in range(2):
            w = 2 * n + c
            rows = slice(c * POS, (c + 1) * POS)
            v_t = mm_nt(wv_t, h1[rows]).astype(bf16)
            q_wide = spread_heads(q_all[rows], head_mask)
            label_col = label_col_ref[:, w : w + 1]
            probs = []
            for low, high in LANE_CUTS:
                scores = mm_nt(k_all[rows], q_wide[low:high])
                allowed = label_col == label_row_ref[w : w + 1, low:high]
                probs.append(masked_softmax(scores, bias_ref[n, :, low:high], allowed))
            probs_low = jnp.concatenate([part.astype(bf16) for part in probs], axis=1)
            probs_out[w] = probs_low
            attended = head_blocks(mm(v_t, probs_low)).astype(bf16).T
            factor = gains_ref[2 + w : 3 + w, :]
            branches.append((mm(attended, wproj_ref[...]) * factor).astype(bf16).astype(f32))
            saved.append(probs)
        y_sum = x + jnp.concatenate(branches, axis=0)
        scaled2, normed2, inverse2 = by_rows(lambda v: norm_parts(v, gain2), LN_ROWS, y_sum)
        act, slope = by_rows(gelu_parts, GELU_ROWS, mm(scaled2.astype(bf16), wup_ref[...]))
        result_out[both, :] = (y_sum + mm_nt(act, wdown_t_ref[...])).astype(bf16)
        grad_up = (mm(cot.astype(bf16), wdown_t_ref[...]) * slope).astype(bf16)
        grad_hidden = mm_nt(grad_up, wup_ref[...])
        (grad_sum,) = by_rows(
            lambda v, g, normed, inverse: (v + norm_back(g, gain2, normed, inverse),),
            LN_ROWS,
            cot,
            grad_hidden,
            normed2,
            inverse2,
        )
        grad_sum_low = grad_sum.astype(bf16)
        grad_sum_out[both, :] = grad_sum_low
        grad_low_in = grad_sum_low.astype(f32)
        folded = [None] * len(LANE_CUTS)
        for c in range(2):
            rows = slice(c * POS, (c + 1) * POS)
            probs = saved[c]
            factor = gains_ref[2 + 2 * n + c : 3 + 2 * n + c, :]
            grad_branch = (grad_low_in[rows] * factor).astype(bf16)
            grad_att = mm_nt(grad_branch, wproj_ref[...]).astype(bf16)
            g_wide = spread_heads(grad_att, head_mask)
            grad_low = []
            for k, (low, high) in enumerate(LANE_CUTS):
                grad_probs = mm_nt(v_all[rows], g_wide[low:high])
                inner_sum = jnp.sum(probs[k] * grad_probs, axis=0, keepdims=True)
                grad_scores = probs[k] * (grad_probs - inner_sum)
                folded[k] = grad_scores if c == 0 else folded[k] + grad_scores
                grad_low.append(grad_scores.astype(bf16))
            grad_low_out[2 * n + c] = jnp.concatenate(grad_low, axis=1)
        folded = jnp.concatenate([part.astype(bf16) for part in folded], axis=1)
        wide[...] = folded.T.astype(f32).reshape(HEADS, POS, POS)
        total = None
        for o in range(WLON):
            left = PAIR * (WLON - 1 - o)
            right = TAB - POS - left
            parts = [wide[:, PAIR * o : PAIR * (o + 1), :]]
            if left:
                parts = [jnp.zeros((HEADS, PAIR, left), f32)] + parts
            if right:
                parts = parts + [jnp.zeros((HEADS, PAIR, right), f32)]
            piece = jnp.concatenate(parts, axis=2)
            total = piece if total is None else total + piece
        total = jnp.concatenate([total, jnp.zeros((HEADS, SLOTS - PAIR, TAB), f32)], axis=1)
        total = total.reshape(HEADS * SLOTS, TAB).astype(bf16)
        total = mm_nt(total, table_perm).astype(bf16)
        total = mm(chunk_perm, total)
        quarters = []
        for k in range(2):
            part = total[k * QUARTER : (k + 1) * QUARTER]
            dense[:QUARTER, :] = part[:, :LANES]
            dense[QUARTER : 2 * QUARTER, :] = part[:, LANES : 2 * LANES]
            rest = [part[HEADS * g : HEADS * (g + 1), 2 * LANES :] for g in range(WLAT)]
            dense[2 * QUARTER : 2 * QUARTER + HEADS, : WLAT * REST] = jnp.concatenate(rest, axis=1)
            quarters.append(dense[...])
        keep_out[n] = jnp.where(odd, quarters[1], quarters[0]).astype(bf16)
        send_out[n] = jnp.where(odd, quarters[0], quarters[1]).astype(bf16)


def rest_kernel(
    x_ref,
    probs_ref,
    grad_low_ref,
    grad_sum_ref,
    result_ref,
    gains_ref,
    wqkv_t_ref,
    wproj_ref,
    own_out,
    lat_out,
    diag_out,
    lon_out,
    lat_buf,
    diag_buf,
    lon_buf,
):
    half = WLAT // 2
    cols = 2 * WLON
    edge = WLON // 2
    inner = cols - edge
    root = 1.0 / math.sqrt(HD)
    gain1 = gains_ref[0:1, :]
    wq_t = wqkv_t_ref[0:C, :]
    wk_t = wqkv_t_ref[C : 2 * C, :]
    wv_t = wqkv_t_ref[2 * C : 3 * C, :]
    head = lax.broadcasted_iota(jnp.int32, (HEADS, C), 0)
    head_mask = (lax.broadcasted_iota(jnp.int32, (HEADS, C), 1) >> 5) == head
    head_mask = head_mask.astype(f32).astype(bf16)
    perm_t = natural_order()
    for n in range(2):
        both = slice(n * 2 * POS, (n + 1) * 2 * POS)
        x = x_ref[both, :].astype(f32)
        scaled1, normed1, inverse1 = by_rows(lambda v: norm_parts(v, gain1), LN_ROWS, x)
        h1 = scaled1.astype(bf16)
        q_all = mm_nt(h1, wq_t).astype(bf16)
        grad_sum = grad_sum_ref[both, :].astype(f32)
        grad_h1 = []
        for c in range(2):
            w = 2 * n + c
            rows = slice(c * POS, (c + 1) * POS)
            q_wide = spread_heads(q_all[rows], head_mask)
            grad_branch = (grad_sum[rows] * gains_ref[2 + w : 3 + w, :]).astype(bf16)
            grad_att = mm_nt(grad_branch, wproj_ref[...]).astype(bf16)
            g_wide = spread_heads(grad_att, head_mask)
            grad_low = grad_low_ref[w]
            k_t = mm_nt(wk_t, h1[rows]).astype(bf16)
            grad_q = (head_blocks(mm(k_t, grad_low)) * root).astype(bf16).T
            grad_k = (mm(grad_low, q_wide) * root).astype(bf16)
            grad_v = mm(probs_ref[w], g_wide).astype(bf16)
            grad_h1.append(mm(grad_q, wq_t) + mm(grad_k, wk_t) + mm(grad_v, wv_t))
        grad_h1 = jnp.concatenate(grad_h1, axis=0).astype(bf16).astype(f32)
        (grad_field,) = by_rows(
            lambda v, g, normed, inverse: (
                (v + norm_back(g, gain1, normed, inverse)).astype(bf16),
            ),
            LN_ROWS,
            grad_sum,
            grad_h1,
            normed1,
            inverse1,
        )
        for t, value in enumerate((result_ref[both, :], grad_field)):
            natural = mm(perm_t, value)
            for dz in range(WZ):
                z = (2 * n + dz + 1) % 4
                for i in range(half):
                    k = z * half + i
                    row = (dz * WLAT + i) * cols
                    slab = natural[row : row + cols]
                    own_out[t, z, i] = slab[:inner].astype(bf16)
                    put(lon_buf, t, k * edge, slab[inner:])
                    row = (dz * WLAT + half + i) * cols
                    slab = natural[row : row + cols]
                    put(lat_buf, t, k * inner, slab[:inner])
                    put(diag_buf, t, k * edge, slab[inner:])
    lat_out[...] = lat_buf[...].astype(bf16)
    diag_out[...] = diag_buf[...].astype(bf16)
    lon_out[...] = lon_buf[...].astype(bf16)


def prepare_kernel(
    table_ref,
    region_ref,
    wqkv_ref,
    gain1_ref,
    gain2_ref,
    keep_ref,
    bias_out,
    label_row_out,
    label_col_out,
    wqkv_t_out,
    gains_out,
    flat,
    rows,
    wide,
    marks,
):
    wqkv_t_out[...] = wqkv_ref[...].astype(f32).T.astype(bf16)
    gains_out[0:1, :] = gain1_ref[...]
    gains_out[1:2, :] = gain2_ref[...]
    for n in range(2):
        for c in range(2):
            factor = keep_ref[n, 0, c].astype(f32) * (1.0 / keep_share)
            row = 2 + 2 * n + c
            gains_out[row : row + 1, :] = jnp.full((1, C), factor, f32)
    lon_index = lax.axis_index("lon")
    for k in range(2):
        bit = ((lon_index >> k) & 1).astype(f32)
        gains_out[6 + k : 7 + k, :] = jnp.full((1, C), bit, f32)
    last = lax.axis_index("lat") == lax.axis_size("lat") - 1
    level = lax.broadcasted_iota(jnp.int32, (4, 2 * WLON), 0)
    for i in range(WLAT):
        wrapped = 2 * (level >= 4 - WZ // 2).astype(jnp.int32)
        if i >= WLAT // 2:
            wrapped = wrapped + last.astype(jnp.int32)
        marks[4 * i : 4 * (i + 1), :] = (4 * region_ref[i] + wrapped).astype(f32)
    place = lax.broadcasted_iota(jnp.int32, (POS, 4 * WLAT), 0)
    lane = lax.broadcasted_iota(jnp.int32, (POS, 4 * WLAT), 1)
    lon = quotient(place, PAIR)
    pair = place - PAIR * lon
    upper = (pair >= WLAT).astype(jnp.int32)
    source = 4 * (pair - WLAT * upper) + upper
    columns = []
    for n in range(2):
        chosen = mm((lane == source + WZ * n).astype(f32).astype(bf16), marks[...].astype(bf16))
        for c in range(2):
            own = jnp.where(lane == lon + WLON * c, chosen, 0.0)
            columns.append(jnp.sum(own, axis=1, keepdims=True))
    label_col_out[...] = jnp.concatenate(columns, axis=1)
    spread = jnp.concatenate([jnp.broadcast_to(v, (POS, LANES)) for v in columns], axis=1).T
    labels = jnp.concatenate([spread[k * LANES : k * LANES + 1] for k in range(4)], axis=0)
    label_row_out[...] = jnp.concatenate([labels] * HEADS, axis=1)
    part = PAIR // WZ * SPREAD
    for k in range(2 * HEADS):
        flat[k : k + 1, :] = table_ref[k]
    rows[...] = jnp.zeros_like(rows)
    for a in range(WZ):
        for c in range(WLAT):
            pieces = []
            for b in range(WZ):
                start = ((a * WZ + b) * WLAT + c) * part
                pieces.append(flat[:, start : start + part])
            row = (a * WLAT + c) * SLOTS
            rows[row : row + 2 * HEADS, :] = jnp.concatenate(pieces, axis=1)
    left = rows[...]
    perm = table_order()
    row_perm = row_order()
    total = None
    for _ in range(3):
        low = left.astype(bf16)
        left = left - low.astype(f32)
        term = mm(row_perm, mm(low, perm).astype(bf16))
        total = term if total is None else total + term
    total = total.reshape(2 * HEADS, SLOTS, TAB)
    for o in range(WLON):
        start = PAIR * (WLON - 1 - o)
        wide[:, PAIR * o : PAIR * (o + 1), :] = total[:, :PAIR, start : start + POS]
    for n in range(2):
        bias_out[n] = wide[n * HEADS : (n + 1) * HEADS].reshape(ROWS, POS).T * LOG2E


def unpack_kernel(mine_ref, other_ref, table_out, flat):
    odd = (lax.axis_index("lon") & 1) != 0
    part = PAIR // WZ * SPREAD
    for n in range(2):
        halves = []
        for k in range(2):
            mine = mine_ref[n].astype(f32)
            other = other_ref[n].astype(f32)
            dense = jnp.where(odd == (k == 1), mine, other)
            rest = dense[2 * QUARTER : 2 * QUARTER + HEADS]
            rest = [rest[:, g * REST : (g + 1) * REST] for g in range(WLAT)]
            rest = jnp.concatenate(rest, axis=0)
            parts = [dense[:QUARTER], dense[QUARTER : 2 * QUARTER], rest]
            halves.append(jnp.concatenate(parts, axis=1))
        for a in range(WZ):
            for c in range(WLAT):
                row = c * HEADS
                chunk = halves[a][row : row + HEADS]
                for b in range(WZ):
                    start = ((a * WZ + b) * WLAT + c) * part
                    flat[n * HEADS : (n + 1) * HEADS, start : start + part] = chunk[
                        :, b * part : (b + 1) * part
                    ]
    for k in range(2 * HEADS):
        table_out[k] = flat[k : k + 1, :]


def halve_kernel(mine_ref, other_ref, gains_ref, keep_out, send_out):
    upper = jnp.broadcast_to(gains_ref[7:8, :LANES], (DENSE, LANES)) > 0.5
    sums = [mine_ref[k].astype(f32) + other_ref[k].astype(f32) for k in range(2)]
    keep_out[0] = jnp.where(upper, sums[1], sums[0]).astype(bf16)
    send_out[0] = jnp.where(upper, sums[0], sums[1]).astype(bf16)


def add_kernel(*refs):
    copies_out = refs[-1]
    parts = [ref[k].astype(f32) for ref in refs[:-1] for k in range(ref.shape[0])]
    while len(parts) > 1:
        parts = [parts[k] + parts[k + 1] for k in range(0, len(parts), 2)]
    total = parts[0].astype(bf16)
    for k in range(copies_out.shape[0]):
        copies_out[k] = total


def finish_kernel(own_ref, lat_ref, diag_ref, lon_ref, out_ref, grad_ref):
    half = WLAT // 2
    edge = WLON // 2
    inner = 2 * WLON - edge
    lat_part = lat_ref[...].astype(f32)
    diag_part = diag_ref[...].astype(f32)
    lon_part = lon_ref[...].astype(f32)
    for t, target in enumerate((out_ref, grad_ref)):
        for z in range(4):
            for i in range(half):
                k = z * half + i
                parts = (get(diag_part, t, k * edge, edge), get(lat_part, t, k * inner, inner))
                slab = [jnp.concatenate([parts[0][j], parts[1][j]], axis=0) for j in range(2)]
                target[z, i] = jnp.concatenate(slab, axis=1).astype(bf16)
                slab = jnp.concatenate(get(lon_part, t, k * edge, edge), axis=1)
                own = own_ref[t, z, i].astype(f32)
                target[z, half + i] = jnp.concatenate([slab, own], axis=0).astype(bf16)


def lon_sum(keep, send, gains, saved, rest_of_backward):
    lons = lax.axis_size("lon")
    far = [[4 * k + j for k in range(lons // 4)] for j in range(4)]
    vmem = pl.BlockSpec(memory_space=pltpu.VMEM)

    def swapped(block, distance):
        return lax.ppermute(block, "lon", [(i, i ^ distance) for i in range(lons)])

    def added(parts, copies):
        return pl.pallas_call(
            add_kernel,
            out_shape=jax.ShapeDtypeStruct((copies,) + parts[0].shape[1:], bf16),
            in_specs=[vmem] * len(parts),
            out_specs=vmem,
            compiler_params=pltpu.CompilerParams(vmem_limit_bytes=VMEM_BYTES),
            name="add",
        )(*parts)

    other, saved = lax.optimization_barrier((swapped(send, 1), saved))
    quarter = jax.ShapeDtypeStruct((1,) + keep.shape[1:], bf16)
    keep, send = pl.pallas_call(
        halve_kernel,
        out_shape=(quarter,) * 2,
        in_specs=[vmem] * 3,
        out_specs=(vmem,) * 2,
        compiler_params=pltpu.CompilerParams(vmem_limit_bytes=VMEM_BYTES),
        name="halve",
    )(keep, other, gains)
    other = swapped(send, 2)
    own, *strips = rest_of_backward(saved)
    parts = added((keep, other), lons // 4)
    parts, strips = lax.optimization_barrier((parts, strips))
    steps = ((1, 0), (1, 1), (0, 1))
    strips = [shifted(strip, *step) for strip, step in zip(strips, steps)]
    parts = lax.all_to_all(parts, "lon", 0, 0, axis_index_groups=far)
    value, strips = lax.optimization_barrier((added((parts,), 1)[0], strips))
    other = swapped(value, 2)
    second = gains[7:8, :LANES] > 0.5
    lower = jnp.where(second, other, value)
    upper = jnp.where(second, value, other)
    value = jnp.stack([lower, upper])
    return (value, swapped(value, 1)), own, strips


def body(
    field_in,
    cotangent,
    ln1_gain,
    w_qkv,
    w_proj,
    ln2_gain,
    w_up,
    w_down,
    bias_table,
    region_ids,
    keep_flags,
):
    levels, lat_rows, lon_cols, channels = field_in.shape
    half = WLAT // 2
    edge = WLON // 2
    inner = lon_cols - edge
    vmem = pl.BlockSpec(memory_space=pltpu.VMEM)
    smem = pl.BlockSpec(memory_space=pltpu.SMEM)
    sizes = [3 * levels * half * size for size in (inner, edge, edge)]
    packed = tuple(jax.ShapeDtypeStruct((size, LANES), bf16) for size in sizes)
    buffers = [pltpu.VMEM((size, LANES), f32) for size in sizes]
    params = pltpu.CompilerParams(vmem_limit_bytes=VMEM_BYTES)
    lat_part = pl.pallas_call(
        pack_lat_kernel,
        out_shape=packed[0],
        in_specs=[pl.BlockSpec(memory_space=pltpu.HBM)] * 2,
        out_specs=vmem,
        scratch_shapes=buffers[:1]
        + [pltpu.VMEM((2, levels, half, lon_cols, C), bf16), pltpu.SemaphoreType.DMA((2,))],
        compiler_params=params,
        name="pack_lat",
    )(field_in, cotangent)
    diag_part, lon_part = pl.pallas_call(
        pack_edge_kernel,
        out_shape=packed[1:],
        in_specs=[vmem] * 2 + [pl.BlockSpec(memory_space=pl.ANY)],
        out_specs=(vmem,) * 2,
        scratch_shapes=buffers[1:],
        compiler_params=params,
        name="pack_edge",
    )(field_in, cotangent, lat_part)
    lat_part = shifted(lat_part, -1, 0)
    diag_part = shifted(diag_part, -1, -1)
    lon_part = shifted(lon_part, 0, -1)

    bias_wide, label_row, label_col, weights_t, gains = pl.pallas_call(
        prepare_kernel,
        out_shape=(
            jax.ShapeDtypeStruct((2, POS, ROWS), f32),
            jax.ShapeDtypeStruct((4, ROWS), f32),
            jax.ShapeDtypeStruct((POS, 4), f32),
            jax.ShapeDtypeStruct((3 * C, C), bf16),
            jax.ShapeDtypeStruct((8, C), f32),
        ),
        in_specs=[vmem] * 5 + [smem],
        out_specs=(vmem,) * 5,
        scratch_shapes=[
            pltpu.VMEM((2 * HEADS, PAIR * TAB), f32),
            pltpu.VMEM((PAIR * SLOTS, TAB), f32),
            pltpu.VMEM((2 * HEADS, POS, POS), f32),
            pltpu.VMEM((4 * WLAT, 2 * WLON), f32),
        ],
        compiler_params=params,
        name="prepare",
    )(
        bias_table.reshape(2 * HEADS, 1, PAIR * TAB),
        region_ids.transpose(1, 0, 2),
        w_qkv,
        ln1_gain.reshape(1, C),
        ln2_gain.reshape(1, C),
        keep_flags,
    )
    positions = levels * lat_rows * lon_cols
    keep, send, *saved = pl.pallas_call(
        scores_kernel,
        out_shape=(
            jax.ShapeDtypeStruct((2, DENSE, LANES), bf16),
            jax.ShapeDtypeStruct((2, DENSE, LANES), bf16),
            jax.ShapeDtypeStruct((positions, C), bf16),
            jax.ShapeDtypeStruct((4, POS, ROWS), bf16),
            jax.ShapeDtypeStruct((4, POS, ROWS), bf16),
            jax.ShapeDtypeStruct((positions, C), bf16),
            jax.ShapeDtypeStruct((positions, C), bf16),
        ),
        in_specs=[vmem] * 13,
        out_specs=(vmem,) * 7,
        scratch_shapes=[
            pltpu.VMEM((2, positions, C), f32),
            pltpu.VMEM((HEADS, POS, POS), f32),
            pltpu.VMEM((DENSE, LANES), f32),
        ],
        compiler_params=params,
        name="scores",
    )(
        field_in,
        cotangent,
        lon_part,
        lat_part,
        diag_part,
        gains,
        weights_t,
        w_proj,
        w_up,
        w_down.T,
        bias_wide,
        label_row,
        label_col,
    )

    def rest_of_backward(saved):
        return pl.pallas_call(
            rest_kernel,
            out_shape=(jax.ShapeDtypeStruct((2, levels, half, inner, C), bf16),) + packed,
            in_specs=[vmem] * 8,
            out_specs=(vmem,) * 4,
            scratch_shapes=buffers,
            compiler_params=params,
            cost_estimate=pl.CostEstimate(
                flops=1_000_000_000, bytes_accessed=8_000_000, transcendentals=0
            ),
            name="rest",
        )(*saved, gains, weights_t, w_proj)

    halves, own, (lat_back, diag_back, lon_back) = lon_sum(keep, send, gains, saved, rest_of_backward)
    grads = pl.pallas_call(
        unpack_kernel,
        out_shape=jax.ShapeDtypeStruct((2 * HEADS, 1, PAIR * TAB), f32),
        in_specs=[vmem] * 2,
        out_specs=vmem,
        scratch_shapes=[pltpu.VMEM((2 * HEADS, PAIR * TAB), f32)],
        compiler_params=params,
        name="unpack",
    )(*halves)
    grads = grads.reshape(2, 1, HEADS, PAIR * TAB)
    result, grad_field = pl.pallas_call(
        finish_kernel,
        out_shape=(jax.ShapeDtypeStruct(field_in.shape, bf16),) * 2,
        in_specs=[vmem] * 4,
        out_specs=(vmem,) * 2,
        compiler_params=params,
        name="finish",
    )(own, lat_back, diag_back, lon_back)
    return (result, grad_field, grads)


def solution(mesh):
    placed = (
        P(None, "lat", "lon", None),
        P(None, "lat", "lon", None),
        P(),
        P(),
        P(),
        P(),
        P(),
        P(),
        P(None, "lat", None, None),
        P(None, "lat", "lon"),
        P(None, "lat", "lon"),
    )
    return jax.shard_map(
        body,
        mesh=mesh,
        in_specs=placed,
        out_specs=(
            P(None, "lat", "lon", None),
            P(None, "lat", "lon", None),
            P(None, "lat", None, None),
        ),
        check_vma=False,
    )
```

```python
import math

import jax
import jax.numpy as jnp
from jax import lax
from jax.experimental import pallas as pl
from jax.experimental.pallas import tpu as pltpu
from jax.sharding import PartitionSpec as P

C = 192
HEADS = 6
HD = 32
FF = 768
WZ = 2
WLAT = 6
WLON = 12
SPREAD = 2 * WLON - 1
POS = WZ * WLAT * WLON
PAIR = WZ * WLAT
TAB = PAIR * SPREAD
ROWS = HEADS * POS
SLOTS = 16
QUARTER = PAIR * HEADS // 2
REST = 20
LN_ROWS = 48
GELU_ROWS = 16
LANE_CUTS = [(k, min(k + 256, ROWS)) for k in range(0, ROWS, 256)]
DENSE = 80
LANES = 128

epsilon = 1e-05
keep_share = 0.8
LOG2E = math.log2(math.e)
gelu_coef = 0.044715
VMEM_BYTES = 16 * 1024 * 1024
bf16 = jnp.bfloat16
f32 = jnp.float32


def shifted(block, lat_step, lon_step):
    lats, lons = lax.axis_size("lat"), lax.axis_size("lon")
    route = []
    for a in range(lats):
        for b in range(lons):
            target = ((a + lat_step) % lats) * lons + (b + lon_step) % lons
            route.append((a * lons + b, target))
    return lax.ppermute(block, ("lat", "lon"), route)


def mm(a, b):
    return lax.dot_general(a, b, (((1,), (0,)), ((), ())), preferred_element_type=f32)


def mm_nt(a, b):
    return lax.dot_general(a, b, (((1,), (1,)), ((), ())), preferred_element_type=f32)


def norm_parts(values, gain):
    row_mean = jnp.mean(values, axis=-1, keepdims=True)
    centred = values - row_mean
    variance = jnp.mean(centred * centred, axis=-1, keepdims=True)
    inverse = lax.rsqrt(variance + epsilon)
    normed = centred * inverse
    return normed * gain, normed, inverse


def norm_back(grad_in, gain, normed, inverse):
    scaled = grad_in * gain
    first_mean = jnp.mean(scaled, axis=-1, keepdims=True)
    second_mean = jnp.mean(scaled * normed, axis=-1, keepdims=True)
    return (scaled - first_mean - normed * second_mean) * inverse


def gelu_parts(values):
    factor = math.sqrt(2.0 / math.pi)
    square = values * values
    tangent = jnp.tanh(values * (factor + (gelu_coef * factor) * square))
    half = 0.5 + 0.5 * tangent
    result = values * half
    derivative = half + result * (1.0 - tangent) * (factor + (3.0 * gelu_coef * factor) * square)
    return result.astype(bf16), derivative


def by_rows(function, size, *arrays):
    rows = arrays[0].shape[0]
    parts = [function(*(v[r : r + size] for v in arrays)) for r in range(0, rows, size)]
    return tuple(jnp.concatenate(part, axis=0) for part in zip(*parts))


def masked_softmax(scores, bias, allowed):
    scores = scores * (LOG2E / math.sqrt(HD)) + bias
    scores = jnp.where(allowed, scores, -1e30)
    weights = jnp.exp2(scores - jnp.max(scores, axis=0, keepdims=True))
    return weights * (1.0 / jnp.sum(weights, axis=0, keepdims=True))


def head_blocks(wide):
    return jnp.concatenate(
        [wide[h * HD : (h + 1) * HD, h * POS : (h + 1) * POS] for h in range(HEADS)], axis=0
    )


def spread_heads(rows, head_mask):
    return jnp.concatenate([rows * head_mask[h : h + 1, :] for h in range(HEADS)], axis=0)


def quotient(values, divisor):
    return (values * (2**20 // divisor + 1)) >> 20


def one_hot(rows, columns, target):
    row = lax.broadcasted_iota(jnp.int32, (rows, 1), 0)
    column = lax.broadcasted_iota(jnp.int32, (rows, columns), 1)
    return (column == target(row)).astype(f32).astype(bf16)


def window_order():
    def target(row):
        c = (row >= POS).astype(jnp.int32)
        row = row - POS * c
        j = quotient(row, PAIR)
        return (row - PAIR * j) * (2 * WLON) + c * WLON + j

    return one_hot(2 * POS, 2 * POS, target)


def natural_order():
    def target(row):
        pair = quotient(row, 2 * WLON)
        lon = row - 2 * WLON * pair
        c = (lon >= WLON).astype(jnp.int32)
        return c * POS + (lon - WLON * c) * PAIR + pair

    return one_hot(2 * POS, 2 * POS, target)


def table_order():
    def target(row):
        pair = quotient(row, SPREAD)
        return (SPREAD - 1 - (row - SPREAD * pair)) * PAIR + pair

    return one_hot(TAB, TAB, target)


def chunk_order():
    def target(row):
        pair = quotient(row, HEADS)
        return (row - HEADS * pair) * SLOTS + pair

    return one_hot(PAIR * HEADS, HEADS * SLOTS, target)


def row_order():
    def target(row):
        head = quotient(row, SLOTS)
        return (row - SLOTS * head) * SLOTS + head

    return one_hot(2 * HEADS * SLOTS, PAIR * SLOTS, target)


def put(packed, t, row, slab):
    third = packed.shape[0] // 3
    size = slab.shape[0]
    rest = C - LANES
    packed[t * third + row : t * third + row + size, :] = slab[:, :LANES]
    packed[2 * third + row : 2 * third + row + size, t * rest : (t + 1) * rest] = slab[:, LANES:]


def get(packed, t, row, size):
    third = packed.shape[0] // 3
    rest = C - LANES
    return (
        packed[t * third + row : t * third + row + size, :],
        packed[2 * third + row : 2 * third + row + size, t * rest : (t + 1) * rest],
    )


def pack_lat_kernel(field_ref, cot_ref, lat_out, lat_buf, rows, arrived):
    half = WLAT // 2
    edge = WLON // 2
    inner = 2 * WLON - edge
    sources = (field_ref, cot_ref)
    copies = [
        pltpu.make_async_copy(sources[t].at[:, pl.ds(0, half)], rows.at[t], arrived.at[t])
        for t in range(2)
    ]
    for copy in copies:
        copy.start()
    for t in range(2):
        copies[t].wait()
        for z in range(4):
            for i in range(half):
                put(lat_buf, t, (z * half + i) * inner, rows[t, z, i].astype(f32)[edge:])
    lat_out[...] = lat_buf[...].astype(bf16)


def pack_edge_kernel(field_ref, cot_ref, after_ref, diag_out, lon_out, diag_buf, lon_buf):
    half = WLAT // 2
    edge = WLON // 2
    for t, source in enumerate((field_ref, cot_ref)):
        for z in range(4):
            for i in range(half):
                row = (z * half + i) * edge
                put(diag_buf, t, row, source[z, i].astype(f32)[:edge])
                put(lon_buf, t, row, source[z, half + i].astype(f32)[:edge])
    diag_out[...] = diag_buf[...].astype(bf16)
    lon_out[...] = lon_buf[...].astype(bf16)


def scores_kernel(
    field_ref,
    cot_ref,
    lon_ref,
    lat_ref,
    diag_ref,
    gains_ref,
    wqkv_t_ref,
    wproj_ref,
    wup_ref,
    wdown_t_ref,
    bias_ref,
    label_row_ref,
    label_col_ref,
    keep_out,
    send_out,
    x_out,
    probs_out,
    grad_low_out,
    grad_sum_out,
    result_out,
    frame,
    wide,
    dense,
):
    half = WLAT // 2
    cols = 2 * WLON
    edge = WLON // 2
    inner = cols - edge
    root = 1.0 / math.sqrt(HD)
    lon_part = lon_ref[...].astype(f32)
    lat_part = lat_ref[...].astype(f32)
    diag_part = diag_ref[...].astype(f32)
    for t, own in enumerate((field_ref, cot_ref)):
        for level in range(4):
            z = (level + 1) % 4
            for i in range(half):
                k = z * half + i
                row = (level * WLAT + i) * cols
                frame[t, row : row + inner, :] = own[z, half + i].astype(f32)[edge:, :]
                main, rest = get(lon_part, t, k * edge, edge)
                frame[t, row + inner : row + cols, :LANES] = main
                frame[t, row + inner : row + cols, LANES:] = rest
                row = (level * WLAT + half + i) * cols
                main, rest = get(lat_part, t, k * inner, inner)
                frame[t, row : row + inner, :LANES] = main
                frame[t, row : row + inner, LANES:] = rest
                main, rest = get(diag_part, t, k * edge, edge)
                frame[t, row + inner : row + cols, :LANES] = main
                frame[t, row + inner : row + cols, LANES:] = rest
    gain1 = gains_ref[0:1, :]
    gain2 = gains_ref[1:2, :]
    wq_t = wqkv_t_ref[0:C, :]
    wk_t = wqkv_t_ref[C : 2 * C, :]
    wv_t = wqkv_t_ref[2 * C : 3 * C, :]
    head = lax.broadcasted_iota(jnp.int32, (HEADS, C), 0)
    head_mask = (lax.broadcasted_iota(jnp.int32, (HEADS, C), 1) >> 5) == head
    head_mask = head_mask.astype(f32).astype(bf16)
    perm = window_order()
    table_perm = table_order()
    chunk_perm = chunk_order()
    dense[...] = jnp.zeros_like(dense)
    odd = jnp.broadcast_to(gains_ref[6:7, :LANES], (DENSE, LANES)) > 0.5
    for n in range(2):
        both = slice(n * 2 * POS, (n + 1) * 2 * POS)
        x = mm(perm, frame[0, both, :].astype(bf16))
        cot = mm(perm, frame[1, both, :].astype(bf16))
        x_out[both, :] = x.astype(bf16)
        (scaled1,) = by_rows(lambda v: norm_parts(v, gain1)[:1], LN_ROWS, x)
        h1 = scaled1.astype(bf16)
        q_all = mm_nt(h1, wq_t).astype(bf16)
        k_all = mm_nt(h1, wk_t).astype(bf16)
        v_all = mm_nt(h1, wv_t).astype(bf16)
        saved = []
        branches = []
        for c in range(2):
            w = 2 * n + c
            rows = slice(c * POS, (c + 1) * POS)
            v_t = mm_nt(wv_t, h1[rows]).astype(bf16)
            q_wide = spread_heads(q_all[rows], head_mask)
            label_col = label_col_ref[:, w : w + 1]
            probs = []
            for low, high in LANE_CUTS:
                scores = mm_nt(k_all[rows], q_wide[low:high])
                for start in range(low, high, LANES):
                    stop = min(start + LANES, high)
                    allowed = label_col == label_row_ref[w : w + 1, start:stop]
                    part = scores[:, start - low : stop - low]
                    probs.append(masked_softmax(part, bias_ref[n, :, start:stop], allowed))
            probs_low = jnp.concatenate([part.astype(bf16) for part in probs], axis=1)
            probs_out[w] = probs_low
            attended = head_blocks(mm(v_t, probs_low)).astype(bf16).T
            factor = gains_ref[2 + w : 3 + w, :]
            branches.append((mm(attended, wproj_ref[...]) * factor).astype(bf16).astype(f32))
            saved.append(probs)
        y_sum = x + jnp.concatenate(branches, axis=0)
        scaled2, normed2, inverse2 = by_rows(lambda v: norm_parts(v, gain2), LN_ROWS, y_sum)
        act, slope = by_rows(gelu_parts, GELU_ROWS, mm(scaled2.astype(bf16), wup_ref[...]))
        result_out[both, :] = (y_sum + mm_nt(act, wdown_t_ref[...])).astype(bf16)
        grad_up = (mm(cot.astype(bf16), wdown_t_ref[...]) * slope).astype(bf16)
        grad_hidden = mm_nt(grad_up, wup_ref[...])
        (grad_sum,) = by_rows(
            lambda v, g, normed, inverse: (v + norm_back(g, gain2, normed, inverse),),
            LN_ROWS,
            cot,
            grad_hidden,
            normed2,
            inverse2,
        )
        grad_sum_low = grad_sum.astype(bf16)
        grad_sum_out[both, :] = grad_sum_low
        grad_low_in = grad_sum_low.astype(f32)
        folded = [None] * -(-ROWS // LANES)
        for c in range(2):
            rows = slice(c * POS, (c + 1) * POS)
            probs = saved[c]
            factor = gains_ref[2 + 2 * n + c : 3 + 2 * n + c, :]
            grad_branch = (grad_low_in[rows] * factor).astype(bf16)
            grad_att = mm_nt(grad_branch, wproj_ref[...]).astype(bf16)
            g_wide = spread_heads(grad_att, head_mask)
            grad_low = []
            for low, high in LANE_CUTS:
                products = mm_nt(v_all[rows], g_wide[low:high])
                for start in range(low, high, LANES):
                    k = start // LANES
                    grad_probs = products[:, start - low : min(start + LANES, high) - low]
                    inner_sum = jnp.sum(probs[k] * grad_probs, axis=0, keepdims=True)
                    grad_scores = probs[k] * (grad_probs - inner_sum)
                    folded[k] = grad_scores if c == 0 else folded[k] + grad_scores
                    grad_low.append(grad_scores.astype(bf16))
            grad_low_out[2 * n + c] = jnp.concatenate(grad_low, axis=1)
        folded = jnp.concatenate([part.astype(bf16) for part in folded], axis=1)
        wide[...] = folded.T.astype(f32).reshape(HEADS, POS, POS)
        total = None
        for o in range(WLON):
            left = PAIR * (WLON - 1 - o)
            right = TAB - POS - left
            parts = [wide[:, PAIR * o : PAIR * (o + 1), :]]
            if left:
                parts = [jnp.zeros((HEADS, PAIR, left), f32)] + parts
            if right:
                parts = parts + [jnp.zeros((HEADS, PAIR, right), f32)]
            piece = jnp.concatenate(parts, axis=2)
            total = piece if total is None else total + piece
        total = jnp.concatenate([total, jnp.zeros((HEADS, SLOTS - PAIR, TAB), f32)], axis=1)
        total = total.reshape(HEADS * SLOTS, TAB).astype(bf16)
        total = mm_nt(total, table_perm).astype(bf16)
        total = mm(chunk_perm, total)
        quarters = []
        for k in range(2):
            part = total[k * QUARTER : (k + 1) * QUARTER]
            dense[:QUARTER, :] = part[:, :LANES]
            dense[QUARTER : 2 * QUARTER, :] = part[:, LANES : 2 * LANES]
            rest = [part[HEADS * g : HEADS * (g + 1), 2 * LANES :] for g in range(WLAT)]
            dense[2 * QUARTER : 2 * QUARTER + HEADS, : WLAT * REST] = jnp.concatenate(rest, axis=1)
            quarters.append(dense[...])
        keep_out[n] = jnp.where(odd, quarters[1], quarters[0]).astype(bf16)
        send_out[n] = jnp.where(odd, quarters[0], quarters[1]).astype(bf16)


def rest_kernel(
    x_ref,
    probs_ref,
    grad_low_ref,
    grad_sum_ref,
    result_ref,
    gains_ref,
    wqkv_t_ref,
    wproj_ref,
    own_out,
    lat_out,
    diag_out,
    lon_out,
    lat_buf,
    diag_buf,
    lon_buf,
):
    half = WLAT // 2
    cols = 2 * WLON
    edge = WLON // 2
    inner = cols - edge
    root = 1.0 / math.sqrt(HD)
    gain1 = gains_ref[0:1, :]
    wq_t = wqkv_t_ref[0:C, :]
    wk_t = wqkv_t_ref[C : 2 * C, :]
    wv_t = wqkv_t_ref[2 * C : 3 * C, :]
    head = lax.broadcasted_iota(jnp.int32, (HEADS, C), 0)
    head_mask = (lax.broadcasted_iota(jnp.int32, (HEADS, C), 1) >> 5) == head
    head_mask = head_mask.astype(f32).astype(bf16)
    perm_t = natural_order()
    for n in range(2):
        both = slice(n * 2 * POS, (n + 1) * 2 * POS)
        x = x_ref[both, :].astype(f32)
        scaled1, normed1, inverse1 = by_rows(lambda v: norm_parts(v, gain1), LN_ROWS, x)
        h1 = scaled1.astype(bf16)
        q_all = mm_nt(h1, wq_t).astype(bf16)
        grad_sum = grad_sum_ref[both, :].astype(f32)
        grad_h1 = []
        for c in range(2):
            w = 2 * n + c
            rows = slice(c * POS, (c + 1) * POS)
            q_wide = spread_heads(q_all[rows], head_mask)
            grad_branch = (grad_sum[rows] * gains_ref[2 + w : 3 + w, :]).astype(bf16)
            grad_att = mm_nt(grad_branch, wproj_ref[...]).astype(bf16)
            g_wide = spread_heads(grad_att, head_mask)
            grad_low = grad_low_ref[w]
            k_t = mm_nt(wk_t, h1[rows]).astype(bf16)
            grad_q = (head_blocks(mm(k_t, grad_low)) * root).astype(bf16).T
            grad_k = (mm(grad_low, q_wide) * root).astype(bf16)
            grad_v = mm(probs_ref[w], g_wide).astype(bf16)
            grad_h1.append(mm(grad_q, wq_t) + mm(grad_k, wk_t) + mm(grad_v, wv_t))
        grad_h1 = jnp.concatenate(grad_h1, axis=0).astype(bf16).astype(f32)
        (grad_field,) = by_rows(
            lambda v, g, normed, inverse: (
                (v + norm_back(g, gain1, normed, inverse)).astype(bf16),
            ),
            LN_ROWS,
            grad_sum,
            grad_h1,
            normed1,
            inverse1,
        )
        for t, value in enumerate((result_ref[both, :], grad_field)):
            natural = mm(perm_t, value)
            for dz in range(WZ):
                z = (2 * n + dz + 1) % 4
                for i in range(half):
                    k = z * half + i
                    row = (dz * WLAT + i) * cols
                    slab = natural[row : row + cols]
                    own_out[t, z, i] = slab[:inner].astype(bf16)
                    put(lon_buf, t, k * edge, slab[inner:])
                    row = (dz * WLAT + half + i) * cols
                    slab = natural[row : row + cols]
                    put(lat_buf, t, k * inner, slab[:inner])
                    put(diag_buf, t, k * edge, slab[inner:])
    lat_out[...] = lat_buf[...].astype(bf16)
    diag_out[...] = diag_buf[...].astype(bf16)
    lon_out[...] = lon_buf[...].astype(bf16)


def prepare_kernel(
    table_ref,
    region_ref,
    wqkv_ref,
    gain1_ref,
    gain2_ref,
    keep_ref,
    bias_out,
    label_row_out,
    label_col_out,
    wqkv_t_out,
    gains_out,
    flat,
    rows,
    wide,
    marks,
):
    wqkv_t_out[...] = wqkv_ref[...].astype(f32).T.astype(bf16)
    gains_out[0:1, :] = gain1_ref[...]
    gains_out[1:2, :] = gain2_ref[...]
    for n in range(2):
        for c in range(2):
            factor = keep_ref[n, 0, c].astype(f32) * (1.0 / keep_share)
            row = 2 + 2 * n + c
            gains_out[row : row + 1, :] = jnp.full((1, C), factor, f32)
    lon_index = lax.axis_index("lon")
    for k in range(2):
        bit = ((lon_index >> k) & 1).astype(f32)
        gains_out[6 + k : 7 + k, :] = jnp.full((1, C), bit, f32)
    last = lax.axis_index("lat") == lax.axis_size("lat") - 1
    level = lax.broadcasted_iota(jnp.int32, (4, 2 * WLON), 0)
    for i in range(WLAT):
        wrapped = 2 * (level >= 4 - WZ // 2).astype(jnp.int32)
        if i >= WLAT // 2:
            wrapped = wrapped + last.astype(jnp.int32)
        marks[4 * i : 4 * (i + 1), :] = (4 * region_ref[i] + wrapped).astype(f32)
    place = lax.broadcasted_iota(jnp.int32, (POS, 4 * WLAT), 0)
    lane = lax.broadcasted_iota(jnp.int32, (POS, 4 * WLAT), 1)
    lon = quotient(place, PAIR)
    pair = place - PAIR * lon
    upper = (pair >= WLAT).astype(jnp.int32)
    source = 4 * (pair - WLAT * upper) + upper
    columns = []
    for n in range(2):
        chosen = mm((lane == source + WZ * n).astype(f32).astype(bf16), marks[...].astype(bf16))
        for c in range(2):
            own = jnp.where(lane == lon + WLON * c, chosen, 0.0)
            columns.append(jnp.sum(own, axis=1, keepdims=True))
    label_col_out[...] = jnp.concatenate(columns, axis=1)
    spread = jnp.concatenate([jnp.broadcast_to(v, (POS, LANES)) for v in columns], axis=1).T
    labels = jnp.concatenate([spread[k * LANES : k * LANES + 1] for k in range(4)], axis=0)
    label_row_out[...] = jnp.concatenate([labels] * HEADS, axis=1)
    part = PAIR // WZ * SPREAD
    for k in range(2 * HEADS):
        flat[k : k + 1, :] = table_ref[k]
    rows[...] = jnp.zeros_like(rows)
    for a in range(WZ):
        for c in range(WLAT):
            pieces = []
            for b in range(WZ):
                start = ((a * WZ + b) * WLAT + c) * part
                pieces.append(flat[:, start : start + part])
            row = (a * WLAT + c) * SLOTS
            rows[row : row + 2 * HEADS, :] = jnp.concatenate(pieces, axis=1)
    left = rows[...]
    perm = table_order()
    row_perm = row_order()
    total = None
    for _ in range(3):
        low = left.astype(bf16)
        left = left - low.astype(f32)
        term = mm(row_perm, mm(low, perm).astype(bf16))
        total = term if total is None else total + term
    total = total.reshape(2 * HEADS, SLOTS, TAB)
    for o in range(WLON):
        start = PAIR * (WLON - 1 - o)
        wide[:, PAIR * o : PAIR * (o + 1), :] = total[:, :PAIR, start : start + POS]
    for n in range(2):
        bias_out[n] = wide[n * HEADS : (n + 1) * HEADS].reshape(ROWS, POS).T * LOG2E


def unpack_kernel(mine_ref, other_ref, table_out, flat):
    odd = (lax.axis_index("lon") & 1) != 0
    part = PAIR // WZ * SPREAD
    for n in range(2):
        halves = []
        for k in range(2):
            mine = mine_ref[n].astype(f32)
            other = other_ref[n].astype(f32)
            dense = jnp.where(odd == (k == 1), mine, other)
            rest = dense[2 * QUARTER : 2 * QUARTER + HEADS]
            rest = [rest[:, g * REST : (g + 1) * REST] for g in range(WLAT)]
            rest = jnp.concatenate(rest, axis=0)
            parts = [dense[:QUARTER], dense[QUARTER : 2 * QUARTER], rest]
            halves.append(jnp.concatenate(parts, axis=1))
        for a in range(WZ):
            for c in range(WLAT):
                row = c * HEADS
                chunk = halves[a][row : row + HEADS]
                for b in range(WZ):
                    start = ((a * WZ + b) * WLAT + c) * part
                    flat[n * HEADS : (n + 1) * HEADS, start : start + part] = chunk[
                        :, b * part : (b + 1) * part
                    ]
    for k in range(2 * HEADS):
        table_out[k] = flat[k : k + 1, :]


def halve_kernel(mine_ref, other_ref, gains_ref, keep_out, send_out):
    upper = jnp.broadcast_to(gains_ref[7:8, :LANES], (DENSE, LANES)) > 0.5
    sums = [mine_ref[k].astype(f32) + other_ref[k].astype(f32) for k in range(2)]
    keep_out[0] = jnp.where(upper, sums[1], sums[0]).astype(bf16)
    send_out[0] = jnp.where(upper, sums[0], sums[1]).astype(bf16)


def add_kernel(*refs):
    copies_out = refs[-1]
    parts = [ref[k].astype(f32) for ref in refs[:-1] for k in range(ref.shape[0])]
    while len(parts) > 1:
        parts = [parts[k] + parts[k + 1] for k in range(0, len(parts), 2)]
    total = parts[0].astype(bf16)
    for k in range(copies_out.shape[0]):
        copies_out[k] = total


def finish_kernel(own_ref, lat_ref, diag_ref, lon_ref, out_ref, grad_ref):
    half = WLAT // 2
    edge = WLON // 2
    inner = 2 * WLON - edge
    lat_part = lat_ref[...].astype(f32)
    diag_part = diag_ref[...].astype(f32)
    lon_part = lon_ref[...].astype(f32)
    for t, target in enumerate((out_ref, grad_ref)):
        for z in range(4):
            for i in range(half):
                k = z * half + i
                parts = (get(diag_part, t, k * edge, edge), get(lat_part, t, k * inner, inner))
                slab = [jnp.concatenate([parts[0][j], parts[1][j]], axis=0) for j in range(2)]
                target[z, i] = jnp.concatenate(slab, axis=1).astype(bf16)
                slab = jnp.concatenate(get(lon_part, t, k * edge, edge), axis=1)
                own = own_ref[t, z, i].astype(f32)
                target[z, half + i] = jnp.concatenate([slab, own], axis=0).astype(bf16)


def lon_sum(keep, send, gains, saved, rest_of_backward):
    lons = lax.axis_size("lon")
    far = [[4 * k + j for k in range(lons // 4)] for j in range(4)]
    vmem = pl.BlockSpec(memory_space=pltpu.VMEM)

    def swapped(block, distance):
        return lax.ppermute(block, "lon", [(i, i ^ distance) for i in range(lons)])

    def added(parts, copies):
        return pl.pallas_call(
            add_kernel,
            out_shape=jax.ShapeDtypeStruct((copies,) + parts[0].shape[1:], bf16),
            in_specs=[vmem] * len(parts),
            out_specs=vmem,
            compiler_params=pltpu.CompilerParams(vmem_limit_bytes=VMEM_BYTES),
            name="add",
        )(*parts)

    other, saved = lax.optimization_barrier((swapped(send, 1), saved))
    quarter = jax.ShapeDtypeStruct((1,) + keep.shape[1:], bf16)
    keep, send = pl.pallas_call(
        halve_kernel,
        out_shape=(quarter,) * 2,
        in_specs=[vmem] * 3,
        out_specs=(vmem,) * 2,
        compiler_params=pltpu.CompilerParams(vmem_limit_bytes=VMEM_BYTES),
        name="halve",
    )(keep, other, gains)
    other = swapped(send, 2)
    own, *strips = rest_of_backward(saved)
    parts = added((keep, other), lons // 4)
    parts, strips = lax.optimization_barrier((parts, strips))
    steps = ((1, 0), (1, 1), (0, 1))
    strips = [shifted(strip, *step) for strip, step in zip(strips, steps)]
    parts = lax.all_to_all(parts, "lon", 0, 0, axis_index_groups=far)
    value, strips = lax.optimization_barrier((added((parts,), 1)[0], strips))
    other = swapped(value, 2)
    second = gains[7:8, :LANES] > 0.5
    lower = jnp.where(second, other, value)
    upper = jnp.where(second, value, other)
    value = jnp.stack([lower, upper])
    return (value, swapped(value, 1)), own, strips


def body(
    field_in,
    cotangent,
    ln1_gain,
    w_qkv,
    w_proj,
    ln2_gain,
    w_up,
    w_down,
    bias_table,
    region_ids,
    keep_flags,
):
    levels, lat_rows, lon_cols, channels = field_in.shape
    half = WLAT // 2
    edge = WLON // 2
    inner = lon_cols - edge
    vmem = pl.BlockSpec(memory_space=pltpu.VMEM)
    smem = pl.BlockSpec(memory_space=pltpu.SMEM)
    sizes = [3 * levels * half * size for size in (inner, edge, edge)]
    packed = tuple(jax.ShapeDtypeStruct((size, LANES), bf16) for size in sizes)
    buffers = [pltpu.VMEM((size, LANES), f32) for size in sizes]
    params = pltpu.CompilerParams(vmem_limit_bytes=VMEM_BYTES)
    lat_part = pl.pallas_call(
        pack_lat_kernel,
        out_shape=packed[0],
        in_specs=[pl.BlockSpec(memory_space=pltpu.HBM)] * 2,
        out_specs=vmem,
        scratch_shapes=buffers[:1]
        + [pltpu.VMEM((2, levels, half, lon_cols, C), bf16), pltpu.SemaphoreType.DMA((2,))],
        compiler_params=params,
        name="pack_lat",
    )(field_in, cotangent)
    diag_part, lon_part = pl.pallas_call(
        pack_edge_kernel,
        out_shape=packed[1:],
        in_specs=[vmem] * 2 + [pl.BlockSpec(memory_space=pl.ANY)],
        out_specs=(vmem,) * 2,
        scratch_shapes=buffers[1:],
        compiler_params=params,
        name="pack_edge",
    )(field_in, cotangent, lat_part)
    lat_part = shifted(lat_part, -1, 0)
    diag_part = shifted(diag_part, -1, -1)
    lon_part = shifted(lon_part, 0, -1)

    bias_wide, label_row, label_col, weights_t, gains = pl.pallas_call(
        prepare_kernel,
        out_shape=(
            jax.ShapeDtypeStruct((2, POS, ROWS), f32),
            jax.ShapeDtypeStruct((4, ROWS), f32),
            jax.ShapeDtypeStruct((POS, 4), f32),
            jax.ShapeDtypeStruct((3 * C, C), bf16),
            jax.ShapeDtypeStruct((8, C), f32),
        ),
        in_specs=[vmem] * 5 + [smem],
        out_specs=(vmem,) * 5,
        scratch_shapes=[
            pltpu.VMEM((2 * HEADS, PAIR * TAB), f32),
            pltpu.VMEM((PAIR * SLOTS, TAB), f32),
            pltpu.VMEM((2 * HEADS, POS, POS), f32),
            pltpu.VMEM((4 * WLAT, 2 * WLON), f32),
        ],
        compiler_params=params,
        name="prepare",
    )(
        bias_table.reshape(2 * HEADS, 1, PAIR * TAB),
        region_ids.transpose(1, 0, 2),
        w_qkv,
        ln1_gain.reshape(1, C),
        ln2_gain.reshape(1, C),
        keep_flags,
    )
    positions = levels * lat_rows * lon_cols
    keep, send, *saved = pl.pallas_call(
        scores_kernel,
        out_shape=(
            jax.ShapeDtypeStruct((2, DENSE, LANES), bf16),
            jax.ShapeDtypeStruct((2, DENSE, LANES), bf16),
            jax.ShapeDtypeStruct((positions, C), bf16),
            jax.ShapeDtypeStruct((4, POS, ROWS), bf16),
            jax.ShapeDtypeStruct((4, POS, ROWS), bf16),
            jax.ShapeDtypeStruct((positions, C), bf16),
            jax.ShapeDtypeStruct((positions, C), bf16),
        ),
        in_specs=[vmem] * 13,
        out_specs=(vmem,) * 7,
        scratch_shapes=[
            pltpu.VMEM((2, positions, C), f32),
            pltpu.VMEM((HEADS, POS, POS), f32),
            pltpu.VMEM((DENSE, LANES), f32),
        ],
        compiler_params=params,
        name="scores",
    )(
        field_in,
        cotangent,
        lon_part,
        lat_part,
        diag_part,
        gains,
        weights_t,
        w_proj,
        w_up,
        w_down.T,
        bias_wide,
        label_row,
        label_col,
    )

    def rest_of_backward(saved):
        return pl.pallas_call(
            rest_kernel,
            out_shape=(jax.ShapeDtypeStruct((2, levels, half, inner, C), bf16),) + packed,
            in_specs=[vmem] * 8,
            out_specs=(vmem,) * 4,
            scratch_shapes=buffers,
            compiler_params=params,
            cost_estimate=pl.CostEstimate(
                flops=1_000_000_000, bytes_accessed=8_000_000, transcendentals=0
            ),
            name="rest",
        )(*saved, gains, weights_t, w_proj)

    halves, own, (lat_back, diag_back, lon_back) = lon_sum(keep, send, gains, saved, rest_of_backward)
    grads = pl.pallas_call(
        unpack_kernel,
        out_shape=jax.ShapeDtypeStruct((2 * HEADS, 1, PAIR * TAB), f32),
        in_specs=[vmem] * 2,
        out_specs=vmem,
        scratch_shapes=[pltpu.VMEM((2 * HEADS, PAIR * TAB), f32)],
        compiler_params=params,
        name="unpack",
    )(*halves)
    grads = grads.reshape(2, 1, HEADS, PAIR * TAB)
    result, grad_field = pl.pallas_call(
        finish_kernel,
        out_shape=(jax.ShapeDtypeStruct(field_in.shape, bf16),) * 2,
        in_specs=[vmem] * 4,
        out_specs=(vmem,) * 2,
        compiler_params=params,
        name="finish",
    )(own, lat_back, diag_back, lon_back)
    return (result, grad_field, grads)


def solution(mesh):
    placed = (
        P(None, "lat", "lon", None),
        P(None, "lat", "lon", None),
        P(),
        P(),
        P(),
        P(),
        P(),
        P(),
        P(None, "lat", None, None),
        P(None, "lat", "lon"),
        P(None, "lat", "lon"),
    )
    return jax.shard_map(
        body,
        mesh=mesh,
        in_specs=placed,
        out_specs=(
            P(None, "lat", "lon", None),
            P(None, "lat", "lon", None),
            P(None, "lat", None, None),
        ),
        check_vma=False,
    )
```

```python
import math

import jax
import jax.numpy as jnp
from jax import lax
from jax.experimental import pallas as pl
from jax.experimental.pallas import tpu as pltpu
from jax.sharding import PartitionSpec as P

C = 192
HEADS = 6
HD = 32
FF = 768
WZ = 2
WLAT = 6
WLON = 12
SPREAD = 2 * WLON - 1
POS = WZ * WLAT * WLON
PAIR = WZ * WLAT
TAB = PAIR * SPREAD
ROWS = HEADS * POS
SLOTS = 16
QUARTER = PAIR * HEADS // 2
REST = 20
LN_ROWS = 96
GELU_ROWS = 48
LANE_CUTS = [(k, min(k + 256, ROWS)) for k in range(0, ROWS, 256)]
DENSE = 80
LANES = 128

epsilon = 1e-05
keep_share = 0.8
LOG2E = math.log2(math.e)
gelu_coef = 0.044715
VMEM_BYTES = 16 * 1024 * 1024
bf16 = jnp.bfloat16
f32 = jnp.float32


def shifted(block, lat_step, lon_step):
    lats, lons = lax.axis_size("lat"), lax.axis_size("lon")
    route = []
    for a in range(lats):
        for b in range(lons):
            target = ((a + lat_step) % lats) * lons + (b + lon_step) % lons
            route.append((a * lons + b, target))
    return lax.ppermute(block, ("lat", "lon"), route)


def mm(a, b):
    return lax.dot_general(a, b, (((1,), (0,)), ((), ())), preferred_element_type=f32)


def mm_nt(a, b):
    return lax.dot_general(a, b, (((1,), (1,)), ((), ())), preferred_element_type=f32)


def norm_parts(values, gain):
    row_mean = jnp.mean(values, axis=-1, keepdims=True)
    centred = values - row_mean
    variance = jnp.mean(centred * centred, axis=-1, keepdims=True)
    inverse = lax.rsqrt(variance + epsilon)
    normed = centred * inverse
    return normed * gain, normed, inverse


def norm_back(grad_in, gain, normed, inverse):
    scaled = grad_in * gain
    first_mean = jnp.mean(scaled, axis=-1, keepdims=True)
    second_mean = jnp.mean(scaled * normed, axis=-1, keepdims=True)
    return (scaled - first_mean - normed * second_mean) * inverse


def gelu_parts(values):
    factor = math.sqrt(2.0 / math.pi)
    square = values * values
    tangent = jnp.tanh(values * (factor + (gelu_coef * factor) * square))
    half = 0.5 + 0.5 * tangent
    result = values * half
    derivative = half + result * (1.0 - tangent) * (factor + (3.0 * gelu_coef * factor) * square)
    return result.astype(bf16), derivative


def by_rows(function, size, *arrays):
    rows = arrays[0].shape[0]
    parts = [function(*(v[r : r + size] for v in arrays)) for r in range(0, rows, size)]
    return tuple(jnp.concatenate(part, axis=0) for part in zip(*parts))


def masked_softmax(scores, bias, allowed):
    scores = scores * (LOG2E / math.sqrt(HD)) + bias
    scores = jnp.where(allowed, scores, -1e30)
    weights = jnp.exp2(scores - jnp.max(scores, axis=0, keepdims=True))
    return weights * (1.0 / jnp.sum(weights, axis=0, keepdims=True))


def head_blocks(wide):
    return jnp.concatenate(
        [wide[h * HD : (h + 1) * HD, h * POS : (h + 1) * POS] for h in range(HEADS)], axis=0
    )


def spread_heads(rows, head_mask):
    return jnp.concatenate([rows * head_mask[h : h + 1, :] for h in range(HEADS)], axis=0)


def quotient(values, divisor):
    return (values * (2**20 // divisor + 1)) >> 20


def one_hot(rows, columns, target):
    row = lax.broadcasted_iota(jnp.int32, (rows, 1), 0)
    column = lax.broadcasted_iota(jnp.int32, (rows, columns), 1)
    return (column == target(row)).astype(f32).astype(bf16)


def window_order():
    def target(row):
        c = (row >= POS).astype(jnp.int32)
        row = row - POS * c
        j = quotient(row, PAIR)
        return (row - PAIR * j) * (2 * WLON) + c * WLON + j

    return one_hot(2 * POS, 2 * POS, target)


def natural_order():
    def target(row):
        pair = quotient(row, 2 * WLON)
        lon = row - 2 * WLON * pair
        c = (lon >= WLON).astype(jnp.int32)
        return c * POS + (lon - WLON * c) * PAIR + pair

    return one_hot(2 * POS, 2 * POS, target)


def table_order():
    def target(row):
        pair = quotient(row, SPREAD)
        return (SPREAD - 1 - (row - SPREAD * pair)) * PAIR + pair

    return one_hot(TAB, TAB, target)


def chunk_order():
    def target(row):
        pair = quotient(row, HEADS)
        return (row - HEADS * pair) * SLOTS + pair

    return one_hot(PAIR * HEADS, HEADS * SLOTS, target)


def row_order():
    def target(row):
        head = quotient(row, SLOTS)
        return (row - SLOTS * head) * SLOTS + head

    return one_hot(2 * HEADS * SLOTS, PAIR * SLOTS, target)


def put(packed, t, row, slab):
    third = packed.shape[0] // 3
    size = slab.shape[0]
    rest = C - LANES
    packed[t * third + row : t * third + row + size, :] = slab[:, :LANES]
    packed[2 * third + row : 2 * third + row + size, t * rest : (t + 1) * rest] = slab[:, LANES:]


def get(packed, t, row, size):
    third = packed.shape[0] // 3
    rest = C - LANES
    return (
        packed[t * third + row : t * third + row + size, :],
        packed[2 * third + row : 2 * third + row + size, t * rest : (t + 1) * rest],
    )


def pack_lat_kernel(field_ref, cot_ref, lat_out, lat_buf, rows, arrived):
    half = WLAT // 2
    edge = WLON // 2
    inner = 2 * WLON - edge
    sources = (field_ref, cot_ref)
    copies = [
        pltpu.make_async_copy(sources[t].at[:, pl.ds(0, half)], rows.at[t], arrived.at[t])
        for t in range(2)
    ]
    for copy in copies:
        copy.start()
    for t in range(2):
        copies[t].wait()
        for z in range(4):
            for i in range(half):
                put(lat_buf, t, (z * half + i) * inner, rows[t, z, i].astype(f32)[edge:])
    lat_out[...] = lat_buf[...].astype(bf16)


def pack_edge_kernel(field_ref, cot_ref, after_ref, diag_out, lon_out, diag_buf, lon_buf):
    half = WLAT // 2
    edge = WLON // 2
    for t, source in enumerate((field_ref, cot_ref)):
        for z in range(4):
            for i in range(half):
                row = (z * half + i) * edge
                put(diag_buf, t, row, source[z, i].astype(f32)[:edge])
                put(lon_buf, t, row, source[z, half + i].astype(f32)[:edge])
    diag_out[...] = diag_buf[...].astype(bf16)
    lon_out[...] = lon_buf[...].astype(bf16)


def scores_kernel(
    field_ref,
    cot_ref,
    lon_ref,
    lat_ref,
    diag_ref,
    gains_ref,
    wqkv_t_ref,
    wproj_ref,
    wup_ref,
    wdown_t_ref,
    bias_ref,
    label_row_ref,
    label_col_ref,
    keep_out,
    send_out,
    x_out,
    probs_out,
    grad_low_out,
    grad_sum_out,
    result_out,
    frame,
    wide,
    dense,
):
    half = WLAT // 2
    cols = 2 * WLON
    edge = WLON // 2
    inner = cols - edge
    root = 1.0 / math.sqrt(HD)
    lon_part = lon_ref[...].astype(f32)
    lat_part = lat_ref[...].astype(f32)
    diag_part = diag_ref[...].astype(f32)
    for t, own in enumerate((field_ref, cot_ref)):
        for level in range(4):
            z = (level + 1) % 4
            for i in range(half):
                k = z * half + i
                row = (level * WLAT + i) * cols
                frame[t, row : row + inner, :] = own[z, half + i].astype(f32)[edge:, :]
                main, rest = get(lon_part, t, k * edge, edge)
                frame[t, row + inner : row + cols, :LANES] = main
                frame[t, row + inner : row + cols, LANES:] = rest
                row = (level * WLAT + half + i) * cols
                main, rest = get(lat_part, t, k * inner, inner)
                frame[t, row : row + inner, :LANES] = main
                frame[t, row : row + inner, LANES:] = rest
                main, rest = get(diag_part, t, k * edge, edge)
                frame[t, row + inner : row + cols, :LANES] = main
                frame[t, row + inner : row + cols, LANES:] = rest
    gain1 = gains_ref[0:1, :]
    gain2 = gains_ref[1:2, :]
    wq_t = wqkv_t_ref[0:C, :]
    wk_t = wqkv_t_ref[C : 2 * C, :]
    wv_t = wqkv_t_ref[2 * C : 3 * C, :]
    head = lax.broadcasted_iota(jnp.int32, (HEADS, C), 0)
    head_mask = (lax.broadcasted_iota(jnp.int32, (HEADS, C), 1) >> 5) == head
    head_mask = head_mask.astype(f32).astype(bf16)
    perm = window_order()
    table_perm = table_order()
    chunk_perm = chunk_order()
    dense[...] = jnp.zeros_like(dense)
    odd = jnp.broadcast_to(gains_ref[6:7, :LANES], (DENSE, LANES)) > 0.5
    for n in range(2):
        both = slice(n * 2 * POS, (n + 1) * 2 * POS)
        x = mm(perm, frame[0, both, :].astype(bf16))
        cot = mm(perm, frame[1, both, :].astype(bf16))
        x_out[both, :] = x.astype(bf16)
        (scaled1,) = by_rows(lambda v: norm_parts(v, gain1)[:1], LN_ROWS, x)
        h1 = scaled1.astype(bf16)
        q_all = mm_nt(h1, wq_t).astype(bf16)
        k_all = mm_nt(h1, wk_t).astype(bf16)
        v_all = mm_nt(h1, wv_t).astype(bf16)
        saved = []
        branches = []
        for c in range(2):
            w = 2 * n + c
            rows = slice(c * POS, (c + 1) * POS)
            v_t = mm_nt(wv_t, h1[rows]).astype(bf16)
            q_wide = spread_heads(q_all[rows], head_mask)
            label_col = label_col_ref[:, w : w + 1]
            probs = []
            for low, high in LANE_CUTS:
                scores = mm_nt(k_all[rows], q_wide[low:high])
                allowed = label_col == label_row_ref[w : w + 1, low:high]
                probs.append(masked_softmax(scores, bias_ref[n, :, low:high], allowed))
            probs_low = jnp.concatenate([part.astype(bf16) for part in probs], axis=1)
            probs_out[w] = probs_low
            attended = head_blocks(mm(v_t, probs_low)).astype(bf16).T
            factor = gains_ref[2 + w : 3 + w, :]
            branches.append((mm(attended, wproj_ref[...]) * factor).astype(bf16).astype(f32))
            saved.append(probs)
        y_sum = x + jnp.concatenate(branches, axis=0)
        scaled2, normed2, inverse2 = by_rows(lambda v: norm_parts(v, gain2), LN_ROWS, y_sum)
        act, slope = by_rows(gelu_parts, GELU_ROWS, mm(scaled2.astype(bf16), wup_ref[...]))
        result_out[both, :] = (y_sum + mm_nt(act, wdown_t_ref[...])).astype(bf16)
        grad_up = (mm(cot.astype(bf16), wdown_t_ref[...]) * slope).astype(bf16)
        grad_hidden = mm_nt(grad_up, wup_ref[...])
        (grad_sum,) = by_rows(
            lambda v, g, normed, inverse: (v + norm_back(g, gain2, normed, inverse),),
            LN_ROWS,
            cot,
            grad_hidden,
            normed2,
            inverse2,
        )
        grad_sum_low = grad_sum.astype(bf16)
        grad_sum_out[both, :] = grad_sum_low
        grad_low_in = grad_sum_low.astype(f32)
        folded = [None] * len(LANE_CUTS)
        for c in range(2):
            rows = slice(c * POS, (c + 1) * POS)
            probs = saved[c]
            factor = gains_ref[2 + 2 * n + c : 3 + 2 * n + c, :]
            grad_branch = (grad_low_in[rows] * factor).astype(bf16)
            grad_att = mm_nt(grad_branch, wproj_ref[...]).astype(bf16)
            g_wide = spread_heads(grad_att, head_mask)
            grad_low = []
            for k, (low, high) in enumerate(LANE_CUTS):
                grad_probs = mm_nt(v_all[rows], g_wide[low:high])
                inner_sum = jnp.sum(probs[k] * grad_probs, axis=0, keepdims=True)
                grad_scores = probs[k] * (grad_probs - inner_sum)
                folded[k] = grad_scores if c == 0 else folded[k] + grad_scores
                grad_low.append(grad_scores.astype(bf16))
            grad_low_out[2 * n + c] = jnp.concatenate(grad_low, axis=1)
        folded = jnp.concatenate([part.astype(bf16) for part in folded], axis=1)
        wide[...] = folded.T.astype(f32).reshape(HEADS, POS, POS)
        total = None
        for o in range(WLON):
            left = PAIR * (WLON - 1 - o)
            right = TAB - POS - left
            parts = [wide[:, PAIR * o : PAIR * (o + 1), :]]
            if left:
                parts = [jnp.zeros((HEADS, PAIR, left), f32)] + parts
            if right:
                parts = parts + [jnp.zeros((HEADS, PAIR, right), f32)]
            piece = jnp.concatenate(parts, axis=2)
            total = piece if total is None else total + piece
        total = jnp.concatenate([total, jnp.zeros((HEADS, SLOTS - PAIR, TAB), f32)], axis=1)
        total = total.reshape(HEADS * SLOTS, TAB).astype(bf16)
        total = mm_nt(total, table_perm).astype(bf16)
        total = mm(chunk_perm, total)
        quarters = []
        for k in range(2):
            part = total[k * QUARTER : (k + 1) * QUARTER]
            dense[:QUARTER, :] = part[:, :LANES]
            dense[QUARTER : 2 * QUARTER, :] = part[:, LANES : 2 * LANES]
            rest = [part[HEADS * g : HEADS * (g + 1), 2 * LANES :] for g in range(WLAT)]
            dense[2 * QUARTER : 2 * QUARTER + HEADS, : WLAT * REST] = jnp.concatenate(rest, axis=1)
            quarters.append(dense[...])
        keep_out[n] = jnp.where(odd, quarters[1], quarters[0]).astype(bf16)
        send_out[n] = jnp.where(odd, quarters[0], quarters[1]).astype(bf16)


def rest_kernel(
    x_ref,
    probs_ref,
    grad_low_ref,
    grad_sum_ref,
    result_ref,
    gains_ref,
    wqkv_t_ref,
    wproj_ref,
    own_out,
    lat_out,
    diag_out,
    lon_out,
    lat_buf,
    diag_buf,
    lon_buf,
):
    half = WLAT // 2
    cols = 2 * WLON
    edge = WLON // 2
    inner = cols - edge
    root = 1.0 / math.sqrt(HD)
    gain1 = gains_ref[0:1, :]
    wq_t = wqkv_t_ref[0:C, :]
    wk_t = wqkv_t_ref[C : 2 * C, :]
    wv_t = wqkv_t_ref[2 * C : 3 * C, :]
    head = lax.broadcasted_iota(jnp.int32, (HEADS, C), 0)
    head_mask = (lax.broadcasted_iota(jnp.int32, (HEADS, C), 1) >> 5) == head
    head_mask = head_mask.astype(f32).astype(bf16)
    perm_t = natural_order()
    for n in range(2):
        both = slice(n * 2 * POS, (n + 1) * 2 * POS)
        x = x_ref[both, :].astype(f32)
        scaled1, normed1, inverse1 = by_rows(lambda v: norm_parts(v, gain1), LN_ROWS, x)
        h1 = scaled1.astype(bf16)
        q_all = mm_nt(h1, wq_t).astype(bf16)
        grad_sum = grad_sum_ref[both, :].astype(f32)
        grad_h1 = []
        for c in range(2):
            w = 2 * n + c
            rows = slice(c * POS, (c + 1) * POS)
            q_wide = spread_heads(q_all[rows], head_mask)
            grad_branch = (grad_sum[rows] * gains_ref[2 + w : 3 + w, :]).astype(bf16)
            grad_att = mm_nt(grad_branch, wproj_ref[...]).astype(bf16)
            g_wide = spread_heads(grad_att, head_mask)
            grad_low = grad_low_ref[w]
            k_t = mm_nt(wk_t, h1[rows]).astype(bf16)
            grad_q = (head_blocks(mm(k_t, grad_low)) * root).astype(bf16).T
            grad_k = (mm(grad_low, q_wide) * root).astype(bf16)
            grad_v = mm(probs_ref[w], g_wide).astype(bf16)
            grad_h1.append(mm(grad_q, wq_t) + mm(grad_k, wk_t) + mm(grad_v, wv_t))
        grad_h1 = jnp.concatenate(grad_h1, axis=0).astype(bf16).astype(f32)
        (grad_field,) = by_rows(
            lambda v, g, normed, inverse: (
                (v + norm_back(g, gain1, normed, inverse)).astype(bf16),
            ),
            LN_ROWS,
            grad_sum,
            grad_h1,
            normed1,
            inverse1,
        )
        for t, value in enumerate((result_ref[both, :], grad_field)):
            natural = mm(perm_t, value)
            for dz in range(WZ):
                z = (2 * n + dz + 1) % 4
                for i in range(half):
                    k = z * half + i
                    row = (dz * WLAT + i) * cols
                    slab = natural[row : row + cols]
                    own_out[t, z, i] = slab[:inner].astype(bf16)
                    put(lon_buf, t, k * edge, slab[inner:])
                    row = (dz * WLAT + half + i) * cols
                    slab = natural[row : row + cols]
                    put(lat_buf, t, k * inner, slab[:inner])
                    put(diag_buf, t, k * edge, slab[inner:])
    lat_out[...] = lat_buf[...].astype(bf16)
    diag_out[...] = diag_buf[...].astype(bf16)
    lon_out[...] = lon_buf[...].astype(bf16)


def prepare_kernel(
    table_ref,
    region_ref,
    wqkv_ref,
    gain1_ref,
    gain2_ref,
    keep_ref,
    bias_out,
    label_row_out,
    label_col_out,
    wqkv_t_out,
    gains_out,
    flat,
    rows,
    wide,
    marks,
):
    wqkv_t_out[...] = wqkv_ref[...].astype(f32).T.astype(bf16)
    gains_out[0:1, :] = gain1_ref[...]
    gains_out[1:2, :] = gain2_ref[...]
    for n in range(2):
        for c in range(2):
            factor = keep_ref[n, 0, c].astype(f32) * (1.0 / keep_share)
            row = 2 + 2 * n + c
            gains_out[row : row + 1, :] = jnp.full((1, C), factor, f32)
    lon_index = lax.axis_index("lon")
    for k in range(2):
        bit = ((lon_index >> k) & 1).astype(f32)
        gains_out[6 + k : 7 + k, :] = jnp.full((1, C), bit, f32)
    last = lax.axis_index("lat") == lax.axis_size("lat") - 1
    level = lax.broadcasted_iota(jnp.int32, (4, 2 * WLON), 0)
    for i in range(WLAT):
        wrapped = 2 * (level >= 4 - WZ // 2).astype(jnp.int32)
        if i >= WLAT // 2:
            wrapped = wrapped + last.astype(jnp.int32)
        marks[4 * i : 4 * (i + 1), :] = (4 * region_ref[i] + wrapped).astype(f32)
    place = lax.broadcasted_iota(jnp.int32, (POS, 4 * WLAT), 0)
    lane = lax.broadcasted_iota(jnp.int32, (POS, 4 * WLAT), 1)
    lon = quotient(place, PAIR)
    pair = place - PAIR * lon
    upper = (pair >= WLAT).astype(jnp.int32)
    source = 4 * (pair - WLAT * upper) + upper
    columns = []
    for n in range(2):
        chosen = mm((lane == source + WZ * n).astype(f32).astype(bf16), marks[...].astype(bf16))
        for c in range(2):
            own = jnp.where(lane == lon + WLON * c, chosen, 0.0)
            columns.append(jnp.sum(own, axis=1, keepdims=True))
    label_col_out[...] = jnp.concatenate(columns, axis=1)
    spread = jnp.concatenate([jnp.broadcast_to(v, (POS, LANES)) for v in columns], axis=1).T
    labels = jnp.concatenate([spread[k * LANES : k * LANES + 1] for k in range(4)], axis=0)
    label_row_out[...] = jnp.concatenate([labels] * HEADS, axis=1)
    part = PAIR // WZ * SPREAD
    for k in range(2 * HEADS):
        flat[k : k + 1, :] = table_ref[k]
    rows[...] = jnp.zeros_like(rows)
    for a in range(WZ):
        for c in range(WLAT):
            pieces = []
            for b in range(WZ):
                start = ((a * WZ + b) * WLAT + c) * part
                pieces.append(flat[:, start : start + part])
            row = (a * WLAT + c) * SLOTS
            rows[row : row + 2 * HEADS, :] = jnp.concatenate(pieces, axis=1)
    left = rows[...]
    perm = table_order()
    row_perm = row_order()
    total = None
    for _ in range(3):
        low = left.astype(bf16)
        left = left - low.astype(f32)
        term = mm(row_perm, mm(low, perm).astype(bf16))
        total = term if total is None else total + term
    total = total.reshape(2 * HEADS, SLOTS, TAB)
    for o in range(WLON):
        start = PAIR * (WLON - 1 - o)
        wide[:, PAIR * o : PAIR * (o + 1), :] = total[:, :PAIR, start : start + POS]
    for n in range(2):
        bias_out[n] = wide[n * HEADS : (n + 1) * HEADS].reshape(ROWS, POS).T * LOG2E


def unpack_kernel(mine_ref, other_ref, table_out, flat):
    odd = (lax.axis_index("lon") & 1) != 0
    part = PAIR // WZ * SPREAD
    for n in range(2):
        halves = []
        for k in range(2):
            mine = mine_ref[n].astype(f32)
            other = other_ref[n].astype(f32)
            dense = jnp.where(odd == (k == 1), mine, other)
            rest = dense[2 * QUARTER : 2 * QUARTER + HEADS]
            rest = [rest[:, g * REST : (g + 1) * REST] for g in range(WLAT)]
            rest = jnp.concatenate(rest, axis=0)
            parts = [dense[:QUARTER], dense[QUARTER : 2 * QUARTER], rest]
            halves.append(jnp.concatenate(parts, axis=1))
        for a in range(WZ):
            for c in range(WLAT):
                row = c * HEADS
                chunk = halves[a][row : row + HEADS]
                for b in range(WZ):
                    start = ((a * WZ + b) * WLAT + c) * part
                    flat[n * HEADS : (n + 1) * HEADS, start : start + part] = chunk[
                        :, b * part : (b + 1) * part
                    ]
    for k in range(2 * HEADS):
        table_out[k] = flat[k : k + 1, :]


def halve_kernel(mine_ref, other_ref, gains_ref, keep_out, send_out):
    upper = jnp.broadcast_to(gains_ref[7:8, :LANES], (DENSE, LANES)) > 0.5
    sums = [mine_ref[k].astype(f32) + other_ref[k].astype(f32) for k in range(2)]
    keep_out[0] = jnp.where(upper, sums[1], sums[0]).astype(bf16)
    send_out[0] = jnp.where(upper, sums[0], sums[1]).astype(bf16)


def add_kernel(*refs):
    copies_out = refs[-1]
    parts = [ref[k].astype(f32) for ref in refs[:-1] for k in range(ref.shape[0])]
    while len(parts) > 1:
        parts = [parts[k] + parts[k + 1] for k in range(0, len(parts), 2)]
    total = parts[0].astype(bf16)
    for k in range(copies_out.shape[0]):
        copies_out[k] = total


def finish_kernel(own_ref, lat_ref, diag_ref, lon_ref, out_ref, grad_ref):
    half = WLAT // 2
    edge = WLON // 2
    inner = 2 * WLON - edge
    lat_part = lat_ref[...].astype(f32)
    diag_part = diag_ref[...].astype(f32)
    lon_part = lon_ref[...].astype(f32)
    for t, target in enumerate((out_ref, grad_ref)):
        for z in range(4):
            for i in range(half):
                k = z * half + i
                parts = (get(diag_part, t, k * edge, edge), get(lat_part, t, k * inner, inner))
                slab = [jnp.concatenate([parts[0][j], parts[1][j]], axis=0) for j in range(2)]
                target[z, i] = jnp.concatenate(slab, axis=1).astype(bf16)
                slab = jnp.concatenate(get(lon_part, t, k * edge, edge), axis=1)
                own = own_ref[t, z, i].astype(f32)
                target[z, half + i] = jnp.concatenate([slab, own], axis=0).astype(bf16)


def lon_sum(keep, send, gains, saved, rest_of_backward):
    lons = lax.axis_size("lon")
    far = [[4 * k + j for k in range(lons // 4)] for j in range(4)]
    vmem = pl.BlockSpec(memory_space=pltpu.VMEM)

    def swapped(block, distance):
        return lax.ppermute(block, "lon", [(i, i ^ distance) for i in range(lons)])

    def added(parts, copies):
        return pl.pallas_call(
            add_kernel,
            out_shape=jax.ShapeDtypeStruct((copies,) + parts[0].shape[1:], bf16),
            in_specs=[vmem] * len(parts),
            out_specs=vmem,
            compiler_params=pltpu.CompilerParams(vmem_limit_bytes=VMEM_BYTES),
            name="add",
        )(*parts)

    other, saved = lax.optimization_barrier((swapped(send, 1), saved))
    quarter = jax.ShapeDtypeStruct((1,) + keep.shape[1:], bf16)
    keep, send = pl.pallas_call(
        halve_kernel,
        out_shape=(quarter,) * 2,
        in_specs=[vmem] * 3,
        out_specs=(vmem,) * 2,
        compiler_params=pltpu.CompilerParams(vmem_limit_bytes=VMEM_BYTES),
        name="halve",
    )(keep, other, gains)
    other = swapped(send, 2)
    own, *strips = rest_of_backward(saved)
    parts = added((keep, other), lons // 4)
    steps = ((1, 0), (1, 1), (0, 1))
    strips = [shifted(strip, *step) for strip, step in zip(strips, steps)]
    parts = lax.all_to_all(parts, "lon", 0, 0, axis_index_groups=far)
    value, strips = lax.optimization_barrier((added((parts,), 1)[0], strips))
    other = swapped(value, 2)
    second = gains[7:8, :LANES] > 0.5
    lower = jnp.where(second, other, value)
    upper = jnp.where(second, value, other)
    value = jnp.stack([lower, upper])
    return (value, swapped(value, 1)), own, strips


def body(
    field_in,
    cotangent,
    ln1_gain,
    w_qkv,
    w_proj,
    ln2_gain,
    w_up,
    w_down,
    bias_table,
    region_ids,
    keep_flags,
):
    levels, lat_rows, lon_cols, channels = field_in.shape
    half = WLAT // 2
    edge = WLON // 2
    inner = lon_cols - edge
    vmem = pl.BlockSpec(memory_space=pltpu.VMEM)
    smem = pl.BlockSpec(memory_space=pltpu.SMEM)
    sizes = [3 * levels * half * size for size in (inner, edge, edge)]
    packed = tuple(jax.ShapeDtypeStruct((size, LANES), bf16) for size in sizes)
    buffers = [pltpu.VMEM((size, LANES), f32) for size in sizes]
    params = pltpu.CompilerParams(vmem_limit_bytes=VMEM_BYTES)
    lat_part = pl.pallas_call(
        pack_lat_kernel,
        out_shape=packed[0],
        in_specs=[pl.BlockSpec(memory_space=pltpu.HBM)] * 2,
        out_specs=vmem,
        scratch_shapes=buffers[:1]
        + [pltpu.VMEM((2, levels, half, lon_cols, C), bf16), pltpu.SemaphoreType.DMA((2,))],
        compiler_params=params,
        name="pack_lat",
    )(field_in, cotangent)
    diag_part, lon_part = pl.pallas_call(
        pack_edge_kernel,
        out_shape=packed[1:],
        in_specs=[vmem] * 2 + [pl.BlockSpec(memory_space=pl.ANY)],
        out_specs=(vmem,) * 2,
        scratch_shapes=buffers[1:],
        compiler_params=params,
        name="pack_edge",
    )(field_in, cotangent, lat_part)
    lat_part = shifted(lat_part, -1, 0)
    diag_part = shifted(diag_part, -1, -1)
    lon_part = shifted(lon_part, 0, -1)

    bias_wide, label_row, label_col, weights_t, gains = pl.pallas_call(
        prepare_kernel,
        out_shape=(
            jax.ShapeDtypeStruct((2, POS, ROWS), f32),
            jax.ShapeDtypeStruct((4, ROWS), f32),
            jax.ShapeDtypeStruct((POS, 4), f32),
            jax.ShapeDtypeStruct((3 * C, C), bf16),
            jax.ShapeDtypeStruct((8, C), f32),
        ),
        in_specs=[vmem] * 5 + [smem],
        out_specs=(vmem,) * 5,
        scratch_shapes=[
            pltpu.VMEM((2 * HEADS, PAIR * TAB), f32),
            pltpu.VMEM((PAIR * SLOTS, TAB), f32),
            pltpu.VMEM((2 * HEADS, POS, POS), f32),
            pltpu.VMEM((4 * WLAT, 2 * WLON), f32),
        ],
        compiler_params=params,
        name="prepare",
    )(
        bias_table.reshape(2 * HEADS, 1, PAIR * TAB),
        region_ids.transpose(1, 0, 2),
        w_qkv,
        ln1_gain.reshape(1, C),
        ln2_gain.reshape(1, C),
        keep_flags,
    )
    positions = levels * lat_rows * lon_cols
    keep, send, *saved = pl.pallas_call(
        scores_kernel,
        out_shape=(
            jax.ShapeDtypeStruct((2, DENSE, LANES), bf16),
            jax.ShapeDtypeStruct((2, DENSE, LANES), bf16),
            jax.ShapeDtypeStruct((positions, C), bf16),
            jax.ShapeDtypeStruct((4, POS, ROWS), bf16),
            jax.ShapeDtypeStruct((4, POS, ROWS), bf16),
            jax.ShapeDtypeStruct((positions, C), bf16),
            jax.ShapeDtypeStruct((positions, C), bf16),
        ),
        in_specs=[vmem] * 13,
        out_specs=(vmem,) * 7,
        scratch_shapes=[
            pltpu.VMEM((2, positions, C), f32),
            pltpu.VMEM((HEADS, POS, POS), f32),
            pltpu.VMEM((DENSE, LANES), f32),
        ],
        compiler_params=params,
        name="scores",
    )(
        field_in,
        cotangent,
        lon_part,
        lat_part,
        diag_part,
        gains,
        weights_t,
        w_proj,
        w_up,
        w_down.T,
        bias_wide,
        label_row,
        label_col,
    )

    def rest_of_backward(saved):
        return pl.pallas_call(
            rest_kernel,
            out_shape=(jax.ShapeDtypeStruct((2, levels, half, inner, C), bf16),) + packed,
            in_specs=[vmem] * 8,
            out_specs=(vmem,) * 4,
            scratch_shapes=buffers,
            compiler_params=params,
            cost_estimate=pl.CostEstimate(
                flops=1_000_000_000, bytes_accessed=8_000_000, transcendentals=0
            ),
            name="rest",
        )(*saved, gains, weights_t, w_proj)

    halves, own, (lat_back, diag_back, lon_back) = lon_sum(keep, send, gains, saved, rest_of_backward)
    grads = pl.pallas_call(
        unpack_kernel,
        out_shape=jax.ShapeDtypeStruct((2 * HEADS, 1, PAIR * TAB), f32),
        in_specs=[vmem] * 2,
        out_specs=vmem,
        scratch_shapes=[pltpu.VMEM((2 * HEADS, PAIR * TAB), f32)],
        compiler_params=params,
        name="unpack",
    )(*halves)
    grads = grads.reshape(2, 1, HEADS, PAIR * TAB)
    result, grad_field = pl.pallas_call(
        finish_kernel,
        out_shape=(jax.ShapeDtypeStruct(field_in.shape, bf16),) * 2,
        in_specs=[vmem] * 4,
        out_specs=(vmem,) * 2,
        compiler_params=params,
        name="finish",
    )(own, lat_back, diag_back, lon_back)
    return (result, grad_field, grads)


def solution(mesh):
    placed = (
        P(None, "lat", "lon", None),
        P(None, "lat", "lon", None),
        P(),
        P(),
        P(),
        P(),
        P(),
        P(),
        P(None, "lat", None, None),
        P(None, "lat", "lon"),
        P(None, "lat", "lon"),
    )
    return jax.shard_map(
        body,
        mesh=mesh,
        in_specs=placed,
        out_specs=(
            P(None, "lat", "lon", None),
            P(None, "lat", "lon", None),
            P(None, "lat", None, None),
        ),
        check_vma=False,
    )
```
